32 devices in a mesh: win: 2 (over x), row: 16 (over z, y, core).
Axes of the slice: x: 2, y: 2, z: 4, core: 2. Of those that a mesh axis runs over, the one named last changes fastest.
Arguments:
- mask_field: float32 [2, 4096, 128], P(None, ('win', 'row')), parts along dimension 1, may hold values from -6 to 6
- target: int32 [4096, 128], P(('win', 'row')), parts along dimension 0, may hold values 0 or 1
- kernel_taps: float32 [24, 2, 128, 128], replicated, may hold values from -0.046875 to 0.046875
- kernel_radii: int32 [24], replicated, may hold values from 16 to 64, as said below
- kernel_group: int32 [24], replicated, may hold values from 0 to 2, as said below
- kernel_weight: float32 [24], replicated, may hold values from 0.1 to 1
Outputs:
- resist: float32 [3, 4096, 128], P(None, ('win', 'row')), parts along dimension 1
- gradient: float32 [2, 4096, 128], P(None, ('win', 'row')), parts along dimension 1
The draws below stay inside these ranges and needn't reach their ends.
There are 2 independent parts, one for each index of `win`. The reference program is written for one: setup_inputs(seed, part) draws one part's arguments, and reference() takes and returns one part's arrays. A program takes and returns all parts, laid end to end along the dimension named above; an argument that names none is the same for every part. Nothing has to cross between parts.
Inputs may be any that keep to these rules, and one draw needn't show every extreme that they name: `kernel_radii`: every radius lies in 16 to 64; some kernel has radius exactly 64 and some exactly 16. `kernel_group`: every one of the 3 process conditions holds at least one kernel.
All inputs are finite; a program needn't handle non-finite values. No bound on the sum of `target` on one device may be relied on, other than what follows from the above.
Results may differ from the reference program's by a relative error of at most 0.0003.
Values sent between devices are 32-bit elements; how exact they have to be, the bound alone decides.
No kernel may reach another device: no remote copies, remote signals or barrier semaphores. Data moves between devices by JAX's collectives and lax.ppermute only.
A program may use at most 128 MiB of HBM per device.

```python
import math
import jax
import jax.numpy as jnp
from jax import lax

COLS = 128
RMAX = 64
RMIN = 16
KERNELS = 24
GROUPS = 3
ROWS = 2048


def draw_kernel_radii(key, part):
    key = jax.random.fold_in(key, 11)
    first_key, second_key = jax.random.split(key)
    values = jax.random.randint(first_key, (KERNELS,), RMIN, RMAX + 1)
    order = jax.random.permutation(second_key, KERNELS)
    values = values.at[order[0]].set(RMAX)
    values = values.at[order[1]].set(RMIN)
    return values.astype(jnp.int32)


def draw_kernel_group(key, part):
    key = jax.random.fold_in(key, 23)
    first_key, second_key = jax.random.split(key)
    values = jax.random.randint(first_key, (KERNELS,), 0, GROUPS)
    order = jax.random.permutation(second_key, KERNELS)
    values = values.at[order[:GROUPS]].set(jnp.arange(GROUPS, dtype=jnp.int32))
    return values.astype(jnp.int32)


def with_ends(result, rng, smallest, top_value):
    longest = result.shape.index(max(result.shape))
    spots = []
    for shift in (0, 1):
        where = [jax.random.randint(jax.random.fold_in(rng, axis), (), 0, length) for axis, length in enumerate(result.shape)]
        where[longest] = (where[longest] + shift) % result.shape[longest]
        spots.append(tuple(where))
    return result.at[spots[0]].set(smallest).at[spots[1]].set(top_value)


def levels(rng, extent, shards, least, high):
    level, own = 1.0, jax.random.fold_in(rng, 6)
    for axis_at, shards_of in shards:
        steps = jnp.exp(jax.random.uniform(jax.random.fold_in(own, axis_at), (shards_of,), jnp.float32, least / len(shards), high / len(shards)))
        level = level * jnp.repeat(steps, extent[axis_at] // shards_of).reshape([-1 if axis == axis_at else 1 for axis in range(len(extent))])
    return level


def normal_values(key, shape, spread, bound, pieces=(), held_as=jnp.bfloat16):
    loudness = levels(key, shape, pieces, -0.22, 0.18) if pieces else 1.0
    drawn = jax.random.normal(key, shape, jnp.float32) * spread * loudness
    return jnp.minimum(jnp.maximum(drawn, -bound), bound).astype(held_as)


def setup_inputs(seed: int = 0, part: int = 0) -> dict:
    key_of = jax.random.split(jax.random.key(seed), 7)
    part_splits = jax.random.split(jax.random.fold_in(key_of[6], part), 7)
    mask_field = normal_values(part_splits[0], (2, ROWS, COLS), 1.0, 6.0, ((1, 16),), jnp.float32)
    target = with_ends((jax.random.randint(part_splits[1], (ROWS, COLS), 0, 2) < 1).astype(jnp.int32), jax.random.fold_in(part_splits[1], 1), 0, 1)
    kernel_taps = normal_values(key_of[2], (KERNELS, 2, 2 * RMAX, 2 * RMAX), (4 * RMAX * RMAX) ** -0.5, 0.046875, (), jnp.float32)
    kernel_radii = draw_kernel_radii(jax.random.fold_in(key_of[6], 71), part)
    kernel_group = draw_kernel_group(jax.random.fold_in(key_of[6], 71), part)
    kernel_weight = jnp.clip(jnp.exp(jax.random.uniform(key_of[5], (KERNELS,), jnp.float32, math.log(0.1), math.log(1.0))), 0.1, 1.0)
    return {"mask_field": mask_field, "target": target, "kernel_taps": kernel_taps, "kernel_radii": kernel_radii, "kernel_group": kernel_group, "kernel_weight": kernel_weight}


steepness = 1.0
threshold = 2.0

def kernel_spectrum(tap_real, tap_imag, radius, grid_rows, grid_cols):
    offsets = jnp.arange(2 * RMAX, dtype=jnp.int32) - RMAX
    inside = ((offsets >= -radius) & (offsets < radius)).astype(jnp.float32)
    kept_taps = inside[:, None] * inside[None, :]
    complex_taps = lax.complex(tap_real * kept_taps, tap_imag * kept_taps)
    placed = jnp.pad(complex_taps, ((0, grid_rows - 2 * RMAX), (0, grid_cols - 2 * RMAX)))
    placed = jnp.roll(placed, (-RMAX, -RMAX), axis=(0, 1))
    return jnp.fft.fft2(placed)

def convolve(mask_real, mask_imag, spectrum):
    total_rows = mask_real.shape[0]
    total_cols = mask_real.shape[1]
    grid = jnp.pad(lax.complex(mask_real, mask_imag), ((0, 2 * RMAX), (0, 2 * RMAX)))
    result_field = jnp.fft.ifft2(jnp.fft.fft2(grid) * spectrum)[:total_rows, :total_cols]
    return (jnp.real(result_field), jnp.imag(result_field))

def reference(mask_field, target, kernel_taps, kernel_radii, kernel_group, kernel_weight):
    total_rows = mask_field.shape[1]
    total_cols = mask_field.shape[2]
    grid_rows = total_rows + 2 * RMAX
    grid_cols = total_cols + 2 * RMAX
    onehot = (kernel_group[:, None] == jnp.arange(GROUPS, dtype=jnp.int32)[None, :]).astype(jnp.float32)
    mixing = kernel_weight[:, None] * onehot
    indices = jnp.arange(KERNELS, dtype=jnp.int32)

    def spectrum_of(index):
        return kernel_spectrum(kernel_taps[index, 0], kernel_taps[index, 1], kernel_radii[index], grid_rows, grid_cols)

    def forward_step(carry, index):
        field_real, field_imag = convolve(mask_field[0], mask_field[1], spectrum_of(index))
        power = field_real * field_real + field_imag * field_imag
        return (carry + mixing[index][:, None, None] * power[None], None)
    intensity, _ = lax.scan(forward_step, jnp.zeros((GROUPS, total_rows, total_cols), jnp.float32), indices)
    resist = jax.nn.sigmoid(steepness * (intensity - threshold))
    slopes = 2.0 * (resist - target.astype(jnp.float32)[None]) * resist * (1.0 - resist) * steepness

    def adjoint_step(carry, index):
        spectrum = spectrum_of(index)

        def linear(first_part, second_part):
            return convolve(first_part, second_part, spectrum)
        (field_real, field_imag), pullback = jax.vjp(linear, mask_field[0], mask_field[1])
        factor = 2.0 * lax.optimization_barrier(jnp.sum(mixing[index][:, None, None] * slopes, axis=0))
        grad_real, grad_imag = pullback((factor * field_real, factor * field_imag))
        return (carry + jnp.stack([grad_real, grad_imag]), None)
    gradient, _ = lax.scan(adjoint_step, jnp.zeros((2, total_rows, total_cols), jnp.float32), indices)
    return (resist, gradient)
```

```python
import math

import jax
import jax.numpy as jnp
import ml_dtypes
import numpy as np
from jax import lax
from jax.experimental import pallas as pl
from jax.experimental.pallas import tpu as pltpu
from jax.sharding import PartitionSpec as P

RMAX = 64
GROUPS = 3
STEEPNESS = 1.0
THRESHOLD = 2.0

f32 = jnp.float32
bf16 = jnp.bfloat16


def halves(table):
    high = table.astype(ml_dtypes.bfloat16)
    low = (table - high.astype(np.float64)).astype(ml_dtypes.bfloat16)
    return np.concatenate([high, low], axis=1)


def analysis(freqs, points, shift):
    f = np.arange(freqs)[:, None]
    n = np.arange(points)[None, :] - shift
    angle = 2.0 * math.pi * ((f * n) % freqs) / freqs
    cos, sin = np.cos(angle), np.sin(angle)
    return np.block([[cos, sin], [-sin, cos]])


def synthesis(freqs, points, shift, scale=1.0):
    return analysis(freqs, points, shift).T * scale


def split(x):
    high = x.astype(bf16)
    low = (x - high.astype(f32)).astype(bf16)
    return high, low


def apply_rows(table, high, low):
    depth = high.shape[0]
    left = table[...]
    left = jnp.concatenate([left, left[:, :depth]], axis=1)
    right = jnp.concatenate([high, high, low], axis=0)
    return lax.dot_general(left, right, (((1,), (0,)), ((), ())), preferred_element_type=f32)


def apply_lanes(table, high, low):
    depth = high.shape[1]
    left = table[...]
    left = jnp.concatenate([left, left[:, :depth]], axis=1)
    right = jnp.concatenate([high, high, low], axis=1)
    return lax.dot_general(left, right, (((1,), (1,)), ((), ())), preferred_element_type=f32)


def side(x, rows):
    return jnp.concatenate([x[:rows], x[rows:]], axis=1)


def body(
    radii, group, weight,
    own, above, below, target, taps,
    row_tab, col_tab, col_inv, row_inv, mask_row, mask_col, grad_col, grad_row,
    resist, grad_own, grad_up, grad_down,
    spec, field, mask_spec, slopes, grad_spec,
):
    kernels, _, span, _ = taps.shape
    count, width = target.shape
    grid_rows = row_tab.shape[0] // 2
    grid_cols = col_tab.shape[0] // 2
    rim = above.shape[1]

    mask = jnp.concatenate([above[0], own[0], below[0], above[1], own[1], below[1]], axis=0)
    half = apply_rows(mask_row, *split(mask))
    mask_spec[...] = apply_lanes(mask_col, *split(side(half, grid_rows)))

    slopes[...] = jnp.zeros(slopes.shape, f32)
    grad_spec[...] = jnp.zeros(grad_spec.shape, f32)

    def spectra(pair):
        half = apply_rows(row_tab, *split(pair))
        out = []
        for j in range(2):
            mine = side(half[:, j * width:(j + 1) * width], grid_rows)
            out.append(apply_lanes(col_tab, *split(mine)))
        return out

    row_at = lax.broadcasted_iota(jnp.int32, (2 * span, span), 0) % span - span // 2
    col_at = lax.broadcasted_iota(jnp.int32, (2 * span, span), 1) - span // 2

    def forward(i, carry):
        planes = []
        for j in range(2):
            k = 2 * i + j
            r = radii[k]
            inside = (row_at >= -r) & (row_at < r) & (col_at >= -r) & (col_at < r)
            planes.append(jnp.where(inside, taps[k].reshape(2 * span, span), 0.0))
        found = spectra(jnp.concatenate(planes, axis=1))
        backs = []
        for j in range(2):
            spec[2 * i + j] = found[j]
            s_re, s_im = found[j][:grid_cols], found[j][grid_cols:]
            m_re, m_im = mask_spec[:grid_cols], mask_spec[grid_cols:]
            product = jnp.concatenate([s_re * m_re - s_im * m_im, s_re * m_im + s_im * m_re], axis=0)
            back = apply_rows(col_inv, *split(product))
            backs.append(side(back, width))
        pair = apply_lanes(row_inv, *split(jnp.concatenate(backs, axis=0)))
        field[i] = pair
        power = pair[:count] * pair[:count] + pair[count:] * pair[count:]
        for j in range(2):
            k = 2 * i + j
            g = group[k]
            slopes[g] = slopes[g] + weight[k] * power[:, j * width:(j + 1) * width]
        return carry

    lax.fori_loop(0, kernels // 2, forward, 0)

    wanted = target[...].astype(f32)
    for g in range(GROUPS):
        seen = jax.nn.sigmoid(STEEPNESS * (slopes[g] - THRESHOLD))
        resist[g] = seen
        slopes[g] = 2.0 * (seen - wanted) * seen * (1.0 - seen) * STEEPNESS

    def backward(i, carry):
        factors = []
        for j in range(2):
            k = 2 * i + j
            factors.append((2.0 * weight[k]) * slopes[group[k]])
        factor = jnp.concatenate(factors, axis=1)
        cot = field[i] * jnp.concatenate([factor, factor], axis=0)
        found = spectra(cot)
        total_re = grad_spec[:grid_cols]
        total_im = grad_spec[grid_cols:]
        for j in range(2):
            s_re, s_im = spec[2 * i + j, :grid_cols], spec[2 * i + j, grid_cols:]
            c_re, c_im = found[j][:grid_cols], found[j][grid_cols:]
            total_re = total_re + (s_re * c_re + s_im * c_im)
            total_im = total_im + (s_re * c_im - s_im * c_re)
        grad_spec[:grid_cols] = total_re
        grad_spec[grid_cols:] = total_im
        return carry

    lax.fori_loop(0, kernels // 2, backward, 0)

    back = apply_rows(grad_col, *split(grad_spec[...]))
    full = apply_lanes(grad_row, *split(side(back, width)))
    for c in range(2):
        base = c * grid_rows
        grad_up[c] = full[base:base + rim]
        grad_own[c] = full[base + rim:base + rim + count]
        grad_down[c] = full[base + rim + count:base + grid_rows]


def on_device(mask_field, target, kernel_taps, kernel_radii, kernel_group, kernel_weight):
    _, count, width = mask_field.shape
    kernels, _, span, _ = kernel_taps.shape
    rim = span // 2
    grid_rows = count + 2 * rim
    grid_cols = width + rim
    assert count == span and width == span and kernels % 2 == 0

    strips = lax.axis_size("row")
    down = [(i, i + 1) for i in range(strips - 1)]
    up = [(i + 1, i) for i in range(strips - 1)]
    above = lax.ppermute(mask_field[:, count - rim:], "row", down)
    below = lax.ppermute(mask_field[:, :rim], "row", up)

    scale = 1.0 / (grid_rows * grid_cols)
    tables = [
        analysis(grid_rows, span, 0),
        analysis(grid_cols, span, 0),
        synthesis(grid_cols, width, 0),
        synthesis(grid_rows, count, 0, scale),
        analysis(grid_rows, grid_rows, 2 * rim),
        analysis(grid_cols, width, rim),
        synthesis(grid_cols, width, rim),
        synthesis(grid_rows, grid_rows, 2 * rim, scale),
    ]
    tables = [jnp.asarray(halves(t)) for t in tables]

    smem = pl.BlockSpec(memory_space=pltpu.SMEM)
    vmem = pl.BlockSpec(memory_space=pltpu.VMEM)
    resist, own, up_rim, down_rim = pl.pallas_call(
        body,
        out_shape=[
            jax.ShapeDtypeStruct((GROUPS, count, width), f32),
            jax.ShapeDtypeStruct((2, count, width), f32),
            jax.ShapeDtypeStruct((2, rim, width), f32),
            jax.ShapeDtypeStruct((2, rim, width), f32),
        ],
        in_specs=[smem] * 3 + [vmem] * 13,
        out_specs=[vmem] * 4,
        scratch_shapes=[
            pltpu.VMEM((kernels, 2 * grid_cols, grid_rows), f32),
            pltpu.VMEM((kernels // 2, 2 * count, 2 * width), f32),
            pltpu.VMEM((2 * grid_cols, grid_rows), f32),
            pltpu.VMEM((GROUPS, count, width), f32),
            pltpu.VMEM((2 * grid_cols, grid_rows), f32),
        ],
        compiler_params=pltpu.CompilerParams(vmem_limit_bytes=56 * 1024 * 1024),
        name="socs",
    )(kernel_radii, kernel_group, kernel_weight, mask_field, above, below, target, kernel_taps, *tables)

    from_below = lax.ppermute(up_rim, "row", up)
    from_above = lax.ppermute(down_rim, "row", down)
    gradient = jnp.concatenate([own[:, :rim] + from_above, own[:, rim:] + from_below], axis=1)
    return resist, gradient


def solution(mesh):
    in_specs = (P(None, ("win", "row"), None), P(("win", "row"), None), P(), P(), P(), P())
    out_specs = (P(None, ("win", "row"), None), P(None, ("win", "row"), None))
    return jax.shard_map(
        on_device, mesh=mesh, in_specs=in_specs, out_specs=out_specs, check_vma=False
    )
```

```python
import math

import jax
import jax.numpy as jnp
import ml_dtypes
import numpy as np
from jax import lax
from jax.experimental import pallas as pl
from jax.experimental.pallas import tpu as pltpu
from jax.sharding import PartitionSpec as P

RMAX = 64
GROUPS = 3
STEEPNESS = 1.0
THRESHOLD = 2.0
BATCH = 4

f32 = jnp.float32
bf16 = jnp.bfloat16


def halves(table):
    high = table.astype(ml_dtypes.bfloat16)
    low = (table - high.astype(np.float64)).astype(ml_dtypes.bfloat16)
    return np.concatenate([high, low], axis=1)


def analysis(freqs, points, shift):
    f = np.arange(freqs)[:, None]
    n = np.arange(points)[None, :] - shift
    angle = 2.0 * math.pi * ((f * n) % freqs) / freqs
    cos, sin = np.cos(angle), np.sin(angle)
    return np.block([[cos, sin], [-sin, cos]])


def synthesis(freqs, points, shift, scale=1.0):
    return analysis(freqs, points, shift).T * scale


def split(x):
    high = x.astype(bf16)
    low = (x - high.astype(f32)).astype(bf16)
    return high, low


def apply_rows(table, high, low):
    depth = high.shape[0]
    left = table[...]
    left = jnp.concatenate([left, left[:, :depth]], axis=1)
    right = jnp.concatenate([high, high, low], axis=0)
    return lax.dot_general(left, right, (((1,), (0,)), ((), ())), preferred_element_type=f32)


def apply_lanes(table, high, low):
    depth = high.shape[1]
    left = table[...]
    left = jnp.concatenate([left, left[:, :depth]], axis=1)
    right = jnp.concatenate([high, high, low], axis=1)
    return lax.dot_general(left, right, (((1,), (1,)), ((), ())), preferred_element_type=f32)


def side(x, rows):
    return jnp.concatenate([x[:rows], x[rows:]], axis=1)


def dft_pair(pair, row_tab, col_tab):
    width = pair.shape[1] // 2
    grid_rows = row_tab.shape[0] // 2
    half = apply_rows(row_tab, *split(pair))
    out = []
    for j in range(2):
        mine = side(half[:, j * width:(j + 1) * width], grid_rows)
        out.append(apply_lanes(col_tab, *split(mine)))
    return out


def spectra_body(radii, taps, row_tab, col_tab, spec):
    batch, _, span, _ = taps.shape
    first = pl.program_id(0) * batch
    row_at = lax.broadcasted_iota(jnp.int32, (span, span), 0) - span // 2
    col_at = lax.broadcasted_iota(jnp.int32, (span, span), 1) - span // 2
    reach = jnp.maximum(jnp.maximum(row_at, -1 - row_at), jnp.maximum(col_at, -1 - col_at))
    for i in range(batch // 2):
        planes = []
        for j in range(2):
            k = 2 * i + j
            inside = reach < radii[first + k]
            parts = [jnp.where(inside, taps[k, c], 0.0) for c in range(2)]
            planes.append(jnp.concatenate(parts, axis=0))
        found = dft_pair(jnp.concatenate(planes, axis=1), row_tab, col_tab)
        for j in range(2):
            spec[2 * i + j] = found[j]


def main_body(
    group, weight,
    own, above, below, target, spec_far,
    row_tab, col_tab, col_inv, row_inv, mask_row, mask_col, grad_col, grad_row,
    resist, grad_own, grad_up, grad_down,
    spec, field, mask_spec, slopes, grad_spec, sems,
):
    kernels = spec.shape[0]
    count, width = target.shape
    grid_rows = row_tab.shape[0] // 2
    grid_cols = col_tab.shape[0] // 2
    rim = (grid_rows - count) // 2
    steps = sems.shape[0]
    batch = kernels // steps

    def fetch(i):
        here = pl.ds(i * batch, batch)
        return pltpu.make_async_copy(spec_far.at[here], spec.at[here], sems.at[i])

    for i in range(steps):
        fetch(i).start()

    mask = jnp.concatenate(
        [part for c in range(2) for part in (above[c, count - rim:], own[c], below[c, :rim])], axis=0
    )
    half = apply_rows(mask_row, *split(mask))
    mask_spec[...] = apply_lanes(mask_col, *split(side(half, grid_rows)))

    slopes[...] = jnp.zeros(slopes.shape, f32)
    grad_spec[...] = jnp.zeros(grad_spec.shape, f32)

    def forward(i, carry):
        fetch(i).wait()
        powers = []
        for p in range(batch // 2):
            backs = []
            for j in range(2):
                k = i * batch + 2 * p + j
                s_re, s_im = spec[k, :grid_cols], spec[k, grid_cols:]
                m_re, m_im = mask_spec[:grid_cols], mask_spec[grid_cols:]
                product = jnp.concatenate([s_re * m_re - s_im * m_im, s_re * m_im + s_im * m_re], axis=0)
                back = apply_rows(col_inv, *split(product))
                backs.append(side(back, width))
            pair = apply_lanes(row_inv, *split(jnp.concatenate(backs, axis=0)))
            field[i * (batch // 2) + p] = pair
            powers.append(pair[:count] * pair[:count] + pair[count:] * pair[count:])
        for p in range(batch // 2):
            for j in range(2):
                k = i * batch + 2 * p + j
                g = group[k]
                slopes[g] = slopes[g] + weight[k] * powers[p][:, j * width:(j + 1) * width]
        return carry

    lax.fori_loop(0, steps, forward, 0)

    wanted = target[...].astype(f32)
    for g in range(GROUPS):
        seen = jax.nn.sigmoid(STEEPNESS * (slopes[g] - THRESHOLD))
        resist[g] = seen
        slopes[g] = 2.0 * (seen - wanted) * seen * (1.0 - seen) * STEEPNESS

    def backward(i, carry):
        total_re = grad_spec[:grid_cols]
        total_im = grad_spec[grid_cols:]
        for p in range(batch // 2):
            factors = []
            for j in range(2):
                k = i * batch + 2 * p + j
                factors.append((2.0 * weight[k]) * slopes[group[k]])
            factor = jnp.concatenate(factors, axis=1)
            cot = field[i * (batch // 2) + p] * jnp.concatenate([factor, factor], axis=0)
            found = dft_pair(cot, row_tab, col_tab)
            for j in range(2):
                k = i * batch + 2 * p + j
                s_re, s_im = spec[k, :grid_cols], spec[k, grid_cols:]
                c_re, c_im = found[j][:grid_cols], found[j][grid_cols:]
                total_re = total_re + (s_re * c_re + s_im * c_im)
                total_im = total_im + (s_re * c_im - s_im * c_re)
        grad_spec[:grid_cols] = total_re
        grad_spec[grid_cols:] = total_im
        return carry

    lax.fori_loop(0, steps, backward, 0)

    back = apply_rows(grad_col, *split(grad_spec[...]))
    full = apply_lanes(grad_row, *split(side(back, width)))
    for c in range(2):
        base = c * grid_rows
        grad_up[c] = full[base:base + rim]
        grad_own[c] = full[base + rim:base + rim + count]
        grad_down[c] = full[base + rim + count:base + grid_rows]


def on_device(mask_field, target, kernel_taps, kernel_radii, kernel_group, kernel_weight):
    _, count, width = mask_field.shape
    kernels, _, span, _ = kernel_taps.shape
    rim = span // 2
    grid_rows = count + 2 * rim
    grid_cols = width + rim
    assert count == span and width == span and kernels % 2 == 0

    assert kernels % BATCH == 0 and BATCH % 2 == 0

    strips = lax.axis_size("row")
    down = [(i, i + 1) for i in range(strips - 1)]
    up = [(i + 1, i) for i in range(strips - 1)]
    above = lax.ppermute(mask_field, "row", down)
    below = lax.ppermute(mask_field, "row", up)

    scale = 1.0 / (grid_rows * grid_cols)
    tables = [
        analysis(grid_rows, span, 0),
        analysis(grid_cols, span, 0),
        synthesis(grid_cols, width, 0),
        synthesis(grid_rows, count, 0, scale),
        analysis(grid_rows, grid_rows, 2 * rim),
        analysis(grid_cols, width, rim),
        synthesis(grid_cols, width, rim),
        synthesis(grid_rows, grid_rows, 2 * rim, scale),
    ]
    tables = [jnp.asarray(halves(t)) for t in tables]

    smem = pl.BlockSpec(memory_space=pltpu.SMEM)
    vmem = pl.BlockSpec(memory_space=pltpu.VMEM)
    spectra = pl.pallas_call(
        spectra_body,
        grid=(kernels // BATCH,),
        out_shape=jax.ShapeDtypeStruct((kernels, 2 * grid_cols, grid_rows), f32),
        in_specs=[smem, pl.BlockSpec((BATCH, 2, span, span), lambda i: (i, 0, 0, 0)), vmem, vmem],
        out_specs=pl.BlockSpec((BATCH, 2 * grid_cols, grid_rows), lambda i: (i, 0, 0)),
        compiler_params=pltpu.CompilerParams(vmem_limit_bytes=24 * 1024 * 1024),
        cost_estimate=pl.CostEstimate(flops=18 * 10**9, bytes_accessed=14 * 10**6, transcendentals=0),
        name="spectra",
    )(kernel_radii, kernel_taps, tables[0], tables[1])

    resist, own, up_rim, down_rim = pl.pallas_call(
        main_body,
        out_shape=[
            jax.ShapeDtypeStruct((GROUPS, count, width), f32),
            jax.ShapeDtypeStruct((2, count, width), f32),
            jax.ShapeDtypeStruct((2, rim, width), f32),
            jax.ShapeDtypeStruct((2, rim, width), f32),
        ],
        in_specs=[smem] * 2 + [vmem] * 4 + [pl.BlockSpec(memory_space=pl.ANY)] + [vmem] * 8,
        out_specs=[vmem] * 4,
        scratch_shapes=[
            pltpu.VMEM((kernels, 2 * grid_cols, grid_rows), f32),
            pltpu.VMEM((kernels // 2, 2 * count, 2 * width), f32),
            pltpu.VMEM((2 * grid_cols, grid_rows), f32),
            pltpu.VMEM((GROUPS, count, width), f32),
            pltpu.VMEM((2 * grid_cols, grid_rows), f32),
            pltpu.SemaphoreType.DMA((kernels // BATCH,)),
        ],
        compiler_params=pltpu.CompilerParams(vmem_limit_bytes=56 * 1024 * 1024),
        name="fields",
    )(kernel_group, kernel_weight, mask_field, above, below, target, spectra, *tables)

    from_below = lax.ppermute(up_rim, "row", up)
    from_above = lax.ppermute(down_rim, "row", down)
    gradient = (
        own
        + jnp.pad(from_above, ((0, 0), (0, count - rim), (0, 0)))
        + jnp.pad(from_below, ((0, 0), (count - rim, 0), (0, 0)))
    )
    return resist, gradient


def solution(mesh):
    in_specs = (P(None, ("win", "row"), None), P(("win", "row"), None), P(), P(), P(), P())
    out_specs = (P(None, ("win", "row"), None), P(None, ("win", "row"), None))
    return jax.shard_map(
        on_device, mesh=mesh, in_specs=in_specs, out_specs=out_specs, check_vma=False
    )
```

```python
import math

import jax
import jax.numpy as jnp
import ml_dtypes
import numpy as np
from jax import lax
from jax.experimental import pallas as pl
from jax.experimental.pallas import tpu as pltpu
from jax.sharding import PartitionSpec as P

RMAX = 64
GROUPS = 3
STEEPNESS = 1.0
THRESHOLD = 2.0
BATCH = 4

f32 = jnp.float32
bf16 = jnp.bfloat16
MIB = 1024 * 1024


def halves(table, axis):
    high = table.astype(ml_dtypes.bfloat16)
    low = (table - high.astype(np.float64)).astype(ml_dtypes.bfloat16)
    return np.concatenate([high, low], axis=axis)


def analysis(freqs, points, shift):
    f = np.arange(freqs)[:, None]
    n = np.arange(points)[None, :] - shift
    angle = 2.0 * math.pi * ((f * n) % freqs) / freqs
    cos, sin = np.cos(angle), np.sin(angle)
    return np.block([[cos, sin], [-sin, cos]])


def synthesis(freqs, points, shift, scale=1.0):
    return analysis(freqs, points, shift).T * scale


def grouped(freqs, lanes):
    head, tail = np.arange(lanes), np.arange(lanes, freqs)
    return np.concatenate([head, freqs + head, tail, freqs + tail])


def split(x):
    high = x.astype(bf16)
    low = (x - high.astype(f32)).astype(bf16)
    return high, low


def dot(left, right):
    return jnp.dot(left, right, preferred_element_type=f32)


def over_rows(table, x):
    high, low = split(x)
    left = table[...]
    left = jnp.concatenate([left, left[:, :x.shape[0]]], axis=1)
    return dot(left, jnp.concatenate([high, high, low], axis=0))


def over_lanes(x, table):
    high, low = split(x)
    right = table[...]
    right = jnp.concatenate([right, right[:x.shape[1]]], axis=0)
    return dot(jnp.concatenate([high, high, low], axis=1), right)


def to_freqs(x, head, tail):
    high, low = split(x)
    depth = x.shape[1]
    right = head[...]
    right = jnp.concatenate([right, right[:depth]], axis=0)
    first = dot(jnp.concatenate([high, high, low], axis=1), right)
    right = tail[...]
    rest = dot(jnp.concatenate([high, low], axis=1), jnp.concatenate([right, right], axis=0))
    lanes = rest.shape[1] // 2
    return first, rest[:, :lanes] + rest[:, lanes:]


def side(x):
    rows = x.shape[0] // 2
    return jnp.concatenate([x[:rows], x[rows:]], axis=1)


def dft(pairs, row_tab, head, tail):
    tiles = []
    for pair in pairs:
        width = pair.shape[1] // 2
        half = over_rows(row_tab, pair)
        tiles += [side(half[:, :width]), side(half[:, width:])]
    rows = tiles[0].shape[0]
    first, rest = to_freqs(jnp.concatenate(tiles, axis=0), head, tail)
    return [(first[j * rows:(j + 1) * rows], rest[j * rows:(j + 1) * rows]) for j in range(len(tiles))]


def swap(x):
    return pltpu.roll(x, x.shape[1] // 2, 1)


def spectra_body(radii, taps, row_tab, head, tail, spec):
    batch, _, span, _ = taps.shape
    first = pl.program_id(0) * batch
    row_at = lax.broadcasted_iota(jnp.int32, (span, span), 0) - span // 2
    col_at = lax.broadcasted_iota(jnp.int32, (span, span), 1) - span // 2
    reach = jnp.maximum(jnp.maximum(row_at, -1 - row_at), jnp.maximum(col_at, -1 - col_at))
    pairs = []
    for i in range(batch // 2):
        planes = []
        for j in range(2):
            inside = reach < radii[first + 2 * i + j]
            parts = [jnp.where(inside, taps[2 * i + j, c], 0.0) for c in range(2)]
            planes.append(jnp.concatenate(parts, axis=0))
        pairs.append(jnp.concatenate(planes, axis=1))
    for k, (a, b) in enumerate(dft(pairs, row_tab, head, tail)):
        spec[k, :, :a.shape[1]] = a
        spec[k, :, a.shape[1]:] = b


def main_body(
    group, weight,
    own, above, below, target, mask_row, mask_head, mask_tail, spec_far, *rest,
):
    tables_far, rest = rest[:7], rest[7:]
    resist, grad_own, grad_up, grad_down = rest[:4]
    spec, field, mask_spec, slopes, grad_spec, spec_sems, table_sems = rest[4:11]
    tables = rest[11:]
    kernels, grid_rows, _ = spec.shape
    count, width = target.shape
    rim = (grid_rows - count) // 2
    steps = spec_sems.shape[0]
    batch = kernels // steps

    def fetch(i):
        here = pl.ds(i * batch, batch)
        return pltpu.make_async_copy(spec_far.at[here], spec.at[here], spec_sems.at[i])

    def fetch_table(i):
        return pltpu.make_async_copy(tables_far[i], tables[i], table_sems.at[i])

    col_inv, row_inv, row_tab, head, tail, grad_col, grad_row = tables
    for i in range(2):
        fetch_table(i).start()
    for i in range(steps):
        fetch(i).start()
    for i in range(2, 7):
        fetch_table(i).start()

    mask = jnp.concatenate(
        [part for c in range(2) for part in (above[c, count - rim:], own[c], below[c, :rim])], axis=0
    )
    m_first, m_rest = to_freqs(side(over_rows(mask_row, mask)), mask_head, mask_tail)
    lane = lax.broadcasted_iota(jnp.int32, m_rest.shape, 1)
    real_half = lane < m_rest.shape[1] // 2
    turned = swap(m_rest)
    mask_spec[:, :2 * width] = m_first
    mask_spec[:, 2 * width:3 * width] = jnp.where(real_half, m_rest, turned)
    mask_spec[:, 3 * width:] = jnp.where(real_half, -turned, m_rest)

    slopes[...] = jnp.zeros(slopes.shape, f32)
    grad_spec[...] = jnp.zeros(grad_spec.shape, f32)
    for i in range(2):
        fetch_table(i).wait()

    def forward(i, carry):
        fetch(i).wait()
        m_re, m_im = mask_spec[:, :width], mask_spec[:, width:2 * width]
        m_same, m_cross = mask_spec[:, 2 * width:3 * width], mask_spec[:, 3 * width:]
        products = []
        for j in range(batch):
            k = i * batch + j
            s_re, s_im, s_rest = spec[k, :, :width], spec[k, :, width:2 * width], spec[k, :, 2 * width:]
            products.append(jnp.concatenate([
                s_re * m_re - s_im * m_im,
                s_re * m_im + s_im * m_re,
                s_rest * m_same + swap(s_rest) * m_cross,
            ], axis=1))
        back = over_lanes(jnp.concatenate(products, axis=0), col_inv)
        for p in range(batch // 2):
            mine = []
            for c in range(2):
                planes = [back[(2 * p + j) * grid_rows:(2 * p + j + 1) * grid_rows, c * width:(c + 1) * width] for j in range(2)]
                mine.append(jnp.concatenate(planes, axis=1))
            pair = over_rows(row_inv, jnp.concatenate(mine, axis=0))
            field[i * (batch // 2) + p] = pair
            power = pair[:count] * pair[:count] + pair[count:] * pair[count:]
            for j in range(2):
                k = i * batch + 2 * p + j
                g = group[k]
                slopes[g] = slopes[g] + weight[k] * power[:, j * width:(j + 1) * width]
        return carry

    lax.fori_loop(0, steps, forward, 0)

    wanted = target[...].astype(f32)
    for g in range(GROUPS):
        seen = jax.nn.sigmoid(STEEPNESS * (slopes[g] - THRESHOLD))
        resist[g] = seen
        slopes[g] = 2.0 * (seen - wanted) * seen * (1.0 - seen) * STEEPNESS
    for i in range(2, 7):
        fetch_table(i).wait()

    def backward(i, carry):
        pairs = []
        for p in range(batch // 2):
            factors = []
            for j in range(2):
                k = i * batch + 2 * p + j
                factors.append((2.0 * weight[k]) * slopes[group[k]])
            factor = jnp.concatenate(factors, axis=1)
            pairs.append(field[i * (batch // 2) + p] * jnp.concatenate([factor, factor], axis=0))
        found = dft(pairs, row_tab, head, tail)
        total = [grad_spec[:, c * width:(c + 1) * width] for c in range(4)]
        for j in range(batch):
            k = i * batch + j
            s_re, s_im, s_rest = spec[k, :, :width], spec[k, :, width:2 * width], spec[k, :, 2 * width:]
            first, rest = found[j]
            c_re, c_im = first[:, :width], first[:, width:]
            total[0] = total[0] + (s_re * c_re + s_im * c_im)
            total[1] = total[1] + (s_re * c_im - s_im * c_re)
            total[2] = total[2] + s_rest * rest
            total[3] = total[3] + s_rest * swap(rest)
        for c in range(4):
            grad_spec[:, c * width:(c + 1) * width] = total[c]
        return carry

    lax.fori_loop(0, steps, backward, 0)

    same, cross = grad_spec[:, 2 * width:3 * width], grad_spec[:, 3 * width:]
    tail_sum = jnp.where(real_half, same + swap(same), swap(cross) - cross)
    total = jnp.concatenate([grad_spec[:, :2 * width], tail_sum], axis=1)
    back = over_lanes(total, grad_col)
    full = over_rows(grad_row, jnp.concatenate([back[:, :width], back[:, width:]], axis=0))
    for c in range(2):
        base = c * grid_rows
        grad_up[c] = full[base:base + rim]
        grad_own[c] = full[base + rim:base + rim + count]
        grad_down[c] = full[base + rim + count:base + grid_rows]


def on_device(mask_field, target, kernel_taps, kernel_radii, kernel_group, kernel_weight):
    _, count, width = mask_field.shape
    kernels, _, span, _ = kernel_taps.shape
    rim = span // 2
    grid_rows = count + 2 * rim
    grid_cols = width + rim
    assert count == span and width == span and kernels % BATCH == 0 and BATCH % 2 == 0

    strips = lax.axis_size("row")
    down = [(i, i + 1) for i in range(strips - 1)]
    up = [(i + 1, i) for i in range(strips - 1)]
    above = lax.ppermute(mask_field, "row", down)
    below = lax.ppermute(mask_field, "row", up)

    scale = 1.0 / (grid_rows * grid_cols)
    order = grouped(grid_cols, width)

    def head_and_tail(shift):
        table = analysis(grid_cols, width, shift).T[:, order]
        return halves(table[:, :2 * width], 0), halves(table[:, 2 * width:], 1)

    row_tab = halves(analysis(grid_rows, span, 0), 1)
    head, tail = head_and_tail(0)
    mask_row = halves(analysis(grid_rows, grid_rows, 2 * rim), 1)
    mask_head, mask_tail = head_and_tail(rim)
    col_inv = halves(synthesis(grid_cols, width, 0).T[order], 0)
    row_inv = halves(synthesis(grid_rows, count, 0, scale), 1)
    grad_col = halves(synthesis(grid_cols, width, rim).T[order], 0)
    grad_row = halves(synthesis(grid_rows, grid_rows, 2 * rim, scale), 1)

    smem = pl.BlockSpec(memory_space=pltpu.SMEM)
    vmem = pl.BlockSpec(memory_space=pltpu.VMEM)
    anywhere = pl.BlockSpec(memory_space=pl.ANY)
    spectra = pl.pallas_call(
        spectra_body,
        grid=(kernels // BATCH,),
        out_shape=jax.ShapeDtypeStruct((kernels, grid_rows, 2 * grid_cols), f32),
        in_specs=[smem, pl.BlockSpec((BATCH, 2, span, span), lambda i: (i, 0, 0, 0)), vmem, vmem, vmem],
        out_specs=pl.BlockSpec((BATCH, grid_rows, 2 * grid_cols), lambda i: (i, 0, 0)),
        compiler_params=pltpu.CompilerParams(vmem_limit_bytes=56 * MIB),
        cost_estimate=pl.CostEstimate(flops=18 * 10**9, bytes_accessed=14 * 10**6, transcendentals=0),
        name="spectra",
    )(kernel_radii, kernel_taps, *map(jnp.asarray, (row_tab, head, tail)))

    far = [jnp.asarray(t) for t in (col_inv, row_inv, row_tab, head, tail, grad_col, grad_row)]
    resist, own, up_rim, down_rim = pl.pallas_call(
        main_body,
        out_shape=[
            jax.ShapeDtypeStruct((GROUPS, count, width), f32),
            jax.ShapeDtypeStruct((2, count, width), f32),
            jax.ShapeDtypeStruct((2, rim, width), f32),
            jax.ShapeDtypeStruct((2, rim, width), f32),
        ],
        in_specs=[smem] * 2 + [vmem] * 7 + [anywhere] * 8,
        out_specs=[vmem] * 4,
        scratch_shapes=[
            pltpu.VMEM((kernels, grid_rows, 2 * grid_cols), f32),
            pltpu.VMEM((kernels // 2, 2 * count, 2 * width), f32),
            pltpu.VMEM((grid_rows, 4 * width), f32),
            pltpu.VMEM((GROUPS, count, width), f32),
            pltpu.VMEM((grid_rows, 4 * width), f32),
            pltpu.SemaphoreType.DMA((kernels // BATCH,)),
            pltpu.SemaphoreType.DMA((len(far),)),
        ] + [pltpu.VMEM(t.shape, bf16) for t in far],
        compiler_params=pltpu.CompilerParams(vmem_limit_bytes=56 * MIB),
        name="fields",
    )(
        kernel_group, kernel_weight, mask_field, above, below, target,
        *map(jnp.asarray, (mask_row, mask_head, mask_tail)), spectra, *far,
    )

    from_below = lax.ppermute(up_rim, "row", up)
    from_above = lax.ppermute(down_rim, "row", down)
    gradient = (
        own
        + jnp.pad(from_above, ((0, 0), (0, count - rim), (0, 0)))
        + jnp.pad(from_below, ((0, 0), (count - rim, 0), (0, 0)))
    )
    return resist, gradient


def solution(mesh):
    in_specs = (P(None, ("win", "row"), None), P(("win", "row"), None), P(), P(), P(), P())
    out_specs = (P(None, ("win", "row"), None), P(None, ("win", "row"), None))
    return jax.shard_map(
        on_device, mesh=mesh, in_specs=in_specs, out_specs=out_specs, check_vma=False
    )
```

```python
import math

import jax
import jax.numpy as jnp
import ml_dtypes
import numpy as np
from jax import lax
from jax.experimental import pallas as pl
from jax.experimental.pallas import tpu as pltpu
from jax.sharding import PartitionSpec as P

RMAX = 64
GROUPS = 3
STEEPNESS = 1.0
THRESHOLD = 2.0
BATCH = 4

f32 = jnp.float32
bf16 = jnp.bfloat16
MIB = 1024 * 1024


def halves(table, axis):
    high = table.astype(ml_dtypes.bfloat16)
    low = (table - high.astype(np.float64)).astype(ml_dtypes.bfloat16)
    return np.concatenate([high, low], axis=axis)


def analysis(freqs, points, shift):
    f = np.arange(freqs)[:, None]
    n = np.arange(points)[None, :] - shift
    angle = 2.0 * math.pi * ((f * n) % freqs) / freqs
    cos, sin = np.cos(angle), np.sin(angle)
    return np.block([[cos, sin], [-sin, cos]])


def synthesis(freqs, points, shift, scale=1.0):
    return analysis(freqs, points, shift).T * scale


def grouped(freqs, lanes):
    head, tail = np.arange(lanes), np.arange(lanes, freqs)
    return np.concatenate([head, freqs + head, tail, freqs + tail])


def split(x):
    high = x.astype(bf16)
    low = (x - high.astype(f32)).astype(bf16)
    return high, low


def dot(left, right):
    return jnp.dot(left, right, preferred_element_type=f32)


def over_rows(table, x):
    high, low = split(x)
    left = table[...]
    left = jnp.concatenate([left, left[:, :x.shape[0]]], axis=1)
    return dot(left, jnp.concatenate([high, high, low], axis=0))


def over_lanes(x, table):
    high, low = split(x)
    right = table[...]
    right = jnp.concatenate([right, right[:x.shape[1]]], axis=0)
    return dot(jnp.concatenate([high, high, low], axis=1), right)


def to_freqs(x, head, tail):
    high, low = split(x)
    depth = x.shape[1]
    right = head[...]
    right = jnp.concatenate([right, right[:depth]], axis=0)
    first = dot(jnp.concatenate([high, high, low], axis=1), right)
    right = tail[...]
    rest = dot(jnp.concatenate([high, low], axis=1), jnp.concatenate([right, right], axis=0))
    lanes = rest.shape[1] // 2
    return first, rest[:, :lanes] + rest[:, lanes:]


def side(x):
    rows = x.shape[0] // 2
    return jnp.concatenate([x[:rows], x[rows:]], axis=1)


def dft(planes, row_tab, head, tail):
    width = planes.shape[0] // 2
    half = over_rows(row_tab, planes)
    tiles = [side(half[:, at:at + width]) for at in range(0, planes.shape[1], width)]
    rows = tiles[0].shape[0]
    first, rest = to_freqs(jnp.concatenate(tiles, axis=0), head, tail)
    return [(first[j * rows:(j + 1) * rows], rest[j * rows:(j + 1) * rows]) for j in range(len(tiles))]


def swap(x):
    return pltpu.roll(x, x.shape[1] // 2, 1)


def spectra_body(radii, taps, row_tab, head, tail, spec):
    batch, _, span, _ = taps.shape
    first = pl.program_id(0) * batch
    row_at = lax.broadcasted_iota(jnp.int32, (span, span), 0) - span // 2
    col_at = lax.broadcasted_iota(jnp.int32, (span, span), 1) - span // 2
    reach = jnp.maximum(jnp.maximum(row_at, -1 - row_at), jnp.maximum(col_at, -1 - col_at))
    planes = []
    for k in range(batch):
        inside = reach < radii[first + k]
        parts = [jnp.where(inside, taps[k, c], 0.0) for c in range(2)]
        planes.append(jnp.concatenate(parts, axis=0))
    for k, (a, b) in enumerate(dft(jnp.concatenate(planes, axis=1), row_tab, head, tail)):
        spec[k, :, :a.shape[1]] = a
        spec[k, :, a.shape[1]:] = b


def main_body(
    group, weight,
    own, above, below, target, mask_row, mask_head, mask_tail, spec_far, *rest,
):
    tables_far, rest = rest[:7], rest[7:]
    resist, grad_own, grad_up, grad_down = rest[:4]
    spec, field, mask_spec, slopes, grad_spec, spec_sems, table_sems = rest[4:11]
    tables = rest[11:]
    kernels, grid_rows, _ = spec.shape
    count, width = target.shape
    rim = (grid_rows - count) // 2
    steps = spec_sems.shape[0]
    batch = kernels // steps

    def fetch(i):
        here = pl.ds(i * batch, batch)
        return pltpu.make_async_copy(spec_far.at[here], spec.at[here], spec_sems.at[i])

    def fetch_table(i):
        return pltpu.make_async_copy(tables_far[i], tables[i], table_sems.at[i])

    col_inv, row_inv, row_tab, head, tail, grad_col, grad_row = tables
    for i in range(2):
        fetch_table(i).start()
    for i in range(steps):
        fetch(i).start()
    for i in range(2, 7):
        fetch_table(i).start()

    mask = jnp.concatenate(
        [part for c in range(2) for part in (above[c, count - rim:], own[c], below[c, :rim])], axis=0
    )
    m_first, m_rest = to_freqs(side(over_rows(mask_row, mask)), mask_head, mask_tail)
    lane = lax.broadcasted_iota(jnp.int32, m_rest.shape, 1)
    real_half = lane < m_rest.shape[1] // 2
    turned = swap(m_rest)
    mask_spec[:, :2 * width] = m_first
    mask_spec[:, 2 * width:3 * width] = jnp.where(real_half, m_rest, turned)
    mask_spec[:, 3 * width:] = jnp.where(real_half, -turned, m_rest)

    slopes[...] = jnp.zeros(slopes.shape, f32)
    grad_spec[...] = jnp.zeros(grad_spec.shape, f32)
    for i in range(2):
        fetch_table(i).wait()

    def forward(i, carry):
        fetch(i).wait()
        m_re, m_im = mask_spec[:, :width], mask_spec[:, width:2 * width]
        m_same, m_cross = mask_spec[:, 2 * width:3 * width], mask_spec[:, 3 * width:]
        products = []
        for j in range(batch):
            k = i * batch + j
            s_re, s_im, s_rest = spec[k, :, :width], spec[k, :, width:2 * width], spec[k, :, 2 * width:]
            products.append(jnp.concatenate([
                s_re * m_re - s_im * m_im,
                s_re * m_im + s_im * m_re,
                s_rest * m_same + swap(s_rest) * m_cross,
            ], axis=1))
        back = over_lanes(jnp.concatenate(products, axis=0), col_inv)
        mine = []
        for c in range(2):
            planes = [back[j * grid_rows:(j + 1) * grid_rows, c * width:(c + 1) * width] for j in range(batch)]
            mine.append(jnp.concatenate(planes, axis=1))
        found = over_rows(row_inv, jnp.concatenate(mine, axis=0))
        field[i] = found
        power = found[:count] * found[:count] + found[count:] * found[count:]
        for j in range(batch):
            k = i * batch + j
            g = group[k]
            slopes[g] = slopes[g] + weight[k] * power[:, j * width:(j + 1) * width]
        return carry

    lax.fori_loop(0, steps, forward, 0)

    wanted = target[...].astype(f32)
    for g in range(GROUPS):
        seen = jax.nn.sigmoid(STEEPNESS * (slopes[g] - THRESHOLD))
        resist[g] = seen
        slopes[g] = 2.0 * (seen - wanted) * seen * (1.0 - seen) * STEEPNESS
    for i in range(2, 7):
        fetch_table(i).wait()

    def backward(i, carry):
        factors = []
        for j in range(batch):
            k = i * batch + j
            factors.append((2.0 * weight[k]) * slopes[group[k]])
        factor = jnp.concatenate(factors, axis=1)
        cot = field[i] * jnp.concatenate([factor, factor], axis=0)
        found = dft(cot, row_tab, head, tail)
        total = [grad_spec[:, c * width:(c + 1) * width] for c in range(4)]
        for j in range(batch):
            k = i * batch + j
            s_re, s_im, s_rest = spec[k, :, :width], spec[k, :, width:2 * width], spec[k, :, 2 * width:]
            first, rest = found[j]
            c_re, c_im = first[:, :width], first[:, width:]
            total[0] = total[0] + (s_re * c_re + s_im * c_im)
            total[1] = total[1] + (s_re * c_im - s_im * c_re)
            total[2] = total[2] + s_rest * rest
            total[3] = total[3] + s_rest * swap(rest)
        for c in range(4):
            grad_spec[:, c * width:(c + 1) * width] = total[c]
        return carry

    lax.fori_loop(0, steps, backward, 0)

    same, cross = grad_spec[:, 2 * width:3 * width], grad_spec[:, 3 * width:]
    tail_sum = jnp.where(real_half, same + swap(same), swap(cross) - cross)
    total = jnp.concatenate([grad_spec[:, :2 * width], tail_sum], axis=1)
    back = over_lanes(total, grad_col)
    full = over_rows(grad_row, jnp.concatenate([back[:, :width], back[:, width:]], axis=0))
    for c in range(2):
        base = c * grid_rows
        grad_up[c] = full[base:base + rim]
        grad_own[c] = full[base + rim:base + rim + count]
        grad_down[c] = full[base + rim + count:base + grid_rows]


def on_device(mask_field, target, kernel_taps, kernel_radii, kernel_group, kernel_weight):
    _, count, width = mask_field.shape
    kernels, _, span, _ = kernel_taps.shape
    rim = span // 2
    grid_rows = count + 2 * rim
    grid_cols = width + rim
    assert count == span and width == span and kernels % BATCH == 0

    strips = lax.axis_size("row")
    down = [(i, i + 1) for i in range(strips - 1)]
    up = [(i + 1, i) for i in range(strips - 1)]
    above = lax.ppermute(mask_field, "row", down)
    below = lax.ppermute(mask_field, "row", up)

    scale = 1.0 / (grid_rows * grid_cols)
    order = grouped(grid_cols, width)

    def head_and_tail(shift):
        table = analysis(grid_cols, width, shift).T[:, order]
        return halves(table[:, :2 * width], 0), halves(table[:, 2 * width:], 1)

    row_tab = halves(analysis(grid_rows, span, 0), 1)
    head, tail = head_and_tail(0)
    mask_row = halves(analysis(grid_rows, grid_rows, 2 * rim), 1)
    mask_head, mask_tail = head_and_tail(rim)
    col_inv = halves(synthesis(grid_cols, width, 0).T[order], 0)
    row_inv = halves(synthesis(grid_rows, count, 0, scale), 1)
    grad_col = halves(synthesis(grid_cols, width, rim).T[order], 0)
    grad_row = halves(synthesis(grid_rows, grid_rows, 2 * rim, scale), 1)

    smem = pl.BlockSpec(memory_space=pltpu.SMEM)
    vmem = pl.BlockSpec(memory_space=pltpu.VMEM)
    anywhere = pl.BlockSpec(memory_space=pl.ANY)
    spectra = pl.pallas_call(
        spectra_body,
        grid=(kernels // BATCH,),
        out_shape=jax.ShapeDtypeStruct((kernels, grid_rows, 2 * grid_cols), f32),
        in_specs=[smem, pl.BlockSpec((BATCH, 2, span, span), lambda i: (i, 0, 0, 0)), vmem, vmem, vmem],
        out_specs=pl.BlockSpec((BATCH, grid_rows, 2 * grid_cols), lambda i: (i, 0, 0)),
        compiler_params=pltpu.CompilerParams(vmem_limit_bytes=56 * MIB),
        cost_estimate=pl.CostEstimate(flops=18 * 10**9, bytes_accessed=14 * 10**6, transcendentals=0),
        name="spectra",
    )(kernel_radii, kernel_taps, *map(jnp.asarray, (row_tab, head, tail)))

    far = [jnp.asarray(t) for t in (col_inv, row_inv, row_tab, head, tail, grad_col, grad_row)]
    resist, own, up_rim, down_rim = pl.pallas_call(
        main_body,
        out_shape=[
            jax.ShapeDtypeStruct((GROUPS, count, width), f32),
            jax.ShapeDtypeStruct((2, count, width), f32),
            jax.ShapeDtypeStruct((2, rim, width), f32),
            jax.ShapeDtypeStruct((2, rim, width), f32),
        ],
        in_specs=[smem] * 2 + [vmem] * 7 + [anywhere] * 8,
        out_specs=[vmem] * 4,
        scratch_shapes=[
            pltpu.VMEM((kernels, grid_rows, 2 * grid_cols), f32),
            pltpu.VMEM((kernels // BATCH, 2 * count, BATCH * width), f32),
            pltpu.VMEM((grid_rows, 4 * width), f32),
            pltpu.VMEM((GROUPS, count, width), f32),
            pltpu.VMEM((grid_rows, 4 * width), f32),
            pltpu.SemaphoreType.DMA((kernels // BATCH,)),
            pltpu.SemaphoreType.DMA((len(far),)),
        ] + [pltpu.VMEM(t.shape, bf16) for t in far],
        compiler_params=pltpu.CompilerParams(vmem_limit_bytes=56 * MIB),
        name="fields",
    )(
        kernel_group, kernel_weight, mask_field, above, below, target,
        *map(jnp.asarray, (mask_row, mask_head, mask_tail)), spectra, *far,
    )

    from_below = lax.ppermute(up_rim, "row", up)
    from_above = lax.ppermute(down_rim, "row", down)
    gradient = (
        own
        + jnp.pad(from_above, ((0, 0), (0, count - rim), (0, 0)))
        + jnp.pad(from_below, ((0, 0), (count - rim, 0), (0, 0)))
    )
    return resist, gradient


def solution(mesh):
    in_specs = (P(None, ("win", "row"), None), P(("win", "row"), None), P(), P(), P(), P())
    out_specs = (P(None, ("win", "row"), None), P(None, ("win", "row"), None))
    return jax.shard_map(
        on_device, mesh=mesh, in_specs=in_specs, out_specs=out_specs, check_vma=False
    )
```

```python
import math

import jax
import jax.numpy as jnp
import ml_dtypes
import numpy as np
from jax import lax
from jax.experimental import pallas as pl
from jax.experimental.pallas import tpu as pltpu
from jax.sharding import PartitionSpec as P

RMAX = 64
GROUPS = 3
STEEPNESS = 1.0
THRESHOLD = 2.0
BATCH = 4

f32 = jnp.float32
bf16 = jnp.bfloat16
MIB = 1024 * 1024


def halves(table, axis):
    high = table.astype(ml_dtypes.bfloat16)
    low = (table - high.astype(np.float64)).astype(ml_dtypes.bfloat16)
    return np.concatenate([high, low], axis=axis)


def analysis(freqs, points, shift):
    f = np.arange(freqs)[:, None]
    n = np.arange(points)[None, :] - shift
    angle = 2.0 * math.pi * ((f * n) % freqs) / freqs
    cos, sin = np.cos(angle), np.sin(angle)
    return np.block([[cos, sin], [-sin, cos]])


def synthesis(freqs, points, shift, scale=1.0):
    return analysis(freqs, points, shift).T * scale


def grouped(freqs, lanes):
    head, tail = np.arange(lanes), np.arange(lanes, freqs)
    return np.concatenate([head, freqs + head, tail, freqs + tail])


def split(x):
    high = x.astype(bf16)
    low = (x - high.astype(f32)).astype(bf16)
    return high, low


def dot(left, right, piece):
    parts = [
        jnp.dot(left[at:at + piece], right, preferred_element_type=f32)
        for at in range(0, left.shape[0], piece)
    ]
    return jnp.concatenate(parts, axis=0)


def over_rows(table, x, piece):
    high, low = split(x)
    left = table[...]
    left = jnp.concatenate([left, left[:, :x.shape[0]]], axis=1)
    return dot(left, jnp.concatenate([high, high, low], axis=0), piece)


def over_lanes(x, table, piece):
    high, low = split(x)
    right = table[...]
    right = jnp.concatenate([right, right[:x.shape[1]]], axis=0)
    return dot(jnp.concatenate([high, high, low], axis=1), right, piece)


def to_freqs(x, head, tail, piece):
    high, low = split(x)
    depth = x.shape[1]
    right = head[...]
    right = jnp.concatenate([right, right[:depth]], axis=0)
    first = dot(jnp.concatenate([high, high, low], axis=1), right, piece)
    right = tail[...]
    rest = dot(jnp.concatenate([high, low], axis=1), jnp.concatenate([right, right], axis=0), piece)
    lanes = rest.shape[1] // 2
    return first, rest[:, :lanes] + rest[:, lanes:]


def side(x):
    rows = x.shape[0] // 2
    return jnp.concatenate([x[:rows], x[rows:]], axis=1)


def dft(planes, row_tab, head, tail, piece):
    width = planes.shape[0] // 2
    half = over_rows(row_tab, planes, piece)
    tiles = [side(half[:, at:at + width]) for at in range(0, planes.shape[1], width)]
    rows = tiles[0].shape[0]
    first, rest = to_freqs(jnp.concatenate(tiles, axis=0), head, tail, piece)
    return [(first[j * rows:(j + 1) * rows], rest[j * rows:(j + 1) * rows]) for j in range(len(tiles))]


def swap(x):
    return pltpu.roll(x, x.shape[1] // 2, 1)


def spectra_body(radii, taps, row_tab, head, tail, spec):
    batch, _, span, _ = taps.shape
    first = pl.program_id(0) * batch
    row_at = lax.broadcasted_iota(jnp.int32, (span, span), 0) - span // 2
    col_at = lax.broadcasted_iota(jnp.int32, (span, span), 1) - span // 2
    reach = jnp.maximum(jnp.maximum(row_at, -1 - row_at), jnp.maximum(col_at, -1 - col_at))
    planes = []
    for k in range(batch):
        inside = reach < radii[first + k]
        parts = [jnp.where(inside, taps[k, c], 0.0) for c in range(2)]
        planes.append(jnp.concatenate(parts, axis=0))
    for k, (a, b) in enumerate(dft(jnp.concatenate(planes, axis=1), row_tab, head, tail, 128)):
        spec[k, :, :a.shape[1]] = a
        spec[k, :, a.shape[1]:] = b


def main_body(
    group, weight,
    own, above, below, target, mask_row, mask_head, mask_tail, spec_far, *rest,
):
    tables_far, rest = rest[:7], rest[7:]
    resist, grad_own, grad_up, grad_down = rest[:4]
    spec, field, mask_spec, slopes, grad_spec, spec_sems, table_sems = rest[4:11]
    tables = rest[11:]
    kernels, grid_rows, _ = spec.shape
    count, width = target.shape
    rim = (grid_rows - count) // 2
    steps = spec_sems.shape[0]
    batch = kernels // steps

    def fetch(i):
        here = pl.ds(i * batch, batch)
        return pltpu.make_async_copy(spec_far.at[here], spec.at[here], spec_sems.at[i])

    def fetch_table(i):
        return pltpu.make_async_copy(tables_far[i], tables[i], table_sems.at[i])

    col_inv, row_inv, row_tab, head, tail, grad_col, grad_row = tables
    for i in range(2):
        fetch_table(i).start()
    for i in range(steps):
        fetch(i).start()
    for i in range(2, 7):
        fetch_table(i).start()

    mask = jnp.concatenate(
        [part for c in range(2) for part in (above[c, count - rim:], own[c], below[c, :rim])], axis=0
    )
    m_first, m_rest = to_freqs(side(over_rows(mask_row, mask, 256)), mask_head, mask_tail, 256)
    lane = lax.broadcasted_iota(jnp.int32, m_rest.shape, 1)
    real_half = lane < m_rest.shape[1] // 2
    turned = swap(m_rest)
    mask_spec[:, :2 * width] = m_first
    mask_spec[:, 2 * width:3 * width] = jnp.where(real_half, m_rest, turned)
    mask_spec[:, 3 * width:] = jnp.where(real_half, -turned, m_rest)

    slopes[...] = jnp.zeros(slopes.shape, f32)
    grad_spec[...] = jnp.zeros(grad_spec.shape, f32)
    for i in range(2):
        fetch_table(i).wait()

    def forward(i, carry):
        fetch(i).wait()
        m_re, m_im = mask_spec[:, :width], mask_spec[:, width:2 * width]
        m_same, m_cross = mask_spec[:, 2 * width:3 * width], mask_spec[:, 3 * width:]
        products = []
        for j in range(batch):
            k = i * batch + j
            s_re, s_im, s_rest = spec[k, :, :width], spec[k, :, width:2 * width], spec[k, :, 2 * width:]
            products.append(jnp.concatenate([
                s_re * m_re - s_im * m_im,
                s_re * m_im + s_im * m_re,
                s_rest * m_same + swap(s_rest) * m_cross,
            ], axis=1))
        back = over_lanes(jnp.concatenate(products, axis=0), col_inv, 256)
        mine = []
        for c in range(2):
            planes = [back[j * grid_rows:(j + 1) * grid_rows, c * width:(c + 1) * width] for j in range(batch)]
            mine.append(jnp.concatenate(planes, axis=1))
        found = over_rows(row_inv, jnp.concatenate(mine, axis=0), 256)
        field[i] = found
        power = found[:count] * found[:count] + found[count:] * found[count:]
        for j in range(batch):
            k = i * batch + j
            g = group[k]
            slopes[g] = slopes[g] + weight[k] * power[:, j * width:(j + 1) * width]
        return carry

    lax.fori_loop(0, steps, forward, 0)

    wanted = target[...].astype(f32)
    for g in range(GROUPS):
        seen = jax.nn.sigmoid(STEEPNESS * (slopes[g] - THRESHOLD))
        resist[g] = seen
        slopes[g] = 2.0 * (seen - wanted) * seen * (1.0 - seen) * STEEPNESS
    for i in range(2, 7):
        fetch_table(i).wait()

    def backward(i, carry):
        factors = []
        for j in range(batch):
            k = i * batch + j
            factors.append((2.0 * weight[k]) * slopes[group[k]])
        factor = jnp.concatenate(factors, axis=1)
        cot = field[i] * jnp.concatenate([factor, factor], axis=0)
        found = dft(cot, row_tab, head, tail, 256)
        total = [grad_spec[:, c * width:(c + 1) * width] for c in range(4)]
        for j in range(batch):
            k = i * batch + j
            s_re, s_im, s_rest = spec[k, :, :width], spec[k, :, width:2 * width], spec[k, :, 2 * width:]
            first, rest = found[j]
            c_re, c_im = first[:, :width], first[:, width:]
            total[0] = total[0] + (s_re * c_re + s_im * c_im)
            total[1] = total[1] + (s_re * c_im - s_im * c_re)
            total[2] = total[2] + s_rest * rest
            total[3] = total[3] + s_rest * swap(rest)
        for c in range(4):
            grad_spec[:, c * width:(c + 1) * width] = total[c]
        return carry

    lax.fori_loop(0, steps, backward, 0)

    same, cross = grad_spec[:, 2 * width:3 * width], grad_spec[:, 3 * width:]
    tail_sum = jnp.where(real_half, same + swap(same), swap(cross) - cross)
    total = jnp.concatenate([grad_spec[:, :2 * width], tail_sum], axis=1)
    back = over_lanes(total, grad_col, 256)
    full = over_rows(grad_row, jnp.concatenate([back[:, :width], back[:, width:]], axis=0), 256)
    for c in range(2):
        base = c * grid_rows
        grad_up[c] = full[base:base + rim]
        grad_own[c] = full[base + rim:base + rim + count]
        grad_down[c] = full[base + rim + count:base + grid_rows]


def on_device(mask_field, target, kernel_taps, kernel_radii, kernel_group, kernel_weight):
    _, count, width = mask_field.shape
    kernels, _, span, _ = kernel_taps.shape
    rim = span // 2
    grid_rows = count + 2 * rim
    grid_cols = width + rim
    assert count == span and width == span and kernels % BATCH == 0

    strips = lax.axis_size("row")
    down = [(i, i + 1) for i in range(strips - 1)]
    up = [(i + 1, i) for i in range(strips - 1)]
    above = lax.ppermute(mask_field, "row", down)
    below = lax.ppermute(mask_field, "row", up)

    scale = 1.0 / (grid_rows * grid_cols)
    order = grouped(grid_cols, width)

    def head_and_tail(shift):
        table = analysis(grid_cols, width, shift).T[:, order]
        return halves(table[:, :2 * width], 0), halves(table[:, 2 * width:], 1)

    row_tab = halves(analysis(grid_rows, span, 0), 1)
    head, tail = head_and_tail(0)
    mask_row = halves(analysis(grid_rows, grid_rows, 2 * rim), 1)
    mask_head, mask_tail = head_and_tail(rim)
    col_inv = halves(synthesis(grid_cols, width, 0).T[order], 0)
    row_inv = halves(synthesis(grid_rows, count, 0, scale), 1)
    grad_col = halves(synthesis(grid_cols, width, rim).T[order], 0)
    grad_row = halves(synthesis(grid_rows, grid_rows, 2 * rim, scale), 1)

    smem = pl.BlockSpec(memory_space=pltpu.SMEM)
    vmem = pl.BlockSpec(memory_space=pltpu.VMEM)
    anywhere = pl.BlockSpec(memory_space=pl.ANY)
    spectra = pl.pallas_call(
        spectra_body,
        grid=(kernels // BATCH,),
        out_shape=jax.ShapeDtypeStruct((kernels, grid_rows, 2 * grid_cols), f32),
        in_specs=[smem, pl.BlockSpec((BATCH, 2, span, span), lambda i: (i, 0, 0, 0)), vmem, vmem, vmem],
        out_specs=pl.BlockSpec((BATCH, grid_rows, 2 * grid_cols), lambda i: (i, 0, 0)),
        compiler_params=pltpu.CompilerParams(vmem_limit_bytes=56 * MIB),
        cost_estimate=pl.CostEstimate(flops=18 * 10**9, bytes_accessed=14 * 10**6, transcendentals=0),
        name="spectra",
    )(kernel_radii, kernel_taps, *map(jnp.asarray, (row_tab, head, tail)))

    far = [jnp.asarray(t) for t in (col_inv, row_inv, row_tab, head, tail, grad_col, grad_row)]
    resist, own, up_rim, down_rim = pl.pallas_call(
        main_body,
        out_shape=[
            jax.ShapeDtypeStruct((GROUPS, count, width), f32),
            jax.ShapeDtypeStruct((2, count, width), f32),
            jax.ShapeDtypeStruct((2, rim, width), f32),
            jax.ShapeDtypeStruct((2, rim, width), f32),
        ],
        in_specs=[smem] * 2 + [vmem] * 7 + [anywhere] * 8,
        out_specs=[vmem] * 4,
        scratch_shapes=[
            pltpu.VMEM((kernels, grid_rows, 2 * grid_cols), f32),
            pltpu.VMEM((kernels // BATCH, 2 * count, BATCH * width), f32),
            pltpu.VMEM((grid_rows, 4 * width), f32),
            pltpu.VMEM((GROUPS, count, width), f32),
            pltpu.VMEM((grid_rows, 4 * width), f32),
            pltpu.SemaphoreType.DMA((kernels // BATCH,)),
            pltpu.SemaphoreType.DMA((len(far),)),
        ] + [pltpu.VMEM(t.shape, bf16) for t in far],
        compiler_params=pltpu.CompilerParams(vmem_limit_bytes=56 * MIB),
        name="fields",
    )(
        kernel_group, kernel_weight, mask_field, above, below, target,
        *map(jnp.asarray, (mask_row, mask_head, mask_tail)), spectra, *far,
    )

    from_below = lax.ppermute(up_rim, "row", up)
    from_above = lax.ppermute(down_rim, "row", down)
    gradient = (
        own
        + jnp.pad(from_above, ((0, 0), (0, count - rim), (0, 0)))
        + jnp.pad(from_below, ((0, 0), (count - rim, 0), (0, 0)))
    )
    return resist, gradient


def solution(mesh):
    in_specs = (P(None, ("win", "row"), None), P(("win", "row"), None), P(), P(), P(), P())
    out_specs = (P(None, ("win", "row"), None), P(None, ("win", "row"), None))
    return jax.shard_map(
        on_device, mesh=mesh, in_specs=in_specs, out_specs=out_specs, check_vma=False
    )
```

```python
import math

import jax
import jax.numpy as jnp
import ml_dtypes
import numpy as np
from jax import lax
from jax.experimental import pallas as pl
from jax.experimental.pallas import tpu as pltpu
from jax.sharding import PartitionSpec as P

RMAX = 64
GROUPS = 3
STEEPNESS = 1.0
THRESHOLD = 2.0
BATCH = 4

f32 = jnp.float32
bf16 = jnp.bfloat16
MIB = 1024 * 1024


def halves(table, axis):
    high = table.astype(ml_dtypes.bfloat16)
    low = (table - high.astype(np.float64)).astype(ml_dtypes.bfloat16)
    return np.concatenate([high, low], axis=axis)


def analysis(freqs, points, shift):
    f = np.arange(freqs)[:, None]
    n = np.arange(points)[None, :] - shift
    angle = 2.0 * math.pi * ((f * n) % freqs) / freqs
    cos, sin = np.cos(angle), np.sin(angle)
    return np.block([[cos, sin], [-sin, cos]])


def synthesis(freqs, points, shift, scale=1.0):
    return analysis(freqs, points, shift).T * scale


def grouped(freqs, lanes):
    head, tail = np.arange(lanes), np.arange(lanes, freqs)
    return np.concatenate([head, freqs + head, tail, freqs + tail])


def split(x):
    high = x.astype(bf16)
    low = (x - high.astype(f32)).astype(bf16)
    return high, low


def dot(left, right, piece):
    parts = [
        jnp.dot(left[at:at + piece], right, preferred_element_type=f32)
        for at in range(0, left.shape[0], piece)
    ]
    return jnp.concatenate(parts, axis=0)


def over_rows(table, x, piece):
    high, low = split(x)
    left = table[...]
    left = jnp.concatenate([left, left[:, :x.shape[0]]], axis=1)
    return dot(left, jnp.concatenate([high, high, low], axis=0), piece)


def over_lanes(x, table, piece):
    high, low = split(x)
    right = table[...]
    right = jnp.concatenate([right, right[:x.shape[1]]], axis=0)
    return dot(jnp.concatenate([high, high, low], axis=1), right, piece)


def to_freqs(x, head, tail, piece):
    high, low = split(x)
    depth = x.shape[1]
    right = head[...]
    right = jnp.concatenate([right, right[:depth]], axis=0)
    first = dot(jnp.concatenate([high, high, low], axis=1), right, piece)
    right = tail[...]
    rest = dot(jnp.concatenate([high, low], axis=1), jnp.concatenate([right, right], axis=0), piece)
    lanes = rest.shape[1] // 2
    return first, rest[:, :lanes] + rest[:, lanes:]


def side(x):
    rows = x.shape[0] // 2
    return jnp.concatenate([x[:rows], x[rows:]], axis=1)


def dft(planes, row_tab, head, tail, piece):
    width = planes.shape[0] // 2
    half = over_rows(row_tab, planes, piece)
    tiles = [side(half[:, at:at + width]) for at in range(0, planes.shape[1], width)]
    rows = tiles[0].shape[0]
    first, rest = to_freqs(jnp.concatenate(tiles, axis=0), head, tail, piece)
    return [(first[j * rows:(j + 1) * rows], rest[j * rows:(j + 1) * rows]) for j in range(len(tiles))]


def swap(x):
    return pltpu.roll(x, x.shape[1] // 2, 1)


def spectra_body(radii, taps, row_tab, head, tail, spec):
    batch, _, span, _ = taps.shape
    first = pl.program_id(0) * batch
    row_at = lax.broadcasted_iota(jnp.int32, (span, span), 0) - span // 2
    col_at = lax.broadcasted_iota(jnp.int32, (span, span), 1) - span // 2
    reach = jnp.maximum(jnp.maximum(row_at, -1 - row_at), jnp.maximum(col_at, -1 - col_at))
    planes = []
    for k in range(batch):
        inside = reach < radii[first + k]
        parts = [jnp.where(inside, taps[k, c], 0.0) for c in range(2)]
        planes.append(jnp.concatenate(parts, axis=0))
    for k, (a, b) in enumerate(dft(jnp.concatenate(planes, axis=1), row_tab, head, tail, 256)):
        spec[k, :, :a.shape[1]] = a
        spec[k, :, a.shape[1]:] = b


def main_body(
    group, weight, place,
    own, near, far, target, mask_row, mask_head, mask_tail, spec_far, *rest,
):
    tables_far, rest = rest[:7], rest[7:]
    resist, grad_own, near_rim, far_rim = rest[:4]
    spec, field, mask_spec, slopes, grad_spec, spec_sems, table_sems = rest[4:11]
    tables = rest[11:]
    kernels, grid_rows, _ = spec.shape
    count, width = target.shape
    rim = (grid_rows - count) // 2
    steps = spec_sems.shape[0]
    batch = kernels // steps

    def fetch(i):
        here = pl.ds(i * batch, batch)
        return pltpu.make_async_copy(spec_far.at[here], spec.at[here], spec_sems.at[i])

    def fetch_table(i):
        return pltpu.make_async_copy(tables_far[i], tables[i], table_sems.at[i])

    col_inv, row_inv, row_tab, head, tail, grad_col, grad_row = tables
    for i in range(2):
        fetch_table(i).start()
    for i in range(steps):
        fetch(i).start()
    for i in range(2, 7):
        fetch_table(i).start()

    odd = place[0] % 2
    has_above = place[0] > 0
    has_below = place[0] < place[1] - 1
    parts = []
    for c in range(2):
        above = jnp.where(odd == 1, near[0, c, count - rim:], far[0, c, count - rim:])
        below = jnp.where(odd == 1, far[1, c, :rim], near[1, c, :rim])
        parts += [jnp.where(has_above, above, 0.0), own[c], jnp.where(has_below, below, 0.0)]
    mask = jnp.concatenate(parts, axis=0)
    m_first, m_rest = to_freqs(side(over_rows(mask_row, mask, 256)), mask_head, mask_tail, 256)
    lane = lax.broadcasted_iota(jnp.int32, m_rest.shape, 1)
    real_half = lane < m_rest.shape[1] // 2
    turned = swap(m_rest)
    mask_spec[:, :2 * width] = m_first
    mask_spec[:, 2 * width:3 * width] = jnp.where(real_half, m_rest, turned)
    mask_spec[:, 3 * width:] = jnp.where(real_half, -turned, m_rest)

    slopes[...] = jnp.zeros(slopes.shape, f32)
    grad_spec[...] = jnp.zeros(grad_spec.shape, f32)
    for i in range(2):
        fetch_table(i).wait()

    def forward(i, carry):
        fetch(i).wait()
        m_re, m_im = mask_spec[:, :width], mask_spec[:, width:2 * width]
        m_same, m_cross = mask_spec[:, 2 * width:3 * width], mask_spec[:, 3 * width:]
        products = []
        for j in range(batch):
            k = i * batch + j
            s_re, s_im, s_rest = spec[k, :, :width], spec[k, :, width:2 * width], spec[k, :, 2 * width:]
            products.append(jnp.concatenate([
                s_re * m_re - s_im * m_im,
                s_re * m_im + s_im * m_re,
                s_rest * m_same + swap(s_rest) * m_cross,
            ], axis=1))
        back = over_lanes(jnp.concatenate(products, axis=0), col_inv, 256)
        mine = []
        for c in range(2):
            planes = [back[j * grid_rows:(j + 1) * grid_rows, c * width:(c + 1) * width] for j in range(batch)]
            mine.append(jnp.concatenate(planes, axis=1))
        found = over_rows(row_inv, jnp.concatenate(mine, axis=0), 256)
        field[i] = found
        power = found[:count] * found[:count] + found[count:] * found[count:]
        for j in range(batch):
            k = i * batch + j
            g = group[k]
            slopes[g] = slopes[g] + weight[k] * power[:, j * width:(j + 1) * width]
        return carry

    lax.fori_loop(0, steps, forward, 0)

    wanted = target[...].astype(f32)
    for g in range(GROUPS):
        seen = jax.nn.sigmoid(STEEPNESS * (slopes[g] - THRESHOLD))
        resist[g] = seen
        slopes[g] = 2.0 * (seen - wanted) * seen * (1.0 - seen) * STEEPNESS
    for i in range(2, 7):
        fetch_table(i).wait()

    def backward(i, carry):
        factors = []
        for j in range(batch):
            k = i * batch + j
            factors.append((2.0 * weight[k]) * slopes[group[k]])
        factor = jnp.concatenate(factors, axis=1)
        cot = field[i] * jnp.concatenate([factor, factor], axis=0)
        found = dft(cot, row_tab, head, tail, 256)
        total = [grad_spec[:, c * width:(c + 1) * width] for c in range(4)]
        for j in range(batch):
            k = i * batch + j
            s_re, s_im, s_rest = spec[k, :, :width], spec[k, :, width:2 * width], spec[k, :, 2 * width:]
            first, rest = found[j]
            c_re, c_im = first[:, :width], first[:, width:]
            total[0] = total[0] + (s_re * c_re + s_im * c_im)
            total[1] = total[1] + (s_re * c_im - s_im * c_re)
            total[2] = total[2] + s_rest * rest
            total[3] = total[3] + s_rest * swap(rest)
        for c in range(4):
            grad_spec[:, c * width:(c + 1) * width] = total[c]
        return carry

    lax.fori_loop(0, steps, backward, 0)

    same, cross = grad_spec[:, 2 * width:3 * width], grad_spec[:, 3 * width:]
    tail_sum = jnp.where(real_half, same + swap(same), swap(cross) - cross)
    total = jnp.concatenate([grad_spec[:, :2 * width], tail_sum], axis=1)
    back = over_lanes(total, grad_col, 256)
    full = over_rows(grad_row, jnp.concatenate([back[:, :width], back[:, width:]], axis=0), 256)
    for c in range(2):
        base = c * grid_rows
        rise, fall = full[base:base + rim], full[base + rim + count:base + grid_rows]
        near_rim[c] = jnp.where(odd == 1, rise, fall)
        far_rim[c] = jnp.where(odd == 1, fall, rise)
        grad_own[c] = full[base + rim:base + rim + count]


def on_device(mask_field, target, kernel_taps, kernel_radii, kernel_group, kernel_weight):
    _, count, width = mask_field.shape
    kernels, _, span, _ = kernel_taps.shape
    rim = span // 2
    grid_rows = count + 2 * rim
    grid_cols = width + rim
    assert count == span and width == span and kernels % BATCH == 0

    strips = lax.axis_size("row")
    assert strips % 2 == 0
    at = lax.axis_index("row")
    odd = at % 2
    near_pairs = [[i, i + 1] for i in range(0, strips, 2)]
    far_pairs = [[i, (i + 1) % strips] for i in range(1, strips, 2)]
    near = lax.all_gather(mask_field, "row", axis_index_groups=near_pairs)
    far = lax.all_gather(mask_field, "row", axis_index_groups=far_pairs)
    place = jnp.stack([at, jnp.int32(strips)]).astype(jnp.int32)

    scale = 1.0 / (grid_rows * grid_cols)
    order = grouped(grid_cols, width)

    def head_and_tail(shift):
        table = analysis(grid_cols, width, shift).T[:, order]
        return halves(table[:, :2 * width], 0), halves(table[:, 2 * width:], 1)

    row_tab = halves(analysis(grid_rows, span, 0), 1)
    head, tail = head_and_tail(0)
    mask_row = halves(analysis(grid_rows, grid_rows, 2 * rim), 1)
    mask_head, mask_tail = head_and_tail(rim)
    col_inv = halves(synthesis(grid_cols, width, 0).T[order], 0)
    row_inv = halves(synthesis(grid_rows, count, 0, scale), 1)
    grad_col = halves(synthesis(grid_cols, width, rim).T[order], 0)
    grad_row = halves(synthesis(grid_rows, grid_rows, 2 * rim, scale), 1)

    smem = pl.BlockSpec(memory_space=pltpu.SMEM)
    vmem = pl.BlockSpec(memory_space=pltpu.VMEM)
    anywhere = pl.BlockSpec(memory_space=pl.ANY)
    spectra = pl.pallas_call(
        spectra_body,
        grid=(kernels // BATCH,),
        out_shape=jax.ShapeDtypeStruct((kernels, grid_rows, 2 * grid_cols), f32),
        in_specs=[smem, pl.BlockSpec((BATCH, 2, span, span), lambda i: (i, 0, 0, 0)), vmem, vmem, vmem],
        out_specs=pl.BlockSpec((BATCH, grid_rows, 2 * grid_cols), lambda i: (i, 0, 0)),
        compiler_params=pltpu.CompilerParams(vmem_limit_bytes=56 * MIB),
        cost_estimate=pl.CostEstimate(flops=18 * 10**9, bytes_accessed=14 * 10**6, transcendentals=0),
        name="spectra",
    )(kernel_radii, kernel_taps, *map(jnp.asarray, (row_tab, head, tail)))

    late = [jnp.asarray(t) for t in (col_inv, row_inv, row_tab, head, tail, grad_col, grad_row)]
    resist, own, near_rim, far_rim = pl.pallas_call(
        main_body,
        out_shape=[
            jax.ShapeDtypeStruct((GROUPS, count, width), f32),
            jax.ShapeDtypeStruct((2, count, width), f32),
            jax.ShapeDtypeStruct((2, rim, width), f32),
            jax.ShapeDtypeStruct((2, rim, width), f32),
        ],
        in_specs=[smem] * 3 + [vmem] * 7 + [anywhere] * 8,
        out_specs=[vmem] * 4,
        scratch_shapes=[
            pltpu.VMEM((kernels, grid_rows, 2 * grid_cols), f32),
            pltpu.VMEM((kernels // BATCH, 2 * count, BATCH * width), f32),
            pltpu.VMEM((grid_rows, 4 * width), f32),
            pltpu.VMEM((GROUPS, count, width), f32),
            pltpu.VMEM((grid_rows, 4 * width), f32),
            pltpu.SemaphoreType.DMA((kernels // BATCH,)),
            pltpu.SemaphoreType.DMA((len(late),)),
        ] + [pltpu.VMEM(t.shape, bf16) for t in late],
        compiler_params=pltpu.CompilerParams(vmem_limit_bytes=56 * MIB),
        name="fields",
    )(
        kernel_group, kernel_weight, place, mask_field, near, far, target,
        *map(jnp.asarray, (mask_row, mask_head, mask_tail)), spectra, *late,
    )

    near_rims = lax.all_gather(near_rim, "row", axis_index_groups=near_pairs)
    far_rims = lax.all_gather(far_rim, "row", axis_index_groups=far_pairs)
    from_above = jnp.where(odd == 1, near_rims[0], far_rims[0])
    from_above = jnp.where(at > 0, from_above, 0.0)
    from_below = jnp.where(odd == 1, far_rims[1], near_rims[1])
    from_below = jnp.where(at < strips - 1, from_below, 0.0)
    gradient = (
        own
        + jnp.pad(from_above, ((0, 0), (0, count - rim), (0, 0)))
        + jnp.pad(from_below, ((0, 0), (count - rim, 0), (0, 0)))
    )
    return resist, gradient


def solution(mesh):
    in_specs = (P(None, ("win", "row"), None), P(("win", "row"), None), P(), P(), P(), P())
    out_specs = (P(None, ("win", "row"), None), P(None, ("win", "row"), None))
    return jax.shard_map(
        on_device, mesh=mesh, in_specs=in_specs, out_specs=out_specs, check_vma=False
    )
```

```python
import math

import jax
import jax.numpy as jnp
import ml_dtypes
import numpy as np
from jax import lax
from jax.experimental import pallas as pl
from jax.experimental.pallas import tpu as pltpu
from jax.sharding import PartitionSpec as P

RMAX = 64
GROUPS = 3
STEEPNESS = 1.0
THRESHOLD = 2.0
BATCH = 4

f32 = jnp.float32
bf16 = jnp.bfloat16
MIB = 1024 * 1024
LIMIT = 40


def halves(table, axis):
    high = table.astype(ml_dtypes.bfloat16)
    low = (table - high.astype(np.float64)).astype(ml_dtypes.bfloat16)
    return np.concatenate([high, low], axis=axis)


def analysis(freqs, points, shift):
    f = np.arange(freqs)[:, None]
    n = np.arange(points)[None, :] - shift
    angle = 2.0 * math.pi * ((f * n) % freqs) / freqs
    cos, sin = np.cos(angle), np.sin(angle)
    return np.block([[cos, sin], [-sin, cos]])


def synthesis(freqs, points, shift, scale=1.0):
    return analysis(freqs, points, shift).T * scale


def grouped(freqs, lanes):
    head, tail = np.arange(lanes), np.arange(lanes, freqs)
    return np.concatenate([head, freqs + head, tail, freqs + tail])


def split(x):
    high = x.astype(bf16)
    low = (x - high.astype(f32)).astype(bf16)
    return high, low


def dot(left, right, piece):
    parts = [
        jnp.dot(left[at:at + piece], right, preferred_element_type=f32)
        for at in range(0, left.shape[0], piece)
    ]
    return jnp.concatenate(parts, axis=0)


def over_rows(table, x, piece):
    high, low = split(x)
    left = table[...]
    left = jnp.concatenate([left, left[:, :x.shape[0]]], axis=1)
    return dot(left, jnp.concatenate([high, high, low], axis=0), piece)


def over_lanes(x, table, piece):
    high, low = split(x)
    right = table[...]
    right = jnp.concatenate([right, right[:x.shape[1]]], axis=0)
    return dot(jnp.concatenate([high, high, low], axis=1), right, piece)


def to_freqs(x, head, tail, piece):
    high, low = split(x)
    depth = x.shape[1]
    right = head[...]
    right = jnp.concatenate([right, right[:depth]], axis=0)
    first = dot(jnp.concatenate([high, high, low], axis=1), right, piece)
    right = tail[...]
    rest = dot(jnp.concatenate([high, low], axis=1), jnp.concatenate([right, right], axis=0), piece)
    lanes = rest.shape[1] // 2
    return first, rest[:, :lanes] + rest[:, lanes:]


def side(x):
    rows = x.shape[0] // 2
    return jnp.concatenate([x[:rows], x[rows:]], axis=1)


def dft(planes, row_tab, head, tail, piece):
    width = planes.shape[0] // 2
    half = over_rows(row_tab, planes, piece)
    tiles = [side(half[:, at:at + width]) for at in range(0, planes.shape[1], width)]
    rows = tiles[0].shape[0]
    first, rest = to_freqs(jnp.concatenate(tiles, axis=0), head, tail, piece)
    return [(first[j * rows:(j + 1) * rows], rest[j * rows:(j + 1) * rows]) for j in range(len(tiles))]


def swap(x):
    return pltpu.roll(x, x.shape[1] // 2, 1)


def spectra_body(radii, taps, row_tab, head, tail, spec):
    batch, _, span, _ = taps.shape
    first = pl.program_id(0) * batch
    row_at = lax.broadcasted_iota(jnp.int32, (span, span), 0) - span // 2
    col_at = lax.broadcasted_iota(jnp.int32, (span, span), 1) - span // 2
    reach = jnp.maximum(jnp.maximum(row_at, -1 - row_at), jnp.maximum(col_at, -1 - col_at))
    planes = []
    for k in range(batch):
        inside = reach < radii[first + k]
        parts = [jnp.where(inside, taps[k, c], 0.0) for c in range(2)]
        planes.append(jnp.concatenate(parts, axis=0))
    for k, (a, b) in enumerate(dft(jnp.concatenate(planes, axis=1), row_tab, head, tail, 256)):
        spec[k, :, :a.shape[1]] = a
        spec[k, :, a.shape[1]:] = b


def main_body(
    group, weight, place,
    own, near, far, target, mask_row, mask_head, mask_tail, spec_far, *rest,
):
    tables_far, rest = rest[:7], rest[7:]
    resist, grad_own, near_rim, far_rim = rest[:4]
    spec, field, mask_spec, slopes, grad_spec, spec_sems, table_sems = rest[4:11]
    tables = rest[11:]
    kernels, grid_rows, _ = spec.shape
    count, width = target.shape
    rim = (grid_rows - count) // 2
    steps = spec_sems.shape[0]
    batch = kernels // steps

    def fetch(i):
        here = pl.ds(i * batch, batch)
        return pltpu.make_async_copy(spec_far.at[here], spec.at[here], spec_sems.at[i])

    def fetch_table(i):
        return pltpu.make_async_copy(tables_far[i], tables[i], table_sems.at[i])

    col_inv, row_inv, row_tab, head, tail, grad_col, grad_row = tables
    for i in range(2):
        fetch_table(i).start()
    for i in range(steps):
        fetch(i).start()
    for i in range(2, 7):
        fetch_table(i).start()

    odd = place[0] % 2 == 1
    parts = []
    for c in range(2):
        above = jnp.where(odd, near[c, count - rim:], far[c, count - rim:])
        below = jnp.where(odd, far[c, :rim], near[c, :rim])
        parts += [above, own[c], below]
    mask = jnp.concatenate(parts, axis=0)
    m_first, m_rest = to_freqs(side(over_rows(mask_row, mask, 256)), mask_head, mask_tail, 256)
    lane = lax.broadcasted_iota(jnp.int32, m_rest.shape, 1)
    real_half = lane < m_rest.shape[1] // 2
    turned = swap(m_rest)
    mask_spec[:, :2 * width] = m_first
    mask_spec[:, 2 * width:3 * width] = jnp.where(real_half, m_rest, turned)
    mask_spec[:, 3 * width:] = jnp.where(real_half, -turned, m_rest)

    slopes[...] = jnp.zeros(slopes.shape, f32)
    grad_spec[...] = jnp.zeros(grad_spec.shape, f32)
    for i in range(2):
        fetch_table(i).wait()

    def forward(i, carry):
        fetch(i).wait()
        m_re, m_im = mask_spec[:, :width], mask_spec[:, width:2 * width]
        m_same, m_cross = mask_spec[:, 2 * width:3 * width], mask_spec[:, 3 * width:]
        products = []
        for j in range(batch):
            k = i * batch + j
            s_re, s_im, s_rest = spec[k, :, :width], spec[k, :, width:2 * width], spec[k, :, 2 * width:]
            products.append(jnp.concatenate([
                s_re * m_re - s_im * m_im,
                s_re * m_im + s_im * m_re,
                s_rest * m_same + swap(s_rest) * m_cross,
            ], axis=1))
        back = over_lanes(jnp.concatenate(products, axis=0), col_inv, 256)
        mine = []
        for c in range(2):
            planes = [back[j * grid_rows:(j + 1) * grid_rows, c * width:(c + 1) * width] for j in range(batch)]
            mine.append(jnp.concatenate(planes, axis=1))
        found = over_rows(row_inv, jnp.concatenate(mine, axis=0), 256)
        field[i] = found
        power = found[:count] * found[:count] + found[count:] * found[count:]
        for j in range(batch):
            k = i * batch + j
            g = group[k]
            slopes[g] = slopes[g] + weight[k] * power[:, j * width:(j + 1) * width]
        return carry

    lax.fori_loop(0, steps, forward, 0)

    wanted = target[...].astype(f32)
    for g in range(GROUPS):
        seen = jax.nn.sigmoid(STEEPNESS * (slopes[g] - THRESHOLD))
        resist[g] = seen
        slopes[g] = 2.0 * (seen - wanted) * seen * (1.0 - seen) * STEEPNESS
    for i in range(2, 7):
        fetch_table(i).wait()

    def backward(i, carry):
        factors = []
        for j in range(batch):
            k = i * batch + j
            factors.append((2.0 * weight[k]) * slopes[group[k]])
        factor = jnp.concatenate(factors, axis=1)
        cot = field[i] * jnp.concatenate([factor, factor], axis=0)
        found = dft(cot, row_tab, head, tail, 256)
        total = [grad_spec[:, c * width:(c + 1) * width] for c in range(4)]
        for j in range(batch):
            k = i * batch + j
            s_re, s_im, s_rest = spec[k, :, :width], spec[k, :, width:2 * width], spec[k, :, 2 * width:]
            first, rest = found[j]
            c_re, c_im = first[:, :width], first[:, width:]
            total[0] = total[0] + (s_re * c_re + s_im * c_im)
            total[1] = total[1] + (s_re * c_im - s_im * c_re)
            total[2] = total[2] + s_rest * rest
            total[3] = total[3] + s_rest * swap(rest)
        for c in range(4):
            grad_spec[:, c * width:(c + 1) * width] = total[c]
        return carry

    lax.fori_loop(0, steps, backward, 0)

    same, cross = grad_spec[:, 2 * width:3 * width], grad_spec[:, 3 * width:]
    tail_sum = jnp.where(real_half, same + swap(same), swap(cross) - cross)
    total = jnp.concatenate([grad_spec[:, :2 * width], tail_sum], axis=1)
    back = over_lanes(total, grad_col, 256)
    full = over_rows(grad_row, jnp.concatenate([back[:, :width], back[:, width:]], axis=0), 256)
    for c in range(2):
        base = c * grid_rows
        rise, fall = full[base:base + rim], full[base + rim + count:base + grid_rows]
        near_rim[c] = jnp.where(odd, rise, fall)
        far_rim[c] = jnp.where(odd, fall, rise)
        grad_own[c] = full[base + rim:base + rim + count]


def on_device(mask_field, target, kernel_taps, kernel_radii, kernel_group, kernel_weight):
    _, count, width = mask_field.shape
    kernels, _, span, _ = kernel_taps.shape
    rim = span // 2
    grid_rows = count + 2 * rim
    grid_cols = width + rim
    assert count == span and width == span and kernels % BATCH == 0

    strips = lax.axis_size("row")
    assert strips % 2 == 0
    at = lax.axis_index("row")
    odd = at % 2 == 1
    near_pairs = [(i, i ^ 1) for i in range(strips)]
    far_pairs = [(i, ((i + 1) ^ 1) - 1) for i in range(1, strips - 1)]
    near = lax.ppermute(mask_field, "row", near_pairs)
    far = lax.ppermute(mask_field, "row", far_pairs)
    place = at.astype(jnp.int32).reshape(1)

    scale = 1.0 / (grid_rows * grid_cols)
    order = grouped(grid_cols, width)

    def head_and_tail(shift):
        table = analysis(grid_cols, width, shift).T[:, order]
        return halves(table[:, :2 * width], 0), halves(table[:, 2 * width:], 1)

    row_tab = halves(analysis(grid_rows, span, 0), 1)
    head, tail = head_and_tail(0)
    mask_row = halves(analysis(grid_rows, grid_rows, 2 * rim), 1)
    mask_head, mask_tail = head_and_tail(rim)
    col_inv = halves(synthesis(grid_cols, width, 0).T[order], 0)
    row_inv = halves(synthesis(grid_rows, count, 0, scale), 1)
    grad_col = halves(synthesis(grid_cols, width, rim).T[order], 0)
    grad_row = halves(synthesis(grid_rows, grid_rows, 2 * rim, scale), 1)

    smem = pl.BlockSpec(memory_space=pltpu.SMEM)
    vmem = pl.BlockSpec(memory_space=pltpu.VMEM)
    anywhere = pl.BlockSpec(memory_space=pl.ANY)
    spectra = pl.pallas_call(
        spectra_body,
        grid=(kernels // BATCH,),
        out_shape=jax.ShapeDtypeStruct((kernels, grid_rows, 2 * grid_cols), f32),
        in_specs=[smem, pl.BlockSpec((BATCH, 2, span, span), lambda i: (i, 0, 0, 0)), vmem, vmem, vmem],
        out_specs=pl.BlockSpec((BATCH, grid_rows, 2 * grid_cols), lambda i: (i, 0, 0)),
        compiler_params=pltpu.CompilerParams(vmem_limit_bytes=56 * MIB),
        cost_estimate=pl.CostEstimate(flops=18 * 10**9, bytes_accessed=14 * 10**6, transcendentals=0),
        name="spectra",
    )(kernel_radii, kernel_taps, *map(jnp.asarray, (row_tab, head, tail)))

    late = [jnp.asarray(t) for t in (col_inv, row_inv, row_tab, head, tail, grad_col, grad_row)]
    resist, own, near_rim, far_rim = pl.pallas_call(
        main_body,
        out_shape=[
            jax.ShapeDtypeStruct((GROUPS, count, width), f32),
            jax.ShapeDtypeStruct((2, count, width), f32),
            jax.ShapeDtypeStruct((2, rim, width), f32),
            jax.ShapeDtypeStruct((2, rim, width), f32),
        ],
        in_specs=[smem] * 3 + [vmem] * 7 + [anywhere] * 8,
        out_specs=[vmem] * 4,
        scratch_shapes=[
            pltpu.VMEM((kernels, grid_rows, 2 * grid_cols), f32),
            pltpu.VMEM((kernels // BATCH, 2 * count, BATCH * width), f32),
            pltpu.VMEM((grid_rows, 4 * width), f32),
            pltpu.VMEM((GROUPS, count, width), f32),
            pltpu.VMEM((grid_rows, 4 * width), f32),
            pltpu.SemaphoreType.DMA((kernels // BATCH,)),
            pltpu.SemaphoreType.DMA((len(late),)),
        ] + [pltpu.VMEM(t.shape, bf16) for t in late],
        compiler_params=pltpu.CompilerParams(vmem_limit_bytes=LIMIT * MIB),
        name="fields",
    )(
        kernel_group, kernel_weight, place, mask_field, near, far, target,
        *map(jnp.asarray, (mask_row, mask_head, mask_tail)), spectra, *late,
    )

    near_in = lax.ppermute(near_rim, "row", near_pairs)
    far_in = lax.ppermute(far_rim, "row", far_pairs)
    from_above = jnp.where(odd, near_in, far_in)
    from_below = jnp.where(odd, far_in, near_in)
    gradient = (
        own
        + jnp.pad(from_above, ((0, 0), (0, count - rim), (0, 0)))
        + jnp.pad(from_below, ((0, 0), (count - rim, 0), (0, 0)))
    )
    return resist, gradient


def solution(mesh):
    in_specs = (P(None, ("win", "row"), None), P(("win", "row"), None), P(), P(), P(), P())
    out_specs = (P(None, ("win", "row"), None), P(None, ("win", "row"), None))
    return jax.shard_map(
        on_device, mesh=mesh, in_specs=in_specs, out_specs=out_specs, check_vma=False
    )
```

```python
import math

import jax
import jax.numpy as jnp
import ml_dtypes
import numpy as np
from jax import lax
from jax.experimental import pallas as pl
from jax.experimental.pallas import tpu as pltpu
from jax.sharding import PartitionSpec as P

RMAX = 64
GROUPS = 3
STEEPNESS = 1.0
THRESHOLD = 2.0
BATCH = 8
PIECE = 256

f32 = jnp.float32
bf16 = jnp.bfloat16
MIB = 1024 * 1024
LIMIT = 40


def halves(table, axis):
    high = table.astype(ml_dtypes.bfloat16)
    low = (table - high.astype(np.float64)).astype(ml_dtypes.bfloat16)
    return np.concatenate([high, low], axis=axis)


def analysis(freqs, points, shift):
    f = np.arange(freqs)[:, None]
    n = np.arange(points)[None, :] - shift
    angle = 2.0 * math.pi * ((f * n) % freqs) / freqs
    cos, sin = np.cos(angle), np.sin(angle)
    return np.block([[cos, sin], [-sin, cos]])


def synthesis(freqs, points, shift, scale=1.0):
    return analysis(freqs, points, shift).T * scale


def grouped(freqs, lanes):
    head, tail = np.arange(lanes), np.arange(lanes, freqs)
    return np.concatenate([head, freqs + head, tail, freqs + tail])


def split(x):
    high = x.astype(bf16)
    low = (x - high.astype(f32)).astype(bf16)
    return high, low


def dot(left, right):
    parts = [
        jnp.dot(left[at:at + PIECE], right, preferred_element_type=f32)
        for at in range(0, left.shape[0], PIECE)
    ]
    return jnp.concatenate(parts, axis=0)


def over_rows(table, x):
    high, low = split(x)
    left = table[...]
    left = jnp.concatenate([left, left[:, :x.shape[0]]], axis=1)
    return dot(left, jnp.concatenate([high, high, low], axis=0))


def over_lanes(x, table):
    high, low = split(x)
    right = table[...]
    right = jnp.concatenate([right, right[:x.shape[1]]], axis=0)
    return dot(jnp.concatenate([high, high, low], axis=1), right)


def to_freqs(x, head, tail):
    high, low = split(x)
    right = head[...]
    right = jnp.concatenate([right, right[:x.shape[1]]], axis=0)
    first = dot(jnp.concatenate([high, high, low], axis=1), right)
    right = tail[...]
    rest = dot(jnp.concatenate([high, low], axis=1), jnp.concatenate([right, right], axis=0))
    lanes = rest.shape[1] // 2
    return first, rest[:, :lanes] + rest[:, lanes:]


def side(x):
    rows = x.shape[0] // 2
    return jnp.concatenate([x[:rows], x[rows:]], axis=1)


def row_stage(pair, row_tab):
    width = pair.shape[1] // 2
    half = over_rows(row_tab, pair)
    return [side(half[:, :width]), side(half[:, width:])]


def staggered(count, first, second):
    held = None
    for i in range(count):
        new = first(i)
        if i:
            second(i - 1, held)
        held = new
    second(count - 1, held)


def swap(x):
    return pltpu.roll(x, x.shape[1] // 2, 1)


def spectra_body(radii, taps, row_tab, head, tail, spec):
    batch, _, span, _ = taps.shape
    first = pl.program_id(0) * batch
    row_at = lax.broadcasted_iota(jnp.int32, (span, span), 0) - span // 2
    col_at = lax.broadcasted_iota(jnp.int32, (span, span), 1) - span // 2
    reach = jnp.maximum(jnp.maximum(row_at, -1 - row_at), jnp.maximum(col_at, -1 - col_at))

    def rows_of(p):
        planes = []
        for k in (2 * p, 2 * p + 1):
            inside = reach < radii[first + k]
            parts = [jnp.where(inside, taps[k, c], 0.0) for c in range(2)]
            planes.append(jnp.concatenate(parts, axis=0))
        return row_stage(jnp.concatenate(planes, axis=1), row_tab)

    def cols_of(p, tiles):
        for j in range(2):
            a, b = to_freqs(tiles[j], head, tail)
            spec[2 * p + j, :, :a.shape[1]] = a
            spec[2 * p + j, :, a.shape[1]:] = b

    staggered(batch // 2, rows_of, cols_of)


def main_body(
    group, weight, place,
    own, near, far, target, mask_row, mask_head, mask_tail, spec_far, *rest,
):
    tables_far, rest = rest[:7], rest[7:]
    resist_far, grad_own, near_rim, far_rim = rest[:4]
    spec, field, mask_spec, resist, slopes, grad_spec, spec_sems, table_sems, out_sem = rest[4:13]
    tables = rest[13:]
    kernels, grid_rows, _ = spec.shape
    count, width = target.shape
    rim = (grid_rows - count) // 2
    steps = spec_sems.shape[0]
    batch = kernels // steps

    def fetch(i):
        here = pl.ds(i * batch, batch)
        return pltpu.make_async_copy(spec_far.at[here], spec.at[here], spec_sems.at[i])

    def fetch_table(i):
        return pltpu.make_async_copy(tables_far[i], tables[i], table_sems.at[i])

    col_inv, row_inv, row_tab, head, tail, grad_col, grad_row = tables
    for i in range(2):
        fetch_table(i).start()
    for i in range(steps):
        fetch(i).start()
    for i in range(2, 7):
        fetch_table(i).start()

    odd = place[0] % 2 == 1
    parts = []
    for c in range(2):
        above = jnp.where(odd, near[c, count - rim:], far[c, count - rim:])
        below = jnp.where(odd, far[c, :rim], near[c, :rim])
        parts += [above, own[c], below]
    mask = jnp.concatenate(parts, axis=0)
    m_first, m_rest = to_freqs(side(over_rows(mask_row, mask)), mask_head, mask_tail)
    lane = lax.broadcasted_iota(jnp.int32, m_rest.shape, 1)
    real_half = lane < m_rest.shape[1] // 2
    turned = swap(m_rest)
    mask_spec[:, :2 * width] = m_first
    mask_spec[:, 2 * width:3 * width] = jnp.where(real_half, m_rest, turned)
    mask_spec[:, 3 * width:] = jnp.where(real_half, -turned, m_rest)

    slopes[...] = jnp.zeros(slopes.shape, f32)
    grad_spec[...] = jnp.zeros(grad_spec.shape, f32)
    for i in range(2):
        fetch_table(i).wait()

    def forward(i, carry):
        fetch(i).wait()
        m_re, m_im = mask_spec[:, :width], mask_spec[:, width:2 * width]
        m_same, m_cross = mask_spec[:, 2 * width:3 * width], mask_spec[:, 3 * width:]

        def cols_of(p):
            planes = []
            for j in range(2):
                k = i * batch + 2 * p + j
                s_re, s_im, s_rest = spec[k, :, :width], spec[k, :, width:2 * width], spec[k, :, 2 * width:]
                product = jnp.concatenate([
                    s_re * m_re - s_im * m_im,
                    s_re * m_im + s_im * m_re,
                    s_rest * m_same + swap(s_rest) * m_cross,
                ], axis=1)
                back = over_lanes(product, col_inv)
                planes.append(jnp.concatenate([back[:, :width], back[:, width:]], axis=0))
            return jnp.concatenate(planes, axis=1)

        def rows_of(p, pair):
            found = over_rows(row_inv, pair)
            field[i * (batch // 2) + p] = found
            power = found[:count] * found[:count] + found[count:] * found[count:]
            for j in range(2):
                k = i * batch + 2 * p + j
                g = group[k]
                slopes[g] = slopes[g] + weight[k] * power[:, j * width:(j + 1) * width]

        staggered(batch // 2, cols_of, rows_of)
        return carry

    lax.fori_loop(0, steps, forward, 0)

    wanted = target[...].astype(f32)
    for g in range(GROUPS):
        seen = jax.nn.sigmoid(STEEPNESS * (slopes[g] - THRESHOLD))
        resist[g] = seen
        slopes[g] = 2.0 * (seen - wanted) * seen * (1.0 - seen) * STEEPNESS
    out = pltpu.make_async_copy(resist, resist_far, out_sem)
    out.start()
    for i in range(2, 7):
        fetch_table(i).wait()

    def backward(i, carry):
        def rows_of(p):
            factors = []
            for j in range(2):
                k = i * batch + 2 * p + j
                factors.append((2.0 * weight[k]) * slopes[group[k]])
            factor = jnp.concatenate(factors, axis=1)
            cot = field[i * (batch // 2) + p] * jnp.concatenate([factor, factor], axis=0)
            return row_stage(cot, row_tab)

        def cols_of(p, tiles):
            total = [grad_spec[:, c * width:(c + 1) * width] for c in range(4)]
            for j in range(2):
                k = i * batch + 2 * p + j
                s_re, s_im, s_rest = spec[k, :, :width], spec[k, :, width:2 * width], spec[k, :, 2 * width:]
                first, rest = to_freqs(tiles[j], head, tail)
                c_re, c_im = first[:, :width], first[:, width:]
                total[0] = total[0] + (s_re * c_re + s_im * c_im)
                total[1] = total[1] + (s_re * c_im - s_im * c_re)
                total[2] = total[2] + s_rest * rest
                total[3] = total[3] + s_rest * swap(rest)
            for c in range(4):
                grad_spec[:, c * width:(c + 1) * width] = total[c]

        staggered(batch // 2, rows_of, cols_of)
        return carry

    lax.fori_loop(0, steps, backward, 0)

    same, cross = grad_spec[:, 2 * width:3 * width], grad_spec[:, 3 * width:]
    tail_sum = jnp.where(real_half, same + swap(same), swap(cross) - cross)
    total = jnp.concatenate([grad_spec[:, :2 * width], tail_sum], axis=1)
    back = over_lanes(total, grad_col)
    full = over_rows(grad_row, jnp.concatenate([back[:, :width], back[:, width:]], axis=0))
    for c in range(2):
        base = c * grid_rows
        rise, fall = full[base:base + rim], full[base + rim + count:base + grid_rows]
        near_rim[c] = jnp.where(odd, rise, fall)
        far_rim[c] = jnp.where(odd, fall, rise)
        grad_own[c] = full[base + rim:base + rim + count]
    out.wait()


def join_body(place, own, near, far, out):
    odd = place[0] % 2 == 1
    rim = near.shape[1]
    count = own.shape[1]
    for c in range(2):
        out[c, :rim] = own[c, :rim] + jnp.where(odd, near[c], far[c])
        if count > 2 * rim:
            out[c, rim:count - rim] = own[c, rim:count - rim]
        out[c, count - rim:] = own[c, count - rim:] + jnp.where(odd, far[c], near[c])


def on_device(mask_field, target, kernel_taps, kernel_radii, kernel_group, kernel_weight):
    _, count, width = mask_field.shape
    kernels, _, span, _ = kernel_taps.shape
    rim = span // 2
    grid_rows = count + 2 * rim
    grid_cols = width + rim
    assert count == span and width == span and kernels % BATCH == 0 and BATCH % 2 == 0 and count >= 2 * rim

    strips = lax.axis_size("row")
    assert strips % 2 == 0
    at = lax.axis_index("row")
    near_pairs = [(i, i ^ 1) for i in range(strips)]
    far_pairs = [(i, ((i + 1) ^ 1) - 1) for i in range(1, strips - 1)]
    near = lax.ppermute(mask_field, "row", near_pairs)
    far = lax.ppermute(mask_field, "row", far_pairs)
    place = at.astype(jnp.int32).reshape(1)

    scale = 1.0 / (grid_rows * grid_cols)
    order = grouped(grid_cols, width)

    def head_and_tail(shift):
        table = analysis(grid_cols, width, shift).T[:, order]
        return halves(table[:, :2 * width], 0), halves(table[:, 2 * width:], 1)

    row_tab = halves(analysis(grid_rows, span, 0), 1)
    head, tail = head_and_tail(0)
    mask_row = halves(analysis(grid_rows, grid_rows, 2 * rim), 1)
    mask_head, mask_tail = head_and_tail(rim)
    col_inv = halves(synthesis(grid_cols, width, 0).T[order], 0)
    row_inv = halves(synthesis(grid_rows, count, 0, scale), 1)
    grad_col = halves(synthesis(grid_cols, width, rim).T[order], 0)
    grad_row = halves(synthesis(grid_rows, grid_rows, 2 * rim, scale), 1)

    smem = pl.BlockSpec(memory_space=pltpu.SMEM)
    vmem = pl.BlockSpec(memory_space=pltpu.VMEM)
    hbm = pl.BlockSpec(memory_space=pltpu.HBM)
    spectra = pl.pallas_call(
        spectra_body,
        grid=(kernels // BATCH,),
        out_shape=jax.ShapeDtypeStruct((kernels, grid_rows, 2 * grid_cols), f32),
        in_specs=[smem, pl.BlockSpec((BATCH, 2, span, span), lambda i: (i, 0, 0, 0)), vmem, vmem, vmem],
        out_specs=pl.BlockSpec((BATCH, grid_rows, 2 * grid_cols), lambda i: (i, 0, 0)),
        compiler_params=pltpu.CompilerParams(vmem_limit_bytes=56 * MIB),
        cost_estimate=pl.CostEstimate(flops=18 * 10**9, bytes_accessed=14 * 10**6, transcendentals=0),
        name="spectra",
    )(kernel_radii, kernel_taps, *map(jnp.asarray, (row_tab, head, tail)))

    late = [jnp.asarray(t) for t in (col_inv, row_inv, row_tab, head, tail, grad_col, grad_row)]
    resist, own, near_rim, far_rim = pl.pallas_call(
        main_body,
        out_shape=[
            jax.ShapeDtypeStruct((GROUPS, count, width), f32),
            jax.ShapeDtypeStruct((2, count, width), f32),
            jax.ShapeDtypeStruct((2, rim, width), f32),
            jax.ShapeDtypeStruct((2, rim, width), f32),
        ],
        in_specs=[smem] * 3 + [vmem] * 7 + [hbm] * 8,
        out_specs=[hbm] + [vmem] * 3,
        scratch_shapes=[
            pltpu.VMEM((kernels, grid_rows, 2 * grid_cols), f32),
            pltpu.VMEM((kernels // 2, 2 * count, 2 * width), f32),
            pltpu.VMEM((grid_rows, 4 * width), f32),
            pltpu.VMEM((GROUPS, count, width), f32),
            pltpu.VMEM((GROUPS, count, width), f32),
            pltpu.VMEM((grid_rows, 4 * width), f32),
            pltpu.SemaphoreType.DMA((kernels // BATCH,)),
            pltpu.SemaphoreType.DMA((len(late),)),
            pltpu.SemaphoreType.DMA,
        ] + [pltpu.VMEM(t.shape, bf16) for t in late],
        compiler_params=pltpu.CompilerParams(vmem_limit_bytes=LIMIT * MIB),
        name="fields",
    )(
        kernel_group, kernel_weight, place, mask_field, near, far, target,
        *map(jnp.asarray, (mask_row, mask_head, mask_tail)), spectra, *late,
    )

    near_in = lax.ppermute(near_rim, "row", near_pairs)
    far_in = lax.ppermute(far_rim, "row", far_pairs)
    gradient = pl.pallas_call(
        join_body,
        out_shape=jax.ShapeDtypeStruct((2, count, width), f32),
        in_specs=[smem] + [vmem] * 3,
        out_specs=vmem,
        name="join",
    )(place, own, near_in, far_in)
    return resist, gradient


def solution(mesh):
    in_specs = (P(None, ("win", "row"), None), P(("win", "row"), None), P(), P(), P(), P())
    out_specs = (P(None, ("win", "row"), None), P(None, ("win", "row"), None))
    return jax.shard_map(
        on_device, mesh=mesh, in_specs=in_specs, out_specs=out_specs, check_vma=False
    )
```

```python
import functools
import math

import jax
import jax.numpy as jnp
import ml_dtypes
import numpy as np
from jax import lax
from jax.experimental import pallas as pl
from jax.experimental.pallas import tpu as pltpu
from jax.sharding import PartitionSpec as P

RMAX = 64
GROUPS = 3
STEEPNESS = 1.0
THRESHOLD = 2.0
BATCH = 8
PIECE = 256

f32 = jnp.float32
bf16 = jnp.bfloat16
MIB = 1024 * 1024
LIMIT = 40


def halves(table, axis):
    high = table.astype(ml_dtypes.bfloat16)
    low = (table - high.astype(np.float64)).astype(ml_dtypes.bfloat16)
    return np.concatenate([high, low], axis=axis)


def analysis(freqs, points, shift):
    f = np.arange(freqs)[:, None]
    n = np.arange(points)[None, :] - shift
    angle = 2.0 * math.pi * ((f * n) % freqs) / freqs
    cos, sin = np.cos(angle), np.sin(angle)
    return np.block([[cos, sin], [-sin, cos]])


def synthesis(freqs, points, shift, scale=1.0):
    return analysis(freqs, points, shift).T * scale


def grouped(freqs, lanes):
    head, tail = np.arange(lanes), np.arange(lanes, freqs)
    return np.concatenate([head, freqs + head, tail, freqs + tail])


def split(x):
    high = x.astype(bf16)
    low = (x - high.astype(f32)).astype(bf16)
    return high, low


def dot(left, right):
    parts = [
        jnp.dot(left[at:at + PIECE], right, preferred_element_type=f32)
        for at in range(0, left.shape[0], PIECE)
    ]
    return jnp.concatenate(parts, axis=0)


def over_rows(table, x):
    high, low = split(x)
    left = jnp.concatenate([table, table[:, :x.shape[0]]], axis=1)
    return dot(left, jnp.concatenate([high, high, low], axis=0))


def over_lanes(x, table):
    high, low = split(x)
    right = jnp.concatenate([table, table[:x.shape[1]]], axis=0)
    return dot(jnp.concatenate([high, high, low], axis=1), right)


def to_freqs(x, head, tail):
    high, low = split(x)
    right = jnp.concatenate([head, head[:x.shape[1]]], axis=0)
    first = dot(jnp.concatenate([high, high, low], axis=1), right)
    rest = dot(jnp.concatenate([high, low], axis=1), jnp.concatenate([tail, tail], axis=0))
    lanes = rest.shape[1] // 2
    return first, rest[:, :lanes] + rest[:, lanes:]


def side(x):
    rows = x.shape[0] // 2
    return jnp.concatenate([x[:rows], x[rows:]], axis=1)


def row_stage(pair, row_tab):
    width = pair.shape[1] // 2
    half = over_rows(row_tab, pair)
    return [side(half[:, :width]), side(half[:, width:])]


def staggered(count, first, second):
    held = None
    for i in range(count):
        new = first(i)
        if i:
            second(i - 1, held)
        held = new
    second(count - 1, held)


def swap(x):
    return pltpu.roll(x, x.shape[1] // 2, 1)


def spectra_body(radii, taps, row_ref, head_ref, tail_ref, spec):
    batch, _, span, _ = taps.shape
    row_tab, head, tail = row_ref[...], head_ref[...], tail_ref[...]
    first = pl.program_id(0) * batch
    row_at = lax.broadcasted_iota(jnp.int32, (span, span), 0) - span // 2
    col_at = lax.broadcasted_iota(jnp.int32, (span, span), 1) - span // 2
    reach = jnp.maximum(jnp.maximum(row_at, -1 - row_at), jnp.maximum(col_at, -1 - col_at))

    def rows_of(p):
        planes = []
        for k in (2 * p, 2 * p + 1):
            inside = reach < radii[first + k]
            parts = [jnp.where(inside, taps[k, c], 0.0) for c in range(2)]
            planes.append(jnp.concatenate(parts, axis=0))
        return row_stage(jnp.concatenate(planes, axis=1), row_tab)

    def cols_of(p, tiles):
        for j in range(2):
            a, b = to_freqs(tiles[j], head, tail)
            spec[2 * p + j, :, :a.shape[1]] = a
            spec[2 * p + j, :, a.shape[1]:] = b

    staggered(batch // 2, rows_of, cols_of)


def main_body(
    group, weight, place,
    own, near, far, target, spec_far, tables_far,
    resist_far, grad_own, near_rim, far_rim,
    spec, field, mask_spec, resist, slopes, grad_spec, tables, spec_sems, table_sems, out_sem,
    *, layout, sections,
):
    kernels, grid_rows, _ = spec.shape
    count, width = target.shape
    rim = (grid_rows - count) // 2
    steps = spec_sems.shape[0]
    batch = kernels // steps

    def fetch(i):
        here = pl.ds(i * batch, batch)
        return pltpu.make_async_copy(spec_far.at[here], spec.at[here], spec_sems.at[i])

    def fetch_table(i):
        here = pl.ds(sections[i][0], sections[i][1])
        return pltpu.make_async_copy(tables_far.at[here], tables.at[here], table_sems.at[i])

    def table(name):
        start, rows, blocks = layout[name]
        parts = [tables[start + b * rows:start + (b + 1) * rows] for b in range(blocks)]
        return jnp.concatenate(parts, axis=1)

    fetch_table(0).start()
    fetch_table(1).start()
    for i in range(steps):
        fetch(i).start()
    fetch_table(2).start()
    fetch_table(0).wait()

    odd = place[0] % 2 == 1
    parts = []
    for c in range(2):
        above = jnp.where(odd, near[c, count - rim:], far[c, count - rim:])
        below = jnp.where(odd, far[c, :rim], near[c, :rim])
        parts += [above, own[c], below]
    mask = jnp.concatenate(parts, axis=0)
    m_first, m_rest = to_freqs(side(over_rows(table("mask_row"), mask)), table("mask_head"), table("mask_tail"))
    lane = lax.broadcasted_iota(jnp.int32, m_rest.shape, 1)
    real_half = lane < m_rest.shape[1] // 2
    turned = swap(m_rest)
    mask_spec[:, :2 * width] = m_first
    mask_spec[:, 2 * width:3 * width] = jnp.where(real_half, m_rest, turned)
    mask_spec[:, 3 * width:] = jnp.where(real_half, -turned, m_rest)

    slopes[...] = jnp.zeros(slopes.shape, f32)
    grad_spec[...] = jnp.zeros(grad_spec.shape, f32)
    fetch_table(1).wait()
    col_inv, row_inv = table("col_inv"), table("row_inv")

    def forward(i, carry):
        fetch(i).wait()
        m_re, m_im = mask_spec[:, :width], mask_spec[:, width:2 * width]
        m_same, m_cross = mask_spec[:, 2 * width:3 * width], mask_spec[:, 3 * width:]

        def cols_of(p):
            planes = []
            for j in range(2):
                k = i * batch + 2 * p + j
                s_re, s_im, s_rest = spec[k, :, :width], spec[k, :, width:2 * width], spec[k, :, 2 * width:]
                product = jnp.concatenate([
                    s_re * m_re - s_im * m_im,
                    s_re * m_im + s_im * m_re,
                    s_rest * m_same + swap(s_rest) * m_cross,
                ], axis=1)
                back = over_lanes(product, col_inv)
                planes.append(jnp.concatenate([back[:, :width], back[:, width:]], axis=0))
            return jnp.concatenate(planes, axis=1)

        def rows_of(p, pair):
            found = over_rows(row_inv, pair)
            field[i * (batch // 2) + p] = found
            power = found[:count] * found[:count] + found[count:] * found[count:]
            for j in range(2):
                k = i * batch + 2 * p + j
                g = group[k]
                slopes[g] = slopes[g] + weight[k] * power[:, j * width:(j + 1) * width]

        staggered(batch // 2, cols_of, rows_of)
        return carry

    lax.fori_loop(0, steps, forward, 0)

    wanted = target[...].astype(f32)
    for g in range(GROUPS):
        seen = jax.nn.sigmoid(STEEPNESS * (slopes[g] - THRESHOLD))
        resist[g] = seen
        slopes[g] = 2.0 * (seen - wanted) * seen * (1.0 - seen) * STEEPNESS
    out = pltpu.make_async_copy(resist, resist_far, out_sem)
    out.start()
    fetch_table(2).wait()
    row_tab, head, tail = table("row_tab"), table("head"), table("tail")

    def backward(i, carry):
        def rows_of(p):
            factors = []
            for j in range(2):
                k = i * batch + 2 * p + j
                factors.append((2.0 * weight[k]) * slopes[group[k]])
            factor = jnp.concatenate(factors, axis=1)
            cot = field[i * (batch // 2) + p] * jnp.concatenate([factor, factor], axis=0)
            return row_stage(cot, row_tab)

        def cols_of(p, tiles):
            total = [grad_spec[:, c * width:(c + 1) * width] for c in range(4)]
            for j in range(2):
                k = i * batch + 2 * p + j
                s_re, s_im, s_rest = spec[k, :, :width], spec[k, :, width:2 * width], spec[k, :, 2 * width:]
                first, rest = to_freqs(tiles[j], head, tail)
                c_re, c_im = first[:, :width], first[:, width:]
                total[0] = total[0] + (s_re * c_re + s_im * c_im)
                total[1] = total[1] + (s_re * c_im - s_im * c_re)
                total[2] = total[2] + s_rest * rest
                total[3] = total[3] + s_rest * swap(rest)
            for c in range(4):
                grad_spec[:, c * width:(c + 1) * width] = total[c]

        staggered(batch // 2, rows_of, cols_of)
        return carry

    lax.fori_loop(0, steps, backward, 0)

    same, cross = grad_spec[:, 2 * width:3 * width], grad_spec[:, 3 * width:]
    tail_sum = jnp.where(real_half, same + swap(same), swap(cross) - cross)
    total = jnp.concatenate([grad_spec[:, :2 * width], tail_sum], axis=1)
    back = over_lanes(total, table("grad_col"))
    full = over_rows(table("grad_row"), jnp.concatenate([back[:, :width], back[:, width:]], axis=0))
    for c in range(2):
        base = c * grid_rows
        rise, fall = full[base:base + rim], full[base + rim + count:base + grid_rows]
        near_rim[c] = jnp.where(odd, rise, fall)
        far_rim[c] = jnp.where(odd, fall, rise)
        grad_own[c] = full[base + rim:base + rim + count]
    out.wait()


def join_body(place, own, near, far, out):
    odd = place[0] % 2 == 1
    rim = near.shape[1]
    count = own.shape[1]
    for c in range(2):
        out[c, :rim] = own[c, :rim] + jnp.where(odd, near[c], far[c])
        if count > 2 * rim:
            out[c, rim:count - rim] = own[c, rim:count - rim]
        out[c, count - rim:] = own[c, count - rim:] + jnp.where(odd, far[c], near[c])


def stacked(groups):
    blocks, layout, sections, at = [], {}, [], 0
    for group in groups:
        start = at
        for name, table in group.items():
            rows, lanes = table.shape
            layout[name] = (at, rows, lanes // 256)
            for b in range(lanes // 256):
                blocks.append(table[:, b * 256:(b + 1) * 256])
            at += rows * (lanes // 256)
        sections.append((start, at - start))
    return np.concatenate(blocks, axis=0), layout, sections


def on_device(mask_field, target, kernel_taps, kernel_radii, kernel_group, kernel_weight):
    _, count, width = mask_field.shape
    kernels, _, span, _ = kernel_taps.shape
    rim = span // 2
    grid_rows = count + 2 * rim
    grid_cols = width + rim
    assert count == span and width == span and kernels % BATCH == 0 and BATCH % 2 == 0 and count >= 2 * rim

    strips = lax.axis_size("row")
    assert strips % 2 == 0
    at = lax.axis_index("row")
    near_pairs = [(i, i ^ 1) for i in range(strips)]
    far_pairs = [(i, ((i + 1) ^ 1) - 1) for i in range(1, strips - 1)]
    near = lax.ppermute(mask_field, "row", near_pairs)
    far = lax.ppermute(mask_field, "row", far_pairs)
    place = at.astype(jnp.int32).reshape(1)

    scale = 1.0 / (grid_rows * grid_cols)
    order = grouped(grid_cols, width)

    def head_and_tail(shift):
        table = analysis(grid_cols, width, shift).T[:, order]
        return halves(table[:, :2 * width], 0), halves(table[:, 2 * width:], 1)

    row_tab = halves(analysis(grid_rows, span, 0), 1)
    head, tail = head_and_tail(0)
    mask_row = halves(analysis(grid_rows, grid_rows, 2 * rim), 1)
    mask_head, mask_tail = head_and_tail(rim)
    col_inv = halves(synthesis(grid_cols, width, 0).T[order], 0)
    row_inv = halves(synthesis(grid_rows, count, 0, scale), 1)
    grad_col = halves(synthesis(grid_cols, width, rim).T[order], 0)
    grad_row = halves(synthesis(grid_rows, grid_rows, 2 * rim, scale), 1)

    smem = pl.BlockSpec(memory_space=pltpu.SMEM)
    vmem = pl.BlockSpec(memory_space=pltpu.VMEM)
    hbm = pl.BlockSpec(memory_space=pltpu.HBM)
    spectra = pl.pallas_call(
        spectra_body,
        grid=(kernels // BATCH,),
        out_shape=jax.ShapeDtypeStruct((kernels, grid_rows, 2 * grid_cols), f32),
        in_specs=[smem, pl.BlockSpec((BATCH, 2, span, span), lambda i: (i, 0, 0, 0)), vmem, vmem, vmem],
        out_specs=pl.BlockSpec((BATCH, grid_rows, 2 * grid_cols), lambda i: (i, 0, 0)),
        compiler_params=pltpu.CompilerParams(vmem_limit_bytes=56 * MIB),
        cost_estimate=pl.CostEstimate(flops=18 * 10**9, bytes_accessed=14 * 10**6, transcendentals=0),
        name="spectra",
    )(kernel_radii, kernel_taps, *map(jnp.asarray, (row_tab, head, tail)))

    tables, layout, sections = stacked([
        {"mask_row": mask_row, "mask_head": mask_head, "mask_tail": mask_tail},
        {"col_inv": col_inv, "row_inv": row_inv},
        {"row_tab": row_tab, "head": head, "tail": tail, "grad_col": grad_col, "grad_row": grad_row},
    ])
    resist, own, near_rim, far_rim = pl.pallas_call(
        functools.partial(main_body, layout=layout, sections=sections),
        out_shape=[
            jax.ShapeDtypeStruct((GROUPS, count, width), f32),
            jax.ShapeDtypeStruct((2, count, width), f32),
            jax.ShapeDtypeStruct((2, rim, width), f32),
            jax.ShapeDtypeStruct((2, rim, width), f32),
        ],
        in_specs=[smem] * 3 + [vmem] * 4 + [hbm] * 2,
        out_specs=[hbm] + [vmem] * 3,
        scratch_shapes=[
            pltpu.VMEM((kernels, grid_rows, 2 * grid_cols), f32),
            pltpu.VMEM((kernels // 2, 2 * count, 2 * width), f32),
            pltpu.VMEM((grid_rows, 4 * width), f32),
            pltpu.VMEM((GROUPS, count, width), f32),
            pltpu.VMEM((GROUPS, count, width), f32),
            pltpu.VMEM((grid_rows, 4 * width), f32),
            pltpu.VMEM(tables.shape, bf16),
            pltpu.SemaphoreType.DMA((kernels // BATCH,)),
            pltpu.SemaphoreType.DMA((len(sections),)),
            pltpu.SemaphoreType.DMA,
        ],
        compiler_params=pltpu.CompilerParams(vmem_limit_bytes=LIMIT * MIB),
        name="fields",
    )(kernel_group, kernel_weight, place, mask_field, near, far, target, spectra, jnp.asarray(tables))

    near_in = lax.ppermute(near_rim, "row", near_pairs)
    far_in = lax.ppermute(far_rim, "row", far_pairs)
    gradient = pl.pallas_call(
        join_body,
        out_shape=jax.ShapeDtypeStruct((2, count, width), f32),
        in_specs=[smem] + [vmem] * 3,
        out_specs=vmem,
        compiler_params=pltpu.CompilerParams(vmem_limit_bytes=4 * MIB),
        name="join",
    )(place, own, near_in, far_in)
    return resist, gradient


def solution(mesh):
    in_specs = (P(None, ("win", "row"), None), P(("win", "row"), None), P(), P(), P(), P())
    out_specs = (P(None, ("win", "row"), None), P(None, ("win", "row"), None))
    return jax.shard_map(
        on_device, mesh=mesh, in_specs=in_specs, out_specs=out_specs, check_vma=False
    )
```

```python
import functools
import math

import jax
import jax.numpy as jnp
import ml_dtypes
import numpy as np
from jax import lax
from jax.experimental import pallas as pl
from jax.experimental.pallas import tpu as pltpu
from jax.sharding import PartitionSpec as P

RMAX = 64
GROUPS = 3
STEEPNESS = 1.0
THRESHOLD = 2.0
BATCH = 8

f32 = jnp.float32
bf16 = jnp.bfloat16
MIB = 1024 * 1024


def halves(table, axis):
    high = table.astype(ml_dtypes.bfloat16)
    low = (table - high.astype(np.float64)).astype(ml_dtypes.bfloat16)
    return np.concatenate([high, low], axis=axis)


def analysis(freqs, points, shift):
    f = np.arange(freqs)[:, None]
    n = np.arange(points)[None, :] - shift
    angle = 2.0 * math.pi * ((f * n) % freqs) / freqs
    cos, sin = np.cos(angle), np.sin(angle)
    return np.block([[cos, sin], [-sin, cos]])


def synthesis(freqs, points, shift, scale=1.0):
    return analysis(freqs, points, shift).T * scale


def grouped(freqs, lanes):
    head, tail = np.arange(lanes), np.arange(lanes, freqs)
    return np.concatenate([head, freqs + head, tail, freqs + tail])


def split(x):
    high = x.astype(bf16)
    low = (x - high.astype(f32)).astype(bf16)
    return high, low


def dot(left, right, piece):
    parts = [
        jnp.dot(left[at:at + piece], right, preferred_element_type=f32)
        for at in range(0, left.shape[0], piece)
    ]
    return jnp.concatenate(parts, axis=0)


def over_rows(table, x, piece=128):
    high, low = split(x)
    left = jnp.concatenate([table, table[:, :x.shape[0]]], axis=1)
    return dot(left, jnp.concatenate([high, high, low], axis=0), piece)


def over_lanes(x, table, piece=128):
    high, low = split(x)
    right = jnp.concatenate([table, table[:x.shape[1]]], axis=0)
    return dot(jnp.concatenate([high, high, low], axis=1), right, piece)


def to_freqs(x, head, tail, piece=128):
    high, low = split(x)
    right = jnp.concatenate([head, head[:x.shape[1]]], axis=0)
    first = dot(jnp.concatenate([high, high, low], axis=1), right, piece)
    rest = dot(jnp.concatenate([high, low], axis=1), jnp.concatenate([tail, tail], axis=0), piece)
    lanes = rest.shape[1] // 2
    return first, rest[:, :lanes] + rest[:, lanes:]


def side(x):
    rows = x.shape[0] // 2
    return jnp.concatenate([x[:rows], x[rows:]], axis=1)


def row_stage(pair, row_tab, piece=128):
    width = pair.shape[1] // 2
    half = over_rows(row_tab, pair, piece)
    return [side(half[:, :width]), side(half[:, width:])]


def staggered(count, first, second):
    held = None
    for i in range(count):
        new = first(i)
        if i:
            second(i - 1, held)
        held = new
    second(count - 1, held)


def swap(x):
    return pltpu.roll(x, x.shape[1] // 2, 1)


def spectra_body(radii, taps, row_ref, head_ref, tail_ref, spec):
    batch, _, span, _ = taps.shape
    row_tab, head, tail = row_ref[...], head_ref[...], tail_ref[...]
    first = pl.program_id(0) * batch
    row_at = lax.broadcasted_iota(jnp.int32, (span, span), 0) - span // 2
    col_at = lax.broadcasted_iota(jnp.int32, (span, span), 1) - span // 2
    reach = jnp.maximum(jnp.maximum(row_at, -1 - row_at), jnp.maximum(col_at, -1 - col_at))

    def rows_of(p):
        planes = []
        for k in (2 * p, 2 * p + 1):
            inside = reach < radii[first + k]
            parts = [jnp.where(inside, taps[k, c], 0.0) for c in range(2)]
            planes.append(jnp.concatenate(parts, axis=0))
        return row_stage(jnp.concatenate(planes, axis=1), row_tab, 64)

    def cols_of(p, tiles):
        for j in range(2):
            a, b = to_freqs(tiles[j], head, tail, 64)
            spec[2 * p + j, :, :a.shape[1]] = a
            spec[2 * p + j, :, a.shape[1]:] = b

    staggered(batch // 2, rows_of, cols_of)


def main_body(
    group, weight, place,
    own, near, far, target, spec_far, tables_far,
    resist_far, grad_own, near_rim, far_rim,
    spec, field, mask_spec, resist, slopes, grad_spec, tables, spec_sems, table_sems, out_sem,
    *, layout, sections,
):
    kernels, grid_rows, _ = spec.shape
    count, width = target.shape
    rim = (grid_rows - count) // 2
    steps = spec_sems.shape[0]
    batch = kernels // steps

    def fetch(i):
        here = pl.ds(i * batch, batch)
        return pltpu.make_async_copy(spec_far.at[here], spec.at[here], spec_sems.at[i])

    def fetch_table(i):
        here = pl.ds(sections[i][0], sections[i][1])
        return pltpu.make_async_copy(tables_far.at[here], tables.at[here], table_sems.at[i])

    def table(name):
        start, rows, blocks = layout[name]
        parts = [tables[start + b * rows:start + (b + 1) * rows] for b in range(blocks)]
        return jnp.concatenate(parts, axis=1)

    fetch_table(0).start()
    fetch_table(1).start()
    for i in range(steps):
        fetch(i).start()
    fetch_table(2).start()
    fetch_table(0).wait()

    odd = place[0] % 2 == 1
    parts = []
    for c in range(2):
        above = jnp.where(odd, near[c, count - rim:], far[c, count - rim:])
        below = jnp.where(odd, far[c, :rim], near[c, :rim])
        parts += [above, own[c], below]
    mask = jnp.concatenate(parts, axis=0)
    m_first, m_rest = to_freqs(side(over_rows(table("mask_row"), mask)), table("mask_head"), table("mask_tail"))
    lane = lax.broadcasted_iota(jnp.int32, m_rest.shape, 1)
    real_half = lane < m_rest.shape[1] // 2
    turned = swap(m_rest)
    mask_spec[:, :2 * width] = m_first
    mask_spec[:, 2 * width:3 * width] = jnp.where(real_half, m_rest, turned)
    mask_spec[:, 3 * width:] = jnp.where(real_half, -turned, m_rest)

    slopes[...] = jnp.zeros(slopes.shape, f32)
    grad_spec[...] = jnp.zeros(grad_spec.shape, f32)
    fetch_table(1).wait()
    col_inv, row_inv = table("col_inv"), table("row_inv")

    def forward(i, carry):
        fetch(i).wait()
        m_re, m_im = mask_spec[:, :width], mask_spec[:, width:2 * width]
        m_same, m_cross = mask_spec[:, 2 * width:3 * width], mask_spec[:, 3 * width:]

        def cols_of(p):
            planes = []
            for j in range(2):
                k = i * batch + 2 * p + j
                s_re, s_im, s_rest = spec[k, :, :width], spec[k, :, width:2 * width], spec[k, :, 2 * width:]
                product = jnp.concatenate([
                    s_re * m_re - s_im * m_im,
                    s_re * m_im + s_im * m_re,
                    s_rest * m_same + swap(s_rest) * m_cross,
                ], axis=1)
                back = over_lanes(product, col_inv)
                planes.append(jnp.concatenate([back[:, :width], back[:, width:]], axis=0))
            return jnp.concatenate(planes, axis=1)

        def rows_of(p, pair):
            found = over_rows(row_inv, pair)
            field[i * (batch // 2) + p] = found
            power = found[:count] * found[:count] + found[count:] * found[count:]
            for j in range(2):
                k = i * batch + 2 * p + j
                g = group[k]
                slopes[g] = slopes[g] + weight[k] * power[:, j * width:(j + 1) * width]

        staggered(batch // 2, cols_of, rows_of)
        return carry

    lax.fori_loop(0, steps, forward, 0)

    wanted = target[...].astype(f32)
    for g in range(GROUPS):
        seen = jax.nn.sigmoid(STEEPNESS * (slopes[g] - THRESHOLD))
        resist[g] = seen
        slopes[g] = 2.0 * (seen - wanted) * seen * (1.0 - seen) * STEEPNESS
    out = pltpu.make_async_copy(resist, resist_far, out_sem)
    out.start()
    fetch_table(2).wait()
    row_tab, head, tail = table("row_tab"), table("head"), table("tail")

    def backward(i, carry):
        def rows_of(p):
            factors = []
            for j in range(2):
                k = i * batch + 2 * p + j
                factors.append((2.0 * weight[k]) * slopes[group[k]])
            factor = jnp.concatenate(factors, axis=1)
            cot = field[i * (batch // 2) + p] * jnp.concatenate([factor, factor], axis=0)
            return row_stage(cot, row_tab)

        def cols_of(p, tiles):
            total = [grad_spec[:, c * width:(c + 1) * width] for c in range(4)]
            for j in range(2):
                k = i * batch + 2 * p + j
                s_re, s_im, s_rest = spec[k, :, :width], spec[k, :, width:2 * width], spec[k, :, 2 * width:]
                first, rest = to_freqs(tiles[j], head, tail)
                c_re, c_im = first[:, :width], first[:, width:]
                total[0] = total[0] + (s_re * c_re + s_im * c_im)
                total[1] = total[1] + (s_re * c_im - s_im * c_re)
                total[2] = total[2] + s_rest * rest
                total[3] = total[3] + s_rest * swap(rest)
            for c in range(4):
                grad_spec[:, c * width:(c + 1) * width] = total[c]

        staggered(batch // 2, rows_of, cols_of)
        return carry

    lax.fori_loop(0, steps, backward, 0)

    same, cross = grad_spec[:, 2 * width:3 * width], grad_spec[:, 3 * width:]
    tail_sum = jnp.where(real_half, same + swap(same), swap(cross) - cross)
    total = jnp.concatenate([grad_spec[:, :2 * width], tail_sum], axis=1)
    back = over_lanes(total, table("grad_col"))
    full = over_rows(table("grad_row"), jnp.concatenate([back[:, :width], back[:, width:]], axis=0))
    for c in range(2):
        base = c * grid_rows
        rise, fall = full[base:base + rim], full[base + rim + count:base + grid_rows]
        near_rim[c] = jnp.where(odd, rise, fall)
        far_rim[c] = jnp.where(odd, fall, rise)
        grad_own[c] = full[base + rim:base + rim + count]
    out.wait()


def join_body(place, own, near, far, out):
    odd = place[0] % 2 == 1
    rim = near.shape[1]
    count = own.shape[1]
    for c in range(2):
        out[c, :rim] = own[c, :rim] + jnp.where(odd, near[c], far[c])
        if count > 2 * rim:
            out[c, rim:count - rim] = own[c, rim:count - rim]
        out[c, count - rim:] = own[c, count - rim:] + jnp.where(odd, far[c], near[c])


def stacked(groups):
    blocks, layout, sections, at = [], {}, [], 0
    for group in groups:
        start = at
        for name, table in group.items():
            rows, lanes = table.shape
            layout[name] = (at, rows, lanes // 256)
            for b in range(lanes // 256):
                blocks.append(table[:, b * 256:(b + 1) * 256])
            at += rows * (lanes // 256)
        sections.append((start, at - start))
    return np.concatenate(blocks, axis=0), layout, sections


def on_device(mask_field, target, kernel_taps, kernel_radii, kernel_group, kernel_weight):
    _, count, width = mask_field.shape
    kernels, _, span, _ = kernel_taps.shape
    rim = span // 2
    grid_rows = count + 2 * rim
    grid_cols = width + rim
    assert count == span and width == span and kernels % BATCH == 0 and BATCH % 2 == 0 and count >= 2 * rim

    strips = lax.axis_size("row")
    assert strips % 2 == 0
    at = lax.axis_index("row")
    near_pairs = [(i, i ^ 1) for i in range(strips)]
    far_pairs = [(i, ((i + 1) ^ 1) - 1) for i in range(1, strips - 1)]
    near = lax.ppermute(mask_field, "row", near_pairs)
    far = lax.ppermute(mask_field, "row", far_pairs)
    place = at.astype(jnp.int32).reshape(1)

    scale = 1.0 / (grid_rows * grid_cols)
    order = grouped(grid_cols, width)

    def head_and_tail(shift):
        table = analysis(grid_cols, width, shift).T[:, order]
        return halves(table[:, :2 * width], 0), halves(table[:, 2 * width:], 1)

    row_tab = halves(analysis(grid_rows, span, 0), 1)
    head, tail = head_and_tail(0)
    mask_row = halves(analysis(grid_rows, grid_rows, 2 * rim), 1)
    mask_head, mask_tail = head_and_tail(rim)
    col_inv = halves(synthesis(grid_cols, width, 0).T[order], 0)
    row_inv = halves(synthesis(grid_rows, count, 0, scale), 1)
    grad_col = halves(synthesis(grid_cols, width, rim).T[order], 0)
    grad_row = halves(synthesis(grid_rows, grid_rows, 2 * rim, scale), 1)

    smem = pl.BlockSpec(memory_space=pltpu.SMEM)
    vmem = pl.BlockSpec(memory_space=pltpu.VMEM)
    hbm = pl.BlockSpec(memory_space=pltpu.HBM)
    spectra = pl.pallas_call(
        spectra_body,
        grid=(kernels // BATCH,),
        out_shape=jax.ShapeDtypeStruct((kernels, grid_rows, 2 * grid_cols), f32),
        in_specs=[smem, pl.BlockSpec((BATCH, 2, span, span), lambda i: (i, 0, 0, 0)), vmem, vmem, vmem],
        out_specs=pl.BlockSpec((BATCH, grid_rows, 2 * grid_cols), lambda i: (i, 0, 0)),
        compiler_params=pltpu.CompilerParams(vmem_limit_bytes=56 * MIB),
        cost_estimate=pl.CostEstimate(flops=18 * 10**9, bytes_accessed=14 * 10**6, transcendentals=0),
        name="spectra",
    )(kernel_radii, kernel_taps, *map(jnp.asarray, (row_tab, head, tail)))

    tables, layout, sections = stacked([
        {"mask_row": mask_row, "mask_head": mask_head, "mask_tail": mask_tail},
        {"col_inv": col_inv, "row_inv": row_inv},
        {"row_tab": row_tab, "head": head, "tail": tail, "grad_col": grad_col, "grad_row": grad_row},
    ])
    resist, own, near_rim, far_rim = pl.pallas_call(
        functools.partial(main_body, layout=layout, sections=sections),
        out_shape=[
            jax.ShapeDtypeStruct((GROUPS, count, width), f32),
            jax.ShapeDtypeStruct((2, count, width), f32),
            jax.ShapeDtypeStruct((2, rim, width), f32),
            jax.ShapeDtypeStruct((2, rim, width), f32),
        ],
        in_specs=[smem] * 3 + [vmem] * 4 + [hbm] * 2,
        out_specs=[hbm] + [vmem] * 3,
        scratch_shapes=[
            pltpu.VMEM((kernels, grid_rows, 2 * grid_cols), f32),
            pltpu.VMEM((kernels // 2, 2 * count, 2 * width), f32),
            pltpu.VMEM((grid_rows, 4 * width), f32),
            pltpu.VMEM((GROUPS, count, width), f32),
            pltpu.VMEM((GROUPS, count, width), f32),
            pltpu.VMEM((grid_rows, 4 * width), f32),
            pltpu.VMEM(tables.shape, bf16),
            pltpu.SemaphoreType.DMA((kernels // BATCH,)),
            pltpu.SemaphoreType.DMA((len(sections),)),
            pltpu.SemaphoreType.DMA,
        ],
        compiler_params=pltpu.CompilerParams(vmem_limit_bytes=56 * MIB),
        name="fields",
    )(kernel_group, kernel_weight, place, mask_field, near, far, target, spectra, jnp.asarray(tables))

    near_in = lax.ppermute(near_rim, "row", near_pairs)
    far_in = lax.ppermute(far_rim, "row", far_pairs)
    gradient = pl.pallas_call(
        join_body,
        out_shape=jax.ShapeDtypeStruct((2, count, width), f32),
        in_specs=[smem] + [vmem] * 3,
        out_specs=vmem,
        compiler_params=pltpu.CompilerParams(vmem_limit_bytes=4 * MIB),
        name="join",
    )(place, own, near_in, far_in)
    return resist, gradient


def solution(mesh):
    in_specs = (P(None, ("win", "row"), None), P(("win", "row"), None), P(), P(), P(), P())
    out_specs = (P(None, ("win", "row"), None), P(None, ("win", "row"), None))
    return jax.shard_map(
        on_device, mesh=mesh, in_specs=in_specs, out_specs=out_specs, check_vma=False
    )
```

```python
import functools
import math

import jax
import jax.numpy as jnp
import ml_dtypes
import numpy as np
from jax import lax
from jax.experimental import pallas as pl
from jax.experimental.pallas import tpu as pltpu
from jax.sharding import PartitionSpec as P

RMAX = 64
GROUPS = 3
STEEPNESS = 1.0
THRESHOLD = 2.0
SPECTRA_BATCH = 12
BATCH = 24
PIECE = 256

f32 = jnp.float32
bf16 = jnp.bfloat16
MIB = 1024 * 1024
LIMIT = 40


def halves(table, axis):
    high = table.astype(ml_dtypes.bfloat16)
    low = (table - high.astype(np.float64)).astype(ml_dtypes.bfloat16)
    return np.concatenate([high, low], axis=axis)


def analysis(freqs, points, shift):
    f = np.arange(freqs)[:, None]
    n = np.arange(points)[None, :] - shift
    angle = 2.0 * math.pi * ((f * n) % freqs) / freqs
    cos, sin = np.cos(angle), np.sin(angle)
    return np.block([[cos, sin], [-sin, cos]])


def synthesis(freqs, points, shift, scale=1.0):
    return analysis(freqs, points, shift).T * scale


def grouped(freqs, lanes):
    head, tail = np.arange(lanes), np.arange(lanes, freqs)
    return np.concatenate([head, freqs + head, tail, freqs + tail])


def split(x):
    high = x.astype(bf16)
    low = (x - high.astype(f32)).astype(bf16)
    return high, low


def dot(left, right):
    parts = [
        jnp.dot(left[at:at + PIECE], right, preferred_element_type=f32)
        for at in range(0, left.shape[0], PIECE)
    ]
    return jnp.concatenate(parts, axis=0)


def over_rows(table, x):
    high, low = split(x)
    left = jnp.concatenate([table, table[:, :x.shape[0]]], axis=1)
    return dot(left, jnp.concatenate([high, high, low], axis=0))


def over_lanes(x, table):
    high, low = split(x)
    right = jnp.concatenate([table, table[:x.shape[1]]], axis=0)
    return dot(jnp.concatenate([high, high, low], axis=1), right)


def to_freqs(x, head, tail):
    high, low = split(x)
    right = jnp.concatenate([head, head[:x.shape[1]]], axis=0)
    first = dot(jnp.concatenate([high, high, low], axis=1), right)
    rest = dot(jnp.concatenate([high, low], axis=1), jnp.concatenate([tail, tail], axis=0))
    lanes = rest.shape[1] // 2
    return first, rest[:, :lanes] + rest[:, lanes:]


def side(x):
    rows = x.shape[0] // 2
    return jnp.concatenate([x[:rows], x[rows:]], axis=1)


def row_stage(pair, row_tab):
    width = pair.shape[1] // 2
    half = over_rows(row_tab, pair)
    return [side(half[:, :width]), side(half[:, width:])]


def loop(steps, body):
    if steps == 1:
        body(0, 0)
    else:
        lax.fori_loop(0, steps, body, 0)


def staggered(count, first, second):
    held = None
    for i in range(count):
        new = first(i)
        if i:
            second(i - 1, held)
        held = new
    second(count - 1, held)


def swap(x):
    return pltpu.roll(x, x.shape[1] // 2, 1)


def spectra_body(radii, taps, row_ref, head_ref, tail_ref, spec):
    batch, _, span, _ = taps.shape
    row_tab, head, tail = row_ref[...], head_ref[...], tail_ref[...]
    first = pl.program_id(0) * batch
    row_at = lax.broadcasted_iota(jnp.int32, (span, span), 0) - span // 2
    col_at = lax.broadcasted_iota(jnp.int32, (span, span), 1) - span // 2
    reach = jnp.maximum(jnp.maximum(row_at, -1 - row_at), jnp.maximum(col_at, -1 - col_at))

    def rows_of(p):
        planes = []
        for k in (2 * p, 2 * p + 1):
            inside = reach < radii[first + k]
            parts = [jnp.where(inside, taps[k, c], 0.0) for c in range(2)]
            planes.append(jnp.concatenate(parts, axis=0))
        return row_stage(jnp.concatenate(planes, axis=1), row_tab)

    def cols_of(p, tiles):
        for j in range(2):
            a, b = to_freqs(tiles[j], head, tail)
            spec[2 * p + j, :, :a.shape[1]] = a
            spec[2 * p + j, :, a.shape[1]:] = b

    staggered(batch // 2, rows_of, cols_of)


def main_body(
    group, weight, place,
    own, near, far, target, spec_far, tables_far,
    resist_far, grad_own, near_rim, far_rim,
    spec, field, mask_spec, resist, slopes, grad_spec, tables, spec_sems, table_sems, out_sem,
    *, layout, sections,
):
    kernels, grid_rows, _ = spec.shape
    count, width = target.shape
    rim = (grid_rows - count) // 2
    batch = BATCH
    steps = kernels // batch

    def fetch(i):
        here = pl.ds(2 * i, 2)
        return pltpu.make_async_copy(spec_far.at[here], spec.at[here], spec_sems.at[i])

    def fetch_table(i):
        here = pl.ds(sections[i][0], sections[i][1])
        return pltpu.make_async_copy(tables_far.at[here], tables.at[here], table_sems.at[i])

    def table(name):
        start, rows, blocks = layout[name]
        parts = [tables[start + b * rows:start + (b + 1) * rows] for b in range(blocks)]
        return jnp.concatenate(parts, axis=1)

    fetch_table(0).start()
    fetch_table(1).start()
    for i in range(kernels // 2):
        fetch(i).start()
    fetch_table(2).start()
    fetch_table(0).wait()

    odd = place[0] % 2 == 1
    parts = []
    for c in range(2):
        above = jnp.where(odd, near[c, count - rim:], far[c, count - rim:])
        below = jnp.where(odd, far[c, :rim], near[c, :rim])
        parts += [above, own[c], below]
    mask = jnp.concatenate(parts, axis=0)
    m_first, m_rest = to_freqs(side(over_rows(table("mask_row"), mask)), table("mask_head"), table("mask_tail"))
    lane = lax.broadcasted_iota(jnp.int32, m_rest.shape, 1)
    real_half = lane < m_rest.shape[1] // 2
    turned = swap(m_rest)
    mask_spec[:, :2 * width] = m_first
    mask_spec[:, 2 * width:3 * width] = jnp.where(real_half, m_rest, turned)
    mask_spec[:, 3 * width:] = jnp.where(real_half, -turned, m_rest)

    slopes[...] = jnp.zeros(slopes.shape, f32)
    grad_spec[...] = jnp.zeros(grad_spec.shape, f32)
    fetch_table(1).wait()
    col_inv, row_inv = table("col_inv"), table("row_inv")

    def forward(i, carry):
        m_re, m_im = mask_spec[:, :width], mask_spec[:, width:2 * width]
        m_same, m_cross = mask_spec[:, 2 * width:3 * width], mask_spec[:, 3 * width:]

        def cols_of(p):
            fetch(i * (batch // 2) + p).wait()
            planes = []
            for j in range(2):
                k = i * batch + 2 * p + j
                s_re, s_im, s_rest = spec[k, :, :width], spec[k, :, width:2 * width], spec[k, :, 2 * width:]
                product = jnp.concatenate([
                    s_re * m_re - s_im * m_im,
                    s_re * m_im + s_im * m_re,
                    s_rest * m_same + swap(s_rest) * m_cross,
                ], axis=1)
                back = over_lanes(product, col_inv)
                planes.append(jnp.concatenate([back[:, :width], back[:, width:]], axis=0))
            return jnp.concatenate(planes, axis=1)

        def rows_of(p, pair):
            found = over_rows(row_inv, pair)
            field[i * (batch // 2) + p] = found
            power = found[:count] * found[:count] + found[count:] * found[count:]
            for j in range(2):
                k = i * batch + 2 * p + j
                g = group[k]
                slopes[g] = slopes[g] + weight[k] * power[:, j * width:(j + 1) * width]

        staggered(batch // 2, cols_of, rows_of)
        return carry

    loop(steps, forward)

    wanted = target[...].astype(f32)
    for g in range(GROUPS):
        seen = jax.nn.sigmoid(STEEPNESS * (slopes[g] - THRESHOLD))
        resist[g] = seen
        slopes[g] = 2.0 * (seen - wanted) * seen * (1.0 - seen) * STEEPNESS
    out = pltpu.make_async_copy(resist, resist_far, out_sem)
    out.start()
    fetch_table(2).wait()
    row_tab, head, tail = table("row_tab"), table("head"), table("tail")

    def backward(i, carry):
        def rows_of(p):
            factors = []
            for j in range(2):
                k = i * batch + 2 * p + j
                factors.append((2.0 * weight[k]) * slopes[group[k]])
            factor = jnp.concatenate(factors, axis=1)
            cot = field[i * (batch // 2) + p] * jnp.concatenate([factor, factor], axis=0)
            return row_stage(cot, row_tab)

        def cols_of(p, tiles):
            total = [grad_spec[:, c * width:(c + 1) * width] for c in range(4)]
            for j in range(2):
                k = i * batch + 2 * p + j
                s_re, s_im, s_rest = spec[k, :, :width], spec[k, :, width:2 * width], spec[k, :, 2 * width:]
                first, rest = to_freqs(tiles[j], head, tail)
                c_re, c_im = first[:, :width], first[:, width:]
                total[0] = total[0] + (s_re * c_re + s_im * c_im)
                total[1] = total[1] + (s_re * c_im - s_im * c_re)
                total[2] = total[2] + s_rest * rest
                total[3] = total[3] + s_rest * swap(rest)
            for c in range(4):
                grad_spec[:, c * width:(c + 1) * width] = total[c]

        staggered(batch // 2, rows_of, cols_of)
        return carry

    loop(steps, backward)

    same, cross = grad_spec[:, 2 * width:3 * width], grad_spec[:, 3 * width:]
    tail_sum = jnp.where(real_half, same + swap(same), swap(cross) - cross)
    total = jnp.concatenate([grad_spec[:, :2 * width], tail_sum], axis=1)
    back = over_lanes(total, table("grad_col"))
    full = over_rows(table("grad_row"), jnp.concatenate([back[:, :width], back[:, width:]], axis=0))
    for c in range(2):
        base = c * grid_rows
        rise, fall = full[base:base + rim], full[base + rim + count:base + grid_rows]
        near_rim[c] = jnp.where(odd, rise, fall)
        far_rim[c] = jnp.where(odd, fall, rise)
        grad_own[c] = full[base + rim:base + rim + count]
    out.wait()


def join_body(place, own, near, far, out):
    odd = place[0] % 2 == 1
    rim = near.shape[1]
    count = own.shape[1]
    for c in range(2):
        out[c, :rim] = own[c, :rim] + jnp.where(odd, near[c], far[c])
        if count > 2 * rim:
            out[c, rim:count - rim] = own[c, rim:count - rim]
        out[c, count - rim:] = own[c, count - rim:] + jnp.where(odd, far[c], near[c])


def stacked(groups):
    blocks, layout, sections, at = [], {}, [], 0
    for group in groups:
        start = at
        for name, table in group.items():
            rows, lanes = table.shape
            layout[name] = (at, rows, lanes // 256)
            for b in range(lanes // 256):
                blocks.append(table[:, b * 256:(b + 1) * 256])
            at += rows * (lanes // 256)
        sections.append((start, at - start))
    return np.concatenate(blocks, axis=0), layout, sections


def on_device(mask_field, target, kernel_taps, kernel_radii, kernel_group, kernel_weight):
    _, count, width = mask_field.shape
    kernels, _, span, _ = kernel_taps.shape
    rim = span // 2
    grid_rows = count + 2 * rim
    grid_cols = width + rim
    assert count == span and width == span and kernels % BATCH == 0 and kernels % SPECTRA_BATCH == 0 and count >= 2 * rim

    strips = lax.axis_size("row")
    assert strips % 2 == 0
    at = lax.axis_index("row")
    near_pairs = [(i, i ^ 1) for i in range(strips)]
    far_pairs = [(i, ((i + 1) ^ 1) - 1) for i in range(1, strips - 1)]
    near = lax.ppermute(mask_field, "row", near_pairs)
    far = lax.ppermute(mask_field, "row", far_pairs)
    place = at.astype(jnp.int32).reshape(1)

    scale = 1.0 / (grid_rows * grid_cols)
    order = grouped(grid_cols, width)

    def head_and_tail(shift):
        table = analysis(grid_cols, width, shift).T[:, order]
        return halves(table[:, :2 * width], 0), halves(table[:, 2 * width:], 1)

    row_tab = halves(analysis(grid_rows, span, 0), 1)
    head, tail = head_and_tail(0)
    mask_row = halves(analysis(grid_rows, grid_rows, 2 * rim), 1)
    mask_head, mask_tail = head_and_tail(rim)
    col_inv = halves(synthesis(grid_cols, width, 0).T[order], 0)
    row_inv = halves(synthesis(grid_rows, count, 0, scale), 1)
    grad_col = halves(synthesis(grid_cols, width, rim).T[order], 0)
    grad_row = halves(synthesis(grid_rows, grid_rows, 2 * rim, scale), 1)

    smem = pl.BlockSpec(memory_space=pltpu.SMEM)
    vmem = pl.BlockSpec(memory_space=pltpu.VMEM)
    hbm = pl.BlockSpec(memory_space=pltpu.HBM)
    spectra = pl.pallas_call(
        spectra_body,
        grid=(kernels // SPECTRA_BATCH,),
        out_shape=jax.ShapeDtypeStruct((kernels, grid_rows, 2 * grid_cols), f32),
        in_specs=[smem, pl.BlockSpec((SPECTRA_BATCH, 2, span, span), lambda i: (i, 0, 0, 0)), vmem, vmem, vmem],
        out_specs=pl.BlockSpec((SPECTRA_BATCH, grid_rows, 2 * grid_cols), lambda i: (i, 0, 0)),
        compiler_params=pltpu.CompilerParams(vmem_limit_bytes=56 * MIB),
        cost_estimate=pl.CostEstimate(flops=18 * 10**9, bytes_accessed=14 * 10**6, transcendentals=0),
        name="spectra",
    )(kernel_radii, kernel_taps, *map(jnp.asarray, (row_tab, head, tail)))

    tables, layout, sections = stacked([
        {"mask_row": mask_row, "mask_head": mask_head, "mask_tail": mask_tail},
        {"col_inv": col_inv, "row_inv": row_inv},
        {"row_tab": row_tab, "head": head, "tail": tail, "grad_col": grad_col, "grad_row": grad_row},
    ])
    resist, own, near_rim, far_rim = pl.pallas_call(
        functools.partial(main_body, layout=layout, sections=sections),
        out_shape=[
            jax.ShapeDtypeStruct((GROUPS, count, width), f32),
            jax.ShapeDtypeStruct((2, count, width), f32),
            jax.ShapeDtypeStruct((2, rim, width), f32),
            jax.ShapeDtypeStruct((2, rim, width), f32),
        ],
        in_specs=[smem] * 3 + [vmem] * 4 + [hbm] * 2,
        out_specs=[hbm] + [vmem] * 3,
        scratch_shapes=[
            pltpu.VMEM((kernels, grid_rows, 2 * grid_cols), f32),
            pltpu.VMEM((kernels // 2, 2 * count, 2 * width), f32),
            pltpu.VMEM((grid_rows, 4 * width), f32),
            pltpu.VMEM((GROUPS, count, width), f32),
            pltpu.VMEM((GROUPS, count, width), f32),
            pltpu.VMEM((grid_rows, 4 * width), f32),
            pltpu.VMEM(tables.shape, bf16),
            pltpu.SemaphoreType.DMA((kernels // 2,)),
            pltpu.SemaphoreType.DMA((len(sections),)),
            pltpu.SemaphoreType.DMA,
        ],
        compiler_params=pltpu.CompilerParams(vmem_limit_bytes=LIMIT * MIB),
        name="fields",
    )(kernel_group, kernel_weight, place, mask_field, near, far, target, spectra, jnp.asarray(tables))

    near_in = lax.ppermute(near_rim, "row", near_pairs)
    far_in = lax.ppermute(far_rim, "row", far_pairs)
    gradient = pl.pallas_call(
        join_body,
        out_shape=jax.ShapeDtypeStruct((2, count, width), f32),
        in_specs=[smem] + [vmem] * 3,
        out_specs=vmem,
        compiler_params=pltpu.CompilerParams(vmem_limit_bytes=4 * MIB),
        name="join",
    )(place, own, near_in, far_in)
    return resist, gradient


def solution(mesh):
    in_specs = (P(None, ("win", "row"), None), P(("win", "row"), None), P(), P(), P(), P())
    out_specs = (P(None, ("win", "row"), None), P(None, ("win", "row"), None))
    return jax.shard_map(
        on_device, mesh=mesh, in_specs=in_specs, out_specs=out_specs, check_vma=False
    )
```

```python
import functools
import math

import jax
import jax.numpy as jnp
import ml_dtypes
import numpy as np
from jax import lax
from jax.experimental import pallas as pl
from jax.experimental.pallas import tpu as pltpu
from jax.sharding import PartitionSpec as P

RMAX = 64
GROUPS = 3
STEEPNESS = 1.0
THRESHOLD = 2.0
BATCH = 8
PIECE = 256

f32 = jnp.float32
bf16 = jnp.bfloat16
MIB = 1024 * 1024
LIMIT = 40


def halves(table, axis):
    high = table.astype(ml_dtypes.bfloat16)
    low = (table - high.astype(np.float64)).astype(ml_dtypes.bfloat16)
    return np.concatenate([high, low], axis=axis)


def analysis(freqs, points, shift):
    f = np.arange(freqs)[:, None]
    n = np.arange(points)[None, :] - shift
    angle = 2.0 * math.pi * ((f * n) % freqs) / freqs
    cos, sin = np.cos(angle), np.sin(angle)
    return np.block([[cos, sin], [-sin, cos]])


def synthesis(freqs, points, shift, scale=1.0):
    return analysis(freqs, points, shift).T * scale


def grouped(freqs, lanes):
    head, tail = np.arange(lanes), np.arange(lanes, freqs)
    return np.concatenate([head, freqs + head, tail, freqs + tail])


def split(x):
    high = x.astype(bf16)
    low = (x - high.astype(f32)).astype(bf16)
    return high, low


def dot(left, right):
    parts = [
        jnp.dot(left[at:at + PIECE], right, preferred_element_type=f32)
        for at in range(0, left.shape[0], PIECE)
    ]
    return jnp.concatenate(parts, axis=0)


def over_rows(table, x, piece=PIECE):
    high, low = split(x)
    depth = x.shape[0]
    parts = []
    for at in range(0, table.shape[0], piece):
        t_high, t_low = table[at:at + piece, :depth], table[at:at + piece, depth:]
        both = jnp.dot(jnp.concatenate([t_high, t_low], axis=0), high, preferred_element_type=f32)
        third = jnp.dot(t_high, low, preferred_element_type=f32)
        parts.append(both[:piece] + (both[piece:] + third))
    return jnp.concatenate(parts, axis=0)


def over_lanes(x, table):
    high, low = split(x)
    right = jnp.concatenate([table, table[:x.shape[1]]], axis=0)
    return dot(jnp.concatenate([high, high, low], axis=1), right)


def to_freqs(x, head, tail, piece=PIECE):
    high, low = split(x)
    depth = x.shape[1]
    lanes = tail.shape[1] // 2
    first, rest = [], []
    for at in range(0, x.shape[0], piece):
        stack = jnp.concatenate([high[at:at + piece], low[at:at + piece]], axis=0)
        both = jnp.dot(stack, head[:depth], preferred_element_type=f32)
        third = jnp.dot(high[at:at + piece], head[depth:], preferred_element_type=f32)
        first.append(both[:piece] + (both[piece:] + third))
        both = jnp.dot(stack, tail, preferred_element_type=f32)
        rest.append(both[:piece, :lanes] + (both[:piece, lanes:] + both[piece:, :lanes]))
    return jnp.concatenate(first, axis=0), jnp.concatenate(rest, axis=0)


def side(x):
    rows = x.shape[0] // 2
    return jnp.concatenate([x[:rows], x[rows:]], axis=1)


def row_stage(pair, row_tab, piece=PIECE):
    width = pair.shape[1] // 2
    half = over_rows(row_tab, pair, piece)
    return [side(half[:, :width]), side(half[:, width:])]


def staggered(count, first, second):
    held = None
    for i in range(count):
        new = first(i)
        if i:
            second(i - 1, held)
        held = new
    second(count - 1, held)


def swap(x):
    return pltpu.roll(x, x.shape[1] // 2, 1)


def spectra_body(radii, taps, row_ref, head_ref, tail_ref, spec):
    batch, _, span, _ = taps.shape
    row_tab, head, tail = row_ref[...], head_ref[...], tail_ref[...]
    first = pl.program_id(0) * batch
    row_at = lax.broadcasted_iota(jnp.int32, (span, span), 0) - span // 2
    col_at = lax.broadcasted_iota(jnp.int32, (span, span), 1) - span // 2
    reach = jnp.maximum(jnp.maximum(row_at, -1 - row_at), jnp.maximum(col_at, -1 - col_at))

    def rows_of(p):
        planes = []
        for k in (2 * p, 2 * p + 1):
            inside = reach < radii[first + k]
            parts = [jnp.where(inside, taps[k, c], 0.0) for c in range(2)]
            planes.append(jnp.concatenate(parts, axis=0))
        return row_stage(jnp.concatenate(planes, axis=1), row_tab, 128)

    def cols_of(p, tiles):
        for j in range(2):
            a, b = to_freqs(tiles[j], head, tail, 128)
            spec[2 * p + j, :, :a.shape[1]] = a
            spec[2 * p + j, :, a.shape[1]:] = b

    staggered(batch // 2, rows_of, cols_of)


def main_body(
    group, weight, place,
    own, near, far, target, spec_far, tables_far,
    resist_far, grad_own, near_rim, far_rim,
    spec, field, mask_spec, resist, slopes, grad_spec, tables, spec_sems, table_sems, out_sem,
    *, layout, sections,
):
    kernels, grid_rows, _ = spec.shape
    count, width = target.shape
    rim = (grid_rows - count) // 2
    steps = spec_sems.shape[0]
    batch = kernels // steps

    def fetch(i):
        here = pl.ds(i * batch, batch)
        return pltpu.make_async_copy(spec_far.at[here], spec.at[here], spec_sems.at[i])

    def fetch_table(i):
        here = pl.ds(sections[i][0], sections[i][1])
        return pltpu.make_async_copy(tables_far.at[here], tables.at[here], table_sems.at[i])

    def table(name):
        start, rows, blocks = layout[name]
        parts = [tables[start + b * rows:start + (b + 1) * rows] for b in range(blocks)]
        return jnp.concatenate(parts, axis=1)

    fetch_table(0).start()
    fetch_table(1).start()
    for i in range(steps):
        fetch(i).start()
    fetch_table(2).start()
    fetch_table(0).wait()

    odd = place[0] % 2 == 1
    parts = []
    for c in range(2):
        above = jnp.where(odd, near[c, count - rim:], far[c, count - rim:])
        below = jnp.where(odd, far[c, :rim], near[c, :rim])
        parts += [above, own[c], below]
    mask = jnp.concatenate(parts, axis=0)
    m_first, m_rest = to_freqs(side(over_rows(table("mask_row"), mask)), table("mask_head"), table("mask_tail"))
    lane = lax.broadcasted_iota(jnp.int32, m_rest.shape, 1)
    real_half = lane < m_rest.shape[1] // 2
    turned = swap(m_rest)
    mask_spec[:, :2 * width] = m_first
    mask_spec[:, 2 * width:3 * width] = jnp.where(real_half, m_rest, turned)
    mask_spec[:, 3 * width:] = jnp.where(real_half, -turned, m_rest)

    slopes[...] = jnp.zeros(slopes.shape, f32)
    grad_spec[...] = jnp.zeros(grad_spec.shape, f32)
    fetch_table(1).wait()
    col_inv, row_inv = table("col_inv"), table("row_inv")

    def forward(i, carry):
        fetch(i).wait()
        m_re, m_im = mask_spec[:, :width], mask_spec[:, width:2 * width]
        m_same, m_cross = mask_spec[:, 2 * width:3 * width], mask_spec[:, 3 * width:]

        def cols_of(p):
            planes = []
            for j in range(2):
                k = i * batch + 2 * p + j
                s_re, s_im, s_rest = spec[k, :, :width], spec[k, :, width:2 * width], spec[k, :, 2 * width:]
                product = jnp.concatenate([
                    s_re * m_re - s_im * m_im,
                    s_re * m_im + s_im * m_re,
                    s_rest * m_same + swap(s_rest) * m_cross,
                ], axis=1)
                back = over_lanes(product, col_inv)
                planes.append(jnp.concatenate([back[:, :width], back[:, width:]], axis=0))
            return jnp.concatenate(planes, axis=1)

        def rows_of(p, pair):
            found = over_rows(row_inv, pair)
            field[i * (batch // 2) + p] = found
            power = found[:count] * found[:count] + found[count:] * found[count:]
            for j in range(2):
                k = i * batch + 2 * p + j
                g = group[k]
                slopes[g] = slopes[g] + weight[k] * power[:, j * width:(j + 1) * width]

        staggered(batch // 2, cols_of, rows_of)
        return carry

    lax.fori_loop(0, steps, forward, 0)

    wanted = target[...].astype(f32)
    for g in range(GROUPS):
        seen = jax.nn.sigmoid(STEEPNESS * (slopes[g] - THRESHOLD))
        resist[g] = seen
        slopes[g] = 2.0 * (seen - wanted) * seen * (1.0 - seen) * STEEPNESS
    out = pltpu.make_async_copy(resist, resist_far, out_sem)
    out.start()
    fetch_table(2).wait()
    row_tab, head, tail = table("row_tab"), table("head"), table("tail")

    def backward(i, carry):
        def rows_of(p):
            factors = []
            for j in range(2):
                k = i * batch + 2 * p + j
                factors.append((2.0 * weight[k]) * slopes[group[k]])
            factor = jnp.concatenate(factors, axis=1)
            cot = field[i * (batch // 2) + p] * jnp.concatenate([factor, factor], axis=0)
            return row_stage(cot, row_tab)

        def cols_of(p, tiles):
            total = [grad_spec[:, c * width:(c + 1) * width] for c in range(4)]
            for j in range(2):
                k = i * batch + 2 * p + j
                s_re, s_im, s_rest = spec[k, :, :width], spec[k, :, width:2 * width], spec[k, :, 2 * width:]
                first, rest = to_freqs(tiles[j], head, tail)
                c_re, c_im = first[:, :width], first[:, width:]
                total[0] = total[0] + (s_re * c_re + s_im * c_im)
                total[1] = total[1] + (s_re * c_im - s_im * c_re)
                total[2] = total[2] + s_rest * rest
                total[3] = total[3] + s_rest * swap(rest)
            for c in range(4):
                grad_spec[:, c * width:(c + 1) * width] = total[c]

        staggered(batch // 2, rows_of, cols_of)
        return carry

    lax.fori_loop(0, steps, backward, 0)

    same, cross = grad_spec[:, 2 * width:3 * width], grad_spec[:, 3 * width:]
    tail_sum = jnp.where(real_half, same + swap(same), swap(cross) - cross)
    total = jnp.concatenate([grad_spec[:, :2 * width], tail_sum], axis=1)
    back = over_lanes(total, table("grad_col"))
    full = over_rows(table("grad_row"), jnp.concatenate([back[:, :width], back[:, width:]], axis=0))
    for c in range(2):
        base = c * grid_rows
        rise, fall = full[base:base + rim], full[base + rim + count:base + grid_rows]
        near_rim[c] = jnp.where(odd, rise, fall)
        far_rim[c] = jnp.where(odd, fall, rise)
        grad_own[c] = full[base + rim:base + rim + count]
    out.wait()


def join_body(place, own, near, far, out):
    odd = place[0] % 2 == 1
    rim = near.shape[1]
    count = own.shape[1]
    for c in range(2):
        out[c, :rim] = own[c, :rim] + jnp.where(odd, near[c], far[c])
        if count > 2 * rim:
            out[c, rim:count - rim] = own[c, rim:count - rim]
        out[c, count - rim:] = own[c, count - rim:] + jnp.where(odd, far[c], near[c])


def stacked(groups):
    blocks, layout, sections, at = [], {}, [], 0
    for group in groups:
        start = at
        for name, table in group.items():
            rows, lanes = table.shape
            layout[name] = (at, rows, lanes // 256)
            for b in range(lanes // 256):
                blocks.append(table[:, b * 256:(b + 1) * 256])
            at += rows * (lanes // 256)
        sections.append((start, at - start))
    return np.concatenate(blocks, axis=0), layout, sections


def on_device(mask_field, target, kernel_taps, kernel_radii, kernel_group, kernel_weight):
    _, count, width = mask_field.shape
    kernels, _, span, _ = kernel_taps.shape
    rim = span // 2
    grid_rows = count + 2 * rim
    grid_cols = width + rim
    assert count == span and width == span and kernels % BATCH == 0 and BATCH % 2 == 0 and count >= 2 * rim

    strips = lax.axis_size("row")
    assert strips % 2 == 0
    at = lax.axis_index("row")
    near_pairs = [(i, i ^ 1) for i in range(strips)]
    far_pairs = [(i, ((i + 1) ^ 1) - 1) for i in range(1, strips - 1)]
    near = lax.ppermute(mask_field, "row", near_pairs)
    far = lax.ppermute(mask_field, "row", far_pairs)
    place = at.astype(jnp.int32).reshape(1)

    scale = 1.0 / (grid_rows * grid_cols)
    order = grouped(grid_cols, width)

    def head_and_tail(shift):
        table = analysis(grid_cols, width, shift).T[:, order]
        return halves(table[:, :2 * width], 0), halves(table[:, 2 * width:], 1)

    row_tab = halves(analysis(grid_rows, span, 0), 1)
    head, tail = head_and_tail(0)
    mask_row = halves(analysis(grid_rows, grid_rows, 2 * rim), 1)
    mask_head, mask_tail = head_and_tail(rim)
    col_inv = halves(synthesis(grid_cols, width, 0).T[order], 0)
    row_inv = halves(synthesis(grid_rows, count, 0, scale), 1)
    grad_col = halves(synthesis(grid_cols, width, rim).T[order], 0)
    grad_row = halves(synthesis(grid_rows, grid_rows, 2 * rim, scale), 1)

    smem = pl.BlockSpec(memory_space=pltpu.SMEM)
    vmem = pl.BlockSpec(memory_space=pltpu.VMEM)
    hbm = pl.BlockSpec(memory_space=pltpu.HBM)
    spectra = pl.pallas_call(
        spectra_body,
        grid=(kernels // BATCH,),
        out_shape=jax.ShapeDtypeStruct((kernels, grid_rows, 2 * grid_cols), f32),
        in_specs=[smem, pl.BlockSpec((BATCH, 2, span, span), lambda i: (i, 0, 0, 0)), vmem, vmem, vmem],
        out_specs=pl.BlockSpec((BATCH, grid_rows, 2 * grid_cols), lambda i: (i, 0, 0)),
        compiler_params=pltpu.CompilerParams(vmem_limit_bytes=56 * MIB),
        cost_estimate=pl.CostEstimate(flops=18 * 10**9, bytes_accessed=14 * 10**6, transcendentals=0),
        name="spectra",
    )(kernel_radii, kernel_taps, *map(jnp.asarray, (row_tab, head, tail)))

    tables, layout, sections = stacked([
        {"mask_row": mask_row, "mask_head": mask_head, "mask_tail": mask_tail},
        {"col_inv": col_inv, "row_inv": row_inv},
        {"row_tab": row_tab, "head": head, "tail": tail, "grad_col": grad_col, "grad_row": grad_row},
    ])
    resist, own, near_rim, far_rim = pl.pallas_call(
        functools.partial(main_body, layout=layout, sections=sections),
        out_shape=[
            jax.ShapeDtypeStruct((GROUPS, count, width), f32),
            jax.ShapeDtypeStruct((2, count, width), f32),
            jax.ShapeDtypeStruct((2, rim, width), f32),
            jax.ShapeDtypeStruct((2, rim, width), f32),
        ],
        in_specs=[smem] * 3 + [vmem] * 4 + [hbm] * 2,
        out_specs=[hbm] + [vmem] * 3,
        scratch_shapes=[
            pltpu.VMEM((kernels, grid_rows, 2 * grid_cols), f32),
            pltpu.VMEM((kernels // 2, 2 * count, 2 * width), f32),
            pltpu.VMEM((grid_rows, 4 * width), f32),
            pltpu.VMEM((GROUPS, count, width), f32),
            pltpu.VMEM((GROUPS, count, width), f32),
            pltpu.VMEM((grid_rows, 4 * width), f32),
            pltpu.VMEM(tables.shape, bf16),
            pltpu.SemaphoreType.DMA((kernels // BATCH,)),
            pltpu.SemaphoreType.DMA((len(sections),)),
            pltpu.SemaphoreType.DMA,
        ],
        compiler_params=pltpu.CompilerParams(vmem_limit_bytes=LIMIT * MIB),
        name="fields",
    )(kernel_group, kernel_weight, place, mask_field, near, far, target, spectra, jnp.asarray(tables))

    near_in = lax.ppermute(near_rim, "row", near_pairs)
    far_in = lax.ppermute(far_rim, "row", far_pairs)
    gradient = pl.pallas_call(
        join_body,
        out_shape=jax.ShapeDtypeStruct((2, count, width), f32),
        in_specs=[smem] + [vmem] * 3,
        out_specs=vmem,
        compiler_params=pltpu.CompilerParams(vmem_limit_bytes=4 * MIB),
        name="join",
    )(place, own, near_in, far_in)
    return resist, gradient


def solution(mesh):
    in_specs = (P(None, ("win", "row"), None), P(("win", "row"), None), P(), P(), P(), P())
    out_specs = (P(None, ("win", "row"), None), P(None, ("win", "row"), None))
    return jax.shard_map(
        on_device, mesh=mesh, in_specs=in_specs, out_specs=out_specs, check_vma=False
    )
```

```python
import functools
import math

import jax
import jax.numpy as jnp
import ml_dtypes
import numpy as np
from jax import lax
from jax.experimental import pallas as pl
from jax.experimental.pallas import tpu as pltpu
from jax.sharding import PartitionSpec as P

RMAX = 64
GROUPS = 3
STEEPNESS = 1.0
THRESHOLD = 2.0
BATCH = 8
PIECE = 256

f32 = jnp.float32
bf16 = jnp.bfloat16
MIB = 1024 * 1024
LIMIT = 53


def halves(table, axis):
    high = table.astype(ml_dtypes.bfloat16)
    low = (table - high.astype(np.float64)).astype(ml_dtypes.bfloat16)
    return np.concatenate([high, low], axis=axis)


def analysis(freqs, points, shift):
    f = np.arange(freqs)[:, None]
    n = np.arange(points)[None, :] - shift
    angle = 2.0 * math.pi * ((f * n) % freqs) / freqs
    cos, sin = np.cos(angle), np.sin(angle)
    return np.block([[cos, sin], [-sin, cos]])


def synthesis(freqs, points, shift, scale=1.0):
    return analysis(freqs, points, shift).T * scale


def grouped(freqs, lanes):
    head, tail = np.arange(lanes), np.arange(lanes, freqs)
    return np.concatenate([head, freqs + head, tail, freqs + tail])


def split(x):
    high = x.astype(bf16)
    low = (x - high.astype(f32)).astype(bf16)
    return high, low


def dot(left, right):
    parts = [
        jnp.dot(left[at:at + PIECE], right, preferred_element_type=f32)
        for at in range(0, left.shape[0], PIECE)
    ]
    return jnp.concatenate(parts, axis=0)


def over_rows(table, parts, piece=PIECE):
    high, low = parts
    depth = high.shape[0]
    pieces = []
    for at in range(0, table.shape[0], piece):
        t_high, t_low = table[at:at + piece, :depth], table[at:at + piece, depth:]
        both = jnp.dot(jnp.concatenate([t_high, t_low], axis=0), high, preferred_element_type=f32)
        third = jnp.dot(t_high, low, preferred_element_type=f32)
        pieces.append(both[:piece] + (both[piece:] + third))
    return pieces


def over_lanes(parts, table):
    high, low = parts
    right = jnp.concatenate([table, table[:high.shape[1]]], axis=0)
    return dot(jnp.concatenate([high, high, low], axis=1), right)


def to_freqs(parts, head, tail):
    high, low = parts
    rows, depth = high.shape
    lanes = tail.shape[1] // 2
    stack = jnp.concatenate([high, low], axis=0)
    both = jnp.dot(stack, head[:depth], preferred_element_type=f32)
    third = jnp.dot(high, head[depth:], preferred_element_type=f32)
    first = both[:rows] + (both[rows:] + third)
    both = jnp.dot(stack, tail, preferred_element_type=f32)
    return first, both[:rows, :lanes] + (both[:rows, lanes:] + both[rows:, :lanes])


def beside(pieces):
    parts = [split(piece) for piece in pieces]
    return [jnp.concatenate(part, axis=1) for part in zip(*parts)]


def row_stage(pair, row_tab):
    width = pair.shape[1] // 2
    pieces = over_rows(row_tab, split(pair), row_tab.shape[0] // 2)
    parts = [split(piece) for piece in pieces]
    return [
        [jnp.concatenate([part[:, at:at + width] for part in both], axis=1) for both in zip(*parts)]
        for at in (0, width)
    ]


def staggered(count, first, second):
    held = None
    for i in range(count):
        new = first(i)
        if i:
            second(i - 1, held)
        held = new
    second(count - 1, held)


def swap(x):
    return pltpu.roll(x, x.shape[1] // 2, 1)


def spectra_body(radii, taps_far, row_ref, head_ref, tail_ref, spec_far, taps, spec, in_sems, out_sems):
    kernels, _, span, _ = taps.shape
    row_tab, head, tail = row_ref[...], head_ref[...], tail_ref[...]
    steps = in_sems.shape[0]
    batch = kernels // steps

    def fetch(i):
        here = pl.ds(i * batch, batch)
        return pltpu.make_async_copy(taps_far.at[here], taps.at[here], in_sems.at[i])

    def put(i):
        here = pl.ds(2 * i, 2)
        return pltpu.make_async_copy(spec.at[here], spec_far.at[here], out_sems.at[i])

    for i in range(steps):
        fetch(i).start()
    row_at = lax.broadcasted_iota(jnp.int32, (span, span), 0) - span // 2
    col_at = lax.broadcasted_iota(jnp.int32, (span, span), 1) - span // 2
    reach = jnp.maximum(jnp.maximum(row_at, -1 - row_at), jnp.maximum(col_at, -1 - col_at))

    def step(i, carry):
        fetch(i).wait()

        def rows_of(p):
            planes = []
            for j in range(2):
                k = i * batch + 2 * p + j
                inside = reach < radii[k]
                parts = [jnp.where(inside, taps[k, c], 0.0) for c in range(2)]
                planes.append(jnp.concatenate(parts, axis=0))
            return row_stage(jnp.concatenate(planes, axis=1), row_tab)

        def cols_of(p, tiles):
            for j in range(2):
                k = i * batch + 2 * p + j
                a, b = to_freqs(tiles[j], head, tail)
                spec[k, :, :a.shape[1]] = a
                spec[k, :, a.shape[1]:] = b
            put(i * (batch // 2) + p).start()

        staggered(batch // 2, rows_of, cols_of)
        return carry

    lax.fori_loop(0, steps, step, 0)
    for i in range(kernels // 2):
        put(i).wait()


def main_body(
    group, weight, place,
    own, near, far, target, spec_far, tables_far,
    resist_far, grad_own, near_rim, far_rim,
    spec, field, mask_spec, resist, slopes, grad_spec, tables, spec_sems, table_sems, out_sem,
    *, layout, sections,
):
    kernels, grid_rows, _ = spec.shape
    count, width = target.shape
    rim = (grid_rows - count) // 2
    steps = spec_sems.shape[0]
    batch = kernels // steps

    def fetch(i):
        here = pl.ds(i * batch, batch)
        return pltpu.make_async_copy(spec_far.at[here], spec.at[here], spec_sems.at[i])

    def fetch_table(i):
        here = pl.ds(sections[i][0], sections[i][1])
        return pltpu.make_async_copy(tables_far.at[here], tables.at[here], table_sems.at[i])

    def table(name):
        start, rows, blocks = layout[name]
        parts = [tables[start + b * rows:start + (b + 1) * rows] for b in range(blocks)]
        return jnp.concatenate(parts, axis=1)

    fetch_table(0).start()
    fetch_table(1).start()
    for i in range(steps):
        fetch(i).start()
    fetch_table(2).start()
    fetch_table(0).wait()

    odd = place[0] % 2 == 1
    parts = []
    for c in range(2):
        above = jnp.where(odd, near[c, count - rim:], far[c, count - rim:])
        below = jnp.where(odd, far[c, :rim], near[c, :rim])
        parts += [above, own[c], below]
    mask = jnp.concatenate(parts, axis=0)
    half = over_rows(table("mask_row"), split(mask), grid_rows)
    m_first, m_rest = to_freqs(beside(half), table("mask_head"), table("mask_tail"))
    lane = lax.broadcasted_iota(jnp.int32, m_rest.shape, 1)
    real_half = lane < m_rest.shape[1] // 2
    turned = swap(m_rest)
    mask_spec[:, :2 * width] = m_first
    mask_spec[:, 2 * width:3 * width] = jnp.where(real_half, m_rest, turned)
    mask_spec[:, 3 * width:] = jnp.where(real_half, -turned, m_rest)

    slopes[...] = jnp.zeros(slopes.shape, f32)
    grad_spec[...] = jnp.zeros(grad_spec.shape, f32)
    fetch_table(1).wait()
    col_inv, row_inv = table("col_inv"), table("row_inv")

    def forward(i, carry):
        fetch(i).wait()
        m_re, m_im = mask_spec[:, :width], mask_spec[:, width:2 * width]
        m_same, m_cross = mask_spec[:, 2 * width:3 * width], mask_spec[:, 3 * width:]

        def cols_of(p):
            planes = []
            for j in range(2):
                k = i * batch + 2 * p + j
                s_re, s_im, s_rest = spec[k, :, :width], spec[k, :, width:2 * width], spec[k, :, 2 * width:]
                product = jnp.concatenate([
                    s_re * m_re - s_im * m_im,
                    s_re * m_im + s_im * m_re,
                    s_rest * m_same + swap(s_rest) * m_cross,
                ], axis=1)
                back = over_lanes(split(product), col_inv)
                planes.append(split(jnp.concatenate([back[:, :width], back[:, width:]], axis=0)))
            return [jnp.concatenate(part, axis=1) for part in zip(*planes)]

        def rows_of(p, pair):
            found, = over_rows(row_inv, pair, 2 * count)
            field[i * (batch // 2) + p] = found
            power = found[:count] * found[:count] + found[count:] * found[count:]
            for j in range(2):
                k = i * batch + 2 * p + j
                g = group[k]
                slopes[g] = slopes[g] + weight[k] * power[:, j * width:(j + 1) * width]

        staggered(batch // 2, cols_of, rows_of)
        return carry

    lax.fori_loop(0, steps, forward, 0)

    wanted = target[...].astype(f32)
    for g in range(GROUPS):
        seen = jax.nn.sigmoid(STEEPNESS * (slopes[g] - THRESHOLD))
        resist[g] = seen
        slopes[g] = 2.0 * (seen - wanted) * seen * (1.0 - seen) * STEEPNESS
    out = pltpu.make_async_copy(resist, resist_far, out_sem)
    out.start()
    fetch_table(2).wait()
    row_tab, head, tail = table("row_tab"), table("head"), table("tail")

    def backward(i, carry):
        def rows_of(p):
            factors = []
            for j in range(2):
                k = i * batch + 2 * p + j
                factors.append((2.0 * weight[k]) * slopes[group[k]])
            factor = jnp.concatenate(factors, axis=1)
            cot = field[i * (batch // 2) + p] * jnp.concatenate([factor, factor], axis=0)
            return row_stage(cot, row_tab)

        def cols_of(p, tiles):
            total = [grad_spec[:, c * width:(c + 1) * width] for c in range(4)]
            for j in range(2):
                k = i * batch + 2 * p + j
                s_re, s_im, s_rest = spec[k, :, :width], spec[k, :, width:2 * width], spec[k, :, 2 * width:]
                first, rest = to_freqs(tiles[j], head, tail)
                c_re, c_im = first[:, :width], first[:, width:]
                total[0] = total[0] + (s_re * c_re + s_im * c_im)
                total[1] = total[1] + (s_re * c_im - s_im * c_re)
                total[2] = total[2] + s_rest * rest
                total[3] = total[3] + s_rest * swap(rest)
            for c in range(4):
                grad_spec[:, c * width:(c + 1) * width] = total[c]

        staggered(batch // 2, rows_of, cols_of)
        return carry

    lax.fori_loop(0, steps, backward, 0)

    same, cross = grad_spec[:, 2 * width:3 * width], grad_spec[:, 3 * width:]
    tail_sum = jnp.where(real_half, same + swap(same), swap(cross) - cross)
    total = jnp.concatenate([grad_spec[:, :2 * width], tail_sum], axis=1)
    back = over_lanes(split(total), table("grad_col"))
    back = split(jnp.concatenate([back[:, :width], back[:, width:]], axis=0))
    full = over_rows(table("grad_row"), back, grid_rows)
    for c in range(2):
        rise, fall = full[c][:rim], full[c][rim + count:]
        near_rim[c] = jnp.where(odd, rise, fall)
        far_rim[c] = jnp.where(odd, fall, rise)
        grad_own[c] = full[c][rim:rim + count]
    out.wait()


def join_body(place, own, near, far, out):
    odd = place[0] % 2 == 1
    rim = near.shape[1]
    count = own.shape[1]
    for c in range(2):
        out[c, :rim] = own[c, :rim] + jnp.where(odd, near[c], far[c])
        if count > 2 * rim:
            out[c, rim:count - rim] = own[c, rim:count - rim]
        out[c, count - rim:] = own[c, count - rim:] + jnp.where(odd, far[c], near[c])


def stacked(groups):
    blocks, layout, sections, at = [], {}, [], 0
    for group in groups:
        start = at
        for name, table in group.items():
            rows, lanes = table.shape
            layout[name] = (at, rows, lanes // 256)
            for b in range(lanes // 256):
                blocks.append(table[:, b * 256:(b + 1) * 256])
            at += rows * (lanes // 256)
        sections.append((start, at - start))
    return np.concatenate(blocks, axis=0), layout, sections


def on_device(mask_field, target, kernel_taps, kernel_radii, kernel_group, kernel_weight):
    _, count, width = mask_field.shape
    kernels, _, span, _ = kernel_taps.shape
    rim = span // 2
    grid_rows = count + 2 * rim
    grid_cols = width + rim
    assert count == span and width == span and kernels % BATCH == 0 and BATCH % 2 == 0 and count >= 2 * rim

    strips = lax.axis_size("row")
    assert strips % 2 == 0
    at = lax.axis_index("row")
    near_pairs = [(i, i ^ 1) for i in range(strips)]
    far_pairs = [(i, ((i + 1) ^ 1) - 1) for i in range(1, strips - 1)]
    near = lax.ppermute(mask_field, "row", near_pairs)
    far = lax.ppermute(mask_field, "row", far_pairs)
    place = at.astype(jnp.int32).reshape(1)

    scale = 1.0 / (grid_rows * grid_cols)
    order = grouped(grid_cols, width)

    def head_and_tail(shift):
        table = analysis(grid_cols, width, shift).T[:, order]
        return halves(table[:, :2 * width], 0), halves(table[:, 2 * width:], 1)

    row_tab = halves(analysis(grid_rows, span, 0), 1)
    head, tail = head_and_tail(0)
    mask_row = halves(analysis(grid_rows, grid_rows, 2 * rim), 1)
    mask_head, mask_tail = head_and_tail(rim)
    col_inv = halves(synthesis(grid_cols, width, 0).T[order], 0)
    row_inv = halves(synthesis(grid_rows, count, 0, scale), 1)
    grad_col = halves(synthesis(grid_cols, width, rim).T[order], 0)
    grad_row = halves(synthesis(grid_rows, grid_rows, 2 * rim, scale), 1)

    smem = pl.BlockSpec(memory_space=pltpu.SMEM)
    vmem = pl.BlockSpec(memory_space=pltpu.VMEM)
    hbm = pl.BlockSpec(memory_space=pltpu.HBM)
    spectra = pl.pallas_call(
        spectra_body,
        out_shape=jax.ShapeDtypeStruct((kernels, grid_rows, 2 * grid_cols), f32),
        in_specs=[smem, hbm, vmem, vmem, vmem],
        out_specs=hbm,
        scratch_shapes=[
            pltpu.VMEM(kernel_taps.shape, f32),
            pltpu.VMEM((kernels, grid_rows, 2 * grid_cols), f32),
            pltpu.SemaphoreType.DMA((kernels // BATCH,)),
            pltpu.SemaphoreType.DMA((kernels // 2,)),
        ],
        compiler_params=pltpu.CompilerParams(vmem_limit_bytes=56 * MIB),
        cost_estimate=pl.CostEstimate(flops=18 * 10**9, bytes_accessed=14 * 10**6, transcendentals=0),
        name="spectra",
    )(kernel_radii, kernel_taps, *map(jnp.asarray, (row_tab, head, tail)))

    tables, layout, sections = stacked([
        {"mask_row": mask_row, "mask_head": mask_head, "mask_tail": mask_tail},
        {"col_inv": col_inv, "row_inv": row_inv},
        {"row_tab": row_tab, "head": head, "tail": tail, "grad_col": grad_col, "grad_row": grad_row},
    ])
    resist, own, near_rim, far_rim = pl.pallas_call(
        functools.partial(main_body, layout=layout, sections=sections),
        out_shape=[
            jax.ShapeDtypeStruct((GROUPS, count, width), f32),
            jax.ShapeDtypeStruct((2, count, width), f32),
            jax.ShapeDtypeStruct((2, rim, width), f32),
            jax.ShapeDtypeStruct((2, rim, width), f32),
        ],
        in_specs=[smem] * 3 + [vmem] * 4 + [hbm] * 2,
        out_specs=[hbm] + [vmem] * 3,
        scratch_shapes=[
            pltpu.VMEM((kernels, grid_rows, 2 * grid_cols), f32),
            pltpu.VMEM((kernels // 2, 2 * count, 2 * width), f32),
            pltpu.VMEM((grid_rows, 4 * width), f32),
            pltpu.VMEM((GROUPS, count, width), f32),
            pltpu.VMEM((GROUPS, count, width), f32),
            pltpu.VMEM((grid_rows, 4 * width), f32),
            pltpu.VMEM(tables.shape, bf16),
            pltpu.SemaphoreType.DMA((kernels // BATCH,)),
            pltpu.SemaphoreType.DMA((len(sections),)),
            pltpu.SemaphoreType.DMA,
        ],
        compiler_params=pltpu.CompilerParams(vmem_limit_bytes=LIMIT * MIB),
        name="fields",
    )(kernel_group, kernel_weight, place, mask_field, near, far, target, spectra, jnp.asarray(tables))

    near_in = lax.ppermute(near_rim, "row", near_pairs)
    far_in = lax.ppermute(far_rim, "row", far_pairs)
    gradient = pl.pallas_call(
        join_body,
        out_shape=jax.ShapeDtypeStruct((2, count, width), f32),
        in_specs=[smem] + [vmem] * 3,
        out_specs=vmem,
        compiler_params=pltpu.CompilerParams(vmem_limit_bytes=4 * MIB),
        name="join",
    )(place, own, near_in, far_in)
    return resist, gradient


def solution(mesh):
    in_specs = (P(None, ("win", "row"), None), P(("win", "row"), None), P(), P(), P(), P())
    out_specs = (P(None, ("win", "row"), None), P(None, ("win", "row"), None))
    return jax.shard_map(
        on_device, mesh=mesh, in_specs=in_specs, out_specs=out_specs, check_vma=False
    )
```

```python
import functools
import math

import jax
import jax.numpy as jnp
import ml_dtypes
import numpy as np
from jax import lax
from jax.experimental import pallas as pl
from jax.experimental.pallas import tpu as pltpu
from jax.sharding import PartitionSpec as P

RMAX = 64
GROUPS = 3
STEEPNESS = 1.0
THRESHOLD = 2.0
BATCH = 8
PIECE = 256

f32 = jnp.float32
bf16 = jnp.bfloat16
MIB = 1024 * 1024
LIMIT = 53


def halves(table, axis):
    high = table.astype(ml_dtypes.bfloat16)
    low = (table - high.astype(np.float64)).astype(ml_dtypes.bfloat16)
    return np.concatenate([high, low], axis=axis)


def analysis(freqs, points, shift):
    f = np.arange(freqs)[:, None]
    n = np.arange(points)[None, :] - shift
    angle = 2.0 * math.pi * ((f * n) % freqs) / freqs
    cos, sin = np.cos(angle), np.sin(angle)
    return np.block([[cos, sin], [-sin, cos]])


def synthesis(freqs, points, shift, scale=1.0):
    return analysis(freqs, points, shift).T * scale


def class_table(freqs, points, c):
    f = np.arange(c, freqs, 4)[:, None]
    n = np.arange(points)[None, :]
    angle = 2.0 * math.pi * ((f * n) % freqs) / freqs
    cos, sin = np.cos(angle), np.sin(angle)
    return np.block([[cos, sin], [-sin, cos]])


def grouped(freqs, lanes):
    head, tail = np.arange(lanes), np.arange(lanes, freqs)
    return np.concatenate([head, freqs + head, tail, freqs + tail])


def split(x):
    high = x.astype(bf16)
    low = (x - high.astype(f32)).astype(bf16)
    return high, low


def dot(left, right):
    parts = [
        jnp.dot(left[at:at + PIECE], right, preferred_element_type=f32)
        for at in range(0, left.shape[0], PIECE)
    ]
    return jnp.concatenate(parts, axis=0)


def class_product(table, c, parts):
    depth = parts[0].shape[0]
    left = table[:, c * depth:(c + 1) * depth]
    found = dot(jnp.concatenate([left, left], axis=1), jnp.concatenate(parts, axis=0))
    half = found.shape[0] // 2
    return found[:half] + found[half:]


def turned(x, sign):
    re, im = x
    return (-im, re) if sign > 0 else (im, -re)


def plus(x, y):
    return x[0] + y[0], x[1] + y[1]


def minus(x, y):
    return x[0] - y[0], x[1] - y[1]


def to_row_freqs(x, table):
    if len(x) == 2:
        even, odd, even_less, odd_less = x[0], x[1], x[0], x[1]
    else:
        even, odd = plus(x[0], x[2]), plus(x[1], x[3])
        even_less, odd_less = minus(x[0], x[2]), minus(x[1], x[3])
    folded = [
        plus(even, odd),
        plus(even_less, turned(odd_less, -1)),
        minus(even, odd),
        plus(even_less, turned(odd_less, 1)),
    ]
    return [class_product(table, c, split(jnp.concatenate(y, axis=0))) for c, y in enumerate(folded)]


def from_row_freqs(classes, table, quarters):
    v = []
    for c, parts in enumerate(classes):
        found = class_product(table, c, parts)
        half = found.shape[0] // 2
        v.append((found[:half], found[half:]))
    out = []
    for q in quarters:
        if q % 2 == 0:
            even, odd = plus(v[0], v[2]), plus(v[1], v[3])
        else:
            even, odd = minus(v[0], v[2]), turned(minus(v[1], v[3]), 1)
        out.append(plus(even, odd) if q < 2 else minus(even, odd))
    return out


def over_lanes(parts, table):
    high, low = parts
    right = jnp.concatenate([table, table[:high.shape[1]]], axis=0)
    return dot(jnp.concatenate([high, high, low], axis=1), right)


def to_freqs(parts, head, tail):
    high, low = parts
    rows, depth = high.shape
    lanes = tail.shape[1] // 2
    stack = jnp.concatenate([high, low], axis=0)
    both = jnp.dot(stack, head[:depth], preferred_element_type=f32)
    third = jnp.dot(high, head[depth:], preferred_element_type=f32)
    first = both[:rows] + (both[rows:] + third)
    both = jnp.dot(stack, tail, preferred_element_type=f32)
    return first, both[:rows, :lanes] + (both[:rows, lanes:] + both[rows:, :lanes])


def beside(classes, at, width):
    tiles = []
    for found in classes:
        half = found.shape[0] // 2
        tiles.append(jnp.concatenate([found[:half, at:at + width], found[half:, at:at + width]], axis=1))
    return split(jnp.concatenate(tiles, axis=0))


def row_stage(quarters, row_fwd, width):
    classes = to_row_freqs(quarters, row_fwd)
    return [beside(classes, at, width) for at in range(0, quarters[0][0].shape[1], width)]


def quarters_of(re, im, quarter):
    return [(re[at:at + quarter], im[at:at + quarter]) for at in range(0, re.shape[0], quarter)]


def staggered(count, first, second):
    held = None
    for i in range(count):
        new = first(i)
        if i:
            second(i - 1, held)
        held = new
    second(count - 1, held)


def side_by_side(planes, c, width):
    quarter = planes[0][0].shape[0] // 4
    rows = slice(c * quarter, (c + 1) * quarter)
    return [
        jnp.concatenate([
            jnp.concatenate([plane[part][rows, at:at + width] for plane in planes], axis=1)
            for at in (0, width)
        ], axis=0)
        for part in range(2)
    ]


def swap(x):
    return pltpu.roll(x, x.shape[1] // 2, 1)


def spectra_body(radii, taps_far, row_ref, head_ref, tail_ref, spec_far, taps, spec, in_sems, out_sems):
    kernels, _, span, _ = taps.shape
    row_fwd, head, tail = row_ref[...], head_ref[...], tail_ref[...]
    steps = in_sems.shape[0]
    batch = kernels // steps

    def fetch(i):
        here = pl.ds(i * batch, batch)
        return pltpu.make_async_copy(taps_far.at[here], taps.at[here], in_sems.at[i])

    def put(i):
        here = pl.ds(2 * i, 2)
        return pltpu.make_async_copy(spec.at[here], spec_far.at[here], out_sems.at[i])

    for i in range(steps):
        fetch(i).start()
    row_at = lax.broadcasted_iota(jnp.int32, (span, span), 0) - span // 2
    col_at = lax.broadcasted_iota(jnp.int32, (span, span), 1) - span // 2
    reach = jnp.maximum(jnp.maximum(row_at, -1 - row_at), jnp.maximum(col_at, -1 - col_at))

    def step(i, carry):
        fetch(i).wait()

        def rows_of(p):
            planes = [[], []]
            for j in range(2):
                k = i * batch + 2 * p + j
                inside = reach < radii[k]
                for c in range(2):
                    planes[c].append(jnp.where(inside, taps[k, c], 0.0))
            re, im = [jnp.concatenate(plane, axis=1) for plane in planes]
            return row_stage(quarters_of(re, im, span // 2), row_fwd, span)

        def cols_of(p, tiles):
            for j in range(2):
                k = i * batch + 2 * p + j
                a, b = to_freqs(tiles[j], head, tail)
                spec[k, :, :a.shape[1]] = a
                spec[k, :, a.shape[1]:] = b
            put(i * (batch // 2) + p).start()

        staggered(batch // 2, rows_of, cols_of)
        return carry

    lax.fori_loop(0, steps, step, 0)
    for i in range(kernels // 2):
        put(i).wait()


def main_body(
    group, weight, place,
    own, near, far, target, spec_far, tables_far,
    resist_far, grad_own, near_rim, far_rim,
    spec, field, mask_spec, resist, slopes, grad_spec, tables, spec_sems, table_sems, out_sem,
    *, layout, sections,
):
    kernels, grid_rows, _ = spec.shape
    count, width = target.shape
    rim = (grid_rows - count) // 2
    steps = spec_sems.shape[0]
    batch = kernels // steps

    def fetch(i):
        here = pl.ds(i * batch, batch)
        return pltpu.make_async_copy(spec_far.at[here], spec.at[here], spec_sems.at[i])

    def fetch_table(i):
        here = pl.ds(sections[i][0], sections[i][1])
        return pltpu.make_async_copy(tables_far.at[here], tables.at[here], table_sems.at[i])

    def table(name):
        start, rows, blocks = layout[name]
        parts = [tables[start + b * rows:start + (b + 1) * rows] for b in range(blocks)]
        return jnp.concatenate(parts, axis=1)

    fetch_table(0).start()
    fetch_table(1).start()
    for i in range(steps):
        fetch(i).start()
    fetch_table(2).start()
    fetch_table(0).wait()

    odd = place[0] % 2 == 1
    row_fwd = table("row_fwd")
    above, below = [], []
    for c in range(2):
        above.append(jnp.where(odd, near[c, count - rim:], far[c, count - rim:]))
        below.append(jnp.where(odd, far[c, :rim], near[c, :rim]))
    upper, lower = quarters_of(own[0], own[1], rim)
    mask, = row_stage([lower, tuple(below), tuple(above), upper], row_fwd, width)
    m_first, m_rest = to_freqs(mask, table("mask_head"), table("mask_tail"))
    lane = lax.broadcasted_iota(jnp.int32, m_rest.shape, 1)
    real_half = lane < m_rest.shape[1] // 2
    turned = swap(m_rest)
    mask_spec[:, :2 * width] = m_first
    mask_spec[:, 2 * width:3 * width] = jnp.where(real_half, m_rest, turned)
    mask_spec[:, 3 * width:] = jnp.where(real_half, -turned, m_rest)

    slopes[...] = jnp.zeros(slopes.shape, f32)
    grad_spec[...] = jnp.zeros(grad_spec.shape, f32)
    fetch_table(1).wait()
    col_inv, row_inv = table("col_inv"), table("row_inv")

    def forward(i, carry):
        fetch(i).wait()
        m_re, m_im = mask_spec[:, :width], mask_spec[:, width:2 * width]
        m_same, m_cross = mask_spec[:, 2 * width:3 * width], mask_spec[:, 3 * width:]

        def cols_of(p):
            planes = []
            for j in range(2):
                k = i * batch + 2 * p + j
                s_re, s_im, s_rest = spec[k, :, :width], spec[k, :, width:2 * width], spec[k, :, 2 * width:]
                product = jnp.concatenate([
                    s_re * m_re - s_im * m_im,
                    s_re * m_im + s_im * m_re,
                    s_rest * m_same + swap(s_rest) * m_cross,
                ], axis=1)
                back = over_lanes(split(product), col_inv)
                planes.append(split(back))
            return [side_by_side(planes, c, width) for c in range(4)]

        def rows_of(p, pair):
            upper, lower = from_row_freqs(pair, row_inv, (0, 1))
            re = jnp.concatenate([upper[0], lower[0]], axis=0)
            im = jnp.concatenate([upper[1], lower[1]], axis=0)
            field[i * (batch // 2) + p, :count] = re
            field[i * (batch // 2) + p, count:] = im
            power = re * re + im * im
            for j in range(2):
                k = i * batch + 2 * p + j
                g = group[k]
                slopes[g] = slopes[g] + weight[k] * power[:, j * width:(j + 1) * width]

        staggered(batch // 2, cols_of, rows_of)
        return carry

    lax.fori_loop(0, steps, forward, 0)

    wanted = target[...].astype(f32)
    for g in range(GROUPS):
        seen = jax.nn.sigmoid(STEEPNESS * (slopes[g] - THRESHOLD))
        resist[g] = seen
        slopes[g] = 2.0 * (seen - wanted) * seen * (1.0 - seen) * STEEPNESS
    out = pltpu.make_async_copy(resist, resist_far, out_sem)
    out.start()
    fetch_table(2).wait()
    head, tail = table("head"), table("tail")

    def backward(i, carry):
        def rows_of(p):
            factors = []
            for j in range(2):
                k = i * batch + 2 * p + j
                factors.append((2.0 * weight[k]) * slopes[group[k]])
            factor = jnp.concatenate(factors, axis=1)
            re = field[i * (batch // 2) + p, :count] * factor
            im = field[i * (batch // 2) + p, count:] * factor
            return row_stage(quarters_of(re, im, rim), row_fwd, width)

        def cols_of(p, tiles):
            total = [grad_spec[:, c * width:(c + 1) * width] for c in range(4)]
            for j in range(2):
                k = i * batch + 2 * p + j
                s_re, s_im, s_rest = spec[k, :, :width], spec[k, :, width:2 * width], spec[k, :, 2 * width:]
                first, rest = to_freqs(tiles[j], head, tail)
                c_re, c_im = first[:, :width], first[:, width:]
                total[0] = total[0] + (s_re * c_re + s_im * c_im)
                total[1] = total[1] + (s_re * c_im - s_im * c_re)
                total[2] = total[2] + s_rest * rest
                total[3] = total[3] + s_rest * swap(rest)
            for c in range(4):
                grad_spec[:, c * width:(c + 1) * width] = total[c]

        staggered(batch // 2, rows_of, cols_of)
        return carry

    lax.fori_loop(0, steps, backward, 0)

    same, cross = grad_spec[:, 2 * width:3 * width], grad_spec[:, 3 * width:]
    tail_sum = jnp.where(real_half, same + swap(same), swap(cross) - cross)
    total = jnp.concatenate([grad_spec[:, :2 * width], tail_sum], axis=1)
    back = split(over_lanes(split(total), table("grad_col")))
    classes = [side_by_side([back], c, width) for c in range(4)]
    rise, upper, lower, fall = from_row_freqs(classes, row_inv, (2, 3, 0, 1))
    for c in range(2):
        near_rim[c] = jnp.where(odd, rise[c], fall[c])
        far_rim[c] = jnp.where(odd, fall[c], rise[c])
        grad_own[c, :rim] = upper[c]
        grad_own[c, rim:] = lower[c]
    out.wait()


def join_body(place, own, near, far, out):
    odd = place[0] % 2 == 1
    rim = near.shape[1]
    count = own.shape[1]
    for c in range(2):
        out[c, :rim] = own[c, :rim] + jnp.where(odd, near[c], far[c])
        if count > 2 * rim:
            out[c, rim:count - rim] = own[c, rim:count - rim]
        out[c, count - rim:] = own[c, count - rim:] + jnp.where(odd, far[c], near[c])


def stacked(groups):
    blocks, layout, sections, at = [], {}, [], 0
    for group in groups:
        start = at
        for name, table in group.items():
            rows, lanes = table.shape
            layout[name] = (at, rows, lanes // 256)
            for b in range(lanes // 256):
                blocks.append(table[:, b * 256:(b + 1) * 256])
            at += rows * (lanes // 256)
        sections.append((start, at - start))
    return np.concatenate(blocks, axis=0), layout, sections


def on_device(mask_field, target, kernel_taps, kernel_radii, kernel_group, kernel_weight):
    _, count, width = mask_field.shape
    kernels, _, span, _ = kernel_taps.shape
    rim = span // 2
    grid_rows = count + 2 * rim
    grid_cols = width + rim
    assert count == span and width == span and kernels % BATCH == 0 and BATCH % 2 == 0 and count == 2 * rim

    strips = lax.axis_size("row")
    assert strips % 2 == 0
    at = lax.axis_index("row")
    near_pairs = [(i, i ^ 1) for i in range(strips)]
    far_pairs = [(i, ((i + 1) ^ 1) - 1) for i in range(1, strips - 1)]
    near = lax.ppermute(mask_field, "row", near_pairs)
    far = lax.ppermute(mask_field, "row", far_pairs)
    place = at.astype(jnp.int32).reshape(1)

    scale = 1.0 / (grid_rows * grid_cols)
    order = grouped(grid_cols, width)

    def head_and_tail(shift):
        table = analysis(grid_cols, width, shift).T[:, order]
        return halves(table[:, :2 * width], 0), halves(table[:, 2 * width:], 1)

    quarter = grid_rows // 4
    by_class = [class_table(grid_rows, quarter, c) for c in range(4)]
    row_fwd = np.concatenate([halves(t, 0) for t in by_class], axis=1)
    row_inv = np.concatenate([halves(t.T * scale, 0) for t in by_class], axis=1)
    head, tail = head_and_tail(0)
    mask_head, mask_tail = head_and_tail(rim)
    col_inv = halves(synthesis(grid_cols, width, 0).T[order], 0)
    grad_col = halves(synthesis(grid_cols, width, rim).T[order], 0)

    smem = pl.BlockSpec(memory_space=pltpu.SMEM)
    vmem = pl.BlockSpec(memory_space=pltpu.VMEM)
    hbm = pl.BlockSpec(memory_space=pltpu.HBM)
    spectra = pl.pallas_call(
        spectra_body,
        out_shape=jax.ShapeDtypeStruct((kernels, grid_rows, 2 * grid_cols), f32),
        in_specs=[smem, hbm, vmem, vmem, vmem],
        out_specs=hbm,
        scratch_shapes=[
            pltpu.VMEM(kernel_taps.shape, f32),
            pltpu.VMEM((kernels, grid_rows, 2 * grid_cols), f32),
            pltpu.SemaphoreType.DMA((kernels // BATCH,)),
            pltpu.SemaphoreType.DMA((kernels // 2,)),
        ],
        compiler_params=pltpu.CompilerParams(vmem_limit_bytes=56 * MIB),
        cost_estimate=pl.CostEstimate(flops=18 * 10**9, bytes_accessed=14 * 10**6, transcendentals=0),
        name="spectra",
    )(kernel_radii, kernel_taps, *map(jnp.asarray, (row_fwd, head, tail)))

    tables, layout, sections = stacked([
        {"row_fwd": row_fwd, "mask_head": mask_head, "mask_tail": mask_tail},
        {"col_inv": col_inv, "row_inv": row_inv},
        {"head": head, "tail": tail, "grad_col": grad_col},
    ])
    resist, own, near_rim, far_rim = pl.pallas_call(
        functools.partial(main_body, layout=layout, sections=sections),
        out_shape=[
            jax.ShapeDtypeStruct((GROUPS, count, width), f32),
            jax.ShapeDtypeStruct((2, count, width), f32),
            jax.ShapeDtypeStruct((2, rim, width), f32),
            jax.ShapeDtypeStruct((2, rim, width), f32),
        ],
        in_specs=[smem] * 3 + [vmem] * 4 + [hbm] * 2,
        out_specs=[hbm] + [vmem] * 3,
        scratch_shapes=[
            pltpu.VMEM((kernels, grid_rows, 2 * grid_cols), f32),
            pltpu.VMEM((kernels // 2, 2 * count, 2 * width), f32),
            pltpu.VMEM((grid_rows, 4 * width), f32),
            pltpu.VMEM((GROUPS, count, width), f32),
            pltpu.VMEM((GROUPS, count, width), f32),
            pltpu.VMEM((grid_rows, 4 * width), f32),
            pltpu.VMEM(tables.shape, bf16),
            pltpu.SemaphoreType.DMA((kernels // BATCH,)),
            pltpu.SemaphoreType.DMA((len(sections),)),
            pltpu.SemaphoreType.DMA,
        ],
        compiler_params=pltpu.CompilerParams(vmem_limit_bytes=LIMIT * MIB),
        name="fields",
    )(kernel_group, kernel_weight, place, mask_field, near, far, target, spectra, jnp.asarray(tables))

    near_in = lax.ppermute(near_rim, "row", near_pairs)
    far_in = lax.ppermute(far_rim, "row", far_pairs)
    gradient = pl.pallas_call(
        join_body,
        out_shape=jax.ShapeDtypeStruct((2, count, width), f32),
        in_specs=[smem] + [vmem] * 3,
        out_specs=vmem,
        compiler_params=pltpu.CompilerParams(vmem_limit_bytes=4 * MIB),
        name="join",
    )(place, own, near_in, far_in)
    return resist, gradient


def solution(mesh):
    in_specs = (P(None, ("win", "row"), None), P(("win", "row"), None), P(), P(), P(), P())
    out_specs = (P(None, ("win", "row"), None), P(None, ("win", "row"), None))
    return jax.shard_map(
        on_device, mesh=mesh, in_specs=in_specs, out_specs=out_specs, check_vma=False
    )
```

```python
import functools
import math

import jax
import jax.numpy as jnp
import ml_dtypes
import numpy as np
from jax import lax
from jax.experimental import pallas as pl
from jax.experimental.pallas import tpu as pltpu
from jax.sharding import PartitionSpec as P

RMAX = 64
GROUPS = 3
STEEPNESS = 1.0
THRESHOLD = 2.0
UNIT = 4
UNITS = 2
PIECE = 256
TURN = math.sqrt(0.75)

f32 = jnp.float32
bf16 = jnp.bfloat16
MIB = 1024 * 1024
LIMIT = 53


def halves(table, axis):
    high = table.astype(ml_dtypes.bfloat16)
    low = (table - high.astype(np.float64)).astype(ml_dtypes.bfloat16)
    return np.concatenate([high, low], axis=axis)


def class_table(freqs, points, c, classes):
    f = np.arange(c, freqs, classes)[:, None]
    n = np.arange(points)[None, :]
    angle = 2.0 * math.pi * ((f * n) % freqs) / freqs
    cos, sin = np.cos(angle), np.sin(angle)
    return np.block([[cos, sin], [-sin, cos]])


def split(x):
    high = x.astype(bf16)
    low = (x - high.astype(f32)).astype(bf16)
    return high, low


def dot(left, right):
    parts = [
        jnp.dot(left[at:at + PIECE], right, preferred_element_type=f32)
        for at in range(0, left.shape[0], PIECE)
    ]
    return jnp.concatenate(parts, axis=0)


def swap(x):
    return pltpu.roll(x, x.shape[1] // 2, 1)


def first_half(x):
    return lax.broadcasted_iota(jnp.int32, x.shape, 1) < x.shape[1] // 2


def exchange(x, y):
    first = first_half(x)
    return jnp.where(first, x, swap(y)), jnp.where(first, swap(x), y)


def turned(x, sign):
    re, im = x
    return (-im, re) if sign > 0 else (im, -re)


def plus(x, y):
    return x[0] + y[0], x[1] + y[1]


def minus(x, y):
    return x[0] - y[0], x[1] - y[1]


def row_product(table, c, x):
    parts = split(x)
    depth = x.shape[0]
    left = table[:, c * depth:(c + 1) * depth]
    found = dot(jnp.concatenate([left, left], axis=1), jnp.concatenate(parts, axis=0))
    half = found.shape[0] // 2
    found = found[:half] + found[half:]
    return found[:half // 2], found[half // 2:]


def to_row_freqs(x, table):
    if len(x) == 2:
        even, odd, even_less, odd_less = x[0], x[1], x[0], x[1]
    else:
        even, odd = plus(x[0], x[2]), plus(x[1], x[3])
        even_less, odd_less = minus(x[0], x[2]), minus(x[1], x[3])
    folded = [
        plus(even, odd),
        plus(even_less, turned(odd_less, -1)),
        minus(even, odd),
        plus(even_less, turned(odd_less, 1)),
    ]
    return [row_product(table, c, jnp.concatenate(y, axis=0)) for c, y in enumerate(folded)]


def from_row_freqs(classes, table, quarters):
    v = [row_product(table, c, jnp.concatenate(y, axis=0)) for c, y in enumerate(classes)]
    out = []
    for q in quarters:
        if q % 2 == 0:
            even, odd = plus(v[0], v[2]), plus(v[1], v[3])
        else:
            even, odd = minus(v[0], v[2]), turned(minus(v[1], v[3]), 1)
        out.append(plus(even, odd) if q < 2 else minus(even, odd))
    return out


def quarters_of(re, im, quarter):
    return [(re[at:at + quarter], im[at:at + quarter]) for at in range(0, re.shape[0], quarter)]


def lane_turned(x):
    return swap(x) * jnp.where(first_half(x), TURN, -TURN)


def col_products(planes, table):
    rows = planes[0][0].shape[0]
    depth = table.shape[0] // 3
    out = [[] for _ in planes]
    for c in range(3):
        high, low = split(jnp.concatenate([plane[c] for plane in planes], axis=0))
        right = table[c * depth:(c + 1) * depth]
        found = dot(jnp.concatenate([high, low], axis=1), jnp.concatenate([right, right], axis=0))
        found = found[:, :depth] + found[:, depth:]
        for k in range(len(planes)):
            out[k].append(found[k * rows:(k + 1) * rows])
    return out


def to_col_freqs(planes, table, shifted=False):
    folded = []
    for left, right in planes:
        if shifted:
            left, right = right, left
        near, far = left - 0.5 * right, lane_turned(right)
        one, two = near + far, near - far
        folded.append([left + right, two, one] if shifted else [left + right, one, two])
    return col_products(folded, table)


def from_col_freqs(planes, table, shifted=False):
    out = []
    for v in col_products(planes, table):
        total, far = v[1] + v[2], lane_turned(v[1] - v[2])
        whole, part = v[0] + total, v[0] - 0.5 * total
        out.append((part + far, whole) if shifted else (whole, part - far))
    return out


def pairs_apart(planes):
    re, im = [], []
    for k in range(0, len(planes), 2):
        for x, y in zip(planes[k], planes[k + 1]):
            r, i = exchange(x, y)
            re.append(r)
            im.append(i)
    return jnp.concatenate(re, axis=1), jnp.concatenate(im, axis=1)


def pairs_together(re, im, width):
    planes = []
    for at in range(0, re.shape[1], 3 * width):
        both = [
            exchange(re[:, at + c * width:at + (c + 1) * width], im[:, at + c * width:at + (c + 1) * width])
            for c in range(3)
        ]
        planes += [[x for x, _ in both], [y for _, y in both]]
    return planes


def staggered(count, first, second):
    held = None
    for i in range(count):
        new = first(i)
        if i:
            second(i - 1, held)
        held = new
    second(count - 1, held)


def spectra_body(radii, taps_far, row_ref, col_ref, spec_far, taps, spec, in_sems, out_sems):
    kernels, _, span, _ = taps.shape
    row_fwd, col_fwd = row_ref[...], col_ref[...]
    quarter = span // 2
    steps = kernels // (UNIT * UNITS)

    def fetch(u):
        here = pl.ds(u * UNIT, UNIT)
        return pltpu.make_async_copy(taps_far.at[here], taps.at[here], in_sems.at[u])

    def put(u):
        return pltpu.make_async_copy(spec.at[u], spec_far.at[u], out_sems.at[u])

    for u in range(kernels // UNIT):
        fetch(u).start()
    row_at = lax.broadcasted_iota(jnp.int32, (span, span), 0) - span // 2
    col_at = lax.broadcasted_iota(jnp.int32, (span, span), 1) - span // 2
    reach = jnp.maximum(jnp.maximum(row_at, -1 - row_at), jnp.maximum(col_at, -1 - col_at))

    def step(i, carry):
        def cols_of(p):
            u = i * UNITS + p
            fetch(u).wait()
            planes = []
            for j in range(UNIT):
                k = u * UNIT + j
                inside = reach < radii[k]
                planes.append(exchange(*[jnp.where(inside, taps[k, c], 0.0) for c in range(2)]))
            return pairs_apart(to_col_freqs(planes, col_fwd))

        def rows_of(p, both):
            u = i * UNITS + p
            for c, found in enumerate(to_row_freqs(quarters_of(*both, quarter), row_fwd)):
                for part in range(2):
                    spec[u, part, c * quarter:(c + 1) * quarter] = found[part]
            put(u).start()

        staggered(UNITS, cols_of, rows_of)
        return carry

    lax.fori_loop(0, steps, step, 0)
    for u in range(kernels // UNIT):
        put(u).wait()


def main_body(
    group, weight, place,
    own, near, far, target, spec_far, tables_far,
    resist_far, grad_own, near_rim, far_rim,
    spec, field, mask_spec, resist, slopes, grad_spec, tables, spec_sems, table_sem, out_sem,
    *, layout,
):
    count, width = target.shape
    rim = count // 2
    units = spec.shape[0]
    steps = units // UNITS

    def fetch(u):
        return pltpu.make_async_copy(spec_far.at[u], spec.at[u], spec_sems.at[u])

    def table(name):
        start, rows, blocks = layout[name]
        parts = [tables[start + b * rows:start + (b + 1) * rows] for b in range(blocks)]
        return jnp.concatenate(parts, axis=1)

    fetch_tables = pltpu.make_async_copy(tables_far, tables, table_sem)
    fetch_tables.start()
    for u in range(units):
        fetch(u).start()
    slopes[...] = jnp.zeros(slopes.shape, f32)
    grad_spec[...] = jnp.zeros(grad_spec.shape, f32)
    fetch_tables.wait()
    row_fwd, row_inv, col_fwd, col_inv = [table(name) for name in ("row_fwd", "row_inv", "col_fwd", "col_inv")]

    odd = place[0] % 2 == 1
    mask = []
    for c in range(2):
        above = jnp.where(odd, near[c, count - rim:], far[c, count - rim:])
        below = jnp.where(odd, far[c, :rim], near[c, :rim])
        mask.append(jnp.concatenate([own[c, rim:], below, above, own[c, :rim]], axis=0))
    plane, = to_col_freqs([exchange(*mask)], col_fwd, shifted=True)
    both = pairs_apart([plane, plane])
    for c, found in enumerate(to_row_freqs(quarters_of(*both, rim), row_fwd)):
        for part in range(2):
            mask_spec[part, c * rim:(c + 1) * rim] = found[part]

    def forward(i, carry):
        def rows_of(p):
            u = i * UNITS + p
            fetch(u).wait()
            classes = []
            for c in range(4):
                here = slice(c * rim, (c + 1) * rim)
                m_re, m_im = [jnp.concatenate([mask_spec[part, here]] * (UNIT // 2), axis=1) for part in range(2)]
                s_re, s_im = spec[u, 0, here], spec[u, 1, here]
                classes.append((s_re * m_re - s_im * m_im, s_re * m_im + s_im * m_re))
            upper, lower = from_row_freqs(classes, row_inv, (0, 1))
            return [jnp.concatenate([upper[part], lower[part]], axis=0) for part in range(2)]

        def cols_of(p, both):
            u = i * UNITS + p
            found = from_col_freqs(pairs_together(*both, width), col_inv)
            for j in range(UNIT):
                k = u * UNIT + j
                for side in range(2):
                    x = found[j][side]
                    field[k, side] = x
                    slopes[group[k], side] = slopes[group[k], side] + weight[k] * (x * x)

        staggered(UNITS, rows_of, cols_of)
        return carry

    lax.fori_loop(0, steps, forward, 0)

    wanted = target[...].astype(f32)
    for g in range(GROUPS):
        left, right = [slopes[g, side] + swap(slopes[g, side]) for side in range(2)]
        seen = jax.nn.sigmoid(STEEPNESS * (jnp.where(first_half(left), left, right) - THRESHOLD))
        resist[g] = seen
        slope = 2.0 * (seen - wanted) * seen * (1.0 - seen) * STEEPNESS
        slopes[g, 0], slopes[g, 1] = exchange(slope, slope)
    out = pltpu.make_async_copy(resist, resist_far, out_sem)
    out.start()

    def backward(i, carry):
        def cols_of(p):
            u = i * UNITS + p
            planes = []
            for j in range(UNIT):
                k = u * UNIT + j
                planes.append([field[k, side] * ((2.0 * weight[k]) * slopes[group[k], side]) for side in range(2)])
            return pairs_apart(to_col_freqs(planes, col_fwd))

        def rows_of(p, both):
            u = i * UNITS + p
            for c, (c_re, c_im) in enumerate(to_row_freqs(quarters_of(*both, rim), row_fwd)):
                here = slice(c * rim, (c + 1) * rim)
                s_re, s_im = spec[u, 0, here], spec[u, 1, here]
                terms = s_re * c_re + s_im * c_im, s_re * c_im - s_im * c_re
                for part in range(2):
                    total = grad_spec[part, here]
                    lanes = total.shape[1]
                    for at in range(0, terms[part].shape[1], lanes):
                        total = total + terms[part][:, at:at + lanes]
                    grad_spec[part, here] = total

        staggered(UNITS, cols_of, rows_of)
        return carry

    lax.fori_loop(0, steps, backward, 0)

    classes = [tuple(grad_spec[part, c * rim:(c + 1) * rim] for part in range(2)) for c in range(4)]
    quarters = from_row_freqs(classes, row_inv, (2, 3, 0, 1))
    re, im = [jnp.concatenate([x[part] for x in quarters], axis=0) for part in range(2)]
    first, second = pairs_together(re, im, width)
    plane = [x + y for x, y in zip(first, second)]
    halves_found, = from_col_freqs([plane], col_inv, shifted=True)
    for c, full in enumerate(exchange(*halves_found)):
        rise, fall = full[:rim], full[rim + count:]
        near_rim[c] = jnp.where(odd, rise, fall)
        far_rim[c] = jnp.where(odd, fall, rise)
        grad_own[c] = full[rim:rim + count]
    out.wait()


def join_body(place, own, near, far, out):
    odd = place[0] % 2 == 1
    rim = near.shape[1]
    for c in range(2):
        out[c, :rim] = own[c, :rim] + jnp.where(odd, near[c], far[c])
        out[c, rim:] = own[c, rim:] + jnp.where(odd, far[c], near[c])


def stacked(tables):
    blocks, layout, at = [], {}, 0
    for name, table in tables.items():
        rows, lanes = table.shape
        layout[name] = (at, rows, lanes // 256)
        for b in range(lanes // 256):
            blocks.append(table[:, b * 256:(b + 1) * 256])
        at += rows * (lanes // 256)
    return np.concatenate(blocks, axis=0), layout


def on_device(mask_field, target, kernel_taps, kernel_radii, kernel_group, kernel_weight):
    _, count, width = mask_field.shape
    kernels, _, span, _ = kernel_taps.shape
    rim = span // 2
    grid_rows = count + 2 * rim
    grid_cols = width + rim
    units = kernels // UNIT
    assert count == span and width == span and kernels % (UNIT * UNITS) == 0 and span == 128

    strips = lax.axis_size("row")
    assert strips % 2 == 0
    at = lax.axis_index("row")
    near_pairs = [(i, i ^ 1) for i in range(strips)]
    far_pairs = [(i, ((i + 1) ^ 1) - 1) for i in range(1, strips - 1)]
    near = lax.ppermute(mask_field, "row", near_pairs)
    far = lax.ppermute(mask_field, "row", far_pairs)
    place = at.astype(jnp.int32).reshape(1)

    scale = 1.0 / (grid_rows * grid_cols)
    row_classes = [class_table(grid_rows, rim, c, 4) for c in range(4)]
    col_classes = [class_table(grid_cols, rim, c, 3) for c in range(3)]
    row_fwd = np.concatenate([halves(t, 0) for t in row_classes], axis=1)
    row_inv = np.concatenate([halves(t.T * scale, 0) for t in row_classes], axis=1)
    col_fwd = np.concatenate([halves(t.T, 1) for t in col_classes], axis=0)
    col_inv = np.concatenate([halves(t, 1) for t in col_classes], axis=0)
    tables, layout = stacked({"row_fwd": row_fwd, "row_inv": row_inv, "col_fwd": col_fwd, "col_inv": col_inv})

    smem = pl.BlockSpec(memory_space=pltpu.SMEM)
    vmem = pl.BlockSpec(memory_space=pltpu.VMEM)
    hbm = pl.BlockSpec(memory_space=pltpu.HBM)
    spec_shape = (units, 2, grid_rows, UNIT * grid_cols)
    spectra = pl.pallas_call(
        spectra_body,
        out_shape=jax.ShapeDtypeStruct(spec_shape, f32),
        in_specs=[smem, hbm, vmem, vmem],
        out_specs=hbm,
        scratch_shapes=[
            pltpu.VMEM(kernel_taps.shape, f32),
            pltpu.VMEM(spec_shape, f32),
            pltpu.SemaphoreType.DMA((units,)),
            pltpu.SemaphoreType.DMA((units,)),
        ],
        compiler_params=pltpu.CompilerParams(vmem_limit_bytes=56 * MIB),
        cost_estimate=pl.CostEstimate(flops=18 * 10**9, bytes_accessed=14 * 10**6, transcendentals=0),
        name="spectra",
    )(kernel_radii, kernel_taps, *map(jnp.asarray, (row_fwd, col_fwd)))

    resist, own, near_rim, far_rim = pl.pallas_call(
        functools.partial(main_body, layout=layout),
        out_shape=[
            jax.ShapeDtypeStruct((GROUPS, count, width), f32),
            jax.ShapeDtypeStruct((2, count, width), f32),
            jax.ShapeDtypeStruct((2, rim, width), f32),
            jax.ShapeDtypeStruct((2, rim, width), f32),
        ],
        in_specs=[smem] * 3 + [vmem] * 4 + [hbm] * 2,
        out_specs=[hbm] + [vmem] * 3,
        scratch_shapes=[
            pltpu.VMEM(spec_shape, f32),
            pltpu.VMEM((kernels, 2, count, width), f32),
            pltpu.VMEM((2, grid_rows, 2 * grid_cols), f32),
            pltpu.VMEM((GROUPS, count, width), f32),
            pltpu.VMEM((GROUPS, 2, count, width), f32),
            pltpu.VMEM((2, grid_rows, 2 * grid_cols), f32),
            pltpu.VMEM(tables.shape, bf16),
            pltpu.SemaphoreType.DMA((units,)),
            pltpu.SemaphoreType.DMA,
            pltpu.SemaphoreType.DMA,
        ],
        compiler_params=pltpu.CompilerParams(vmem_limit_bytes=LIMIT * MIB),
        name="fields",
    )(kernel_group, kernel_weight, place, mask_field, near, far, target, spectra, jnp.asarray(tables))

    near_in = lax.ppermute(near_rim, "row", near_pairs)
    far_in = lax.ppermute(far_rim, "row", far_pairs)
    gradient = pl.pallas_call(
        join_body,
        out_shape=jax.ShapeDtypeStruct((2, count, width), f32),
        in_specs=[smem] + [vmem] * 3,
        out_specs=vmem,
        compiler_params=pltpu.CompilerParams(vmem_limit_bytes=4 * MIB),
        name="join",
    )(place, own, near_in, far_in)
    return resist, gradient


def solution(mesh):
    in_specs = (P(None, ("win", "row"), None), P(("win", "row"), None), P(), P(), P(), P())
    out_specs = (P(None, ("win", "row"), None), P(None, ("win", "row"), None))
    return jax.shard_map(
        on_device, mesh=mesh, in_specs=in_specs, out_specs=out_specs, check_vma=False
    )
```

```python
import functools
import math

import jax
import jax.numpy as jnp
import ml_dtypes
import numpy as np
from jax import lax
from jax.experimental import pallas as pl
from jax.experimental.pallas import tpu as pltpu
from jax.sharding import PartitionSpec as P

RMAX = 64
GROUPS = 3
STEEPNESS = 1.0
THRESHOLD = 2.0
UNIT = 4
SPECTRA_UNITS = 6
UNITS = 3
PIECE = 256
TURN = math.sqrt(0.75)

f32 = jnp.float32
bf16 = jnp.bfloat16
MIB = 1024 * 1024
LIMIT = 53


def halves(table, axis):
    high = table.astype(ml_dtypes.bfloat16)
    low = (table - high.astype(np.float64)).astype(ml_dtypes.bfloat16)
    return np.concatenate([high, low], axis=axis)


def class_table(freqs, points, c, classes):
    f = np.arange(c, freqs, classes)[:, None]
    n = np.arange(points)[None, :]
    angle = 2.0 * math.pi * ((f * n) % freqs) / freqs
    cos, sin = np.cos(angle), np.sin(angle)
    return np.block([[cos, sin], [-sin, cos]])


def split(x):
    high = x.astype(bf16)
    low = (x - high.astype(f32)).astype(bf16)
    return high, low


def dot(left, right):
    parts = [
        jnp.dot(left[at:at + PIECE], right, preferred_element_type=f32)
        for at in range(0, left.shape[0], PIECE)
    ]
    return jnp.concatenate(parts, axis=0)


def swap(x):
    return pltpu.roll(x, x.shape[1] // 2, 1)


def first_half(x):
    return lax.broadcasted_iota(jnp.int32, x.shape, 1) < x.shape[1] // 2


def exchange(x, y):
    first = first_half(x)
    return jnp.where(first, x, swap(y)), jnp.where(first, swap(x), y)


def turned(x, sign):
    re, im = x
    return (-im, re) if sign > 0 else (im, -re)


def plus(x, y):
    return x[0] + y[0], x[1] + y[1]


def minus(x, y):
    return x[0] - y[0], x[1] - y[1]


def row_product(table, c, x):
    parts = split(x)
    depth = x.shape[0]
    left = table[:, c * depth:(c + 1) * depth]
    found = dot(jnp.concatenate([left, left], axis=1), jnp.concatenate(parts, axis=0))
    half = found.shape[0] // 2
    found = found[:half] + found[half:]
    return found[:half // 2], found[half // 2:]


def to_row_freqs(x, table):
    if len(x) == 2:
        even, odd, even_less, odd_less = x[0], x[1], x[0], x[1]
    else:
        even, odd = plus(x[0], x[2]), plus(x[1], x[3])
        even_less, odd_less = minus(x[0], x[2]), minus(x[1], x[3])
    folded = [
        plus(even, odd),
        plus(even_less, turned(odd_less, -1)),
        minus(even, odd),
        plus(even_less, turned(odd_less, 1)),
    ]
    return [row_product(table, c, jnp.concatenate(y, axis=0)) for c, y in enumerate(folded)]


def from_row_freqs(classes, table, quarters):
    v = [row_product(table, c, jnp.concatenate(y, axis=0)) for c, y in enumerate(classes)]
    out = []
    for q in quarters:
        if q % 2 == 0:
            even, odd = plus(v[0], v[2]), plus(v[1], v[3])
        else:
            even, odd = minus(v[0], v[2]), turned(minus(v[1], v[3]), 1)
        out.append(plus(even, odd) if q < 2 else minus(even, odd))
    return out


def quarters_of(re, im, quarter):
    return [(re[at:at + quarter], im[at:at + quarter]) for at in range(0, re.shape[0], quarter)]


def lane_turned(x):
    return swap(x) * jnp.where(first_half(x), TURN, -TURN)


def col_products(planes, table):
    rows = planes[0][0].shape[0]
    depth = table.shape[0] // 3
    out = [[] for _ in planes]
    for c in range(3):
        high, low = split(jnp.concatenate([plane[c] for plane in planes], axis=0))
        right = table[c * depth:(c + 1) * depth]
        found = dot(jnp.concatenate([high, low], axis=1), jnp.concatenate([right, right], axis=0))
        found = found[:, :depth] + found[:, depth:]
        for k in range(len(planes)):
            out[k].append(found[k * rows:(k + 1) * rows])
    return out


def to_col_freqs(planes, table, shifted=False):
    folded = []
    for left, right in planes:
        if shifted:
            left, right = right, left
        near, far = left - 0.5 * right, lane_turned(right)
        one, two = near + far, near - far
        folded.append([left + right, two, one] if shifted else [left + right, one, two])
    return col_products(folded, table)


def from_col_freqs(planes, table, shifted=False):
    out = []
    for v in col_products(planes, table):
        total, far = v[1] + v[2], lane_turned(v[1] - v[2])
        whole, part = v[0] + total, v[0] - 0.5 * total
        out.append((part + far, whole) if shifted else (whole, part - far))
    return out


def pairs_apart(planes):
    re, im = [], []
    for k in range(0, len(planes), 2):
        for x, y in zip(planes[k], planes[k + 1]):
            r, i = exchange(x, y)
            re.append(r)
            im.append(i)
    return jnp.concatenate(re, axis=1), jnp.concatenate(im, axis=1)


def pairs_together(re, im, width):
    planes = []
    for at in range(0, re.shape[1], 3 * width):
        both = [
            exchange(re[:, at + c * width:at + (c + 1) * width], im[:, at + c * width:at + (c + 1) * width])
            for c in range(3)
        ]
        planes += [[x for x, _ in both], [y for _, y in both]]
    return planes


def loop(steps, body):
    if steps == 1:
        body(0, 0)
    else:
        lax.fori_loop(0, steps, body, 0)


def staggered(count, first, second):
    held = None
    for i in range(count):
        new = first(i)
        if i:
            second(i - 1, held)
        held = new
    second(count - 1, held)


def spectra_body(radii, taps_far, row_ref, col_ref, spec_far, taps, spec, in_sems, out_sems):
    kernels, _, span, _ = taps.shape
    row_fwd, col_fwd = row_ref[...], col_ref[...]
    quarter = span // 2
    steps = kernels // (UNIT * SPECTRA_UNITS)

    def fetch(u):
        here = pl.ds(u * UNIT, UNIT)
        return pltpu.make_async_copy(taps_far.at[here], taps.at[here], in_sems.at[u])

    def put(u):
        return pltpu.make_async_copy(spec.at[u], spec_far.at[u], out_sems.at[u])

    for u in range(kernels // UNIT):
        fetch(u).start()
    row_at = lax.broadcasted_iota(jnp.int32, (span, span), 0) - span // 2
    col_at = lax.broadcasted_iota(jnp.int32, (span, span), 1) - span // 2
    reach = jnp.maximum(jnp.maximum(row_at, -1 - row_at), jnp.maximum(col_at, -1 - col_at))

    def step(i, carry):
        def cols_of(p):
            u = i * SPECTRA_UNITS + p
            fetch(u).wait()
            planes = []
            for j in range(UNIT):
                k = u * UNIT + j
                inside = reach < radii[k]
                planes.append(exchange(*[jnp.where(inside, taps[k, c], 0.0) for c in range(2)]))
            return pairs_apart(to_col_freqs(planes, col_fwd))

        def rows_of(p, both):
            u = i * SPECTRA_UNITS + p
            for c, found in enumerate(to_row_freqs(quarters_of(*both, quarter), row_fwd)):
                for part in range(2):
                    spec[u, part, c * quarter:(c + 1) * quarter] = found[part]
            put(u).start()

        staggered(SPECTRA_UNITS, cols_of, rows_of)
        return carry

    loop(steps, step)
    for u in range(kernels // UNIT):
        put(u).wait()


def main_body(
    group, weight, place,
    own, near, far, target, spec_far, tables_far,
    resist_far, grad_own, near_rim, far_rim,
    spec, field, mask_spec, resist, slopes, grad_spec, tables, spec_sems, table_sem, out_sem,
    *, layout,
):
    count, width = target.shape
    rim = count // 2
    units = spec.shape[0]
    steps = units // UNITS

    def fetch(u):
        return pltpu.make_async_copy(spec_far.at[u], spec.at[u], spec_sems.at[u])

    def table(name):
        start, rows, blocks = layout[name]
        parts = [tables[start + b * rows:start + (b + 1) * rows] for b in range(blocks)]
        return jnp.concatenate(parts, axis=1)

    fetch_tables = pltpu.make_async_copy(tables_far, tables, table_sem)
    fetch_tables.start()
    for u in range(units):
        fetch(u).start()
    slopes[...] = jnp.zeros(slopes.shape, f32)
    grad_spec[...] = jnp.zeros(grad_spec.shape, f32)
    fetch_tables.wait()
    row_fwd, row_inv, col_fwd, col_inv = [table(name) for name in ("row_fwd", "row_inv", "col_fwd", "col_inv")]

    odd = place[0] % 2 == 1
    mask = []
    for c in range(2):
        above = jnp.where(odd, near[c, count - rim:], far[c, count - rim:])
        below = jnp.where(odd, far[c, :rim], near[c, :rim])
        mask.append(jnp.concatenate([own[c, rim:], below, above, own[c, :rim]], axis=0))
    plane, = to_col_freqs([exchange(*mask)], col_fwd, shifted=True)
    both = pairs_apart([plane, plane])
    for c, found in enumerate(to_row_freqs(quarters_of(*both, rim), row_fwd)):
        for part in range(2):
            mask_spec[part, c * rim:(c + 1) * rim] = found[part]

    def forward(i, carry):
        def rows_of(p):
            u = i * UNITS + p
            fetch(u).wait()
            classes = []
            for c in range(4):
                here = slice(c * rim, (c + 1) * rim)
                m_re, m_im = [jnp.concatenate([mask_spec[part, here]] * (UNIT // 2), axis=1) for part in range(2)]
                s_re, s_im = spec[u, 0, here], spec[u, 1, here]
                classes.append((s_re * m_re - s_im * m_im, s_re * m_im + s_im * m_re))
            upper, lower = from_row_freqs(classes, row_inv, (0, 1))
            return [jnp.concatenate([upper[part], lower[part]], axis=0) for part in range(2)]

        def cols_of(p, both):
            u = i * UNITS + p
            found = from_col_freqs(pairs_together(*both, width), col_inv)
            for j in range(UNIT):
                k = u * UNIT + j
                for side in range(2):
                    x = found[j][side]
                    field[k, side] = x
                    slopes[group[k], side] = slopes[group[k], side] + weight[k] * (x * x)

        staggered(UNITS, rows_of, cols_of)
        return carry

    loop(steps, forward)

    wanted = target[...].astype(f32)
    for g in range(GROUPS):
        left, right = [slopes[g, side] + swap(slopes[g, side]) for side in range(2)]
        seen = jax.nn.sigmoid(STEEPNESS * (jnp.where(first_half(left), left, right) - THRESHOLD))
        resist[g] = seen
        slope = 2.0 * (seen - wanted) * seen * (1.0 - seen) * STEEPNESS
        slopes[g, 0], slopes[g, 1] = exchange(slope, slope)
    out = pltpu.make_async_copy(resist, resist_far, out_sem)
    out.start()

    def backward(i, carry):
        def cols_of(p):
            u = i * UNITS + p
            planes = []
            for j in range(UNIT):
                k = u * UNIT + j
                planes.append([field[k, side] * ((2.0 * weight[k]) * slopes[group[k], side]) for side in range(2)])
            return pairs_apart(to_col_freqs(planes, col_fwd))

        def rows_of(p, both):
            u = i * UNITS + p
            for c, (c_re, c_im) in enumerate(to_row_freqs(quarters_of(*both, rim), row_fwd)):
                here = slice(c * rim, (c + 1) * rim)
                s_re, s_im = spec[u, 0, here], spec[u, 1, here]
                terms = s_re * c_re + s_im * c_im, s_re * c_im - s_im * c_re
                for part in range(2):
                    total = grad_spec[part, here]
                    lanes = total.shape[1]
                    for at in range(0, terms[part].shape[1], lanes):
                        total = total + terms[part][:, at:at + lanes]
                    grad_spec[part, here] = total

        staggered(UNITS, cols_of, rows_of)
        return carry

    loop(steps, backward)

    classes = [tuple(grad_spec[part, c * rim:(c + 1) * rim] for part in range(2)) for c in range(4)]
    quarters = from_row_freqs(classes, row_inv, (2, 3, 0, 1))
    re, im = [jnp.concatenate([x[part] for x in quarters], axis=0) for part in range(2)]
    first, second = pairs_together(re, im, width)
    plane = [x + y for x, y in zip(first, second)]
    halves_found, = from_col_freqs([plane], col_inv, shifted=True)
    for c, full in enumerate(exchange(*halves_found)):
        rise, fall = full[:rim], full[rim + count:]
        near_rim[c] = jnp.where(odd, rise, fall)
        far_rim[c] = jnp.where(odd, fall, rise)
        grad_own[c] = full[rim:rim + count]
    out.wait()


def join_body(place, own, near, far, out):
    odd = place[0] % 2 == 1
    rim = near.shape[1]
    for c in range(2):
        out[c, :rim] = own[c, :rim] + jnp.where(odd, near[c], far[c])
        out[c, rim:] = own[c, rim:] + jnp.where(odd, far[c], near[c])


def stacked(tables):
    blocks, layout, at = [], {}, 0
    for name, table in tables.items():
        rows, lanes = table.shape
        layout[name] = (at, rows, lanes // 256)
        for b in range(lanes // 256):
            blocks.append(table[:, b * 256:(b + 1) * 256])
        at += rows * (lanes // 256)
    return np.concatenate(blocks, axis=0), layout


def on_device(mask_field, target, kernel_taps, kernel_radii, kernel_group, kernel_weight):
    _, count, width = mask_field.shape
    kernels, _, span, _ = kernel_taps.shape
    rim = span // 2
    grid_rows = count + 2 * rim
    grid_cols = width + rim
    units = kernels // UNIT
    assert count == span and width == span and units % UNITS == 0 and units % SPECTRA_UNITS == 0 and kernels % UNIT == 0 and span == 128

    strips = lax.axis_size("row")
    assert strips % 2 == 0
    at = lax.axis_index("row")
    near_pairs = [(i, i ^ 1) for i in range(strips)]
    far_pairs = [(i, ((i + 1) ^ 1) - 1) for i in range(1, strips - 1)]
    near = lax.ppermute(mask_field, "row", near_pairs)
    far = lax.ppermute(mask_field, "row", far_pairs)
    place = at.astype(jnp.int32).reshape(1)

    scale = 1.0 / (grid_rows * grid_cols)
    row_classes = [class_table(grid_rows, rim, c, 4) for c in range(4)]
    col_classes = [class_table(grid_cols, rim, c, 3) for c in range(3)]
    row_fwd = np.concatenate([halves(t, 0) for t in row_classes], axis=1)
    row_inv = np.concatenate([halves(t.T * scale, 0) for t in row_classes], axis=1)
    col_fwd = np.concatenate([halves(t.T, 1) for t in col_classes], axis=0)
    col_inv = np.concatenate([halves(t, 1) for t in col_classes], axis=0)
    tables, layout = stacked({"row_fwd": row_fwd, "row_inv": row_inv, "col_fwd": col_fwd, "col_inv": col_inv})

    smem = pl.BlockSpec(memory_space=pltpu.SMEM)
    vmem = pl.BlockSpec(memory_space=pltpu.VMEM)
    hbm = pl.BlockSpec(memory_space=pltpu.HBM)
    spec_shape = (units, 2, grid_rows, UNIT * grid_cols)
    spectra = pl.pallas_call(
        spectra_body,
        out_shape=jax.ShapeDtypeStruct(spec_shape, f32),
        in_specs=[smem, hbm, vmem, vmem],
        out_specs=hbm,
        scratch_shapes=[
            pltpu.VMEM(kernel_taps.shape, f32),
            pltpu.VMEM(spec_shape, f32),
            pltpu.SemaphoreType.DMA((units,)),
            pltpu.SemaphoreType.DMA((units,)),
        ],
        compiler_params=pltpu.CompilerParams(vmem_limit_bytes=56 * MIB),
        cost_estimate=pl.CostEstimate(flops=18 * 10**9, bytes_accessed=14 * 10**6, transcendentals=0),
        name="spectra",
    )(kernel_radii, kernel_taps, *map(jnp.asarray, (row_fwd, col_fwd)))

    resist, own, near_rim, far_rim = pl.pallas_call(
        functools.partial(main_body, layout=layout),
        out_shape=[
            jax.ShapeDtypeStruct((GROUPS, count, width), f32),
            jax.ShapeDtypeStruct((2, count, width), f32),
            jax.ShapeDtypeStruct((2, rim, width), f32),
            jax.ShapeDtypeStruct((2, rim, width), f32),
        ],
        in_specs=[smem] * 3 + [vmem] * 4 + [hbm] * 2,
        out_specs=[hbm] + [vmem] * 3,
        scratch_shapes=[
            pltpu.VMEM(spec_shape, f32),
            pltpu.VMEM((kernels, 2, count, width), f32),
            pltpu.VMEM((2, grid_rows, 2 * grid_cols), f32),
            pltpu.VMEM((GROUPS, count, width), f32),
            pltpu.VMEM((GROUPS, 2, count, width), f32),
            pltpu.VMEM((2, grid_rows, 2 * grid_cols), f32),
            pltpu.VMEM(tables.shape, bf16),
            pltpu.SemaphoreType.DMA((units,)),
            pltpu.SemaphoreType.DMA,
            pltpu.SemaphoreType.DMA,
        ],
        compiler_params=pltpu.CompilerParams(vmem_limit_bytes=LIMIT * MIB),
        name="fields",
    )(kernel_group, kernel_weight, place, mask_field, near, far, target, spectra, jnp.asarray(tables))

    near_in = lax.ppermute(near_rim, "row", near_pairs)
    far_in = lax.ppermute(far_rim, "row", far_pairs)
    gradient = pl.pallas_call(
        join_body,
        out_shape=jax.ShapeDtypeStruct((2, count, width), f32),
        in_specs=[smem] + [vmem] * 3,
        out_specs=vmem,
        compiler_params=pltpu.CompilerParams(vmem_limit_bytes=4 * MIB),
        name="join",
    )(place, own, near_in, far_in)
    return resist, gradient


def solution(mesh):
    in_specs = (P(None, ("win", "row"), None), P(("win", "row"), None), P(), P(), P(), P())
    out_specs = (P(None, ("win", "row"), None), P(None, ("win", "row"), None))
    return jax.shard_map(
        on_device, mesh=mesh, in_specs=in_specs, out_specs=out_specs, check_vma=False
    )
```

```python
import functools
import math

import jax
import jax.numpy as jnp
import ml_dtypes
import numpy as np
from jax import lax
from jax.experimental import pallas as pl
from jax.experimental.pallas import tpu as pltpu
from jax.sharding import PartitionSpec as P

RMAX = 64
GROUPS = 3
STEEPNESS = 1.0
THRESHOLD = 2.0
UNIT = 4
SPECTRA_UNITS = 3
UNITS = 2
PIECE = 256
TURN = math.sqrt(0.75)

f32 = jnp.float32
bf16 = jnp.bfloat16
MIB = 1024 * 1024
LIMIT = 53


def halves(table, axis):
    high = table.astype(ml_dtypes.bfloat16)
    low = (table - high.astype(np.float64)).astype(ml_dtypes.bfloat16)
    return np.concatenate([high, low], axis=axis)


def class_table(freqs, points, c, classes):
    f = np.arange(c, freqs, classes)[:, None]
    n = np.arange(points)[None, :]
    angle = 2.0 * math.pi * ((f * n) % freqs) / freqs
    cos, sin = np.cos(angle), np.sin(angle)
    return np.block([[cos, sin], [-sin, cos]])


def split(x, dtype):
    if dtype == f32:
        wide = x * 65537.0
        high = wide - (wide - x)
        return high, x - high
    high = x.astype(bf16)
    low = (x - high.astype(f32)).astype(bf16)
    return high, low


def dot(left, right):
    parts = [
        jnp.dot(left[at:at + PIECE], right, preferred_element_type=f32)
        for at in range(0, left.shape[0], PIECE)
    ]
    return jnp.concatenate(parts, axis=0)


def swap(x):
    return pltpu.roll(x, x.shape[1] // 2, 1)


def first_half(x):
    return lax.broadcasted_iota(jnp.int32, x.shape, 1) < x.shape[1] // 2


def exchange(x, y):
    first = first_half(x)
    return jnp.where(first, x, swap(y)), jnp.where(first, swap(x), y)


def turned(x, sign):
    re, im = x
    return (-im, re) if sign > 0 else (im, -re)


def plus(x, y):
    return x[0] + y[0], x[1] + y[1]


def minus(x, y):
    return x[0] - y[0], x[1] - y[1]


def row_product(table, c, x):
    parts = split(x, table.dtype)
    depth = x.shape[0]
    left = table[:, c * depth:(c + 1) * depth]
    found = dot(jnp.concatenate([left, left], axis=1), jnp.concatenate(parts, axis=0))
    half = found.shape[0] // 2
    found = found[:half] + found[half:]
    return found[:half // 2], found[half // 2:]


def to_row_freqs(x, table):
    if len(x) == 2:
        even, odd, even_less, odd_less = x[0], x[1], x[0], x[1]
    else:
        even, odd = plus(x[0], x[2]), plus(x[1], x[3])
        even_less, odd_less = minus(x[0], x[2]), minus(x[1], x[3])
    folded = [
        plus(even, odd),
        plus(even_less, turned(odd_less, -1)),
        minus(even, odd),
        plus(even_less, turned(odd_less, 1)),
    ]
    return [row_product(table, c, jnp.concatenate(y, axis=0)) for c, y in enumerate(folded)]


def from_row_freqs(classes, table, quarters):
    v = [row_product(table, c, jnp.concatenate(y, axis=0)) for c, y in enumerate(classes)]
    out = []
    for q in quarters:
        if q % 2 == 0:
            even, odd = plus(v[0], v[2]), plus(v[1], v[3])
        else:
            even, odd = minus(v[0], v[2]), turned(minus(v[1], v[3]), 1)
        out.append(plus(even, odd) if q < 2 else minus(even, odd))
    return out


def quarters_of(re, im, quarter):
    return [(re[at:at + quarter], im[at:at + quarter]) for at in range(0, re.shape[0], quarter)]


def lane_turned(x):
    return swap(x) * jnp.where(first_half(x), TURN, -TURN)


def col_products(planes, table):
    rows = planes[0][0].shape[0]
    depth = table.shape[0] // 3
    out = [[] for _ in planes]
    for c in range(3):
        high, low = split(jnp.concatenate([plane[c] for plane in planes], axis=0), table.dtype)
        right = table[c * depth:(c + 1) * depth]
        found = dot(jnp.concatenate([high, low], axis=1), jnp.concatenate([right, right], axis=0))
        found = found[:, :depth] + found[:, depth:]
        for k in range(len(planes)):
            out[k].append(found[k * rows:(k + 1) * rows])
    return out


def to_col_freqs(planes, table, shifted=False):
    folded = []
    for left, right in planes:
        if shifted:
            left, right = right, left
        near, far = left - 0.5 * right, lane_turned(right)
        one, two = near + far, near - far
        folded.append([left + right, two, one] if shifted else [left + right, one, two])
    return col_products(folded, table)


def from_col_freqs(planes, table, shifted=False):
    out = []
    for v in col_products(planes, table):
        total, far = v[1] + v[2], lane_turned(v[1] - v[2])
        whole, part = v[0] + total, v[0] - 0.5 * total
        out.append((part + far, whole) if shifted else (whole, part - far))
    return out


def pairs_apart(planes):
    re, im = [], []
    for k in range(0, len(planes), 2):
        for x, y in zip(planes[k], planes[k + 1]):
            r, i = exchange(x, y)
            re.append(r)
            im.append(i)
    return jnp.concatenate(re, axis=1), jnp.concatenate(im, axis=1)


def pairs_together(re, im, width):
    planes = []
    for at in range(0, re.shape[1], 3 * width):
        both = [
            exchange(re[:, at + c * width:at + (c + 1) * width], im[:, at + c * width:at + (c + 1) * width])
            for c in range(3)
        ]
        planes += [[x for x, _ in both], [y for _, y in both]]
    return planes


def loop(steps, body):
    if steps == 1:
        body(0, 0)
    else:
        lax.fori_loop(0, steps, body, 0)


def staggered(count, first, second):
    held = None
    for i in range(count):
        new = first(i)
        if i:
            second(i - 1, held)
        held = new
    second(count - 1, held)


def spectra_body(radii, taps_far, row_ref, col_ref, spec_far, taps, spec, in_sems, out_sems):
    kernels, _, span, _ = taps.shape
    row_fwd, col_fwd = row_ref[...], col_ref[...]
    quarter = span // 2
    steps = kernels // (UNIT * SPECTRA_UNITS)

    def fetch(u):
        here = pl.ds(u * UNIT, UNIT)
        return pltpu.make_async_copy(taps_far.at[here], taps.at[here], in_sems.at[u])

    def put(u):
        return pltpu.make_async_copy(spec.at[u], spec_far.at[u], out_sems.at[u])

    for u in range(kernels // UNIT):
        fetch(u).start()
    row_at = lax.broadcasted_iota(jnp.int32, (span, span), 0) - span // 2
    col_at = lax.broadcasted_iota(jnp.int32, (span, span), 1) - span // 2
    reach = jnp.maximum(jnp.maximum(row_at, -1 - row_at), jnp.maximum(col_at, -1 - col_at))

    def step(i, carry):
        def cols_of(p):
            u = i * SPECTRA_UNITS + p
            fetch(u).wait()
            planes = []
            for j in range(UNIT):
                k = u * UNIT + j
                inside = reach < radii[k]
                planes.append(exchange(*[jnp.where(inside, taps[k, c], 0.0) for c in range(2)]))
            return pairs_apart(to_col_freqs(planes, col_fwd))

        def rows_of(p, both):
            u = i * SPECTRA_UNITS + p
            for c, found in enumerate(to_row_freqs(quarters_of(*both, quarter), row_fwd)):
                for part in range(2):
                    spec[u, part, c * quarter:(c + 1) * quarter] = found[part]
            put(u).start()

        staggered(SPECTRA_UNITS, cols_of, rows_of)
        return carry

    loop(steps, step)
    for u in range(kernels // UNIT):
        put(u).wait()


def main_body(
    group, weight, place,
    own, near, far, target, spec_far, tables_far,
    resist_far, grad_own, near_rim, far_rim,
    spec, field, mask_spec, resist, slopes, grad_spec, tables, spec_sems, table_sem, out_sem,
    *, layout,
):
    count, width = target.shape
    rim = count // 2
    units = spec.shape[0]
    steps = units // UNITS

    def fetch(u):
        return pltpu.make_async_copy(spec_far.at[u], spec.at[u], spec_sems.at[u])

    def table(name):
        start, rows, blocks = layout[name]
        parts = [tables[start + b * rows:start + (b + 1) * rows] for b in range(blocks)]
        return jnp.concatenate(parts, axis=1)

    fetch_tables = pltpu.make_async_copy(tables_far, tables, table_sem)
    fetch_tables.start()
    for u in range(units):
        fetch(u).start()
    slopes[...] = jnp.zeros(slopes.shape, f32)
    grad_spec[...] = jnp.zeros(grad_spec.shape, f32)
    fetch_tables.wait()
    row_fwd, row_inv, col_fwd, col_inv = [table(name) for name in ("row_fwd", "row_inv", "col_fwd", "col_inv")]

    odd = place[0] % 2 == 1
    mask = []
    for c in range(2):
        above = jnp.where(odd, near[c, count - rim:], far[c, count - rim:])
        below = jnp.where(odd, far[c, :rim], near[c, :rim])
        mask.append(jnp.concatenate([own[c, rim:], below, above, own[c, :rim]], axis=0))
    plane, = to_col_freqs([exchange(*mask)], col_fwd, shifted=True)
    both = pairs_apart([plane, plane])
    for c, found in enumerate(to_row_freqs(quarters_of(*both, rim), row_fwd)):
        for part in range(2):
            mask_spec[part, c * rim:(c + 1) * rim] = found[part]

    def forward(i, carry):
        def rows_of(p):
            u = i * UNITS + p
            fetch(u).wait()
            classes = []
            for c in range(4):
                here = slice(c * rim, (c + 1) * rim)
                m_re, m_im = [jnp.concatenate([mask_spec[part, here]] * (UNIT // 2), axis=1) for part in range(2)]
                s_re, s_im = spec[u, 0, here], spec[u, 1, here]
                classes.append((s_re * m_re - s_im * m_im, s_re * m_im + s_im * m_re))
            upper, lower = from_row_freqs(classes, row_inv, (0, 1))
            return [jnp.concatenate([upper[part], lower[part]], axis=0) for part in range(2)]

        def cols_of(p, both):
            u = i * UNITS + p
            found = from_col_freqs(pairs_together(*both, width), col_inv)
            for j in range(UNIT):
                k = u * UNIT + j
                for side in range(2):
                    x = found[j][side]
                    field[k, side] = x
                    slopes[group[k], side] = slopes[group[k], side] + weight[k] * (x * x)

        staggered(UNITS, rows_of, cols_of)
        return carry

    loop(steps, forward)

    wanted = target[...].astype(f32)
    for g in range(GROUPS):
        left, right = [slopes[g, side] + swap(slopes[g, side]) for side in range(2)]
        seen = jax.nn.sigmoid(STEEPNESS * (jnp.where(first_half(left), left, right) - THRESHOLD))
        resist[g] = seen
        slope = 2.0 * (seen - wanted) * seen * (1.0 - seen) * STEEPNESS
        slopes[g, 0], slopes[g, 1] = exchange(slope, slope)
    out = pltpu.make_async_copy(resist, resist_far, out_sem)
    out.start()

    def backward(i, carry):
        def cols_of(p):
            u = i * UNITS + p
            planes = []
            for j in range(UNIT):
                k = u * UNIT + j
                planes.append([field[k, side] * ((2.0 * weight[k]) * slopes[group[k], side]) for side in range(2)])
            return pairs_apart(to_col_freqs(planes, col_fwd))

        def rows_of(p, both):
            u = i * UNITS + p
            for c, (c_re, c_im) in enumerate(to_row_freqs(quarters_of(*both, rim), row_fwd)):
                here = slice(c * rim, (c + 1) * rim)
                s_re, s_im = spec[u, 0, here], spec[u, 1, here]
                terms = s_re * c_re + s_im * c_im, s_re * c_im - s_im * c_re
                for part in range(2):
                    total = grad_spec[part, here]
                    lanes = total.shape[1]
                    for at in range(0, terms[part].shape[1], lanes):
                        total = total + terms[part][:, at:at + lanes]
                    grad_spec[part, here] = total

        staggered(UNITS, cols_of, rows_of)
        return carry

    loop(steps, backward)

    classes = [tuple(grad_spec[part, c * rim:(c + 1) * rim] for part in range(2)) for c in range(4)]
    quarters = from_row_freqs(classes, row_inv, (2, 3, 0, 1))
    re, im = [jnp.concatenate([x[part] for x in quarters], axis=0) for part in range(2)]
    first, second = pairs_together(re, im, width)
    plane = [x + y for x, y in zip(first, second)]
    halves_found, = from_col_freqs([plane], col_inv, shifted=True)
    for c, full in enumerate(exchange(*halves_found)):
        rise, fall = full[:rim], full[rim + count:]
        near_rim[c] = jnp.where(odd, rise, fall)
        far_rim[c] = jnp.where(odd, fall, rise)
        grad_own[c] = full[rim:rim + count]
    out.wait()


def join_body(place, own, near, far, out):
    odd = place[0] % 2 == 1
    rim = near.shape[1]
    for c in range(2):
        out[c, :rim] = own[c, :rim] + jnp.where(odd, near[c], far[c])
        out[c, rim:] = own[c, rim:] + jnp.where(odd, far[c], near[c])


def stacked(tables):
    blocks, layout, at = [], {}, 0
    for name, table in tables.items():
        rows, lanes = table.shape
        layout[name] = (at, rows, lanes // 256)
        for b in range(lanes // 256):
            blocks.append(table[:, b * 256:(b + 1) * 256])
        at += rows * (lanes // 256)
    return np.concatenate(blocks, axis=0), layout


def on_device(mask_field, target, kernel_taps, kernel_radii, kernel_group, kernel_weight):
    _, count, width = mask_field.shape
    kernels, _, span, _ = kernel_taps.shape
    rim = span // 2
    grid_rows = count + 2 * rim
    grid_cols = width + rim
    units = kernels // UNIT
    assert count == span and width == span and units % UNITS == 0 and units % SPECTRA_UNITS == 0 and kernels % UNIT == 0 and span == 128

    strips = lax.axis_size("row")
    assert strips % 2 == 0
    at = lax.axis_index("row")
    near_pairs = [(i, i ^ 1) for i in range(strips)]
    far_pairs = [(i, ((i + 1) ^ 1) - 1) for i in range(1, strips - 1)]
    near = lax.ppermute(mask_field, "row", near_pairs)
    far = lax.ppermute(mask_field, "row", far_pairs)
    place = at.astype(jnp.int32).reshape(1)

    scale = 1.0 / (grid_rows * grid_cols)
    row_classes = [class_table(grid_rows, rim, c, 4) for c in range(4)]
    col_classes = [class_table(grid_cols, rim, c, 3) for c in range(3)]
    row_fwd = np.concatenate([halves(t, 0) for t in row_classes], axis=1)
    row_inv = np.concatenate([halves(t.T * scale, 0) for t in row_classes], axis=1)
    col_fwd = np.concatenate([halves(t.T, 1) for t in col_classes], axis=0)
    col_inv = np.concatenate([halves(t, 1) for t in col_classes], axis=0)
    tables, layout = stacked({"row_fwd": row_fwd, "row_inv": row_inv, "col_fwd": col_fwd, "col_inv": col_inv})

    smem = pl.BlockSpec(memory_space=pltpu.SMEM)
    vmem = pl.BlockSpec(memory_space=pltpu.VMEM)
    hbm = pl.BlockSpec(memory_space=pltpu.HBM)
    spec_shape = (units, 2, grid_rows, UNIT * grid_cols)
    spectra = pl.pallas_call(
        spectra_body,
        out_shape=jax.ShapeDtypeStruct(spec_shape, f32),
        in_specs=[smem, hbm, vmem, vmem],
        out_specs=hbm,
        scratch_shapes=[
            pltpu.VMEM(kernel_taps.shape, f32),
            pltpu.VMEM(spec_shape, f32),
            pltpu.SemaphoreType.DMA((units,)),
            pltpu.SemaphoreType.DMA((units,)),
        ],
        compiler_params=pltpu.CompilerParams(vmem_limit_bytes=56 * MIB),
        cost_estimate=pl.CostEstimate(flops=18 * 10**9, bytes_accessed=14 * 10**6, transcendentals=0),
        name="spectra",
    )(kernel_radii, kernel_taps, *[jnp.asarray(t.astype(np.float32)) for t in (row_fwd, col_fwd)])

    resist, own, near_rim, far_rim = pl.pallas_call(
        functools.partial(main_body, layout=layout),
        out_shape=[
            jax.ShapeDtypeStruct((GROUPS, count, width), f32),
            jax.ShapeDtypeStruct((2, count, width), f32),
            jax.ShapeDtypeStruct((2, rim, width), f32),
            jax.ShapeDtypeStruct((2, rim, width), f32),
        ],
        in_specs=[smem] * 3 + [vmem] * 4 + [hbm] * 2,
        out_specs=[hbm] + [vmem] * 3,
        scratch_shapes=[
            pltpu.VMEM(spec_shape, f32),
            pltpu.VMEM((kernels, 2, count, width), f32),
            pltpu.VMEM((2, grid_rows, 2 * grid_cols), f32),
            pltpu.VMEM((GROUPS, count, width), f32),
            pltpu.VMEM((GROUPS, 2, count, width), f32),
            pltpu.VMEM((2, grid_rows, 2 * grid_cols), f32),
            pltpu.VMEM(tables.shape, bf16),
            pltpu.SemaphoreType.DMA((units,)),
            pltpu.SemaphoreType.DMA,
            pltpu.SemaphoreType.DMA,
        ],
        compiler_params=pltpu.CompilerParams(vmem_limit_bytes=LIMIT * MIB),
        name="fields",
    )(kernel_group, kernel_weight, place, mask_field, near, far, target, spectra, jnp.asarray(tables))

    near_in = lax.ppermute(near_rim, "row", near_pairs)
    far_in = lax.ppermute(far_rim, "row", far_pairs)
    gradient = pl.pallas_call(
        join_body,
        out_shape=jax.ShapeDtypeStruct((2, count, width), f32),
        in_specs=[smem] + [vmem] * 3,
        out_specs=vmem,
        compiler_params=pltpu.CompilerParams(vmem_limit_bytes=4 * MIB),
        name="join",
    )(place, own, near_in, far_in)
    return resist, gradient


def solution(mesh):
    in_specs = (P(None, ("win", "row"), None), P(("win", "row"), None), P(), P(), P(), P())
    out_specs = (P(None, ("win", "row"), None), P(None, ("win", "row"), None))
    return jax.shard_map(
        on_device, mesh=mesh, in_specs=in_specs, out_specs=out_specs, check_vma=False
    )
```

```python
import functools
import math

import jax
import jax.numpy as jnp
import ml_dtypes
import numpy as np
from jax import lax
from jax.experimental import pallas as pl
from jax.experimental.pallas import tpu as pltpu
from jax.sharding import PartitionSpec as P

RMAX = 64
GROUPS = 3
STEEPNESS = 1.0
THRESHOLD = 2.0
UNIT = 4
SPECTRA_UNITS = 3
UNITS = 3
CHUNK = 32
PIECE = 256
TURN = math.sqrt(0.75)

f32 = jnp.float32
bf16 = jnp.bfloat16
MIB = 1024 * 1024
LIMIT = 53


def halves(table, axis):
    high = table.astype(ml_dtypes.bfloat16)
    low = (table - high.astype(np.float64)).astype(ml_dtypes.bfloat16)
    return np.concatenate([high, low], axis=axis)


def class_table(freqs, points, c, classes):
    f = np.arange(c, freqs, classes)[:, None]
    n = np.arange(points)[None, :]
    angle = 2.0 * math.pi * ((f * n) % freqs) / freqs
    cos, sin = np.cos(angle), np.sin(angle)
    return np.block([[cos, sin], [-sin, cos]])


def split(x):
    high = x.astype(bf16)
    low = (x - high.astype(f32)).astype(bf16)
    return high, low


def dot(left, right):
    parts = [
        jnp.dot(left[at:at + PIECE], right, preferred_element_type=f32)
        for at in range(0, left.shape[0], PIECE)
    ]
    return jnp.concatenate(parts, axis=0)


def swap(x):
    return pltpu.roll(x, x.shape[1] // 2, 1)


def first_half(x):
    return lax.broadcasted_iota(jnp.int32, x.shape, 1) < x.shape[1] // 2


def exchange(x, y):
    first = first_half(x)
    return jnp.where(first, x, swap(y)), jnp.where(first, swap(x), y)


def turned(x, sign):
    re, im = x
    return (-im, re) if sign > 0 else (im, -re)


def plus(x, y):
    return x[0] + y[0], x[1] + y[1]


def minus(x, y):
    return x[0] - y[0], x[1] - y[1]


def row_product(table, c, x):
    parts = split(x)
    depth = x.shape[0]
    left = table[:, c * depth:(c + 1) * depth]
    found = dot(jnp.concatenate([left, left], axis=1), jnp.concatenate(parts, axis=0))
    half = found.shape[0] // 2
    found = found[:half] + found[half:]
    return found[:half // 2], found[half // 2:]


def fold_rows(x):
    if len(x) == 2:
        even, odd, even_less, odd_less = x[0], x[1], x[0], x[1]
    else:
        even, odd = plus(x[0], x[2]), plus(x[1], x[3])
        even_less, odd_less = minus(x[0], x[2]), minus(x[1], x[3])
    return [
        plus(even, odd),
        plus(even_less, turned(odd_less, -1)),
        minus(even, odd),
        plus(even_less, turned(odd_less, 1)),
    ]


def unfold_rows(v, quarters):
    out = []
    for q in quarters:
        if q % 2 == 0:
            even, odd = plus(v[0], v[2]), plus(v[1], v[3])
        else:
            even, odd = minus(v[0], v[2]), turned(minus(v[1], v[3]), 1)
        out.append(plus(even, odd) if q < 2 else minus(even, odd))
    return out


def to_row_freqs(x, table):
    return [row_product(table, c, jnp.concatenate(y, axis=0)) for c, y in enumerate(fold_rows(x))]


def from_row_freqs(classes, table, quarters):
    v = [row_product(table, c, jnp.concatenate(y, axis=0)) for c, y in enumerate(classes)]
    return unfold_rows(v, quarters)


def quarters_of(re, im, quarter):
    return [(re[at:at + quarter], im[at:at + quarter]) for at in range(0, re.shape[0], quarter)]


def lane_turned(x):
    return swap(x) * jnp.where(first_half(x), TURN, -TURN)


def col_products(planes, table):
    rows = planes[0][0].shape[0]
    depth = table.shape[0] // 3
    out = [[] for _ in planes]
    for c in range(3):
        high, low = split(jnp.concatenate([plane[c] for plane in planes], axis=0))
        right = table[c * depth:(c + 1) * depth]
        found = dot(jnp.concatenate([high, low], axis=1), jnp.concatenate([right, right], axis=0))
        found = found[:, :depth] + found[:, depth:]
        for k in range(len(planes)):
            out[k].append(found[k * rows:(k + 1) * rows])
    return out


def fold_cols(left, right, shifted=False):
    if shifted:
        left, right = right, left
    near, far = left - 0.5 * right, lane_turned(right)
    one, two = near + far, near - far
    return [left + right, two, one] if shifted else [left + right, one, two]


def unfold_cols(v, shifted=False):
    total, far = v[1] + v[2], lane_turned(v[1] - v[2])
    whole, part = v[0] + total, v[0] - 0.5 * total
    return (part + far, whole) if shifted else (whole, part - far)


def to_col_freqs(planes, table, shifted=False):
    return col_products([fold_cols(*halves_of, shifted) for halves_of in planes], table)


def from_col_freqs(planes, table, shifted=False):
    return [unfold_cols(v, shifted) for v in col_products(planes, table)]


def pairs_apart(planes):
    re, im = [], []
    for k in range(0, len(planes), 2):
        for x, y in zip(planes[k], planes[k + 1]):
            r, i = exchange(x, y)
            re.append(r)
            im.append(i)
    return jnp.concatenate(re, axis=1), jnp.concatenate(im, axis=1)


def pairs_together(re, im, width):
    planes = []
    for at in range(0, re.shape[1], 3 * width):
        both = [
            exchange(re[:, at + c * width:at + (c + 1) * width], im[:, at + c * width:at + (c + 1) * width])
            for c in range(3)
        ]
        planes += [[x for x, _ in both], [y for _, y in both]]
    return planes


def loop(steps, body):
    if steps == 1:
        body(0, 0)
    else:
        lax.fori_loop(0, steps, body, 0)


def staggered(count, first, second):
    for i in range(count + 1):
        ahead = list_of(first, i) if i < count else iter(())
        behind = list_of(second, i - 1) if i else iter(())
        more = True
        while more:
            more = False
            for steps in (ahead, behind):
                for _ in steps:
                    more = True
                    break


def list_of(stage, i):
    return iter(stage(i))


def put_cols(buf, c, row, x):
    high, low = split(x)
    lanes = x.shape[1]
    buf[c, row:row + x.shape[0], :lanes] = high
    buf[c, row:row + x.shape[0], lanes:] = low


def put_rows(buf, c, row_class, pair, row, parts):
    lanes = parts[0].shape[1]
    quarter = buf.shape[2] // 4
    here = slice(pair * lanes, (pair + 1) * lanes)
    for part, x in enumerate(parts):
        high, low = split(x)
        at = part * quarter + row
        buf[c, row_class, at:at + x.shape[0], here] = high
        buf[c, row_class, 2 * quarter + at:2 * quarter + at + x.shape[0], here] = low


def col_dot(buf, c, pair, table):
    depth = table.shape[0] // 3
    rows = 2 * buf.shape[1] // UNIT
    right = table[c * depth:(c + 1) * depth]
    left = buf[c, pair * rows:(pair + 1) * rows]
    found = jnp.dot(left, jnp.concatenate([right, right], axis=0), preferred_element_type=f32)
    return found[:, :depth] + found[:, depth:]


def row_dot(buf, c, row_class, table):
    depth = table.shape[1] // 4
    left = table[:, row_class * depth:(row_class + 1) * depth]
    found = jnp.dot(jnp.concatenate([left, left], axis=1), buf[c, row_class], preferred_element_type=f32)
    half = found.shape[0] // 2
    return found[:half] + found[half:]


def cols_to_rows(col_buf, row_buf, table):
    rows = col_buf.shape[1] // UNIT
    quarter = rows // 2
    for c in range(3):
        for pair in range(UNIT // 2):
            z = col_dot(col_buf, c, pair, table)
            for r in range(0, quarter, CHUNK):
                parts = [
                    exchange(z[at + r:at + r + CHUNK], z[rows + at + r:rows + at + r + CHUNK])
                    for at in (0, quarter)
                ]
                for row_class, y in enumerate(fold_rows(parts)):
                    put_rows(row_buf, c, row_class, pair, r, y)
            yield


def spectra_body(radii, taps_far, row_ref, col_ref, spec_far, taps, spec, col_buf, row_bufs, in_sems, out_sems):
    kernels, _, span, _ = taps.shape
    row_fwd, col_fwd = row_ref[...], col_ref[...]
    quarter = span // 2
    steps = kernels // (UNIT * SPECTRA_UNITS)

    def fetch(u):
        here = pl.ds(u * UNIT, UNIT)
        return pltpu.make_async_copy(taps_far.at[here], taps.at[here], in_sems.at[u])

    def put(u):
        return pltpu.make_async_copy(spec.at[u], spec_far.at[u], out_sems.at[u])

    for u in range(kernels // UNIT):
        fetch(u).start()
    col_at = lax.broadcasted_iota(jnp.int32, (CHUNK, span), 1) - span // 2
    col_reach = jnp.maximum(col_at, -1 - col_at)

    def step(i, carry):
        def cols_of(p):
            u = i * SPECTRA_UNITS + p
            fetch(u).wait()
            for j in range(UNIT):
                k = u * UNIT + j
                for r in range(0, span, CHUNK):
                    row_at = lax.broadcasted_iota(jnp.int32, (CHUNK, span), 0) + (r - span // 2)
                    inside = jnp.maximum(jnp.maximum(row_at, -1 - row_at), col_reach) < radii[k]
                    planes = [jnp.where(inside, taps[k, c, r:r + CHUNK], 0.0) for c in range(2)]
                    for c, y in enumerate(fold_cols(*exchange(*planes))):
                        put_cols(col_buf, c, j * span + r, y)
                yield
            yield from cols_to_rows(col_buf, row_bufs.at[p % 2], col_fwd)

        def rows_of(p):
            u = i * SPECTRA_UNITS + p
            for c in range(3):
                lanes = slice(c * 2 * span, (c + 1) * 2 * span)
                for row_class in range(4):
                    found = row_dot(row_bufs.at[p % 2], c, row_class, row_fwd)
                    for part in range(2):
                        spec[u, part, row_class * quarter:(row_class + 1) * quarter, lanes] = found[part * quarter:(part + 1) * quarter]
                    yield
            put(u).start()

        staggered(SPECTRA_UNITS, cols_of, rows_of)
        return carry

    loop(steps, step)
    for u in range(kernels // UNIT):
        put(u).wait()


def main_body(
    group, weight, place,
    own, near, far, target, spec_far, tables_far,
    resist_far, grad_own, near_rim, far_rim,
    spec, field, mask_spec, resist, slopes, grad_spec, tables, col_buf, row_buf, row_sums, col_sums,
    spec_sems, table_sem, out_sem,
    *, layout,
):
    count, width = target.shape
    rim = count // 2
    units = spec.shape[0]
    steps = units // UNITS

    def fetch(u):
        return pltpu.make_async_copy(spec_far.at[u], spec.at[u], spec_sems.at[u])

    def table(name):
        start, rows, blocks = layout[name]
        parts = [tables[start + b * rows:start + (b + 1) * rows] for b in range(blocks)]
        return jnp.concatenate(parts, axis=1)

    fetch_tables = pltpu.make_async_copy(tables_far, tables, table_sem)
    fetch_tables.start()
    for u in range(units):
        fetch(u).start()
    slopes[...] = jnp.zeros(slopes.shape, f32)
    grad_spec[...] = jnp.zeros(grad_spec.shape, f32)
    fetch_tables.wait()
    row_fwd, row_inv, col_fwd, col_inv = [table(name) for name in ("row_fwd", "row_inv", "col_fwd", "col_inv")]

    odd = place[0] % 2 == 1
    mask = []
    for c in range(2):
        above = jnp.where(odd, near[c, count - rim:], far[c, count - rim:])
        below = jnp.where(odd, far[c, :rim], near[c, :rim])
        mask.append(jnp.concatenate([own[c, rim:], below, above, own[c, :rim]], axis=0))
    plane, = to_col_freqs([exchange(*mask)], col_fwd, shifted=True)
    both = pairs_apart([plane, plane])
    for c, found in enumerate(to_row_freqs(quarters_of(*both, rim), row_fwd)):
        for part in range(2):
            mask_spec[part, c * rim:(c + 1) * rim] = found[part]

    def forward(i, carry):
        def rows_of(p):
            u = i * UNITS + p
            buf, sums, cols = row_buf.at[p % 2], row_sums.at[p % 2], col_buf.at[p % 2]
            fetch(u).wait()
            for c in range(3):
                for row_class in range(4):
                    for r in range(0, rim, CHUNK):
                        here = slice(row_class * rim + r, row_class * rim + r + CHUNK)
                        m_re, m_im = [mask_spec[part, here, c * width:(c + 1) * width] for part in range(2)]
                        for pair in range(UNIT // 2):
                            lanes = slice((2 * c + pair) * width, (2 * c + pair + 1) * width)
                            s_re, s_im = spec[u, 0, here, lanes], spec[u, 1, here, lanes]
                            product = s_re * m_re - s_im * m_im, s_re * m_im + s_im * m_re
                            put_rows(buf, c, row_class, pair, r, product)
                    yield
                for row_class in range(4):
                    sums[c, row_class] = row_dot(buf, c, row_class, row_inv)
                    yield
                for pair in range(UNIT // 2):
                    lanes = slice(pair * width, (pair + 1) * width)
                    for r in range(0, rim, CHUNK // 2):
                        v = [
                            [sums[c, row_class, part * rim + r:part * rim + r + CHUNK // 2, lanes] for part in range(2)]
                            for row_class in range(4)
                        ]
                        for q, (re, im) in enumerate(unfold_rows(v, (0, 1))):
                            for j, x in enumerate(exchange(re, im)):
                                put_cols(cols, c, (2 * pair + j) * count + q * rim + r, x)
                    yield

        def cols_of(p):
            u = i * UNITS + p
            cols = col_buf.at[p % 2]
            for pair in range(UNIT // 2):
                for c in range(3):
                    col_sums[c] = col_dot(cols, c, pair, col_inv)
                    yield
                for j in range(2):
                    k = u * UNIT + 2 * pair + j
                    for r in range(0, count, CHUNK):
                        here = slice(r, r + CHUNK)
                        v = [col_sums[c, j * count + r:j * count + r + CHUNK] for c in range(3)]
                        for side, x in enumerate(unfold_cols(v)):
                            field[k, side, here] = x
                            slopes[group[k], side, here] = slopes[group[k], side, here] + weight[k] * (x * x)
                    yield

        staggered(UNITS, rows_of, cols_of)
        return carry

    loop(steps, forward)

    wanted = target[...].astype(f32)
    for g in range(GROUPS):
        left, right = [slopes[g, side] + swap(slopes[g, side]) for side in range(2)]
        seen = jax.nn.sigmoid(STEEPNESS * (jnp.where(first_half(left), left, right) - THRESHOLD))
        resist[g] = seen
        slope = 2.0 * (seen - wanted) * seen * (1.0 - seen) * STEEPNESS
        slopes[g, 0], slopes[g, 1] = exchange(slope, slope)
    out = pltpu.make_async_copy(resist, resist_far, out_sem)
    out.start()

    def backward(i, carry):
        def cols_of(p):
            u = i * UNITS + p
            cols = col_buf.at[0]
            for j in range(UNIT):
                k = u * UNIT + j
                for r in range(0, count, CHUNK):
                    here = slice(r, r + CHUNK)
                    halves_of = [field[k, side, here] * ((2.0 * weight[k]) * slopes[group[k], side, here]) for side in range(2)]
                    for c, y in enumerate(fold_cols(*halves_of)):
                        put_cols(cols, c, j * count + r, y)
                yield
            yield from cols_to_rows(cols, row_buf.at[p % 2], col_fwd)

        def rows_of(p):
            u = i * UNITS + p
            for c in range(3):
                for row_class in range(4):
                    found = row_dot(row_buf.at[p % 2], c, row_class, row_fwd)
                    for r in range(0, rim, CHUNK):
                        here = slice(row_class * rim + r, row_class * rim + r + CHUNK)
                        totals = [grad_spec[part, here, c * width:(c + 1) * width] for part in range(2)]
                        for pair in range(UNIT // 2):
                            lanes = slice((2 * c + pair) * width, (2 * c + pair + 1) * width)
                            s_re, s_im = spec[u, 0, here, lanes], spec[u, 1, here, lanes]
                            c_re, c_im = [
                                found[part * rim + r:part * rim + r + CHUNK, pair * width:(pair + 1) * width]
                                for part in range(2)
                            ]
                            totals = [totals[0] + (s_re * c_re + s_im * c_im), totals[1] + (s_re * c_im - s_im * c_re)]
                        for part in range(2):
                            grad_spec[part, here, c * width:(c + 1) * width] = totals[part]
                    yield

        staggered(UNITS, cols_of, rows_of)
        return carry

    loop(steps, backward)

    classes = [tuple(grad_spec[part, c * rim:(c + 1) * rim] for part in range(2)) for c in range(4)]
    quarters = from_row_freqs(classes, row_inv, (2, 3, 0, 1))
    re, im = [jnp.concatenate([x[part] for x in quarters], axis=0) for part in range(2)]
    first, second = pairs_together(re, im, width)
    plane = [x + y for x, y in zip(first, second)]
    halves_found, = from_col_freqs([plane], col_inv, shifted=True)
    for c, full in enumerate(exchange(*halves_found)):
        rise, fall = full[:rim], full[rim + count:]
        near_rim[c] = jnp.where(odd, rise, fall)
        far_rim[c] = jnp.where(odd, fall, rise)
        grad_own[c] = full[rim:rim + count]
    out.wait()


def join_body(place, own, near, far, out):
    odd = place[0] % 2 == 1
    rim = near.shape[1]
    for c in range(2):
        out[c, :rim] = own[c, :rim] + jnp.where(odd, near[c], far[c])
        out[c, rim:] = own[c, rim:] + jnp.where(odd, far[c], near[c])


def stacked(tables):
    blocks, layout, at = [], {}, 0
    for name, table in tables.items():
        rows, lanes = table.shape
        layout[name] = (at, rows, lanes // 256)
        for b in range(lanes // 256):
            blocks.append(table[:, b * 256:(b + 1) * 256])
        at += rows * (lanes // 256)
    return np.concatenate(blocks, axis=0), layout


def on_device(mask_field, target, kernel_taps, kernel_radii, kernel_group, kernel_weight):
    _, count, width = mask_field.shape
    kernels, _, span, _ = kernel_taps.shape
    rim = span // 2
    grid_rows = count + 2 * rim
    grid_cols = width + rim
    units = kernels // UNIT
    assert count == span and width == span and units % UNITS == 0 and units % SPECTRA_UNITS == 0 and kernels % UNIT == 0 and span == 128 and UNIT == 4

    strips = lax.axis_size("row")
    assert strips % 2 == 0
    at = lax.axis_index("row")
    near_pairs = [(i, i ^ 1) for i in range(strips)]
    far_pairs = [(i, ((i + 1) ^ 1) - 1) for i in range(1, strips - 1)]
    near = lax.ppermute(mask_field, "row", near_pairs)
    far = lax.ppermute(mask_field, "row", far_pairs)
    place = at.astype(jnp.int32).reshape(1)

    scale = 1.0 / (grid_rows * grid_cols)
    row_classes = [class_table(grid_rows, rim, c, 4) for c in range(4)]
    col_classes = [class_table(grid_cols, rim, c, 3) for c in range(3)]
    row_fwd = np.concatenate([halves(t, 0) for t in row_classes], axis=1)
    row_inv = np.concatenate([halves(t.T * scale, 0) for t in row_classes], axis=1)
    col_fwd = np.concatenate([halves(t.T, 1) for t in col_classes], axis=0)
    col_inv = np.concatenate([halves(t, 1) for t in col_classes], axis=0)
    tables, layout = stacked({"row_fwd": row_fwd, "row_inv": row_inv, "col_fwd": col_fwd, "col_inv": col_inv})

    smem = pl.BlockSpec(memory_space=pltpu.SMEM)
    vmem = pl.BlockSpec(memory_space=pltpu.VMEM)
    hbm = pl.BlockSpec(memory_space=pltpu.HBM)
    spec_shape = (units, 2, grid_rows, UNIT * grid_cols)
    spectra = pl.pallas_call(
        spectra_body,
        out_shape=jax.ShapeDtypeStruct(spec_shape, f32),
        in_specs=[smem, hbm, vmem, vmem],
        out_specs=hbm,
        scratch_shapes=[
            pltpu.VMEM(kernel_taps.shape, f32),
            pltpu.VMEM(spec_shape, f32),
            pltpu.VMEM((3, UNIT * count, 2 * width), bf16),
            pltpu.VMEM((2, 3, 4, grid_rows, 2 * width), bf16),
            pltpu.SemaphoreType.DMA((units,)),
            pltpu.SemaphoreType.DMA((units,)),
        ],
        compiler_params=pltpu.CompilerParams(vmem_limit_bytes=56 * MIB),
        cost_estimate=pl.CostEstimate(flops=18 * 10**9, bytes_accessed=14 * 10**6, transcendentals=0),
        name="spectra",
    )(kernel_radii, kernel_taps, *map(jnp.asarray, (row_fwd, col_fwd)))

    resist, own, near_rim, far_rim = pl.pallas_call(
        functools.partial(main_body, layout=layout),
        out_shape=[
            jax.ShapeDtypeStruct((GROUPS, count, width), f32),
            jax.ShapeDtypeStruct((2, count, width), f32),
            jax.ShapeDtypeStruct((2, rim, width), f32),
            jax.ShapeDtypeStruct((2, rim, width), f32),
        ],
        in_specs=[smem] * 3 + [vmem] * 4 + [hbm] * 2,
        out_specs=[hbm] + [vmem] * 3,
        scratch_shapes=[
            pltpu.VMEM(spec_shape, f32),
            pltpu.VMEM((kernels, 2, count, width), f32),
            pltpu.VMEM((2, grid_rows, 2 * grid_cols), f32),
            pltpu.VMEM((GROUPS, count, width), f32),
            pltpu.VMEM((GROUPS, 2, count, width), f32),
            pltpu.VMEM((2, grid_rows, 2 * grid_cols), f32),
            pltpu.VMEM(tables.shape, bf16),
            pltpu.VMEM((2, 3, UNIT * count, 2 * width), bf16),
            pltpu.VMEM((2, 3, 4, grid_rows, 2 * width), bf16),
            pltpu.VMEM((2, 3, 4, count, 2 * width), f32),
            pltpu.VMEM((3, 2 * count, width), f32),
            pltpu.SemaphoreType.DMA((units,)),
            pltpu.SemaphoreType.DMA,
            pltpu.SemaphoreType.DMA,
        ],
        compiler_params=pltpu.CompilerParams(vmem_limit_bytes=LIMIT * MIB),
        name="fields",
    )(kernel_group, kernel_weight, place, mask_field, near, far, target, spectra, jnp.asarray(tables))

    near_in = lax.ppermute(near_rim, "row", near_pairs)
    far_in = lax.ppermute(far_rim, "row", far_pairs)
    gradient = pl.pallas_call(
        join_body,
        out_shape=jax.ShapeDtypeStruct((2, count, width), f32),
        in_specs=[smem] + [vmem] * 3,
        out_specs=vmem,
        compiler_params=pltpu.CompilerParams(vmem_limit_bytes=4 * MIB),
        name="join",
    )(place, own, near_in, far_in)
    return resist, gradient


def solution(mesh):
    in_specs = (P(None, ("win", "row"), None), P(("win", "row"), None), P(), P(), P(), P())
    out_specs = (P(None, ("win", "row"), None), P(None, ("win", "row"), None))
    return jax.shard_map(
        on_device, mesh=mesh, in_specs=in_specs, out_specs=out_specs, check_vma=False
    )
```

```python
import functools
import math

import jax
import jax.numpy as jnp
import ml_dtypes
import numpy as np
from jax import lax
from jax.experimental import pallas as pl
from jax.experimental.pallas import tpu as pltpu
from jax.sharding import PartitionSpec as P

RMAX = 64
GROUPS = 3
STEEPNESS = 1.0
THRESHOLD = 2.0
UNIT = 4
SPECTRA_UNITS = 3
UNITS = 2
PIECE = 256
TURN = math.sqrt(0.75)

f32 = jnp.float32
bf16 = jnp.bfloat16
MIB = 1024 * 1024
LIMIT = 53


def halves(table, axis):
    high = table.astype(ml_dtypes.bfloat16)
    low = (table - high.astype(np.float64)).astype(ml_dtypes.bfloat16)
    return np.concatenate([high, low], axis=axis)


def class_table(freqs, points, c, classes):
    f = np.arange(c, freqs, classes)[:, None]
    n = np.arange(points)[None, :]
    angle = 2.0 * math.pi * ((f * n) % freqs) / freqs
    cos, sin = np.cos(angle), np.sin(angle)
    return np.block([[cos, sin], [-sin, cos]])


def rounded(x):
    half = jnp.full(x.shape, 0x8000, jnp.uint32)
    return pltpu.stochastic_round(x, half, target_dtype=bf16)


def split(x):
    high = rounded(x)
    low = rounded(x - high.astype(f32))
    return high, low


def dot(left, right):
    parts = [
        jnp.dot(left[at:at + PIECE], right, preferred_element_type=f32)
        for at in range(0, left.shape[0], PIECE)
    ]
    return jnp.concatenate(parts, axis=0)


def swap(x):
    return pltpu.roll(x, x.shape[1] // 2, 1)


def first_half(x):
    return lax.broadcasted_iota(jnp.int32, x.shape, 1) < x.shape[1] // 2


def exchange(x, y):
    first = first_half(x)
    return jnp.where(first, x, swap(y)), jnp.where(first, swap(x), y)


def turned(x, sign):
    re, im = x
    return (-im, re) if sign > 0 else (im, -re)


def plus(x, y):
    return x[0] + y[0], x[1] + y[1]


def minus(x, y):
    return x[0] - y[0], x[1] - y[1]


def row_product(table, c, x):
    parts = split(x)
    depth = x.shape[0]
    left = table[:, c * depth:(c + 1) * depth]
    found = dot(jnp.concatenate([left, left], axis=1), jnp.concatenate(parts, axis=0))
    half = found.shape[0] // 2
    found = found[:half] + found[half:]
    return found[:half // 2], found[half // 2:]


def to_row_freqs(x, table):
    if len(x) == 2:
        even, odd, even_less, odd_less = x[0], x[1], x[0], x[1]
    else:
        even, odd = plus(x[0], x[2]), plus(x[1], x[3])
        even_less, odd_less = minus(x[0], x[2]), minus(x[1], x[3])
    folded = [
        plus(even, odd),
        plus(even_less, turned(odd_less, -1)),
        minus(even, odd),
        plus(even_less, turned(odd_less, 1)),
    ]
    return [row_product(table, c, jnp.concatenate(y, axis=0)) for c, y in enumerate(folded)]


def from_row_freqs(classes, table, quarters):
    v = [row_product(table, c, jnp.concatenate(y, axis=0)) for c, y in enumerate(classes)]
    out = []
    for q in quarters:
        if q % 2 == 0:
            even, odd = plus(v[0], v[2]), plus(v[1], v[3])
        else:
            even, odd = minus(v[0], v[2]), turned(minus(v[1], v[3]), 1)
        out.append(plus(even, odd) if q < 2 else minus(even, odd))
    return out


def quarters_of(re, im, quarter):
    return [(re[at:at + quarter], im[at:at + quarter]) for at in range(0, re.shape[0], quarter)]


def lane_turned(x):
    return swap(x) * jnp.where(first_half(x), TURN, -TURN)


def col_products(planes, table):
    rows = planes[0][0].shape[0]
    depth = table.shape[0] // 3
    out = [[] for _ in planes]
    for c in range(3):
        high, low = split(jnp.concatenate([plane[c] for plane in planes], axis=0))
        right = table[c * depth:(c + 1) * depth]
        found = dot(jnp.concatenate([high, low], axis=1), jnp.concatenate([right, right], axis=0))
        found = found[:, :depth] + found[:, depth:]
        for k in range(len(planes)):
            out[k].append(found[k * rows:(k + 1) * rows])
    return out


def to_col_freqs(planes, table, shifted=False):
    folded = []
    for left, right in planes:
        if shifted:
            left, right = right, left
        near, far = left - 0.5 * right, lane_turned(right)
        one, two = near + far, near - far
        folded.append([left + right, two, one] if shifted else [left + right, one, two])
    return col_products(folded, table)


def from_col_freqs(planes, table, shifted=False):
    out = []
    for v in col_products(planes, table):
        total, far = v[1] + v[2], lane_turned(v[1] - v[2])
        whole, part = v[0] + total, v[0] - 0.5 * total
        out.append((part + far, whole) if shifted else (whole, part - far))
    return out


def pairs_apart(planes):
    re, im = [], []
    for k in range(0, len(planes), 2):
        for x, y in zip(planes[k], planes[k + 1]):
            r, i = exchange(x, y)
            re.append(r)
            im.append(i)
    return jnp.concatenate(re, axis=1), jnp.concatenate(im, axis=1)


def pairs_together(re, im, width):
    planes = []
    for at in range(0, re.shape[1], 3 * width):
        both = [
            exchange(re[:, at + c * width:at + (c + 1) * width], im[:, at + c * width:at + (c + 1) * width])
            for c in range(3)
        ]
        planes += [[x for x, _ in both], [y for _, y in both]]
    return planes


def loop(steps, body):
    if steps == 1:
        body(0, 0)
    else:
        lax.fori_loop(0, steps, body, 0)


def staggered(count, first, second):
    held = None
    for i in range(count):
        new = first(i)
        if i:
            second(i - 1, held)
        held = new
    second(count - 1, held)


def spectra_body(radii, taps_far, row_ref, col_ref, spec_far, taps, spec, in_sems, out_sems):
    kernels, _, span, _ = taps.shape
    row_fwd, col_fwd = row_ref[...], col_ref[...]
    quarter = span // 2
    steps = kernels // (UNIT * SPECTRA_UNITS)

    def fetch(u):
        here = pl.ds(u * UNIT, UNIT)
        return pltpu.make_async_copy(taps_far.at[here], taps.at[here], in_sems.at[u])

    def put(u):
        return pltpu.make_async_copy(spec.at[u], spec_far.at[u], out_sems.at[u])

    for u in range(kernels // UNIT):
        fetch(u).start()
    row_at = lax.broadcasted_iota(jnp.int32, (span, span), 0) - span // 2
    col_at = lax.broadcasted_iota(jnp.int32, (span, span), 1) - span // 2
    reach = jnp.maximum(jnp.maximum(row_at, -1 - row_at), jnp.maximum(col_at, -1 - col_at))

    def step(i, carry):
        def cols_of(p):
            u = i * SPECTRA_UNITS + p
            fetch(u).wait()
            planes = []
            for j in range(UNIT):
                k = u * UNIT + j
                inside = reach < radii[k]
                planes.append(exchange(*[jnp.where(inside, taps[k, c], 0.0) for c in range(2)]))
            return pairs_apart(to_col_freqs(planes, col_fwd))

        def rows_of(p, both):
            u = i * SPECTRA_UNITS + p
            for c, found in enumerate(to_row_freqs(quarters_of(*both, quarter), row_fwd)):
                for part in range(2):
                    spec[u, part, c * quarter:(c + 1) * quarter] = found[part]
            put(u).start()

        staggered(SPECTRA_UNITS, cols_of, rows_of)
        return carry

    loop(steps, step)
    for u in range(kernels // UNIT):
        put(u).wait()


def main_body(
    group, weight, place,
    own, near, far, target, spec_far, tables_far,
    resist_far, grad_own, near_rim, far_rim,
    spec, field, mask_spec, resist, slopes, grad_spec, tables, spec_sems, table_sem, out_sem,
    *, layout,
):
    count, width = target.shape
    rim = count // 2
    units = spec.shape[0]
    steps = units // UNITS

    def fetch(u):
        return pltpu.make_async_copy(spec_far.at[u], spec.at[u], spec_sems.at[u])

    def table(name):
        start, rows, blocks = layout[name]
        parts = [tables[start + b * rows:start + (b + 1) * rows] for b in range(blocks)]
        return jnp.concatenate(parts, axis=1)

    fetch_tables = pltpu.make_async_copy(tables_far, tables, table_sem)
    fetch_tables.start()
    for u in range(units):
        fetch(u).start()
    slopes[...] = jnp.zeros(slopes.shape, f32)
    grad_spec[...] = jnp.zeros(grad_spec.shape, f32)
    fetch_tables.wait()
    row_fwd, row_inv, col_fwd, col_inv = [table(name) for name in ("row_fwd", "row_inv", "col_fwd", "col_inv")]

    odd = place[0] % 2 == 1
    mask = []
    for c in range(2):
        above = jnp.where(odd, near[c, count - rim:], far[c, count - rim:])
        below = jnp.where(odd, far[c, :rim], near[c, :rim])
        mask.append(jnp.concatenate([own[c, rim:], below, above, own[c, :rim]], axis=0))
    plane, = to_col_freqs([exchange(*mask)], col_fwd, shifted=True)
    both = pairs_apart([plane, plane])
    for c, found in enumerate(to_row_freqs(quarters_of(*both, rim), row_fwd)):
        for part in range(2):
            mask_spec[part, c * rim:(c + 1) * rim] = found[part]

    def forward(i, carry):
        def rows_of(p):
            u = i * UNITS + p
            fetch(u).wait()
            classes = []
            for c in range(4):
                here = slice(c * rim, (c + 1) * rim)
                m_re, m_im = [jnp.concatenate([mask_spec[part, here]] * (UNIT // 2), axis=1) for part in range(2)]
                s_re, s_im = spec[u, 0, here], spec[u, 1, here]
                classes.append((s_re * m_re - s_im * m_im, s_re * m_im + s_im * m_re))
            upper, lower = from_row_freqs(classes, row_inv, (0, 1))
            return [jnp.concatenate([upper[part], lower[part]], axis=0) for part in range(2)]

        def cols_of(p, both):
            u = i * UNITS + p
            found = from_col_freqs(pairs_together(*both, width), col_inv)
            for j in range(UNIT):
                k = u * UNIT + j
                for side in range(2):
                    x = found[j][side]
                    field[k, side] = x
                    slopes[group[k], side] = slopes[group[k], side] + weight[k] * (x * x)

        staggered(UNITS, rows_of, cols_of)
        return carry

    loop(steps, forward)

    wanted = target[...].astype(f32)
    for g in range(GROUPS):
        left, right = [slopes[g, side] + swap(slopes[g, side]) for side in range(2)]
        seen = jax.nn.sigmoid(STEEPNESS * (jnp.where(first_half(left), left, right) - THRESHOLD))
        resist[g] = seen
        slope = 2.0 * (seen - wanted) * seen * (1.0 - seen) * STEEPNESS
        slopes[g, 0], slopes[g, 1] = exchange(slope, slope)
    out = pltpu.make_async_copy(resist, resist_far, out_sem)
    out.start()

    def backward(i, carry):
        def cols_of(p):
            u = i * UNITS + p
            planes = []
            for j in range(UNIT):
                k = u * UNIT + j
                planes.append([field[k, side] * ((2.0 * weight[k]) * slopes[group[k], side]) for side in range(2)])
            return pairs_apart(to_col_freqs(planes, col_fwd))

        def rows_of(p, both):
            u = i * UNITS + p
            for c, (c_re, c_im) in enumerate(to_row_freqs(quarters_of(*both, rim), row_fwd)):
                here = slice(c * rim, (c + 1) * rim)
                s_re, s_im = spec[u, 0, here], spec[u, 1, here]
                terms = s_re * c_re + s_im * c_im, s_re * c_im - s_im * c_re
                for part in range(2):
                    total = grad_spec[part, here]
                    lanes = total.shape[1]
                    for at in range(0, terms[part].shape[1], lanes):
                        total = total + terms[part][:, at:at + lanes]
                    grad_spec[part, here] = total

        staggered(UNITS, cols_of, rows_of)
        return carry

    loop(steps, backward)

    classes = [tuple(grad_spec[part, c * rim:(c + 1) * rim] for part in range(2)) for c in range(4)]
    quarters = from_row_freqs(classes, row_inv, (2, 3, 0, 1))
    re, im = [jnp.concatenate([x[part] for x in quarters], axis=0) for part in range(2)]
    first, second = pairs_together(re, im, width)
    plane = [x + y for x, y in zip(first, second)]
    halves_found, = from_col_freqs([plane], col_inv, shifted=True)
    for c, full in enumerate(exchange(*halves_found)):
        rise, fall = full[:rim], full[rim + count:]
        near_rim[c] = jnp.where(odd, rise, fall)
        far_rim[c] = jnp.where(odd, fall, rise)
        grad_own[c] = full[rim:rim + count]
    out.wait()


def join_body(place, own, near, far, out):
    odd = place[0] % 2 == 1
    rim = near.shape[1]
    for c in range(2):
        out[c, :rim] = own[c, :rim] + jnp.where(odd, near[c], far[c])
        out[c, rim:] = own[c, rim:] + jnp.where(odd, far[c], near[c])


def stacked(tables):
    blocks, layout, at = [], {}, 0
    for name, table in tables.items():
        rows, lanes = table.shape
        layout[name] = (at, rows, lanes // 256)
        for b in range(lanes // 256):
            blocks.append(table[:, b * 256:(b + 1) * 256])
        at += rows * (lanes // 256)
    return np.concatenate(blocks, axis=0), layout


def on_device(mask_field, target, kernel_taps, kernel_radii, kernel_group, kernel_weight):
    _, count, width = mask_field.shape
    kernels, _, span, _ = kernel_taps.shape
    rim = span // 2
    grid_rows = count + 2 * rim
    grid_cols = width + rim
    units = kernels // UNIT
    assert count == span and width == span and units % UNITS == 0 and units % SPECTRA_UNITS == 0 and kernels % UNIT == 0 and span == 128

    strips = lax.axis_size("row")
    assert strips % 2 == 0
    at = lax.axis_index("row")
    near_pairs = [(i, i ^ 1) for i in range(strips)]
    far_pairs = [(i, ((i + 1) ^ 1) - 1) for i in range(1, strips - 1)]
    near = lax.ppermute(mask_field, "row", near_pairs)
    far = lax.ppermute(mask_field, "row", far_pairs)
    place = at.astype(jnp.int32).reshape(1)

    scale = 1.0 / (grid_rows * grid_cols)
    row_classes = [class_table(grid_rows, rim, c, 4) for c in range(4)]
    col_classes = [class_table(grid_cols, rim, c, 3) for c in range(3)]
    row_fwd = np.concatenate([halves(t, 0) for t in row_classes], axis=1)
    row_inv = np.concatenate([halves(t.T * scale, 0) for t in row_classes], axis=1)
    col_fwd = np.concatenate([halves(t.T, 1) for t in col_classes], axis=0)
    col_inv = np.concatenate([halves(t, 1) for t in col_classes], axis=0)
    tables, layout = stacked({"row_fwd": row_fwd, "row_inv": row_inv, "col_fwd": col_fwd, "col_inv": col_inv})

    smem = pl.BlockSpec(memory_space=pltpu.SMEM)
    vmem = pl.BlockSpec(memory_space=pltpu.VMEM)
    hbm = pl.BlockSpec(memory_space=pltpu.HBM)
    spec_shape = (units, 2, grid_rows, UNIT * grid_cols)
    spectra = pl.pallas_call(
        spectra_body,
        out_shape=jax.ShapeDtypeStruct(spec_shape, f32),
        in_specs=[smem, hbm, vmem, vmem],
        out_specs=hbm,
        scratch_shapes=[
            pltpu.VMEM(kernel_taps.shape, f32),
            pltpu.VMEM(spec_shape, f32),
            pltpu.SemaphoreType.DMA((units,)),
            pltpu.SemaphoreType.DMA((units,)),
        ],
        compiler_params=pltpu.CompilerParams(vmem_limit_bytes=56 * MIB),
        cost_estimate=pl.CostEstimate(flops=18 * 10**9, bytes_accessed=14 * 10**6, transcendentals=0),
        name="spectra",
    )(kernel_radii, kernel_taps, *map(jnp.asarray, (row_fwd, col_fwd)))

    resist, own, near_rim, far_rim = pl.pallas_call(
        functools.partial(main_body, layout=layout),
        out_shape=[
            jax.ShapeDtypeStruct((GROUPS, count, width), f32),
            jax.ShapeDtypeStruct((2, count, width), f32),
            jax.ShapeDtypeStruct((2, rim, width), f32),
            jax.ShapeDtypeStruct((2, rim, width), f32),
        ],
        in_specs=[smem] * 3 + [vmem] * 4 + [hbm] * 2,
        out_specs=[hbm] + [vmem] * 3,
        scratch_shapes=[
            pltpu.VMEM(spec_shape, f32),
            pltpu.VMEM((kernels, 2, count, width), f32),
            pltpu.VMEM((2, grid_rows, 2 * grid_cols), f32),
            pltpu.VMEM((GROUPS, count, width), f32),
            pltpu.VMEM((GROUPS, 2, count, width), f32),
            pltpu.VMEM((2, grid_rows, 2 * grid_cols), f32),
            pltpu.VMEM(tables.shape, bf16),
            pltpu.SemaphoreType.DMA((units,)),
            pltpu.SemaphoreType.DMA,
            pltpu.SemaphoreType.DMA,
        ],
        compiler_params=pltpu.CompilerParams(vmem_limit_bytes=LIMIT * MIB),
        name="fields",
    )(kernel_group, kernel_weight, place, mask_field, near, far, target, spectra, jnp.asarray(tables))

    near_in = lax.ppermute(near_rim, "row", near_pairs)
    far_in = lax.ppermute(far_rim, "row", far_pairs)
    gradient = pl.pallas_call(
        join_body,
        out_shape=jax.ShapeDtypeStruct((2, count, width), f32),
        in_specs=[smem] + [vmem] * 3,
        out_specs=vmem,
        compiler_params=pltpu.CompilerParams(vmem_limit_bytes=4 * MIB),
        name="join",
    )(place, own, near_in, far_in)
    return resist, gradient


def solution(mesh):
    in_specs = (P(None, ("win", "row"), None), P(("win", "row"), None), P(), P(), P(), P())
    out_specs = (P(None, ("win", "row"), None), P(None, ("win", "row"), None))
    return jax.shard_map(
        on_device, mesh=mesh, in_specs=in_specs, out_specs=out_specs, check_vma=False
    )
```

```python
import functools
import math

import jax
import jax.numpy as jnp
import ml_dtypes
import numpy as np
from jax import lax
from jax.experimental import pallas as pl
from jax.experimental.pallas import tpu as pltpu
from jax.sharding import PartitionSpec as P

RMAX = 64
GROUPS = 3
STEEPNESS = 1.0
THRESHOLD = 2.0
UNIT = 4
SPECTRA_UNITS = 3
UNITS = 2
PIECE = 256
TURN = math.sqrt(0.75)

f32 = jnp.float32
bf16 = jnp.bfloat16
MIB = 1024 * 1024
LIMIT = 53


def halves(table, axis):
    high = table.astype(ml_dtypes.bfloat16)
    low = (table - high.astype(np.float64)).astype(ml_dtypes.bfloat16)
    return np.concatenate([high, low], axis=axis)


def class_table(freqs, points, c, classes):
    f = np.arange(c, freqs, classes)[:, None]
    n = np.arange(points)[None, :]
    angle = 2.0 * math.pi * ((f * n) % freqs) / freqs
    cos, sin = np.cos(angle), np.sin(angle)
    return np.block([[cos, sin], [-sin, cos]])


def for_two(table):
    half = table.shape[0] // 2
    both = np.eye(2)
    return np.block([
        [np.kron(both, table[i:i + half, j:j + half]) for j in (0, half)] for i in (0, half)
    ])


def split(x):
    high = x.astype(bf16)
    low = (x - high.astype(f32)).astype(bf16)
    return high, low


def dot(left, right):
    parts = [
        jnp.dot(left[at:at + PIECE], right, preferred_element_type=f32)
        for at in range(0, left.shape[0], PIECE)
    ]
    return jnp.concatenate(parts, axis=0)


def swap(x):
    return pltpu.roll(x, x.shape[1] // 2, 1)


def first_half(x):
    return lax.broadcasted_iota(jnp.int32, x.shape, 1) < x.shape[1] // 2


def exchange(x, y):
    first = first_half(x)
    return jnp.where(first, x, swap(y)), jnp.where(first, swap(x), y)


def turned(x, sign):
    re, im = x
    return (-im, re) if sign > 0 else (im, -re)


def plus(x, y):
    return x[0] + y[0], x[1] + y[1]


def minus(x, y):
    return x[0] - y[0], x[1] - y[1]


def row_product(table, c, x):
    parts = split(x)
    depth = x.shape[0]
    left = table[:, c * depth:(c + 1) * depth]
    found = dot(jnp.concatenate([left, left], axis=1), jnp.concatenate(parts, axis=0))
    half = found.shape[0] // 2
    found = found[:half] + found[half:]
    return found[:half // 2], found[half // 2:]


def to_row_freqs(x, table):
    if len(x) == 2:
        even, odd, even_less, odd_less = x[0], x[1], x[0], x[1]
    else:
        even, odd = plus(x[0], x[2]), plus(x[1], x[3])
        even_less, odd_less = minus(x[0], x[2]), minus(x[1], x[3])
    folded = [
        plus(even, odd),
        plus(even_less, turned(odd_less, -1)),
        minus(even, odd),
        plus(even_less, turned(odd_less, 1)),
    ]
    return [row_product(table, c, jnp.concatenate(y, axis=0)) for c, y in enumerate(folded)]


def from_row_freqs(classes, table, quarters):
    v = [row_product(table, c, jnp.concatenate(y, axis=0)) for c, y in enumerate(classes)]
    out = []
    for q in quarters:
        if q % 2 == 0:
            even, odd = plus(v[0], v[2]), plus(v[1], v[3])
        else:
            even, odd = minus(v[0], v[2]), turned(minus(v[1], v[3]), 1)
        out.append(plus(even, odd) if q < 2 else minus(even, odd))
    return out


def quarters_of(re, im, quarter):
    return [(re[at:at + quarter], im[at:at + quarter]) for at in range(0, re.shape[0], quarter)]


def scaled(x, by):
    return x[0] * by, x[1] * by


def col_products(pairs, table):
    rows, lanes = pairs[0][0][0].shape
    depth = 2 * lanes
    out = [[] for _ in pairs]
    for c in range(3):
        x = jnp.concatenate([jnp.concatenate(pair[c], axis=1) for pair in pairs], axis=0)
        high, low = split(x)
        t_high, t_low = table[2 * c * depth:(2 * c + 1) * depth], table[(2 * c + 1) * depth:(2 * c + 2) * depth]
        both = dot(jnp.concatenate([high, low], axis=0), t_high)
        found = both[:x.shape[0]] + (both[x.shape[0]:] + dot(high, t_low))
        for k in range(len(pairs)):
            mine = found[k * rows:(k + 1) * rows]
            out[k].append((mine[:, :lanes], mine[:, lanes:]))
    return out


def fold_cols(left, right, shifted=False):
    if shifted:
        left, right = right, left
    near, far = minus(left, scaled(right, 0.5)), scaled(turned(right, -1), TURN)
    one, two = plus(near, far), minus(near, far)
    return [plus(left, right), two, one] if shifted else [plus(left, right), one, two]


def unfold_cols(v, shifted=False):
    total, far = plus(v[1], v[2]), scaled(turned(minus(v[1], v[2]), -1), TURN)
    whole, part = plus(v[0], total), minus(v[0], scaled(total, 0.5))
    return (plus(part, far), whole) if shifted else (whole, minus(part, far))


def to_col_freqs(pairs, table, shifted=False):
    found = col_products([fold_cols(*pair, shifted) for pair in pairs], table)
    return [jnp.concatenate([x[part] for pair in found for x in pair], axis=1) for part in range(2)]


def from_col_freqs(both, table, lanes, shifted=False):
    pairs = [
        [tuple(x[:, at + c * lanes:at + (c + 1) * lanes] for x in both) for c in range(3)]
        for at in range(0, both[0].shape[1], 3 * lanes)
    ]
    return [unfold_cols(v, shifted) for v in col_products(pairs, table)]


def shared(x, y):
    re, im = [exchange(x[part], y[part]) for part in range(2)]
    return (re[0], im[0]), (re[1], im[1])


def loop(steps, body):
    if steps == 1:
        body(0, 0)
    else:
        lax.fori_loop(0, steps, body, 0)


def staggered(count, first, second):
    held = None
    for i in range(count):
        new = first(i)
        if i:
            second(i - 1, held)
        held = new
    second(count - 1, held)


def spectra_body(radii, taps_far, row_ref, col_ref, spec_far, taps, spec, in_sems, out_sems):
    kernels, _, span, _ = taps.shape
    row_fwd, col_fwd = row_ref[...], col_ref[...]
    quarter = span // 2
    steps = kernels // (UNIT * SPECTRA_UNITS)

    def fetch(u):
        here = pl.ds(u * UNIT, UNIT)
        return pltpu.make_async_copy(taps_far.at[here], taps.at[here], in_sems.at[u])

    def put(u):
        return pltpu.make_async_copy(spec.at[u], spec_far.at[u], out_sems.at[u])

    for u in range(kernels // UNIT):
        fetch(u).start()
    row_at = lax.broadcasted_iota(jnp.int32, (span, span), 0) - span // 2
    col_at = lax.broadcasted_iota(jnp.int32, (span, span), 1) - span // 2
    reach = jnp.maximum(jnp.maximum(row_at, -1 - row_at), jnp.maximum(col_at, -1 - col_at))

    def step(i, carry):
        def cols_of(p):
            u = i * SPECTRA_UNITS + p
            fetch(u).wait()
            planes = []
            for j in range(UNIT):
                k = u * UNIT + j
                inside = reach < radii[k]
                planes.append([jnp.where(inside, taps[k, c], 0.0) for c in range(2)])
            return to_col_freqs([shared(planes[j], planes[j + 1]) for j in range(0, UNIT, 2)], col_fwd)

        def rows_of(p, both):
            u = i * SPECTRA_UNITS + p
            for c, found in enumerate(to_row_freqs(quarters_of(*both, quarter), row_fwd)):
                for part in range(2):
                    spec[u, part, c * quarter:(c + 1) * quarter] = found[part]
            put(u).start()

        staggered(SPECTRA_UNITS, cols_of, rows_of)
        return carry

    loop(steps, step)
    for u in range(kernels // UNIT):
        put(u).wait()


def main_body(
    group, weight, place,
    own, near, far, target, spec_far, tables_far,
    resist_far, grad_own, near_rim, far_rim,
    spec, field, mask_spec, resist, slopes, grad_spec, tables, spec_sems, table_sem, out_sem,
    *, layout,
):
    count, width = target.shape
    rim = count // 2
    units = spec.shape[0]
    steps = units // UNITS

    def fetch(u):
        return pltpu.make_async_copy(spec_far.at[u], spec.at[u], spec_sems.at[u])

    def table(name):
        start, rows, blocks = layout[name]
        parts = [tables[start + b * rows:start + (b + 1) * rows] for b in range(blocks)]
        return jnp.concatenate(parts, axis=1)

    fetch_tables = pltpu.make_async_copy(tables_far, tables, table_sem)
    fetch_tables.start()
    for u in range(units):
        fetch(u).start()
    slopes[...] = jnp.zeros(slopes.shape, f32)
    grad_spec[...] = jnp.zeros(grad_spec.shape, f32)
    fetch_tables.wait()
    row_fwd, row_inv, col_fwd, col_inv = [table(name) for name in ("row_fwd", "row_inv", "col_fwd", "col_inv")]

    odd = place[0] % 2 == 1
    mask = []
    for c in range(2):
        above = jnp.where(odd, near[c, count - rim:], far[c, count - rim:])
        below = jnp.where(odd, far[c, :rim], near[c, :rim])
        mask.append(jnp.concatenate([own[c, rim:], below, above, own[c, :rim]], axis=0))
    both = to_col_freqs([shared(mask, mask)], col_fwd, shifted=True)
    for c, found in enumerate(to_row_freqs(quarters_of(*both, rim), row_fwd)):
        for part in range(2):
            mask_spec[part, c * rim:(c + 1) * rim] = found[part]

    def forward(i, carry):
        def rows_of(p):
            u = i * UNITS + p
            fetch(u).wait()
            classes = []
            for c in range(4):
                here = slice(c * rim, (c + 1) * rim)
                m_re, m_im = [jnp.concatenate([mask_spec[part, here]] * (UNIT // 2), axis=1) for part in range(2)]
                s_re, s_im = spec[u, 0, here], spec[u, 1, here]
                classes.append((s_re * m_re - s_im * m_im, s_re * m_im + s_im * m_re))
            upper, lower = from_row_freqs(classes, row_inv, (0, 1))
            return [jnp.concatenate([upper[part], lower[part]], axis=0) for part in range(2)]

        def cols_of(p, both):
            u = i * UNITS + p
            for pair, sides in enumerate(from_col_freqs(both, col_inv, width)):
                first = first_half(sides[0][0])
                for side, (re, im) in enumerate(sides):
                    at = u * (UNIT // 2) + pair
                    field[at, side, 0], field[at, side, 1] = re, im
                    power = re * re + im * im
                    for j in range(2):
                        k = u * UNIT + 2 * pair + j
                        mine = jnp.where(first, power, 0.0) if j == 0 else jnp.where(first, 0.0, power)
                        slopes[group[k], side] = slopes[group[k], side] + weight[k] * mine

        staggered(UNITS, rows_of, cols_of)
        return carry

    loop(steps, forward)

    wanted = target[...].astype(f32)
    for g in range(GROUPS):
        left, right = [slopes[g, side] + swap(slopes[g, side]) for side in range(2)]
        seen = jax.nn.sigmoid(STEEPNESS * (jnp.where(first_half(left), left, right) - THRESHOLD))
        resist[g] = seen
        slope = 2.0 * (seen - wanted) * seen * (1.0 - seen) * STEEPNESS
        slopes[g, 0], slopes[g, 1] = exchange(slope, slope)
    out = pltpu.make_async_copy(resist, resist_far, out_sem)
    out.start()

    def backward(i, carry):
        def cols_of(p):
            u = i * UNITS + p
            pairs = []
            for pair in range(UNIT // 2):
                at = u * (UNIT // 2) + pair
                sides = []
                for side in range(2):
                    one, two = [
                        (2.0 * weight[u * UNIT + 2 * pair + j]) * slopes[group[u * UNIT + 2 * pair + j], side]
                        for j in range(2)
                    ]
                    factor = jnp.where(first_half(one), one, two)
                    sides.append((field[at, side, 0] * factor, field[at, side, 1] * factor))
                pairs.append(sides)
            return to_col_freqs(pairs, col_fwd)

        def rows_of(p, both):
            u = i * UNITS + p
            for c, (c_re, c_im) in enumerate(to_row_freqs(quarters_of(*both, rim), row_fwd)):
                here = slice(c * rim, (c + 1) * rim)
                s_re, s_im = spec[u, 0, here], spec[u, 1, here]
                terms = s_re * c_re + s_im * c_im, s_re * c_im - s_im * c_re
                for part in range(2):
                    total = grad_spec[part, here]
                    lanes = total.shape[1]
                    for at in range(0, terms[part].shape[1], lanes):
                        total = total + terms[part][:, at:at + lanes]
                    grad_spec[part, here] = total

        staggered(UNITS, cols_of, rows_of)
        return carry

    loop(steps, backward)

    classes = [tuple(grad_spec[part, c * rim:(c + 1) * rim] for part in range(2)) for c in range(4)]
    quarters = from_row_freqs(classes, row_inv, (2, 3, 0, 1))
    re, im = [jnp.concatenate([x[part] for x in quarters], axis=0) for part in range(2)]
    (left, right), = from_col_freqs((re, im), col_inv, width, shifted=True)
    for c in range(2):
        full = jnp.where(first_half(left[c]), left[c] + swap(left[c]), right[c] + swap(right[c]))
        rise, fall = full[:rim], full[rim + count:]
        near_rim[c] = jnp.where(odd, rise, fall)
        far_rim[c] = jnp.where(odd, fall, rise)
        grad_own[c] = full[rim:rim + count]
    out.wait()


def join_body(place, own, near, far, out):
    odd = place[0] % 2 == 1
    rim = near.shape[1]
    for c in range(2):
        out[c, :rim] = own[c, :rim] + jnp.where(odd, near[c], far[c])
        out[c, rim:] = own[c, rim:] + jnp.where(odd, far[c], near[c])


def stacked(tables):
    blocks, layout, at = [], {}, 0
    for name, table in tables.items():
        rows, lanes = table.shape
        layout[name] = (at, rows, lanes // 256)
        for b in range(lanes // 256):
            blocks.append(table[:, b * 256:(b + 1) * 256])
        at += rows * (lanes // 256)
    return np.concatenate(blocks, axis=0), layout


def on_device(mask_field, target, kernel_taps, kernel_radii, kernel_group, kernel_weight):
    _, count, width = mask_field.shape
    kernels, _, span, _ = kernel_taps.shape
    rim = span // 2
    grid_rows = count + 2 * rim
    grid_cols = width + rim
    units = kernels // UNIT
    assert count == span and width == span and units % UNITS == 0 and units % SPECTRA_UNITS == 0 and kernels % UNIT == 0 and span == 128

    strips = lax.axis_size("row")
    assert strips % 2 == 0
    at = lax.axis_index("row")
    near_pairs = [(i, i ^ 1) for i in range(strips)]
    far_pairs = [(i, ((i + 1) ^ 1) - 1) for i in range(1, strips - 1)]
    near = lax.ppermute(mask_field, "row", near_pairs)
    far = lax.ppermute(mask_field, "row", far_pairs)
    place = at.astype(jnp.int32).reshape(1)

    scale = 1.0 / (grid_rows * grid_cols)
    row_classes = [class_table(grid_rows, rim, c, 4) for c in range(4)]
    col_classes = [class_table(grid_cols, rim, c, 3) for c in range(3)]
    row_fwd = np.concatenate([halves(t, 0) for t in row_classes], axis=1)
    row_inv = np.concatenate([halves(t.T * scale, 0) for t in row_classes], axis=1)
    col_fwd = np.concatenate([halves(for_two(t.T), 0) for t in col_classes], axis=0)
    col_inv = np.concatenate([halves(for_two(t), 0) for t in col_classes], axis=0)
    tables, layout = stacked({"row_fwd": row_fwd, "row_inv": row_inv, "col_fwd": col_fwd, "col_inv": col_inv})

    smem = pl.BlockSpec(memory_space=pltpu.SMEM)
    vmem = pl.BlockSpec(memory_space=pltpu.VMEM)
    hbm = pl.BlockSpec(memory_space=pltpu.HBM)
    spec_shape = (units, 2, grid_rows, UNIT * grid_cols)
    spectra = pl.pallas_call(
        spectra_body,
        out_shape=jax.ShapeDtypeStruct(spec_shape, f32),
        in_specs=[smem, hbm, vmem, vmem],
        out_specs=hbm,
        scratch_shapes=[
            pltpu.VMEM(kernel_taps.shape, f32),
            pltpu.VMEM(spec_shape, f32),
            pltpu.SemaphoreType.DMA((units,)),
            pltpu.SemaphoreType.DMA((units,)),
        ],
        compiler_params=pltpu.CompilerParams(vmem_limit_bytes=56 * MIB),
        cost_estimate=pl.CostEstimate(flops=18 * 10**9, bytes_accessed=14 * 10**6, transcendentals=0),
        name="spectra",
    )(kernel_radii, kernel_taps, *map(jnp.asarray, (row_fwd, col_fwd)))

    resist, own, near_rim, far_rim = pl.pallas_call(
        functools.partial(main_body, layout=layout),
        out_shape=[
            jax.ShapeDtypeStruct((GROUPS, count, width), f32),
            jax.ShapeDtypeStruct((2, count, width), f32),
            jax.ShapeDtypeStruct((2, rim, width), f32),
            jax.ShapeDtypeStruct((2, rim, width), f32),
        ],
        in_specs=[smem] * 3 + [vmem] * 4 + [hbm] * 2,
        out_specs=[hbm] + [vmem] * 3,
        scratch_shapes=[
            pltpu.VMEM(spec_shape, f32),
            pltpu.VMEM((kernels // 2, 2, 2, count, width), f32),
            pltpu.VMEM((2, grid_rows, 2 * grid_cols), f32),
            pltpu.VMEM((GROUPS, count, width), f32),
            pltpu.VMEM((GROUPS, 2, count, width), f32),
            pltpu.VMEM((2, grid_rows, 2 * grid_cols), f32),
            pltpu.VMEM(tables.shape, bf16),
            pltpu.SemaphoreType.DMA((units,)),
            pltpu.SemaphoreType.DMA,
            pltpu.SemaphoreType.DMA,
        ],
        compiler_params=pltpu.CompilerParams(vmem_limit_bytes=LIMIT * MIB),
        name="fields",
    )(kernel_group, kernel_weight, place, mask_field, near, far, target, spectra, jnp.asarray(tables))

    near_in = lax.ppermute(near_rim, "row", near_pairs)
    far_in = lax.ppermute(far_rim, "row", far_pairs)
    gradient = pl.pallas_call(
        join_body,
        out_shape=jax.ShapeDtypeStruct((2, count, width), f32),
        in_specs=[smem] + [vmem] * 3,
        out_specs=vmem,
        compiler_params=pltpu.CompilerParams(vmem_limit_bytes=4 * MIB),
        name="join",
    )(place, own, near_in, far_in)
    return resist, gradient


def solution(mesh):
    in_specs = (P(None, ("win", "row"), None), P(("win", "row"), None), P(), P(), P(), P())
    out_specs = (P(None, ("win", "row"), None), P(None, ("win", "row"), None))
    return jax.shard_map(
        on_device, mesh=mesh, in_specs=in_specs, out_specs=out_specs, check_vma=False
    )
```

```python
import functools
import math

import jax
import jax.numpy as jnp
import ml_dtypes
import numpy as np
from jax import lax
from jax.experimental import pallas as pl
from jax.experimental.pallas import tpu as pltpu
from jax.sharding import PartitionSpec as P

RMAX = 64
GROUPS = 3
STEEPNESS = 1.0
THRESHOLD = 2.0
BATCH = 8
PIECE = 256

f32 = jnp.float32
bf16 = jnp.bfloat16
MIB = 1024 * 1024
LIMIT = 53


def halves(table, axis):
    high = table.astype(ml_dtypes.bfloat16)
    low = (table - high.astype(np.float64)).astype(ml_dtypes.bfloat16)
    return np.concatenate([high, low], axis=axis)


def analysis(freqs, points, shift):
    f = np.arange(freqs)[:, None]
    n = np.arange(points)[None, :] - shift
    angle = 2.0 * math.pi * ((f * n) % freqs) / freqs
    cos, sin = np.cos(angle), np.sin(angle)
    return np.block([[cos, sin], [-sin, cos]])


def synthesis(freqs, points, shift, scale=1.0):
    return analysis(freqs, points, shift).T * scale


def class_table(freqs, points, c):
    f = np.arange(c, freqs, 4)[:, None]
    n = np.arange(points)[None, :]
    angle = 2.0 * math.pi * ((f * n) % freqs) / freqs
    cos, sin = np.cos(angle), np.sin(angle)
    return np.block([[cos, sin], [-sin, cos]])


def grouped(freqs, lanes):
    head, tail = np.arange(lanes), np.arange(lanes, freqs)
    return np.concatenate([head, freqs + head, tail, freqs + tail])


def split(x):
    high = x.astype(bf16)
    low = (x - high.astype(f32)).astype(bf16)
    return high, low


def dot(left, right):
    parts = [
        jnp.dot(left[at:at + PIECE], right, preferred_element_type=f32)
        for at in range(0, left.shape[0], PIECE)
    ]
    return jnp.concatenate(parts, axis=0)


def class_product(table, c, parts):
    depth = parts[0].shape[0]
    left = table[:, c * depth:(c + 1) * depth]
    found = dot(jnp.concatenate([left, left], axis=1), jnp.concatenate(parts, axis=0))
    half = found.shape[0] // 2
    return found[:half] + found[half:]


def turned(x, sign):
    re, im = x
    return (-im, re) if sign > 0 else (im, -re)


def plus(x, y):
    return x[0] + y[0], x[1] + y[1]


def minus(x, y):
    return x[0] - y[0], x[1] - y[1]


def to_row_freqs(x, table):
    if len(x) == 2:
        even, odd, even_less, odd_less = x[0], x[1], x[0], x[1]
    else:
        even, odd = plus(x[0], x[2]), plus(x[1], x[3])
        even_less, odd_less = minus(x[0], x[2]), minus(x[1], x[3])
    folded = [
        plus(even, odd),
        plus(even_less, turned(odd_less, -1)),
        minus(even, odd),
        plus(even_less, turned(odd_less, 1)),
    ]
    return [class_product(table, c, split(jnp.concatenate(y, axis=0))) for c, y in enumerate(folded)]


def from_row_freqs(classes, table, quarters):
    v = []
    for c, parts in enumerate(classes):
        found = class_product(table, c, parts)
        half = found.shape[0] // 2
        v.append((found[:half], found[half:]))
    out = []
    for q in quarters:
        if q % 2 == 0:
            even, odd = plus(v[0], v[2]), plus(v[1], v[3])
        else:
            even, odd = minus(v[0], v[2]), turned(minus(v[1], v[3]), 1)
        out.append(plus(even, odd) if q < 2 else minus(even, odd))
    return out


def over_lanes(parts, table):
    high, low = parts
    right = jnp.concatenate([table, table[:high.shape[1]]], axis=0)
    return dot(jnp.concatenate([high, high, low], axis=1), right)


def to_freqs(parts, head, tail):
    high, low = parts
    rows, depth = high.shape
    lanes = tail.shape[1] // 2
    stack = jnp.concatenate([high, low], axis=0)
    both = jnp.dot(stack, head[:depth], preferred_element_type=f32)
    third = jnp.dot(high, head[depth:], preferred_element_type=f32)
    first = both[:rows] + (both[rows:] + third)
    both = jnp.dot(stack, tail, preferred_element_type=f32)
    return first, both[:rows, :lanes] + (both[:rows, lanes:] + both[rows:, :lanes])


def beside(classes, at, width):
    tiles = []
    for found in classes:
        half = found.shape[0] // 2
        tiles.append(jnp.concatenate([found[:half, at:at + width], found[half:, at:at + width]], axis=1))
    return split(jnp.concatenate(tiles, axis=0))


def row_stage(quarters, row_fwd, width):
    classes = to_row_freqs(quarters, row_fwd)
    return [beside(classes, at, width) for at in range(0, quarters[0][0].shape[1], width)]


def quarters_of(re, im, quarter):
    return [(re[at:at + quarter], im[at:at + quarter]) for at in range(0, re.shape[0], quarter)]


def staggered(count, first, second):
    held = None
    for i in range(count):
        new = first(i)
        if i:
            second(i - 1, held)
        held = new
    second(count - 1, held)


def side_by_side(planes, c, width):
    quarter = planes[0][0].shape[0] // 4
    rows = slice(c * quarter, (c + 1) * quarter)
    return [
        jnp.concatenate([
            jnp.concatenate([plane[part][rows, at:at + width] for plane in planes], axis=1)
            for at in (0, width)
        ], axis=0)
        for part in range(2)
    ]


def swap(x):
    return pltpu.roll(x, x.shape[1] // 2, 1)


def spectra_body(radii, taps_far, row_far, head_far, tail_far, spec_far, taps, spec, row_ref, head_ref, tail_ref, in_sems, out_sems, table_sems):
    kernels, _, span, _ = taps.shape
    batch = BATCH
    steps = kernels // batch
    moves = [
        pltpu.make_async_copy(far, here, table_sems.at[i])
        for i, (far, here) in enumerate([(row_far, row_ref), (head_far, head_ref), (tail_far, tail_ref)])
    ]

    def fetch(i):
        here = pl.ds(2 * i, 2)
        return pltpu.make_async_copy(taps_far.at[here], taps.at[here], in_sems.at[i])

    def put(i):
        here = pl.ds(2 * i, 2)
        return pltpu.make_async_copy(spec.at[here], spec_far.at[here], out_sems.at[i])

    moves[0].start()
    fetch(0).start()
    moves[1].start()
    moves[2].start()
    for i in range(1, kernels // 2):
        fetch(i).start()
    row_at = lax.broadcasted_iota(jnp.int32, (span, span), 0) - span // 2
    col_at = lax.broadcasted_iota(jnp.int32, (span, span), 1) - span // 2
    reach = jnp.maximum(jnp.maximum(row_at, -1 - row_at), jnp.maximum(col_at, -1 - col_at))

    for move in moves:
        move.wait()
    row_fwd, head, tail = row_ref[...], head_ref[...], tail_ref[...]

    def step(i, carry):
        def rows_of(p):
            fetch(i * (batch // 2) + p).wait()
            planes = [[], []]
            for j in range(2):
                k = i * batch + 2 * p + j
                inside = reach < radii[k]
                for c in range(2):
                    planes[c].append(jnp.where(inside, taps[k, c], 0.0))
            re, im = [jnp.concatenate(plane, axis=1) for plane in planes]
            return row_stage(quarters_of(re, im, span // 2), row_fwd, span)

        def cols_of(p, tiles):
            for j in range(2):
                k = i * batch + 2 * p + j
                a, b = to_freqs(tiles[j], head, tail)
                spec[k, :, :a.shape[1]] = a
                spec[k, :, a.shape[1]:] = b
            put(i * (batch // 2) + p).start()

        staggered(batch // 2, rows_of, cols_of)
        return carry

    lax.fori_loop(0, steps, step, 0)
    for i in range(kernels // 2):
        put(i).wait()


def main_body(
    group, weight, place,
    own, target, near_out, far_out, spec_far, tables_far,
    resist_far, grad_own, near_rim, far_rim,
    spec, field, mask_spec, resist, slopes, grad_spec, tables, near, far, spec_sems, table_sems, halo_sems, out_sem,
    *, layout, sections,
):
    kernels, grid_rows, _ = spec.shape
    count, width = target.shape
    rim = (grid_rows - count) // 2
    steps = spec_sems.shape[0]
    batch = kernels // steps

    def fetch(i):
        here = pl.ds(i * batch, batch)
        return pltpu.make_async_copy(spec_far.at[here], spec.at[here], spec_sems.at[i])

    def fetch_table(i):
        here = pl.ds(sections[i][0], sections[i][1])
        return pltpu.make_async_copy(tables_far.at[here], tables.at[here], table_sems.at[i])

    def table(name):
        start, rows, blocks = layout[name]
        parts = [tables[start + b * rows:start + (b + 1) * rows] for b in range(blocks)]
        return jnp.concatenate(parts, axis=1)

    halos = [
        pltpu.make_async_copy(out, here, halo_sems.at[i])
        for i, (out, here) in enumerate([(near_out, near), (far_out, far)])
    ]
    for halo in halos:
        halo.start()
    fetch_table(0).start()
    fetch_table(1).start()
    for i in range(steps):
        fetch(i).start()
    fetch_table(2).start()
    slopes[...] = jnp.zeros(slopes.shape, f32)
    grad_spec[...] = jnp.zeros(grad_spec.shape, f32)
    for halo in halos:
        halo.wait()
    fetch_table(0).wait()

    odd = place[0] % 2 == 1
    row_fwd = table("row_fwd")
    above, below = [], []
    for c in range(2):
        above.append(jnp.where(odd, near[c, count - rim:], far[c, count - rim:]))
        below.append(jnp.where(odd, far[c, :rim], near[c, :rim]))
    upper, lower = quarters_of(own[0], own[1], rim)
    mask, = row_stage([lower, tuple(below), tuple(above), upper], row_fwd, width)
    m_first, m_rest = to_freqs(mask, table("mask_head"), table("mask_tail"))
    lane = lax.broadcasted_iota(jnp.int32, m_rest.shape, 1)
    real_half = lane < m_rest.shape[1] // 2
    turned = swap(m_rest)
    mask_spec[:, :2 * width] = m_first
    mask_spec[:, 2 * width:3 * width] = jnp.where(real_half, m_rest, turned)
    mask_spec[:, 3 * width:] = jnp.where(real_half, -turned, m_rest)

    fetch_table(1).wait()
    col_inv, row_inv = table("col_inv"), table("row_inv")

    def forward(i, carry):
        fetch(i).wait()
        m_re, m_im = mask_spec[:, :width], mask_spec[:, width:2 * width]
        m_same, m_cross = mask_spec[:, 2 * width:3 * width], mask_spec[:, 3 * width:]

        def cols_of(p):
            planes = []
            for j in range(2):
                k = i * batch + 2 * p + j
                s_re, s_im, s_rest = spec[k, :, :width], spec[k, :, width:2 * width], spec[k, :, 2 * width:]
                product = jnp.concatenate([
                    s_re * m_re - s_im * m_im,
                    s_re * m_im + s_im * m_re,
                    s_rest * m_same + swap(s_rest) * m_cross,
                ], axis=1)
                back = over_lanes(split(product), col_inv)
                planes.append(split(back))
            return [side_by_side(planes, c, width) for c in range(4)]

        def rows_of(p, pair):
            upper, lower = from_row_freqs(pair, row_inv, (0, 1))
            re = jnp.concatenate([upper[0], lower[0]], axis=0)
            im = jnp.concatenate([upper[1], lower[1]], axis=0)
            field[i * (batch // 2) + p, :count] = re
            field[i * (batch // 2) + p, count:] = im
            power = re * re + im * im
            for j in range(2):
                k = i * batch + 2 * p + j
                g = group[k]
                slopes[g] = slopes[g] + weight[k] * power[:, j * width:(j + 1) * width]

        staggered(batch // 2, cols_of, rows_of)
        return carry

    lax.fori_loop(0, steps, forward, 0)

    wanted = target[...].astype(f32)
    for g in range(GROUPS):
        seen = jax.nn.sigmoid(STEEPNESS * (slopes[g] - THRESHOLD))
        resist[g] = seen
        slopes[g] = 2.0 * (seen - wanted) * seen * (1.0 - seen) * STEEPNESS
    out = pltpu.make_async_copy(resist, resist_far, out_sem)
    out.start()
    fetch_table(2).wait()
    head, tail = table("head"), table("tail")

    def backward(i, carry):
        def rows_of(p):
            factors = []
            for j in range(2):
                k = i * batch + 2 * p + j
                factors.append((2.0 * weight[k]) * slopes[group[k]])
            factor = jnp.concatenate(factors, axis=1)
            re = field[i * (batch // 2) + p, :count] * factor
            im = field[i * (batch // 2) + p, count:] * factor
            return row_stage(quarters_of(re, im, rim), row_fwd, width)

        def cols_of(p, tiles):
            total = [grad_spec[:, c * width:(c + 1) * width] for c in range(4)]
            for j in range(2):
                k = i * batch + 2 * p + j
                s_re, s_im, s_rest = spec[k, :, :width], spec[k, :, width:2 * width], spec[k, :, 2 * width:]
                first, rest = to_freqs(tiles[j], head, tail)
                c_re, c_im = first[:, :width], first[:, width:]
                total[0] = total[0] + (s_re * c_re + s_im * c_im)
                total[1] = total[1] + (s_re * c_im - s_im * c_re)
                total[2] = total[2] + s_rest * rest
                total[3] = total[3] + s_rest * swap(rest)
            for c in range(4):
                grad_spec[:, c * width:(c + 1) * width] = total[c]

        staggered(batch // 2, rows_of, cols_of)
        return carry

    lax.fori_loop(0, steps, backward, 0)

    same, cross = grad_spec[:, 2 * width:3 * width], grad_spec[:, 3 * width:]
    tail_sum = jnp.where(real_half, same + swap(same), swap(cross) - cross)
    total = jnp.concatenate([grad_spec[:, :2 * width], tail_sum], axis=1)
    back = split(over_lanes(split(total), table("grad_col")))
    classes = [side_by_side([back], c, width) for c in range(4)]
    rise, upper, lower, fall = from_row_freqs(classes, row_inv, (2, 3, 0, 1))
    for c in range(2):
        near_rim[c] = jnp.where(odd, rise[c], fall[c])
        far_rim[c] = jnp.where(odd, fall[c], rise[c])
        grad_own[c, :rim] = upper[c]
        grad_own[c, rim:] = lower[c]
    out.wait()


def join_body(place, own, near, far, out):
    odd = place[0] % 2 == 1
    rim = near.shape[1]
    count = own.shape[1]
    for c in range(2):
        out[c, :rim] = own[c, :rim] + jnp.where(odd, near[c], far[c])
        if count > 2 * rim:
            out[c, rim:count - rim] = own[c, rim:count - rim]
        out[c, count - rim:] = own[c, count - rim:] + jnp.where(odd, far[c], near[c])


def stacked(groups):
    blocks, layout, sections, at = [], {}, [], 0
    for group in groups:
        start = at
        for name, table in group.items():
            rows, lanes = table.shape
            layout[name] = (at, rows, lanes // 256)
            for b in range(lanes // 256):
                blocks.append(table[:, b * 256:(b + 1) * 256])
            at += rows * (lanes // 256)
        sections.append((start, at - start))
    return np.concatenate(blocks, axis=0), layout, sections


def on_device(mask_field, target, kernel_taps, kernel_radii, kernel_group, kernel_weight):
    _, count, width = mask_field.shape
    kernels, _, span, _ = kernel_taps.shape
    rim = span // 2
    grid_rows = count + 2 * rim
    grid_cols = width + rim
    assert count == span and width == span and kernels % BATCH == 0 and BATCH % 2 == 0 and count == 2 * rim

    strips = lax.axis_size("row")
    assert strips % 2 == 0
    at = lax.axis_index("row")
    near_pairs = [(i, i ^ 1) for i in range(strips)]
    far_pairs = [(i, ((i + 1) ^ 1) - 1) for i in range(1, strips - 1)]
    near = lax.ppermute(mask_field, "row", near_pairs)
    far = lax.ppermute(mask_field, "row", far_pairs)
    place = at.astype(jnp.int32).reshape(1)

    scale = 1.0 / (grid_rows * grid_cols)
    order = grouped(grid_cols, width)

    def head_and_tail(shift):
        table = analysis(grid_cols, width, shift).T[:, order]
        return halves(table[:, :2 * width], 0), halves(table[:, 2 * width:], 1)

    quarter = grid_rows // 4
    by_class = [class_table(grid_rows, quarter, c) for c in range(4)]
    row_fwd = np.concatenate([halves(t, 0) for t in by_class], axis=1)
    row_inv = np.concatenate([halves(t.T * scale, 0) for t in by_class], axis=1)
    head, tail = head_and_tail(0)
    mask_head, mask_tail = head_and_tail(rim)
    col_inv = halves(synthesis(grid_cols, width, 0).T[order], 0)
    grad_col = halves(synthesis(grid_cols, width, rim).T[order], 0)

    smem = pl.BlockSpec(memory_space=pltpu.SMEM)
    vmem = pl.BlockSpec(memory_space=pltpu.VMEM)
    hbm = pl.BlockSpec(memory_space=pltpu.HBM)
    spectra = pl.pallas_call(
        spectra_body,
        out_shape=jax.ShapeDtypeStruct((kernels, grid_rows, 2 * grid_cols), f32),
        in_specs=[smem] + [hbm] * 4,
        out_specs=hbm,
        scratch_shapes=[
            pltpu.VMEM(kernel_taps.shape, f32),
            pltpu.VMEM((kernels, grid_rows, 2 * grid_cols), f32),
            pltpu.VMEM(row_fwd.shape, bf16),
            pltpu.VMEM(head.shape, bf16),
            pltpu.VMEM(tail.shape, bf16),
            pltpu.SemaphoreType.DMA((kernels // 2,)),
            pltpu.SemaphoreType.DMA((kernels // 2,)),
            pltpu.SemaphoreType.DMA((3,)),
        ],
        compiler_params=pltpu.CompilerParams(vmem_limit_bytes=56 * MIB),
        cost_estimate=pl.CostEstimate(flops=18 * 10**9, bytes_accessed=14 * 10**6, transcendentals=0),
        name="spectra",
    )(kernel_radii, kernel_taps, *map(jnp.asarray, (row_fwd, head, tail)))

    tables, layout, sections = stacked([
        {"row_fwd": row_fwd, "mask_head": mask_head, "mask_tail": mask_tail},
        {"col_inv": col_inv, "row_inv": row_inv},
        {"head": head, "tail": tail, "grad_col": grad_col},
    ])
    resist, own, near_rim, far_rim = pl.pallas_call(
        functools.partial(main_body, layout=layout, sections=sections),
        out_shape=[
            jax.ShapeDtypeStruct((GROUPS, count, width), f32),
            jax.ShapeDtypeStruct((2, count, width), f32),
            jax.ShapeDtypeStruct((2, rim, width), f32),
            jax.ShapeDtypeStruct((2, rim, width), f32),
        ],
        in_specs=[smem] * 3 + [vmem] * 2 + [hbm] * 4,
        out_specs=[hbm] + [vmem] * 3,
        scratch_shapes=[
            pltpu.VMEM((kernels, grid_rows, 2 * grid_cols), f32),
            pltpu.VMEM((kernels // 2, 2 * count, 2 * width), f32),
            pltpu.VMEM((grid_rows, 4 * width), f32),
            pltpu.VMEM((GROUPS, count, width), f32),
            pltpu.VMEM((GROUPS, count, width), f32),
            pltpu.VMEM((grid_rows, 4 * width), f32),
            pltpu.VMEM(tables.shape, bf16),
            pltpu.VMEM(mask_field.shape, f32),
            pltpu.VMEM(mask_field.shape, f32),
            pltpu.SemaphoreType.DMA((kernels // BATCH,)),
            pltpu.SemaphoreType.DMA((len(sections),)),
            pltpu.SemaphoreType.DMA((2,)),
            pltpu.SemaphoreType.DMA,
        ],
        compiler_params=pltpu.CompilerParams(vmem_limit_bytes=LIMIT * MIB),
        name="fields",
    )(kernel_group, kernel_weight, place, mask_field, target, near, far, spectra, jnp.asarray(tables))

    near_in = lax.ppermute(near_rim, "row", near_pairs)
    far_in = lax.ppermute(far_rim, "row", far_pairs)
    gradient = pl.pallas_call(
        join_body,
        out_shape=jax.ShapeDtypeStruct((2, count, width), f32),
        in_specs=[smem] + [vmem] * 3,
        out_specs=vmem,
        compiler_params=pltpu.CompilerParams(vmem_limit_bytes=4 * MIB),
        name="join",
    )(place, own, near_in, far_in)
    return resist, gradient


def solution(mesh):
    in_specs = (P(None, ("win", "row"), None), P(("win", "row"), None), P(), P(), P(), P())
    out_specs = (P(None, ("win", "row"), None), P(None, ("win", "row"), None))
    return jax.shard_map(
        on_device, mesh=mesh, in_specs=in_specs, out_specs=out_specs, check_vma=False
    )
```

```python
import functools
import math

import jax
import jax.numpy as jnp
import ml_dtypes
import numpy as np
from jax import lax
from jax.experimental import pallas as pl
from jax.experimental.pallas import tpu as pltpu
from jax.sharding import PartitionSpec as P

RMAX = 64
GROUPS = 3
STEEPNESS = 1.0
THRESHOLD = 2.0
UNIT = 4
SPECTRA_UNITS = 3
UNITS = 3
PIECE = 256
TURN = math.sqrt(0.75)

f32 = jnp.float32
bf16 = jnp.bfloat16
MIB = 1024 * 1024
LIMIT = 53


def halves(table, axis):
    high = table.astype(ml_dtypes.bfloat16)
    low = (table - high.astype(np.float64)).astype(ml_dtypes.bfloat16)
    return np.concatenate([high, low], axis=axis)


def class_table(freqs, points, c, classes):
    f = np.arange(c, freqs, classes)[:, None]
    n = np.arange(points)[None, :]
    angle = 2.0 * math.pi * ((f * n) % freqs) / freqs
    cos, sin = np.cos(angle), np.sin(angle)
    return np.block([[cos, sin], [-sin, cos]])


def split(x):
    high = x.astype(bf16)
    low = (x - high.astype(f32)).astype(bf16)
    return high, low


def dot(left, right):
    parts = [
        jnp.dot(left[at:at + PIECE], right, preferred_element_type=f32)
        for at in range(0, left.shape[0], PIECE)
    ]
    return jnp.concatenate(parts, axis=0)


def swap(x):
    return pltpu.roll(x, x.shape[1] // 2, 1)


def first_half(x):
    return lax.broadcasted_iota(jnp.int32, x.shape, 1) < x.shape[1] // 2


def exchange(x, y):
    first = first_half(x)
    return jnp.where(first, x, swap(y)), jnp.where(first, swap(x), y)


def turned(x, sign):
    re, im = x
    return (-im, re) if sign > 0 else (im, -re)


def plus(x, y):
    return x[0] + y[0], x[1] + y[1]


def minus(x, y):
    return x[0] - y[0], x[1] - y[1]


def row_product(table, c, x):
    parts = split(x)
    depth = x.shape[0]
    left = table[:, c * depth:(c + 1) * depth]
    found = dot(jnp.concatenate([left, left], axis=1), jnp.concatenate(parts, axis=0))
    half = found.shape[0] // 2
    found = found[:half] + found[half:]
    return found[:half // 2], found[half // 2:]


def to_row_freqs(x, table):
    if len(x) == 2:
        even, odd, even_less, odd_less = x[0], x[1], x[0], x[1]
    else:
        even, odd = plus(x[0], x[2]), plus(x[1], x[3])
        even_less, odd_less = minus(x[0], x[2]), minus(x[1], x[3])
    folded = [
        plus(even, odd),
        plus(even_less, turned(odd_less, -1)),
        minus(even, odd),
        plus(even_less, turned(odd_less, 1)),
    ]
    return [row_product(table, c, jnp.concatenate(y, axis=0)) for c, y in enumerate(folded)]


def from_row_freqs(classes, table, quarters):
    v = [row_product(table, c, jnp.concatenate(y, axis=0)) for c, y in enumerate(classes)]
    out = []
    for q in quarters:
        if q % 2 == 0:
            even, odd = plus(v[0], v[2]), plus(v[1], v[3])
        else:
            even, odd = minus(v[0], v[2]), turned(minus(v[1], v[3]), 1)
        out.append(plus(even, odd) if q < 2 else minus(even, odd))
    return out


def quarters_of(re, im, quarter):
    return [(re[at:at + quarter], im[at:at + quarter]) for at in range(0, re.shape[0], quarter)]


def lane_turned(x):
    return swap(x) * jnp.where(first_half(x), TURN, -TURN)


def col_products(planes, table):
    rows = planes[0][0].shape[0]
    depth = table.shape[0] // 3
    out = [[] for _ in planes]
    for c in range(3):
        high, low = split(jnp.concatenate([plane[c] for plane in planes], axis=0))
        right = table[c * depth:(c + 1) * depth]
        found = dot(jnp.concatenate([high, low], axis=1), jnp.concatenate([right, right], axis=0))
        found = found[:, :depth] + found[:, depth:]
        for k in range(len(planes)):
            out[k].append(found[k * rows:(k + 1) * rows])
    return out


def to_col_freqs(planes, table, shifted=False):
    folded = []
    for left, right in planes:
        if shifted:
            left, right = right, left
        near, far = left - 0.5 * right, lane_turned(right)
        one, two = near + far, near - far
        folded.append([left + right, two, one] if shifted else [left + right, one, two])
    return col_products(folded, table)


def from_col_freqs(planes, table, shifted=False):
    out = []
    for v in col_products(planes, table):
        total, far = v[1] + v[2], lane_turned(v[1] - v[2])
        whole, part = v[0] + total, v[0] - 0.5 * total
        out.append((part + far, whole) if shifted else (whole, part - far))
    return out


def pairs_apart(planes):
    re, im = [], []
    for k in range(0, len(planes), 2):
        for x, y in zip(planes[k], planes[k + 1]):
            r, i = exchange(x, y)
            re.append(r)
            im.append(i)
    return jnp.concatenate(re, axis=1), jnp.concatenate(im, axis=1)


def pairs_together(re, im, width):
    planes = []
    for at in range(0, re.shape[1], 3 * width):
        both = [
            exchange(re[:, at + c * width:at + (c + 1) * width], im[:, at + c * width:at + (c + 1) * width])
            for c in range(3)
        ]
        planes += [[x for x, _ in both], [y for _, y in both]]
    return planes


def loop(steps, body):
    if steps == 1:
        body(0, 0)
    else:
        lax.fori_loop(0, steps, body, 0)


def staggered(count, first, second):
    held = None
    for i in range(count):
        new = first(i)
        if i:
            second(i - 1, held)
        held = new
    second(count - 1, held)


def spectra_body(radii, taps_far, row_ref, col_ref, spec_far, taps, spec, in_sems, out_sems):
    kernels, _, span, _ = taps.shape
    row_fwd, col_fwd = row_ref[...], col_ref[...]
    quarter = span // 2
    steps = kernels // (UNIT * SPECTRA_UNITS)

    def fetch(u):
        here = pl.ds(u * UNIT, UNIT)
        return pltpu.make_async_copy(taps_far.at[here], taps.at[here], in_sems.at[u])

    def put(u):
        return pltpu.make_async_copy(spec.at[u], spec_far.at[u], out_sems.at[u])

    for u in range(kernels // UNIT):
        fetch(u).start()
    row_at = lax.broadcasted_iota(jnp.int32, (span, span), 0) - span // 2
    col_at = lax.broadcasted_iota(jnp.int32, (span, span), 1) - span // 2
    reach = jnp.maximum(jnp.maximum(row_at, -1 - row_at), jnp.maximum(col_at, -1 - col_at))

    def step(i, carry):
        def cols_of(p):
            u = i * SPECTRA_UNITS + p
            planes = []
            for j in range(UNIT):
                k = u * UNIT + j
                inside = reach < radii[k]
                planes.append(exchange(*[jnp.where(inside, taps[k, c], 0.0) for c in range(2)]))
            return pairs_apart(to_col_freqs(planes, col_fwd))

        def rows_of(p, both):
            u = i * SPECTRA_UNITS + p
            for c, found in enumerate(to_row_freqs(quarters_of(*both, quarter), row_fwd)):
                for part in range(2):
                    spec[u, part, c * quarter:(c + 1) * quarter] = found[part]

        for p in range(SPECTRA_UNITS):
            fetch(i * SPECTRA_UNITS + p).wait()
        staggered(SPECTRA_UNITS, cols_of, rows_of)
        for p in range(SPECTRA_UNITS):
            put(i * SPECTRA_UNITS + p).start()
        return carry

    loop(steps, step)
    for u in range(kernels // UNIT):
        put(u).wait()


def main_body(
    group, weight, place,
    own, near, far, target, spec_far, tables_far,
    resist_far, grad_own, near_rim, far_rim,
    spec, field, mask_spec, resist, slopes, grad_spec, tables, spec_sems, table_sem, out_sem,
    *, layout,
):
    count, width = target.shape
    rim = count // 2
    units = spec.shape[0]
    steps = units // UNITS

    def fetch(u):
        return pltpu.make_async_copy(spec_far.at[u], spec.at[u], spec_sems.at[u])

    def table(name):
        start, rows, blocks = layout[name]
        parts = [tables[start + b * rows:start + (b + 1) * rows] for b in range(blocks)]
        return jnp.concatenate(parts, axis=1)

    fetch_tables = pltpu.make_async_copy(tables_far, tables, table_sem)
    fetch_tables.start()
    for u in range(units):
        fetch(u).start()
    slopes[...] = jnp.zeros(slopes.shape, f32)
    grad_spec[...] = jnp.zeros(grad_spec.shape, f32)
    fetch_tables.wait()
    row_fwd, row_inv, col_fwd, col_inv = [table(name) for name in ("row_fwd", "row_inv", "col_fwd", "col_inv")]

    odd = place[0] % 2 == 1
    mask = []
    for c in range(2):
        above = jnp.where(odd, near[c, count - rim:], far[c, count - rim:])
        below = jnp.where(odd, far[c, :rim], near[c, :rim])
        mask.append(jnp.concatenate([own[c, rim:], below, above, own[c, :rim]], axis=0))
    plane, = to_col_freqs([exchange(*mask)], col_fwd, shifted=True)
    both = pairs_apart([plane, plane])
    for c, found in enumerate(to_row_freqs(quarters_of(*both, rim), row_fwd)):
        for part in range(2):
            mask_spec[part, c * rim:(c + 1) * rim] = found[part]

    def forward(i, carry):
        def rows_of(p):
            u = i * UNITS + p
            classes = []
            for c in range(4):
                here = slice(c * rim, (c + 1) * rim)
                m_re, m_im = [jnp.concatenate([mask_spec[part, here]] * (UNIT // 2), axis=1) for part in range(2)]
                s_re, s_im = spec[u, 0, here], spec[u, 1, here]
                classes.append((s_re * m_re - s_im * m_im, s_re * m_im + s_im * m_re))
            upper, lower = from_row_freqs(classes, row_inv, (0, 1))
            return [jnp.concatenate([upper[part], lower[part]], axis=0) for part in range(2)]

        def cols_of(p, both):
            u = i * UNITS + p
            found = from_col_freqs(pairs_together(*both, width), col_inv)
            for j in range(UNIT):
                k = u * UNIT + j
                for side in range(2):
                    x = found[j][side]
                    field[k, side] = x
                    slopes[group[k], side] = slopes[group[k], side] + weight[k] * (x * x)

        for p in range(UNITS):
            fetch(i * UNITS + p).wait()
        staggered(UNITS, rows_of, cols_of)
        return carry

    loop(steps, forward)

    wanted = target[...].astype(f32)
    for g in range(GROUPS):
        left, right = [slopes[g, side] + swap(slopes[g, side]) for side in range(2)]
        seen = jax.nn.sigmoid(STEEPNESS * (jnp.where(first_half(left), left, right) - THRESHOLD))
        resist[g] = seen
        slope = 2.0 * (seen - wanted) * seen * (1.0 - seen) * STEEPNESS
        slopes[g, 0], slopes[g, 1] = exchange(slope, slope)
    out = pltpu.make_async_copy(resist, resist_far, out_sem)
    out.start()

    def backward(i, carry):
        def cols_of(p):
            u = i * UNITS + p
            planes = []
            for j in range(UNIT):
                k = u * UNIT + j
                planes.append([field[k, side] * ((2.0 * weight[k]) * slopes[group[k], side]) for side in range(2)])
            return pairs_apart(to_col_freqs(planes, col_fwd))

        def rows_of(p, both):
            u = i * UNITS + p
            for c, (c_re, c_im) in enumerate(to_row_freqs(quarters_of(*both, rim), row_fwd)):
                here = slice(c * rim, (c + 1) * rim)
                s_re, s_im = spec[u, 0, here], spec[u, 1, here]
                terms = s_re * c_re + s_im * c_im, s_re * c_im - s_im * c_re
                for part in range(2):
                    total = grad_spec[part, here]
                    lanes = total.shape[1]
                    for at in range(0, terms[part].shape[1], lanes):
                        total = total + terms[part][:, at:at + lanes]
                    grad_spec[part, here] = total

        staggered(UNITS, cols_of, rows_of)
        return carry

    loop(steps, backward)

    classes = [tuple(grad_spec[part, c * rim:(c + 1) * rim] for part in range(2)) for c in range(4)]
    quarters = from_row_freqs(classes, row_inv, (2, 3, 0, 1))
    re, im = [jnp.concatenate([x[part] for x in quarters], axis=0) for part in range(2)]
    first, second = pairs_together(re, im, width)
    plane = [x + y for x, y in zip(first, second)]
    halves_found, = from_col_freqs([plane], col_inv, shifted=True)
    for c, full in enumerate(exchange(*halves_found)):
        rise, fall = full[:rim], full[rim + count:]
        near_rim[c] = jnp.where(odd, rise, fall)
        far_rim[c] = jnp.where(odd, fall, rise)
        grad_own[c] = full[rim:rim + count]
    out.wait()


def join_body(place, own, near, far, out):
    odd = place[0] % 2 == 1
    rim = near.shape[1]
    for c in range(2):
        out[c, :rim] = own[c, :rim] + jnp.where(odd, near[c], far[c])
        out[c, rim:] = own[c, rim:] + jnp.where(odd, far[c], near[c])


def stacked(tables):
    blocks, layout, at = [], {}, 0
    for name, table in tables.items():
        rows, lanes = table.shape
        layout[name] = (at, rows, lanes // 256)
        for b in range(lanes // 256):
            blocks.append(table[:, b * 256:(b + 1) * 256])
        at += rows * (lanes // 256)
    return np.concatenate(blocks, axis=0), layout


def on_device(mask_field, target, kernel_taps, kernel_radii, kernel_group, kernel_weight):
    _, count, width = mask_field.shape
    kernels, _, span, _ = kernel_taps.shape
    rim = span // 2
    grid_rows = count + 2 * rim
    grid_cols = width + rim
    units = kernels // UNIT
    assert count == span and width == span and units % UNITS == 0 and units % SPECTRA_UNITS == 0 and kernels % UNIT == 0 and span == 128

    strips = lax.axis_size("row")
    assert strips % 2 == 0
    at = lax.axis_index("row")
    near_pairs = [(i, i ^ 1) for i in range(strips)]
    far_pairs = [(i, ((i + 1) ^ 1) - 1) for i in range(1, strips - 1)]
    near = lax.ppermute(mask_field, "row", near_pairs)
    far = lax.ppermute(mask_field, "row", far_pairs)
    place = at.astype(jnp.int32).reshape(1)

    scale = 1.0 / (grid_rows * grid_cols)
    row_classes = [class_table(grid_rows, rim, c, 4) for c in range(4)]
    col_classes = [class_table(grid_cols, rim, c, 3) for c in range(3)]
    row_fwd = np.concatenate([halves(t, 0) for t in row_classes], axis=1)
    row_inv = np.concatenate([halves(t.T * scale, 0) for t in row_classes], axis=1)
    col_fwd = np.concatenate([halves(t.T, 1) for t in col_classes], axis=0)
    col_inv = np.concatenate([halves(t, 1) for t in col_classes], axis=0)
    tables, layout = stacked({"row_fwd": row_fwd, "row_inv": row_inv, "col_fwd": col_fwd, "col_inv": col_inv})

    smem = pl.BlockSpec(memory_space=pltpu.SMEM)
    vmem = pl.BlockSpec(memory_space=pltpu.VMEM)
    hbm = pl.BlockSpec(memory_space=pltpu.HBM)
    spec_shape = (units, 2, grid_rows, UNIT * grid_cols)
    spectra = pl.pallas_call(
        spectra_body,
        out_shape=jax.ShapeDtypeStruct(spec_shape, f32),
        in_specs=[smem, hbm, vmem, vmem],
        out_specs=hbm,
        scratch_shapes=[
            pltpu.VMEM(kernel_taps.shape, f32),
            pltpu.VMEM(spec_shape, f32),
            pltpu.SemaphoreType.DMA((units,)),
            pltpu.SemaphoreType.DMA((units,)),
        ],
        compiler_params=pltpu.CompilerParams(vmem_limit_bytes=56 * MIB),
        cost_estimate=pl.CostEstimate(flops=18 * 10**9, bytes_accessed=14 * 10**6, transcendentals=0),
        name="spectra",
    )(kernel_radii, kernel_taps, *map(jnp.asarray, (row_fwd, col_fwd)))

    resist, own, near_rim, far_rim = pl.pallas_call(
        functools.partial(main_body, layout=layout),
        out_shape=[
            jax.ShapeDtypeStruct((GROUPS, count, width), f32),
            jax.ShapeDtypeStruct((2, count, width), f32),
            jax.ShapeDtypeStruct((2, rim, width), f32),
            jax.ShapeDtypeStruct((2, rim, width), f32),
        ],
        in_specs=[smem] * 3 + [vmem] * 4 + [hbm] * 2,
        out_specs=[hbm] + [vmem] * 3,
        scratch_shapes=[
            pltpu.VMEM(spec_shape, f32),
            pltpu.VMEM((kernels, 2, count, width), f32),
            pltpu.VMEM((2, grid_rows, 2 * grid_cols), f32),
            pltpu.VMEM((GROUPS, count, width), f32),
            pltpu.VMEM((GROUPS, 2, count, width), f32),
            pltpu.VMEM((2, grid_rows, 2 * grid_cols), f32),
            pltpu.VMEM(tables.shape, bf16),
            pltpu.SemaphoreType.DMA((units,)),
            pltpu.SemaphoreType.DMA,
            pltpu.SemaphoreType.DMA,
        ],
        compiler_params=pltpu.CompilerParams(vmem_limit_bytes=LIMIT * MIB),
        name="fields",
    )(kernel_group, kernel_weight, place, mask_field, near, far, target, spectra, jnp.asarray(tables))

    near_in = lax.ppermute(near_rim, "row", near_pairs)
    far_in = lax.ppermute(far_rim, "row", far_pairs)
    gradient = pl.pallas_call(
        join_body,
        out_shape=jax.ShapeDtypeStruct((2, count, width), f32),
        in_specs=[smem] + [vmem] * 3,
        out_specs=vmem,
        compiler_params=pltpu.CompilerParams(vmem_limit_bytes=4 * MIB),
        name="join",
    )(place, own, near_in, far_in)
    return resist, gradient


def solution(mesh):
    in_specs = (P(None, ("win", "row"), None), P(("win", "row"), None), P(), P(), P(), P())
    out_specs = (P(None, ("win", "row"), None), P(None, ("win", "row"), None))
    return jax.shard_map(
        on_device, mesh=mesh, in_specs=in_specs, out_specs=out_specs, check_vma=False
    )
```

```python
import functools
import math

import jax
import jax.numpy as jnp
import ml_dtypes
import numpy as np
from jax import lax
from jax.experimental import pallas as pl
from jax.experimental.pallas import tpu as pltpu
from jax.sharding import PartitionSpec as P

RMAX = 64
GROUPS = 3
STEEPNESS = 1.0
THRESHOLD = 2.0
BATCH = 8
PIECE = 256

f32 = jnp.float32
bf16 = jnp.bfloat16
MIB = 1024 * 1024
SPECTRA_LIMIT = 45
LIMIT = 34


def halves(table, axis):
    high = table.astype(ml_dtypes.bfloat16)
    low = (table - high.astype(np.float64)).astype(ml_dtypes.bfloat16)
    return np.concatenate([high, low], axis=axis)


def analysis(freqs, points, shift):
    f = np.arange(freqs)[:, None]
    n = np.arange(points)[None, :] - shift
    angle = 2.0 * math.pi * ((f * n) % freqs) / freqs
    cos, sin = np.cos(angle), np.sin(angle)
    return np.block([[cos, sin], [-sin, cos]])


def synthesis(freqs, points, shift, scale=1.0):
    return analysis(freqs, points, shift).T * scale


def class_table(freqs, points, c):
    f = np.arange(c, freqs, 4)[:, None]
    n = np.arange(points)[None, :]
    angle = 2.0 * math.pi * ((f * n) % freqs) / freqs
    cos, sin = np.cos(angle), np.sin(angle)
    return np.block([[cos, sin], [-sin, cos]])


def grouped(freqs, lanes):
    head, tail = np.arange(lanes), np.arange(lanes, freqs)
    return np.concatenate([head, freqs + head, tail, freqs + tail])


def split(x):
    high = x.astype(bf16)
    low = (x - high.astype(f32)).astype(bf16)
    return high, low


def dot(left, right):
    parts = [
        jnp.dot(left[at:at + PIECE], right, preferred_element_type=f32)
        for at in range(0, left.shape[0], PIECE)
    ]
    return jnp.concatenate(parts, axis=0)


def class_product(table, c, parts):
    depth = parts[0].shape[0]
    left = table[:, c * depth:(c + 1) * depth]
    found = dot(jnp.concatenate([left, left], axis=1), jnp.concatenate(parts, axis=0))
    half = found.shape[0] // 2
    return found[:half] + found[half:]


def turned(x, sign):
    re, im = x
    return (-im, re) if sign > 0 else (im, -re)


def plus(x, y):
    return x[0] + y[0], x[1] + y[1]


def minus(x, y):
    return x[0] - y[0], x[1] - y[1]


def to_row_freqs(x, table):
    if len(x) == 2:
        even, odd, even_less, odd_less = x[0], x[1], x[0], x[1]
    else:
        even, odd = plus(x[0], x[2]), plus(x[1], x[3])
        even_less, odd_less = minus(x[0], x[2]), minus(x[1], x[3])
    folded = [
        plus(even, odd),
        plus(even_less, turned(odd_less, -1)),
        minus(even, odd),
        plus(even_less, turned(odd_less, 1)),
    ]
    return [class_product(table, c, split(jnp.concatenate(y, axis=0))) for c, y in enumerate(folded)]


def from_row_freqs(classes, table, quarters):
    v = []
    for c, parts in enumerate(classes):
        found = class_product(table, c, parts)
        half = found.shape[0] // 2
        v.append((found[:half], found[half:]))
    out = []
    for q in quarters:
        if q % 2 == 0:
            even, odd = plus(v[0], v[2]), plus(v[1], v[3])
        else:
            even, odd = minus(v[0], v[2]), turned(minus(v[1], v[3]), 1)
        out.append(plus(even, odd) if q < 2 else minus(even, odd))
    return out


def over_lanes(parts, table):
    high, low = parts
    right = jnp.concatenate([table, table[:high.shape[1]]], axis=0)
    return dot(jnp.concatenate([high, high, low], axis=1), right)


def to_freqs(parts, head, tail):
    high, low = parts
    rows, depth = high.shape
    lanes = tail.shape[1] // 2
    stack = jnp.concatenate([high, low], axis=0)
    both = jnp.dot(stack, head[:depth], preferred_element_type=f32)
    third = jnp.dot(high, head[depth:], preferred_element_type=f32)
    first = both[:rows] + (both[rows:] + third)
    both = jnp.dot(stack, tail, preferred_element_type=f32)
    return first, both[:rows, :lanes] + (both[:rows, lanes:] + both[rows:, :lanes])


def beside(classes, at, width):
    tiles = []
    for found in classes:
        half = found.shape[0] // 2
        tiles.append(jnp.concatenate([found[:half, at:at + width], found[half:, at:at + width]], axis=1))
    return split(jnp.concatenate(tiles, axis=0))


def row_stage(quarters, row_fwd, width):
    classes = to_row_freqs(quarters, row_fwd)
    return [beside(classes, at, width) for at in range(0, quarters[0][0].shape[1], width)]


def quarters_of(re, im, quarter):
    return [(re[at:at + quarter], im[at:at + quarter]) for at in range(0, re.shape[0], quarter)]


def staggered(count, first, second):
    held = None
    for i in range(count):
        new = first(i)
        if i:
            second(i - 1, held)
        held = new
    second(count - 1, held)


def side_by_side(planes, c, width):
    quarter = planes[0][0].shape[0] // 4
    rows = slice(c * quarter, (c + 1) * quarter)
    return [
        jnp.concatenate([
            jnp.concatenate([plane[part][rows, at:at + width] for plane in planes], axis=1)
            for at in (0, width)
        ], axis=0)
        for part in range(2)
    ]


def swap(x):
    return pltpu.roll(x, x.shape[1] // 2, 1)


def spectra_body(radii, taps_far, row_ref, head_ref, tail_ref, spec, taps, in_sems):
    kernels, _, span, _ = taps.shape
    row_fwd, head, tail = row_ref[...], head_ref[...], tail_ref[...]
    steps = in_sems.shape[0]
    batch = kernels // steps

    def fetch(i):
        here = pl.ds(i * batch, batch)
        return pltpu.make_async_copy(taps_far.at[here], taps.at[here], in_sems.at[i])

    for i in range(steps):
        fetch(i).start()
    row_at = lax.broadcasted_iota(jnp.int32, (span, span), 0) - span // 2
    col_at = lax.broadcasted_iota(jnp.int32, (span, span), 1) - span // 2
    reach = jnp.maximum(jnp.maximum(row_at, -1 - row_at), jnp.maximum(col_at, -1 - col_at))

    def step(i, carry):
        fetch(i).wait()

        def rows_of(p):
            planes = [[], []]
            for j in range(2):
                k = i * batch + 2 * p + j
                inside = reach < radii[k]
                for c in range(2):
                    planes[c].append(jnp.where(inside, taps[k, c], 0.0))
            re, im = [jnp.concatenate(plane, axis=1) for plane in planes]
            return row_stage(quarters_of(re, im, span // 2), row_fwd, span)

        def cols_of(p, tiles):
            for j in range(2):
                k = i * batch + 2 * p + j
                a, b = to_freqs(tiles[j], head, tail)
                spec[k, :, :a.shape[1]] = a
                spec[k, :, a.shape[1]:] = b

        staggered(batch // 2, rows_of, cols_of)
        return carry

    lax.fori_loop(0, steps, step, 0)


def main_body(
    group, weight, place,
    own, near, far, target, spec, tables_far,
    resist_far, grad_own, near_rim, far_rim,
    field, mask_spec, resist, slopes, grad_spec, tables, table_sems, out_sem,
    *, layout, sections,
):
    kernels, grid_rows, _ = spec.shape
    count, width = target.shape
    rim = (grid_rows - count) // 2
    batch = BATCH
    steps = kernels // batch

    def fetch_table(i):
        here = pl.ds(sections[i][0], sections[i][1])
        return pltpu.make_async_copy(tables_far.at[here], tables.at[here], table_sems.at[i])

    def table(name):
        start, rows, blocks = layout[name]
        parts = [tables[start + b * rows:start + (b + 1) * rows] for b in range(blocks)]
        return jnp.concatenate(parts, axis=1)

    fetch_table(0).start()
    fetch_table(1).start()
    fetch_table(2).start()
    fetch_table(0).wait()

    odd = place[0] % 2 == 1
    row_fwd = table("row_fwd")
    above, below = [], []
    for c in range(2):
        above.append(jnp.where(odd, near[c, count - rim:], far[c, count - rim:]))
        below.append(jnp.where(odd, far[c, :rim], near[c, :rim]))
    upper, lower = quarters_of(own[0], own[1], rim)
    mask, = row_stage([lower, tuple(below), tuple(above), upper], row_fwd, width)
    m_first, m_rest = to_freqs(mask, table("mask_head"), table("mask_tail"))
    lane = lax.broadcasted_iota(jnp.int32, m_rest.shape, 1)
    real_half = lane < m_rest.shape[1] // 2
    turned = swap(m_rest)
    mask_spec[:, :2 * width] = m_first
    mask_spec[:, 2 * width:3 * width] = jnp.where(real_half, m_rest, turned)
    mask_spec[:, 3 * width:] = jnp.where(real_half, -turned, m_rest)

    slopes[...] = jnp.zeros(slopes.shape, f32)
    grad_spec[...] = jnp.zeros(grad_spec.shape, f32)
    fetch_table(1).wait()
    col_inv, row_inv = table("col_inv"), table("row_inv")

    def forward(i, carry):
        m_re, m_im = mask_spec[:, :width], mask_spec[:, width:2 * width]
        m_same, m_cross = mask_spec[:, 2 * width:3 * width], mask_spec[:, 3 * width:]

        def cols_of(p):
            planes = []
            for j in range(2):
                k = i * batch + 2 * p + j
                s_re, s_im, s_rest = spec[k, :, :width], spec[k, :, width:2 * width], spec[k, :, 2 * width:]
                product = jnp.concatenate([
                    s_re * m_re - s_im * m_im,
                    s_re * m_im + s_im * m_re,
                    s_rest * m_same + swap(s_rest) * m_cross,
                ], axis=1)
                back = over_lanes(split(product), col_inv)
                planes.append(split(back))
            return [side_by_side(planes, c, width) for c in range(4)]

        def rows_of(p, pair):
            upper, lower = from_row_freqs(pair, row_inv, (0, 1))
            re = jnp.concatenate([upper[0], lower[0]], axis=0)
            im = jnp.concatenate([upper[1], lower[1]], axis=0)
            field[i * (batch // 2) + p, :count] = re
            field[i * (batch // 2) + p, count:] = im
            power = re * re + im * im
            for j in range(2):
                k = i * batch + 2 * p + j
                g = group[k]
                slopes[g] = slopes[g] + weight[k] * power[:, j * width:(j + 1) * width]

        staggered(batch // 2, cols_of, rows_of)
        return carry

    lax.fori_loop(0, steps, forward, 0)

    wanted = target[...].astype(f32)
    for g in range(GROUPS):
        seen = jax.nn.sigmoid(STEEPNESS * (slopes[g] - THRESHOLD))
        resist[g] = seen
        slopes[g] = 2.0 * (seen - wanted) * seen * (1.0 - seen) * STEEPNESS
    out = pltpu.make_async_copy(resist, resist_far, out_sem)
    out.start()
    fetch_table(2).wait()
    head, tail = table("head"), table("tail")

    def backward(i, carry):
        def rows_of(p):
            factors = []
            for j in range(2):
                k = i * batch + 2 * p + j
                factors.append((2.0 * weight[k]) * slopes[group[k]])
            factor = jnp.concatenate(factors, axis=1)
            re = field[i * (batch // 2) + p, :count] * factor
            im = field[i * (batch // 2) + p, count:] * factor
            return row_stage(quarters_of(re, im, rim), row_fwd, width)

        def cols_of(p, tiles):
            total = [grad_spec[:, c * width:(c + 1) * width] for c in range(4)]
            for j in range(2):
                k = i * batch + 2 * p + j
                s_re, s_im, s_rest = spec[k, :, :width], spec[k, :, width:2 * width], spec[k, :, 2 * width:]
                first, rest = to_freqs(tiles[j], head, tail)
                c_re, c_im = first[:, :width], first[:, width:]
                total[0] = total[0] + (s_re * c_re + s_im * c_im)
                total[1] = total[1] + (s_re * c_im - s_im * c_re)
                total[2] = total[2] + s_rest * rest
                total[3] = total[3] + s_rest * swap(rest)
            for c in range(4):
                grad_spec[:, c * width:(c + 1) * width] = total[c]

        staggered(batch // 2, rows_of, cols_of)
        return carry

    lax.fori_loop(0, steps, backward, 0)

    same, cross = grad_spec[:, 2 * width:3 * width], grad_spec[:, 3 * width:]
    tail_sum = jnp.where(real_half, same + swap(same), swap(cross) - cross)
    total = jnp.concatenate([grad_spec[:, :2 * width], tail_sum], axis=1)
    back = split(over_lanes(split(total), table("grad_col")))
    classes = [side_by_side([back], c, width) for c in range(4)]
    rise, upper, lower, fall = from_row_freqs(classes, row_inv, (2, 3, 0, 1))
    for c in range(2):
        near_rim[c] = jnp.where(odd, rise[c], fall[c])
        far_rim[c] = jnp.where(odd, fall[c], rise[c])
        grad_own[c, :rim] = upper[c]
        grad_own[c, rim:] = lower[c]
    out.wait()


def join_body(place, own, near, far, out):
    odd = place[0] % 2 == 1
    rim = near.shape[1]
    count = own.shape[1]
    for c in range(2):
        out[c, :rim] = own[c, :rim] + jnp.where(odd, near[c], far[c])
        if count > 2 * rim:
            out[c, rim:count - rim] = own[c, rim:count - rim]
        out[c, count - rim:] = own[c, count - rim:] + jnp.where(odd, far[c], near[c])


def stacked(groups):
    blocks, layout, sections, at = [], {}, [], 0
    for group in groups:
        start = at
        for name, table in group.items():
            rows, lanes = table.shape
            layout[name] = (at, rows, lanes // 256)
            for b in range(lanes // 256):
                blocks.append(table[:, b * 256:(b + 1) * 256])
            at += rows * (lanes // 256)
        sections.append((start, at - start))
    return np.concatenate(blocks, axis=0), layout, sections


def on_device(mask_field, target, kernel_taps, kernel_radii, kernel_group, kernel_weight):
    _, count, width = mask_field.shape
    kernels, _, span, _ = kernel_taps.shape
    rim = span // 2
    grid_rows = count + 2 * rim
    grid_cols = width + rim
    assert count == span and width == span and kernels % BATCH == 0 and BATCH % 2 == 0 and count == 2 * rim

    strips = lax.axis_size("row")
    assert strips % 2 == 0
    at = lax.axis_index("row")
    near_pairs = [(i, i ^ 1) for i in range(strips)]
    far_pairs = [(i, ((i + 1) ^ 1) - 1) for i in range(1, strips - 1)]
    near = lax.ppermute(mask_field, "row", near_pairs)
    far = lax.ppermute(mask_field, "row", far_pairs)
    place = at.astype(jnp.int32).reshape(1)

    scale = 1.0 / (grid_rows * grid_cols)
    order = grouped(grid_cols, width)

    def head_and_tail(shift):
        table = analysis(grid_cols, width, shift).T[:, order]
        return halves(table[:, :2 * width], 0), halves(table[:, 2 * width:], 1)

    quarter = grid_rows // 4
    by_class = [class_table(grid_rows, quarter, c) for c in range(4)]
    row_fwd = np.concatenate([halves(t, 0) for t in by_class], axis=1)
    row_inv = np.concatenate([halves(t.T * scale, 0) for t in by_class], axis=1)
    head, tail = head_and_tail(0)
    mask_head, mask_tail = head_and_tail(rim)
    col_inv = halves(synthesis(grid_cols, width, 0).T[order], 0)
    grad_col = halves(synthesis(grid_cols, width, rim).T[order], 0)

    smem = pl.BlockSpec(memory_space=pltpu.SMEM)
    vmem = pl.BlockSpec(memory_space=pltpu.VMEM)
    hbm = pl.BlockSpec(memory_space=pltpu.HBM)
    spectra = pl.pallas_call(
        spectra_body,
        out_shape=jax.ShapeDtypeStruct((kernels, grid_rows, 2 * grid_cols), f32),
        in_specs=[smem, hbm] + [vmem] * 3,
        out_specs=vmem,
        scratch_shapes=[
            pltpu.VMEM(kernel_taps.shape, f32),
            pltpu.SemaphoreType.DMA((kernels // BATCH,)),
        ],
        compiler_params=pltpu.CompilerParams(vmem_limit_bytes=SPECTRA_LIMIT * MIB),
        cost_estimate=pl.CostEstimate(flops=18 * 10**9, bytes_accessed=14 * 10**6, transcendentals=0),
        name="spectra",
    )(kernel_radii, kernel_taps, *map(jnp.asarray, (row_fwd, head, tail)))

    tables, layout, sections = stacked([
        {"row_fwd": row_fwd, "mask_head": mask_head, "mask_tail": mask_tail},
        {"col_inv": col_inv, "row_inv": row_inv},
        {"head": head, "tail": tail, "grad_col": grad_col},
    ])
    resist, own, near_rim, far_rim = pl.pallas_call(
        functools.partial(main_body, layout=layout, sections=sections),
        out_shape=[
            jax.ShapeDtypeStruct((GROUPS, count, width), f32),
            jax.ShapeDtypeStruct((2, count, width), f32),
            jax.ShapeDtypeStruct((2, rim, width), f32),
            jax.ShapeDtypeStruct((2, rim, width), f32),
        ],
        in_specs=[smem] * 3 + [vmem] * 5 + [hbm],
        out_specs=[hbm] + [vmem] * 3,
        scratch_shapes=[
            pltpu.VMEM((kernels // 2, 2 * count, 2 * width), f32),
            pltpu.VMEM((grid_rows, 4 * width), f32),
            pltpu.VMEM((GROUPS, count, width), f32),
            pltpu.VMEM((GROUPS, count, width), f32),
            pltpu.VMEM((grid_rows, 4 * width), f32),
            pltpu.VMEM(tables.shape, bf16),
            pltpu.SemaphoreType.DMA((len(sections),)),
            pltpu.SemaphoreType.DMA,
        ],
        compiler_params=pltpu.CompilerParams(vmem_limit_bytes=LIMIT * MIB),
        name="fields",
    )(kernel_group, kernel_weight, place, mask_field, near, far, target, spectra, jnp.asarray(tables))

    near_in = lax.ppermute(near_rim, "row", near_pairs)
    far_in = lax.ppermute(far_rim, "row", far_pairs)
    gradient = pl.pallas_call(
        join_body,
        out_shape=jax.ShapeDtypeStruct((2, count, width), f32),
        in_specs=[smem] + [vmem] * 3,
        out_specs=vmem,
        compiler_params=pltpu.CompilerParams(vmem_limit_bytes=4 * MIB),
        name="join",
    )(place, own, near_in, far_in)
    return resist, gradient


def solution(mesh):
    in_specs = (P(None, ("win", "row"), None), P(("win", "row"), None), P(), P(), P(), P())
    out_specs = (P(None, ("win", "row"), None), P(None, ("win", "row"), None))
    return jax.shard_map(
        on_device, mesh=mesh, in_specs=in_specs, out_specs=out_specs, check_vma=False
    )
```

```python
import functools
import math

import jax
import jax.numpy as jnp
import ml_dtypes
import numpy as np
from jax import lax
from jax.experimental import pallas as pl
from jax.experimental.pallas import tpu as pltpu
from jax.sharding import PartitionSpec as P

RMAX = 64
GROUPS = 3
STEEPNESS = 1.0
THRESHOLD = 2.0
BATCH = 12
PIECE = 256

f32 = jnp.float32
bf16 = jnp.bfloat16
MIB = 1024 * 1024
LIMIT = 53


def halves(table, axis):
    high = table.astype(ml_dtypes.bfloat16)
    low = (table - high.astype(np.float64)).astype(ml_dtypes.bfloat16)
    return np.concatenate([high, low], axis=axis)


def analysis(freqs, points, shift):
    f = np.arange(freqs)[:, None]
    n = np.arange(points)[None, :] - shift
    angle = 2.0 * math.pi * ((f * n) % freqs) / freqs
    cos, sin = np.cos(angle), np.sin(angle)
    return np.block([[cos, sin], [-sin, cos]])


def synthesis(freqs, points, shift, scale=1.0):
    return analysis(freqs, points, shift).T * scale


def class_table(freqs, points, c):
    f = np.arange(c, freqs, 4)[:, None]
    n = np.arange(points)[None, :]
    angle = 2.0 * math.pi * ((f * n) % freqs) / freqs
    cos, sin = np.cos(angle), np.sin(angle)
    return np.block([[cos, sin], [-sin, cos]])


def grouped(freqs, lanes):
    head, tail = np.arange(lanes), np.arange(lanes, freqs)
    return np.concatenate([head, freqs + head, tail, freqs + tail])


def split(x):
    high = x.astype(bf16)
    low = (x - high.astype(f32)).astype(bf16)
    return high, low


def dot(left, right):
    parts = [
        jnp.dot(left[at:at + PIECE], right, preferred_element_type=f32)
        for at in range(0, left.shape[0], PIECE)
    ]
    return jnp.concatenate(parts, axis=0)


def class_product(table, c, parts):
    depth = parts[0].shape[0]
    left = table[:, c * depth:(c + 1) * depth]
    found = dot(jnp.concatenate([left, left], axis=1), jnp.concatenate(parts, axis=0))
    half = found.shape[0] // 2
    return found[:half] + found[half:]


def turned(x, sign):
    re, im = x
    return (-im, re) if sign > 0 else (im, -re)


def plus(x, y):
    return x[0] + y[0], x[1] + y[1]


def minus(x, y):
    return x[0] - y[0], x[1] - y[1]


def to_row_freqs(x, table):
    if len(x) == 2:
        even, odd, even_less, odd_less = x[0], x[1], x[0], x[1]
    else:
        even, odd = plus(x[0], x[2]), plus(x[1], x[3])
        even_less, odd_less = minus(x[0], x[2]), minus(x[1], x[3])
    folded = [
        plus(even, odd),
        plus(even_less, turned(odd_less, -1)),
        minus(even, odd),
        plus(even_less, turned(odd_less, 1)),
    ]
    return [class_product(table, c, split(jnp.concatenate(y, axis=0))) for c, y in enumerate(folded)]


def from_row_freqs(classes, table, quarters):
    v = []
    for c, parts in enumerate(classes):
        found = class_product(table, c, parts)
        half = found.shape[0] // 2
        v.append((found[:half], found[half:]))
    out = []
    for q in quarters:
        if q % 2 == 0:
            even, odd = plus(v[0], v[2]), plus(v[1], v[3])
        else:
            even, odd = minus(v[0], v[2]), turned(minus(v[1], v[3]), 1)
        out.append(plus(even, odd) if q < 2 else minus(even, odd))
    return out


def over_lanes(parts, table):
    high, low = parts
    right = jnp.concatenate([table, table[:high.shape[1]]], axis=0)
    return dot(jnp.concatenate([high, high, low], axis=1), right)


def to_freqs(parts, head, tail):
    high, low = parts
    rows, depth = high.shape
    lanes = tail.shape[1] // 2
    stack = jnp.concatenate([high, low], axis=0)
    both = jnp.dot(stack, head[:depth], preferred_element_type=f32)
    third = jnp.dot(high, head[depth:], preferred_element_type=f32)
    first = both[:rows] + (both[rows:] + third)
    both = jnp.dot(stack, tail, preferred_element_type=f32)
    return first, both[:rows, :lanes] + (both[:rows, lanes:] + both[rows:, :lanes])


def beside(classes, at, width):
    tiles = []
    for found in classes:
        half = found.shape[0] // 2
        tiles.append(jnp.concatenate([found[:half, at:at + width], found[half:, at:at + width]], axis=1))
    return split(jnp.concatenate(tiles, axis=0))


def row_stage(quarters, row_fwd, width):
    classes = to_row_freqs(quarters, row_fwd)
    return [beside(classes, at, width) for at in range(0, quarters[0][0].shape[1], width)]


def quarters_of(re, im, quarter):
    return [(re[at:at + quarter], im[at:at + quarter]) for at in range(0, re.shape[0], quarter)]


def staggered(count, first, second):
    held = None
    for i in range(count):
        new = first(i)
        if i:
            second(i - 1, held)
        held = new
    second(count - 1, held)


def side_by_side(planes, c, width):
    quarter = planes[0][0].shape[0] // 4
    rows = slice(c * quarter, (c + 1) * quarter)
    return [
        jnp.concatenate([
            jnp.concatenate([plane[part][rows, at:at + width] for plane in planes], axis=1)
            for at in (0, width)
        ], axis=0)
        for part in range(2)
    ]


def swap(x):
    return pltpu.roll(x, x.shape[1] // 2, 1)


def spectra_body(radii, taps_far, row_ref, head_ref, tail_ref, spec_far, taps, spec, in_sems, out_sems):
    kernels, _, span, _ = taps.shape
    row_fwd, head, tail = row_ref[...], head_ref[...], tail_ref[...]
    steps = in_sems.shape[0]
    batch = kernels // steps

    def fetch(i):
        here = pl.ds(i * batch, batch)
        return pltpu.make_async_copy(taps_far.at[here], taps.at[here], in_sems.at[i])

    def put(i):
        here = pl.ds(2 * i, 2)
        return pltpu.make_async_copy(spec.at[here], spec_far.at[here], out_sems.at[i])

    for i in range(steps):
        fetch(i).start()
    row_at = lax.broadcasted_iota(jnp.int32, (span, span), 0) - span // 2
    col_at = lax.broadcasted_iota(jnp.int32, (span, span), 1) - span // 2
    reach = jnp.maximum(jnp.maximum(row_at, -1 - row_at), jnp.maximum(col_at, -1 - col_at))

    def step(i, carry):
        fetch(i).wait()

        def rows_of(p):
            planes = [[], []]
            for j in range(2):
                k = i * batch + 2 * p + j
                inside = reach < radii[k]
                for c in range(2):
                    planes[c].append(jnp.where(inside, taps[k, c], 0.0))
            re, im = [jnp.concatenate(plane, axis=1) for plane in planes]
            return row_stage(quarters_of(re, im, span // 2), row_fwd, span)

        def cols_of(p, tiles):
            for j in range(2):
                k = i * batch + 2 * p + j
                a, b = to_freqs(tiles[j], head, tail)
                spec[k, :, :a.shape[1]] = a
                spec[k, :, a.shape[1]:] = b
            put(i * (batch // 2) + p).start()

        staggered(batch // 2, rows_of, cols_of)
        return carry

    lax.fori_loop(0, steps, step, 0)
    for i in range(kernels // 2):
        put(i).wait()


def main_body(
    group, weight, place,
    own, near, far, target, spec_far, tables_far,
    resist_far, grad_own, near_rim, far_rim,
    spec, field, mask_spec, resist, slopes, grad_spec, tables, spec_sems, table_sems, out_sem,
    *, layout, sections,
):
    kernels, grid_rows, _ = spec.shape
    count, width = target.shape
    rim = (grid_rows - count) // 2
    steps = spec_sems.shape[0]
    batch = kernels // steps

    def fetch(i):
        here = pl.ds(i * batch, batch)
        return pltpu.make_async_copy(spec_far.at[here], spec.at[here], spec_sems.at[i])

    def fetch_table(i):
        here = pl.ds(sections[i][0], sections[i][1])
        return pltpu.make_async_copy(tables_far.at[here], tables.at[here], table_sems.at[i])

    def table(name):
        start, rows, blocks = layout[name]
        parts = [tables[start + b * rows:start + (b + 1) * rows] for b in range(blocks)]
        return jnp.concatenate(parts, axis=1)

    fetch_table(0).start()
    fetch_table(1).start()
    for i in range(steps):
        fetch(i).start()
    fetch_table(2).start()
    fetch_table(0).wait()

    odd = place[0] % 2 == 1
    row_fwd = table("row_fwd")
    above, below = [], []
    for c in range(2):
        above.append(jnp.where(odd, near[c, count - rim:], far[c, count - rim:]))
        below.append(jnp.where(odd, far[c, :rim], near[c, :rim]))
    upper, lower = quarters_of(own[0], own[1], rim)
    mask, = row_stage([lower, tuple(below), tuple(above), upper], row_fwd, width)
    m_first, m_rest = to_freqs(mask, table("mask_head"), table("mask_tail"))
    lane = lax.broadcasted_iota(jnp.int32, m_rest.shape, 1)
    real_half = lane < m_rest.shape[1] // 2
    turned = swap(m_rest)
    mask_spec[:, :2 * width] = m_first
    mask_spec[:, 2 * width:3 * width] = jnp.where(real_half, m_rest, turned)
    mask_spec[:, 3 * width:] = jnp.where(real_half, -turned, m_rest)

    slopes[...] = jnp.zeros(slopes.shape, f32)
    grad_spec[...] = jnp.zeros(grad_spec.shape, f32)
    fetch_table(1).wait()
    col_inv, row_inv = table("col_inv"), table("row_inv")

    def forward(i, carry):
        fetch(i).wait()
        m_re, m_im = mask_spec[:, :width], mask_spec[:, width:2 * width]
        m_same, m_cross = mask_spec[:, 2 * width:3 * width], mask_spec[:, 3 * width:]

        def cols_of(p):
            planes = []
            for j in range(2):
                k = i * batch + 2 * p + j
                s_re, s_im, s_rest = spec[k, :, :width], spec[k, :, width:2 * width], spec[k, :, 2 * width:]
                product = jnp.concatenate([
                    s_re * m_re - s_im * m_im,
                    s_re * m_im + s_im * m_re,
                    s_rest * m_same + swap(s_rest) * m_cross,
                ], axis=1)
                back = over_lanes(split(product), col_inv)
                planes.append(split(back))
            return [side_by_side(planes, c, width) for c in range(4)]

        def rows_of(p, pair):
            upper, lower = from_row_freqs(pair, row_inv, (0, 1))
            re = jnp.concatenate([upper[0], lower[0]], axis=0)
            im = jnp.concatenate([upper[1], lower[1]], axis=0)
            field[i * (batch // 2) + p, :count] = re
            field[i * (batch // 2) + p, count:] = im
            power = re * re + im * im
            for j in range(2):
                k = i * batch + 2 * p + j
                g = group[k]
                slopes[g] = slopes[g] + weight[k] * power[:, j * width:(j + 1) * width]

        staggered(batch // 2, cols_of, rows_of)
        return carry

    lax.fori_loop(0, steps, forward, 0)

    wanted = target[...].astype(f32)
    for g in range(GROUPS):
        seen = jax.nn.sigmoid(STEEPNESS * (slopes[g] - THRESHOLD))
        resist[g] = seen
        slopes[g] = 2.0 * (seen - wanted) * seen * (1.0 - seen) * STEEPNESS
    out = pltpu.make_async_copy(resist, resist_far, out_sem)
    out.start()
    fetch_table(2).wait()
    head, tail = table("head"), table("tail")

    def backward(i, carry):
        def rows_of(p):
            factors = []
            for j in range(2):
                k = i * batch + 2 * p + j
                factors.append((2.0 * weight[k]) * slopes[group[k]])
            factor = jnp.concatenate(factors, axis=1)
            re = field[i * (batch // 2) + p, :count] * factor
            im = field[i * (batch // 2) + p, count:] * factor
            return row_stage(quarters_of(re, im, rim), row_fwd, width)

        def cols_of(p, tiles):
            total = [grad_spec[:, c * width:(c + 1) * width] for c in range(4)]
            for j in range(2):
                k = i * batch + 2 * p + j
                s_re, s_im, s_rest = spec[k, :, :width], spec[k, :, width:2 * width], spec[k, :, 2 * width:]
                first, rest = to_freqs(tiles[j], head, tail)
                c_re, c_im = first[:, :width], first[:, width:]
                total[0] = total[0] + (s_re * c_re + s_im * c_im)
                total[1] = total[1] + (s_re * c_im - s_im * c_re)
                total[2] = total[2] + s_rest * rest
                total[3] = total[3] + s_rest * swap(rest)
            for c in range(4):
                grad_spec[:, c * width:(c + 1) * width] = total[c]

        staggered(batch // 2, rows_of, cols_of)
        return carry

    lax.fori_loop(0, steps, backward, 0)

    same, cross = grad_spec[:, 2 * width:3 * width], grad_spec[:, 3 * width:]
    tail_sum = jnp.where(real_half, same + swap(same), swap(cross) - cross)
    total = jnp.concatenate([grad_spec[:, :2 * width], tail_sum], axis=1)
    back = split(over_lanes(split(total), table("grad_col")))
    classes = [side_by_side([back], c, width) for c in range(4)]
    rise, upper, lower, fall = from_row_freqs(classes, row_inv, (2, 3, 0, 1))
    for c in range(2):
        near_rim[c] = jnp.where(odd, rise[c], fall[c])
        far_rim[c] = jnp.where(odd, fall[c], rise[c])
        grad_own[c, :rim] = upper[c]
        grad_own[c, rim:] = lower[c]
    out.wait()


def join_body(place, own, near, far, out):
    odd = place[0] % 2 == 1
    rim = near.shape[1]
    count = own.shape[1]
    for c in range(2):
        out[c, :rim] = own[c, :rim] + jnp.where(odd, near[c], far[c])
        if count > 2 * rim:
            out[c, rim:count - rim] = own[c, rim:count - rim]
        out[c, count - rim:] = own[c, count - rim:] + jnp.where(odd, far[c], near[c])


def stacked(groups):
    blocks, layout, sections, at = [], {}, [], 0
    for group in groups:
        start = at
        for name, table in group.items():
            rows, lanes = table.shape
            layout[name] = (at, rows, lanes // 256)
            for b in range(lanes // 256):
                blocks.append(table[:, b * 256:(b + 1) * 256])
            at += rows * (lanes // 256)
        sections.append((start, at - start))
    return np.concatenate(blocks, axis=0), layout, sections


def on_device(mask_field, target, kernel_taps, kernel_radii, kernel_group, kernel_weight):
    _, count, width = mask_field.shape
    kernels, _, span, _ = kernel_taps.shape
    rim = span // 2
    grid_rows = count + 2 * rim
    grid_cols = width + rim
    assert count == span and width == span and kernels % BATCH == 0 and BATCH % 2 == 0 and count == 2 * rim

    strips = lax.axis_size("row")
    assert strips % 2 == 0
    at = lax.axis_index("row")
    near_pairs = [(i, i ^ 1) for i in range(strips)]
    far_pairs = [(i, ((i + 1) ^ 1) - 1) for i in range(1, strips - 1)]
    near = lax.ppermute(mask_field, "row", near_pairs)
    far = lax.ppermute(mask_field, "row", far_pairs)
    place = at.astype(jnp.int32).reshape(1)

    scale = 1.0 / (grid_rows * grid_cols)
    order = grouped(grid_cols, width)

    def head_and_tail(shift):
        table = analysis(grid_cols, width, shift).T[:, order]
        return halves(table[:, :2 * width], 0), halves(table[:, 2 * width:], 1)

    quarter = grid_rows // 4
    by_class = [class_table(grid_rows, quarter, c) for c in range(4)]
    row_fwd = np.concatenate([halves(t, 0) for t in by_class], axis=1)
    row_inv = np.concatenate([halves(t.T * scale, 0) for t in by_class], axis=1)
    head, tail = head_and_tail(0)
    mask_head, mask_tail = head_and_tail(rim)
    col_inv = halves(synthesis(grid_cols, width, 0).T[order], 0)
    grad_col = halves(synthesis(grid_cols, width, rim).T[order], 0)

    smem = pl.BlockSpec(memory_space=pltpu.SMEM)
    vmem = pl.BlockSpec(memory_space=pltpu.VMEM)
    hbm = pl.BlockSpec(memory_space=pltpu.HBM)
    spectra = pl.pallas_call(
        spectra_body,
        out_shape=jax.ShapeDtypeStruct((kernels, grid_rows, 2 * grid_cols), f32),
        in_specs=[smem, hbm, vmem, vmem, vmem],
        out_specs=hbm,
        scratch_shapes=[
            pltpu.VMEM(kernel_taps.shape, f32),
            pltpu.VMEM((kernels, grid_rows, 2 * grid_cols), f32),
            pltpu.SemaphoreType.DMA((kernels // BATCH,)),
            pltpu.SemaphoreType.DMA((kernels // 2,)),
        ],
        compiler_params=pltpu.CompilerParams(vmem_limit_bytes=56 * MIB),
        cost_estimate=pl.CostEstimate(flops=18 * 10**9, bytes_accessed=14 * 10**6, transcendentals=0),
        name="spectra",
    )(kernel_radii, kernel_taps, *map(jnp.asarray, (row_fwd, head, tail)))

    tables, layout, sections = stacked([
        {"row_fwd": row_fwd, "mask_head": mask_head, "mask_tail": mask_tail},
        {"col_inv": col_inv, "row_inv": row_inv},
        {"head": head, "tail": tail, "grad_col": grad_col},
    ])
    resist, own, near_rim, far_rim = pl.pallas_call(
        functools.partial(main_body, layout=layout, sections=sections),
        out_shape=[
            jax.ShapeDtypeStruct((GROUPS, count, width), f32),
            jax.ShapeDtypeStruct((2, count, width), f32),
            jax.ShapeDtypeStruct((2, rim, width), f32),
            jax.ShapeDtypeStruct((2, rim, width), f32),
        ],
        in_specs=[smem] * 3 + [vmem] * 4 + [hbm] * 2,
        out_specs=[hbm] + [vmem] * 3,
        scratch_shapes=[
            pltpu.VMEM((kernels, grid_rows, 2 * grid_cols), f32),
            pltpu.VMEM((kernels // 2, 2 * count, 2 * width), f32),
            pltpu.VMEM((grid_rows, 4 * width), f32),
            pltpu.VMEM((GROUPS, count, width), f32),
            pltpu.VMEM((GROUPS, count, width), f32),
            pltpu.VMEM((grid_rows, 4 * width), f32),
            pltpu.VMEM(tables.shape, bf16),
            pltpu.SemaphoreType.DMA((kernels // BATCH,)),
            pltpu.SemaphoreType.DMA((len(sections),)),
            pltpu.SemaphoreType.DMA,
        ],
        compiler_params=pltpu.CompilerParams(vmem_limit_bytes=LIMIT * MIB),
        name="fields",
    )(kernel_group, kernel_weight, place, mask_field, near, far, target, spectra, jnp.asarray(tables))

    near_in = lax.ppermute(near_rim, "row", near_pairs)
    far_in = lax.ppermute(far_rim, "row", far_pairs)
    gradient = pl.pallas_call(
        join_body,
        out_shape=jax.ShapeDtypeStruct((2, count, width), f32),
        in_specs=[smem] + [vmem] * 3,
        out_specs=vmem,
        compiler_params=pltpu.CompilerParams(vmem_limit_bytes=4 * MIB),
        name="join",
    )(place, own, near_in, far_in)
    return resist, gradient


def solution(mesh):
    in_specs = (P(None, ("win", "row"), None), P(("win", "row"), None), P(), P(), P(), P())
    out_specs = (P(None, ("win", "row"), None), P(None, ("win", "row"), None))
    return jax.shard_map(
        on_device, mesh=mesh, in_specs=in_specs, out_specs=out_specs, check_vma=False
    )
```

```python
import functools
import math

import jax
import jax.numpy as jnp
import ml_dtypes
import numpy as np
from jax import lax
from jax.experimental import pallas as pl
from jax.experimental.pallas import tpu as pltpu
from jax.sharding import PartitionSpec as P

RMAX = 64
GROUPS = 3
STEEPNESS = 1.0
THRESHOLD = 2.0
BATCH = 12
EARLY = 4
LATE_BATCH = 10
PIECE = 256

f32 = jnp.float32
bf16 = jnp.bfloat16
MIB = 1024 * 1024
LIMIT = 53


def halves(table, axis):
    high = table.astype(ml_dtypes.bfloat16)
    low = (table - high.astype(np.float64)).astype(ml_dtypes.bfloat16)
    return np.concatenate([high, low], axis=axis)


def analysis(freqs, points, shift):
    f = np.arange(freqs)[:, None]
    n = np.arange(points)[None, :] - shift
    angle = 2.0 * math.pi * ((f * n) % freqs) / freqs
    cos, sin = np.cos(angle), np.sin(angle)
    return np.block([[cos, sin], [-sin, cos]])


def synthesis(freqs, points, shift, scale=1.0):
    return analysis(freqs, points, shift).T * scale


def class_table(freqs, points, c):
    f = np.arange(c, freqs, 4)[:, None]
    n = np.arange(points)[None, :]
    angle = 2.0 * math.pi * ((f * n) % freqs) / freqs
    cos, sin = np.cos(angle), np.sin(angle)
    return np.block([[cos, sin], [-sin, cos]])


def grouped(freqs, lanes):
    head, tail = np.arange(lanes), np.arange(lanes, freqs)
    return np.concatenate([head, freqs + head, tail, freqs + tail])


def split(x):
    high = x.astype(bf16)
    low = (x - high.astype(f32)).astype(bf16)
    return high, low


def dot(left, right):
    parts = [
        jnp.dot(left[at:at + PIECE], right, preferred_element_type=f32)
        for at in range(0, left.shape[0], PIECE)
    ]
    return jnp.concatenate(parts, axis=0)


def class_product(table, c, parts):
    depth = parts[0].shape[0]
    left = table[:, c * depth:(c + 1) * depth]
    found = dot(jnp.concatenate([left, left], axis=1), jnp.concatenate(parts, axis=0))
    half = found.shape[0] // 2
    return found[:half] + found[half:]


def turned(x, sign):
    re, im = x
    return (-im, re) if sign > 0 else (im, -re)


def plus(x, y):
    return x[0] + y[0], x[1] + y[1]


def minus(x, y):
    return x[0] - y[0], x[1] - y[1]


def to_row_freqs(x, table):
    if len(x) == 2:
        even, odd, even_less, odd_less = x[0], x[1], x[0], x[1]
    else:
        even, odd = plus(x[0], x[2]), plus(x[1], x[3])
        even_less, odd_less = minus(x[0], x[2]), minus(x[1], x[3])
    folded = [
        plus(even, odd),
        plus(even_less, turned(odd_less, -1)),
        minus(even, odd),
        plus(even_less, turned(odd_less, 1)),
    ]
    return [class_product(table, c, split(jnp.concatenate(y, axis=0))) for c, y in enumerate(folded)]


def from_row_freqs(classes, table, quarters):
    v = []
    for c, parts in enumerate(classes):
        found = class_product(table, c, parts)
        half = found.shape[0] // 2
        v.append((found[:half], found[half:]))
    out = []
    for q in quarters:
        if q % 2 == 0:
            even, odd = plus(v[0], v[2]), plus(v[1], v[3])
        else:
            even, odd = minus(v[0], v[2]), turned(minus(v[1], v[3]), 1)
        out.append(plus(even, odd) if q < 2 else minus(even, odd))
    return out


def over_lanes(parts, table):
    high, low = parts
    right = jnp.concatenate([table, table[:high.shape[1]]], axis=0)
    return dot(jnp.concatenate([high, high, low], axis=1), right)


def to_freqs(parts, head, tail):
    high, low = parts
    rows, depth = high.shape
    lanes = tail.shape[1] // 2
    stack = jnp.concatenate([high, low], axis=0)
    both = jnp.dot(stack, head[:depth], preferred_element_type=f32)
    third = jnp.dot(high, head[depth:], preferred_element_type=f32)
    first = both[:rows] + (both[rows:] + third)
    both = jnp.dot(stack, tail, preferred_element_type=f32)
    return first, both[:rows, :lanes] + (both[:rows, lanes:] + both[rows:, :lanes])


def beside(classes, at, width):
    tiles = []
    for found in classes:
        half = found.shape[0] // 2
        tiles.append(jnp.concatenate([found[:half, at:at + width], found[half:, at:at + width]], axis=1))
    return split(jnp.concatenate(tiles, axis=0))


def row_stage(quarters, row_fwd, width):
    classes = to_row_freqs(quarters, row_fwd)
    return [beside(classes, at, width) for at in range(0, quarters[0][0].shape[1], width)]


def quarters_of(re, im, quarter):
    return [(re[at:at + quarter], im[at:at + quarter]) for at in range(0, re.shape[0], quarter)]


def staggered(count, first, second):
    held = None
    for i in range(count):
        new = first(i)
        if i:
            second(i - 1, held)
        held = new
    second(count - 1, held)


def side_by_side(planes, c, width):
    quarter = planes[0][0].shape[0] // 4
    rows = slice(c * quarter, (c + 1) * quarter)
    return [
        jnp.concatenate([
            jnp.concatenate([plane[part][rows, at:at + width] for plane in planes], axis=1)
            for at in (0, width)
        ], axis=0)
        for part in range(2)
    ]


def swap(x):
    return pltpu.roll(x, x.shape[1] // 2, 1)


def spectra_of(radii, taps, spec, first, batch, row_fwd, head, tail):
    span = taps.shape[2]
    row_at = lax.broadcasted_iota(jnp.int32, (span, span), 0) - span // 2
    col_at = lax.broadcasted_iota(jnp.int32, (span, span), 1) - span // 2
    reach = jnp.maximum(jnp.maximum(row_at, -1 - row_at), jnp.maximum(col_at, -1 - col_at))

    def rows_of(p):
        planes = [[], []]
        for j in range(2):
            k = first + 2 * p + j
            inside = reach < radii[k]
            for c in range(2):
                planes[c].append(jnp.where(inside, taps[k, c], 0.0))
        re, im = [jnp.concatenate(plane, axis=1) for plane in planes]
        return row_stage(quarters_of(re, im, span // 2), row_fwd, span)

    def cols_of(p, tiles):
        for j in range(2):
            k = first + 2 * p + j
            a, b = to_freqs(tiles[j], head, tail)
            spec[k, :, :a.shape[1]] = a
            spec[k, :, a.shape[1]:] = b

    staggered(batch // 2, rows_of, cols_of)


def spectra_body(radii, taps_far, row_ref, head_ref, tail_ref, spec_far, taps, spec, in_sem, out_sem):
    early = spec.shape[0]
    fetch = pltpu.make_async_copy(taps_far.at[pl.ds(0, early)], taps, in_sem)
    fetch.start()
    fetch.wait()
    spectra_of(radii, taps, spec, 0, early, row_ref[...], head_ref[...], tail_ref[...])
    put = pltpu.make_async_copy(spec, spec_far, out_sem)
    put.start()
    put.wait()


def main_body(
    group, weight, place, radii,
    own, near, far, target, taps_far, spec_far, tables_far,
    resist_far, grad_own, near_rim, far_rim,
    spec, taps, field, mask_spec, resist, slopes, grad_spec, tables, spec_sem, taps_sems, table_sems, out_sem,
    *, layout, sections,
):
    kernels, grid_rows, _ = spec.shape
    count, width = target.shape
    rim = (grid_rows - count) // 2
    batch = BATCH
    steps = kernels // batch
    early = spec_far.shape[0]
    late_steps = taps_sems.shape[0]
    late = (kernels - early) // late_steps

    fetch_early = pltpu.make_async_copy(spec_far, spec.at[pl.ds(0, early)], spec_sem)

    def fetch_taps(i):
        here = pl.ds(early + i * late, late)
        return pltpu.make_async_copy(taps_far.at[here], taps.at[here], taps_sems.at[i])

    def fetch_table(i):
        here = pl.ds(sections[i][0], sections[i][1])
        return pltpu.make_async_copy(tables_far.at[here], tables.at[here], table_sems.at[i])

    def table(name):
        start, rows, blocks = layout[name]
        parts = [tables[start + b * rows:start + (b + 1) * rows] for b in range(blocks)]
        return jnp.concatenate(parts, axis=1)

    fetch_table(0).start()
    for i in range(late_steps):
        fetch_taps(i).start()
    fetch_table(1).start()
    fetch_early.start()
    slopes[...] = jnp.zeros(slopes.shape, f32)
    grad_spec[...] = jnp.zeros(grad_spec.shape, f32)
    fetch_table(0).wait()
    row_fwd, head, tail = table("row_fwd"), table("head"), table("tail")

    def spectra(i, carry):
        fetch_taps(i).wait()
        spectra_of(radii, taps, spec, early + i * late, late, row_fwd, head, tail)
        return carry

    lax.fori_loop(0, late_steps, spectra, 0)
    fetch_table(1).wait()
    fetch_early.wait()

    odd = place[0] % 2 == 1
    above, below = [], []
    for c in range(2):
        above.append(jnp.where(odd, near[c, count - rim:], far[c, count - rim:]))
        below.append(jnp.where(odd, far[c, :rim], near[c, :rim]))
    upper, lower = quarters_of(own[0], own[1], rim)
    mask, = row_stage([lower, tuple(below), tuple(above), upper], row_fwd, width)
    m_first, m_rest = to_freqs(mask, table("mask_head"), table("mask_tail"))
    lane = lax.broadcasted_iota(jnp.int32, m_rest.shape, 1)
    real_half = lane < m_rest.shape[1] // 2
    turned = swap(m_rest)
    mask_spec[:, :2 * width] = m_first
    mask_spec[:, 2 * width:3 * width] = jnp.where(real_half, m_rest, turned)
    mask_spec[:, 3 * width:] = jnp.where(real_half, -turned, m_rest)

    col_inv, row_inv = table("col_inv"), table("row_inv")

    def forward(i, carry):
        m_re, m_im = mask_spec[:, :width], mask_spec[:, width:2 * width]
        m_same, m_cross = mask_spec[:, 2 * width:3 * width], mask_spec[:, 3 * width:]

        def cols_of(p):
            planes = []
            for j in range(2):
                k = i * batch + 2 * p + j
                s_re, s_im, s_rest = spec[k, :, :width], spec[k, :, width:2 * width], spec[k, :, 2 * width:]
                product = jnp.concatenate([
                    s_re * m_re - s_im * m_im,
                    s_re * m_im + s_im * m_re,
                    s_rest * m_same + swap(s_rest) * m_cross,
                ], axis=1)
                back = over_lanes(split(product), col_inv)
                planes.append(split(back))
            return [side_by_side(planes, c, width) for c in range(4)]

        def rows_of(p, pair):
            upper, lower = from_row_freqs(pair, row_inv, (0, 1))
            re = jnp.concatenate([upper[0], lower[0]], axis=0)
            im = jnp.concatenate([upper[1], lower[1]], axis=0)
            field[i * (batch // 2) + p, :count] = re
            field[i * (batch // 2) + p, count:] = im
            power = re * re + im * im
            for j in range(2):
                k = i * batch + 2 * p + j
                g = group[k]
                slopes[g] = slopes[g] + weight[k] * power[:, j * width:(j + 1) * width]

        staggered(batch // 2, cols_of, rows_of)
        return carry

    lax.fori_loop(0, steps, forward, 0)

    wanted = target[...].astype(f32)
    for g in range(GROUPS):
        seen = jax.nn.sigmoid(STEEPNESS * (slopes[g] - THRESHOLD))
        resist[g] = seen
        slopes[g] = 2.0 * (seen - wanted) * seen * (1.0 - seen) * STEEPNESS
    out = pltpu.make_async_copy(resist, resist_far, out_sem)
    out.start()

    def backward(i, carry):
        def rows_of(p):
            factors = []
            for j in range(2):
                k = i * batch + 2 * p + j
                factors.append((2.0 * weight[k]) * slopes[group[k]])
            factor = jnp.concatenate(factors, axis=1)
            re = field[i * (batch // 2) + p, :count] * factor
            im = field[i * (batch // 2) + p, count:] * factor
            return row_stage(quarters_of(re, im, rim), row_fwd, width)

        def cols_of(p, tiles):
            total = [grad_spec[:, c * width:(c + 1) * width] for c in range(4)]
            for j in range(2):
                k = i * batch + 2 * p + j
                s_re, s_im, s_rest = spec[k, :, :width], spec[k, :, width:2 * width], spec[k, :, 2 * width:]
                first, rest = to_freqs(tiles[j], head, tail)
                c_re, c_im = first[:, :width], first[:, width:]
                total[0] = total[0] + (s_re * c_re + s_im * c_im)
                total[1] = total[1] + (s_re * c_im - s_im * c_re)
                total[2] = total[2] + s_rest * rest
                total[3] = total[3] + s_rest * swap(rest)
            for c in range(4):
                grad_spec[:, c * width:(c + 1) * width] = total[c]

        staggered(batch // 2, rows_of, cols_of)
        return carry

    lax.fori_loop(0, steps, backward, 0)

    same, cross = grad_spec[:, 2 * width:3 * width], grad_spec[:, 3 * width:]
    tail_sum = jnp.where(real_half, same + swap(same), swap(cross) - cross)
    total = jnp.concatenate([grad_spec[:, :2 * width], tail_sum], axis=1)
    back = split(over_lanes(split(total), table("grad_col")))
    classes = [side_by_side([back], c, width) for c in range(4)]
    rise, upper, lower, fall = from_row_freqs(classes, row_inv, (2, 3, 0, 1))
    for c in range(2):
        near_rim[c] = jnp.where(odd, rise[c], fall[c])
        far_rim[c] = jnp.where(odd, fall[c], rise[c])
        grad_own[c, :rim] = upper[c]
        grad_own[c, rim:] = lower[c]
    out.wait()


def join_body(place, own, near, far, out):
    odd = place[0] % 2 == 1
    rim = near.shape[1]
    count = own.shape[1]
    for c in range(2):
        out[c, :rim] = own[c, :rim] + jnp.where(odd, near[c], far[c])
        if count > 2 * rim:
            out[c, rim:count - rim] = own[c, rim:count - rim]
        out[c, count - rim:] = own[c, count - rim:] + jnp.where(odd, far[c], near[c])


def stacked(groups):
    blocks, layout, sections, at = [], {}, [], 0
    for group in groups:
        start = at
        for name, table in group.items():
            rows, lanes = table.shape
            layout[name] = (at, rows, lanes // 256)
            for b in range(lanes // 256):
                blocks.append(table[:, b * 256:(b + 1) * 256])
            at += rows * (lanes // 256)
        sections.append((start, at - start))
    return np.concatenate(blocks, axis=0), layout, sections


def on_device(mask_field, target, kernel_taps, kernel_radii, kernel_group, kernel_weight):
    _, count, width = mask_field.shape
    kernels, _, span, _ = kernel_taps.shape
    rim = span // 2
    grid_rows = count + 2 * rim
    grid_cols = width + rim
    assert count == span and width == span and kernels % BATCH == 0 and (kernels - EARLY) % LATE_BATCH == 0 and count == 2 * rim

    strips = lax.axis_size("row")
    assert strips % 2 == 0
    at = lax.axis_index("row")
    near_pairs = [(i, i ^ 1) for i in range(strips)]
    far_pairs = [(i, ((i + 1) ^ 1) - 1) for i in range(1, strips - 1)]
    near = lax.ppermute(mask_field, "row", near_pairs)
    far = lax.ppermute(mask_field, "row", far_pairs)
    place = at.astype(jnp.int32).reshape(1)

    scale = 1.0 / (grid_rows * grid_cols)
    order = grouped(grid_cols, width)

    def head_and_tail(shift):
        table = analysis(grid_cols, width, shift).T[:, order]
        return halves(table[:, :2 * width], 0), halves(table[:, 2 * width:], 1)

    quarter = grid_rows // 4
    by_class = [class_table(grid_rows, quarter, c) for c in range(4)]
    row_fwd = np.concatenate([halves(t, 0) for t in by_class], axis=1)
    row_inv = np.concatenate([halves(t.T * scale, 0) for t in by_class], axis=1)
    head, tail = head_and_tail(0)
    mask_head, mask_tail = head_and_tail(rim)
    col_inv = halves(synthesis(grid_cols, width, 0).T[order], 0)
    grad_col = halves(synthesis(grid_cols, width, rim).T[order], 0)

    smem = pl.BlockSpec(memory_space=pltpu.SMEM)
    vmem = pl.BlockSpec(memory_space=pltpu.VMEM)
    hbm = pl.BlockSpec(memory_space=pltpu.HBM)
    spectra = pl.pallas_call(
        spectra_body,
        out_shape=jax.ShapeDtypeStruct((EARLY, grid_rows, 2 * grid_cols), f32),
        in_specs=[smem, hbm, vmem, vmem, vmem],
        out_specs=hbm,
        scratch_shapes=[
            pltpu.VMEM((EARLY,) + kernel_taps.shape[1:], f32),
            pltpu.VMEM((EARLY, grid_rows, 2 * grid_cols), f32),
            pltpu.SemaphoreType.DMA,
            pltpu.SemaphoreType.DMA,
        ],
        compiler_params=pltpu.CompilerParams(vmem_limit_bytes=56 * MIB),
        cost_estimate=pl.CostEstimate(flops=3 * 10**9, bytes_accessed=3 * 10**6, transcendentals=0),
        name="spectra",
    )(kernel_radii, kernel_taps, *map(jnp.asarray, (row_fwd, head, tail)))

    tables, layout, sections = stacked([
        {"row_fwd": row_fwd, "head": head, "tail": tail},
        {"mask_head": mask_head, "mask_tail": mask_tail, "col_inv": col_inv, "row_inv": row_inv, "grad_col": grad_col},
    ])
    resist, own, near_rim, far_rim = pl.pallas_call(
        functools.partial(main_body, layout=layout, sections=sections),
        out_shape=[
            jax.ShapeDtypeStruct((GROUPS, count, width), f32),
            jax.ShapeDtypeStruct((2, count, width), f32),
            jax.ShapeDtypeStruct((2, rim, width), f32),
            jax.ShapeDtypeStruct((2, rim, width), f32),
        ],
        in_specs=[smem] * 4 + [vmem] * 4 + [hbm] * 3,
        out_specs=[hbm] + [vmem] * 3,
        scratch_shapes=[
            pltpu.VMEM((kernels, grid_rows, 2 * grid_cols), f32),
            pltpu.VMEM(kernel_taps.shape, f32),
            pltpu.VMEM((kernels // 2, 2 * count, 2 * width), f32),
            pltpu.VMEM((grid_rows, 4 * width), f32),
            pltpu.VMEM((GROUPS, count, width), f32),
            pltpu.VMEM((GROUPS, count, width), f32),
            pltpu.VMEM((grid_rows, 4 * width), f32),
            pltpu.VMEM(tables.shape, bf16),
            pltpu.SemaphoreType.DMA,
            pltpu.SemaphoreType.DMA(((kernels - EARLY) // LATE_BATCH,)),
            pltpu.SemaphoreType.DMA((len(sections),)),
            pltpu.SemaphoreType.DMA,
        ],
        compiler_params=pltpu.CompilerParams(vmem_limit_bytes=LIMIT * MIB),
        name="fields",
    )(kernel_group, kernel_weight, place, kernel_radii, mask_field, near, far, target, kernel_taps, spectra, jnp.asarray(tables))

    near_in = lax.ppermute(near_rim, "row", near_pairs)
    far_in = lax.ppermute(far_rim, "row", far_pairs)
    gradient = pl.pallas_call(
        join_body,
        out_shape=jax.ShapeDtypeStruct((2, count, width), f32),
        in_specs=[smem] + [vmem] * 3,
        out_specs=vmem,
        compiler_params=pltpu.CompilerParams(vmem_limit_bytes=4 * MIB),
        name="join",
    )(place, own, near_in, far_in)
    return resist, gradient


def solution(mesh):
    in_specs = (P(None, ("win", "row"), None), P(("win", "row"), None), P(), P(), P(), P())
    out_specs = (P(None, ("win", "row"), None), P(None, ("win", "row"), None))
    return jax.shard_map(
        on_device, mesh=mesh, in_specs=in_specs, out_specs=out_specs, check_vma=False
    )
```

```python
import functools
import math

import jax
import jax.numpy as jnp
import ml_dtypes
import numpy as np
from jax import lax
from jax.experimental import pallas as pl
from jax.experimental.pallas import tpu as pltpu
from jax.sharding import PartitionSpec as P

RMAX = 64
GROUPS = 3
STEEPNESS = 1.0
THRESHOLD = 2.0
BATCH = 12
EARLY = 4
LATE_BATCH = 10
PIECE = 256

f32 = jnp.float32
bf16 = jnp.bfloat16
MIB = 1024 * 1024
LIMIT = 53


def halves(table, axis):
    high = table.astype(ml_dtypes.bfloat16)
    low = (table - high.astype(np.float64)).astype(ml_dtypes.bfloat16)
    return np.concatenate([high, low], axis=axis)


def analysis(freqs, points, shift):
    f = np.arange(freqs)[:, None]
    n = np.arange(points)[None, :] - shift
    angle = 2.0 * math.pi * ((f * n) % freqs) / freqs
    cos, sin = np.cos(angle), np.sin(angle)
    return np.block([[cos, sin], [-sin, cos]])


def synthesis(freqs, points, shift, scale=1.0):
    return analysis(freqs, points, shift).T * scale


def class_table(freqs, points, c):
    f = np.arange(c, freqs, 4)[:, None]
    n = np.arange(points)[None, :]
    angle = 2.0 * math.pi * ((f * n) % freqs) / freqs
    cos, sin = np.cos(angle), np.sin(angle)
    return np.block([[cos, sin], [-sin, cos]])


def grouped(freqs, lanes):
    head, tail = np.arange(lanes), np.arange(lanes, freqs)
    return np.concatenate([head, freqs + head, tail, freqs + tail])


def split(x):
    high = x.astype(bf16)
    low = (x - high.astype(f32)).astype(bf16)
    return high, low


def dot(left, right):
    parts = [
        jnp.dot(left[at:at + PIECE], right, preferred_element_type=f32)
        for at in range(0, left.shape[0], PIECE)
    ]
    return jnp.concatenate(parts, axis=0)


def class_product(table, c, parts):
    depth = parts[0].shape[0]
    left = table[:, c * depth:(c + 1) * depth]
    found = dot(jnp.concatenate([left, left], axis=1), jnp.concatenate(parts, axis=0))
    half = found.shape[0] // 2
    return found[:half] + found[half:]


def turned(x, sign):
    re, im = x
    return (-im, re) if sign > 0 else (im, -re)


def plus(x, y):
    return x[0] + y[0], x[1] + y[1]


def minus(x, y):
    return x[0] - y[0], x[1] - y[1]


def to_row_freqs(x, table):
    if len(x) == 2:
        even, odd, even_less, odd_less = x[0], x[1], x[0], x[1]
    else:
        even, odd = plus(x[0], x[2]), plus(x[1], x[3])
        even_less, odd_less = minus(x[0], x[2]), minus(x[1], x[3])
    folded = [
        plus(even, odd),
        plus(even_less, turned(odd_less, -1)),
        minus(even, odd),
        plus(even_less, turned(odd_less, 1)),
    ]
    return [class_product(table, c, split(jnp.concatenate(y, axis=0))) for c, y in enumerate(folded)]


def from_row_freqs(classes, table, quarters):
    v = []
    for c, parts in enumerate(classes):
        found = class_product(table, c, parts)
        half = found.shape[0] // 2
        v.append((found[:half], found[half:]))
    out = []
    for q in quarters:
        if q % 2 == 0:
            even, odd = plus(v[0], v[2]), plus(v[1], v[3])
        else:
            even, odd = minus(v[0], v[2]), turned(minus(v[1], v[3]), 1)
        out.append(plus(even, odd) if q < 2 else minus(even, odd))
    return out


def over_lanes(parts, table):
    high, low = parts
    right = jnp.concatenate([table, table[:high.shape[1]]], axis=0)
    return dot(jnp.concatenate([high, high, low], axis=1), right)


def to_freqs(parts, head, tail):
    high, low = parts
    rows, depth = high.shape
    lanes = tail.shape[1] // 2
    right = jnp.concatenate([head, head[:depth]], axis=0)
    first = dot(jnp.concatenate([high, high, low], axis=1), right)
    rest = dot(jnp.concatenate([high, low], axis=1), jnp.concatenate([tail, tail], axis=0))
    return first, rest[:, :lanes] + rest[:, lanes:]


def beside(classes, at, width):
    tiles = []
    for found in classes:
        half = found.shape[0] // 2
        tiles.append(jnp.concatenate([found[:half, at:at + width], found[half:, at:at + width]], axis=1))
    return split(jnp.concatenate(tiles, axis=0))


def row_stage(quarters, row_fwd, width):
    classes = to_row_freqs(quarters, row_fwd)
    return [beside(classes, at, width) for at in range(0, quarters[0][0].shape[1], width)]


def quarters_of(re, im, quarter):
    return [(re[at:at + quarter], im[at:at + quarter]) for at in range(0, re.shape[0], quarter)]


def staggered(count, first, second):
    held = None
    for i in range(count):
        new = first(i)
        if i:
            second(i - 1, held)
        held = new
    second(count - 1, held)


def side_by_side(planes, c, width):
    quarter = planes[0][0].shape[0] // 4
    rows = slice(c * quarter, (c + 1) * quarter)
    return [
        jnp.concatenate([
            jnp.concatenate([plane[part][rows, at:at + width] for plane in planes], axis=1)
            for at in (0, width)
        ], axis=0)
        for part in range(2)
    ]


def swap(x):
    return pltpu.roll(x, x.shape[1] // 2, 1)


def spectra_of(radii, taps, spec, first, batch, row_fwd, head, tail):
    span = taps.shape[2]
    row_at = lax.broadcasted_iota(jnp.int32, (span, span), 0) - span // 2
    col_at = lax.broadcasted_iota(jnp.int32, (span, span), 1) - span // 2
    reach = jnp.maximum(jnp.maximum(row_at, -1 - row_at), jnp.maximum(col_at, -1 - col_at))

    def rows_of(p):
        planes = [[], []]
        for j in range(2):
            k = first + 2 * p + j
            inside = reach < radii[k]
            for c in range(2):
                planes[c].append(jnp.where(inside, taps[k, c], 0.0))
        re, im = [jnp.concatenate(plane, axis=1) for plane in planes]
        return row_stage(quarters_of(re, im, span // 2), row_fwd, span)

    def cols_of(p, tiles):
        for j in range(2):
            k = first + 2 * p + j
            a, b = to_freqs(tiles[j], head, tail)
            spec[k, :, :a.shape[1]] = a
            spec[k, :, a.shape[1]:] = b

    staggered(batch // 2, rows_of, cols_of)


def spectra_body(radii, taps_far, row_ref, head_ref, tail_ref, spec_far, taps, spec, in_sem, out_sem):
    early = spec.shape[0]
    fetch = pltpu.make_async_copy(taps_far.at[pl.ds(0, early)], taps, in_sem)
    fetch.start()
    fetch.wait()
    spectra_of(radii, taps, spec, 0, early, row_ref[...], head_ref[...], tail_ref[...])
    put = pltpu.make_async_copy(spec, spec_far, out_sem)
    put.start()
    put.wait()


def main_body(
    group, weight, place, radii,
    own, near, far, target, taps_far, spec_far, tables_far,
    resist_far, grad_own, near_rim, far_rim,
    spec, taps, field, mask_spec, resist, slopes, grad_spec, tables, spec_sem, taps_sems, table_sems, out_sem,
    *, layout, sections,
):
    kernels, grid_rows, _ = spec.shape
    count, width = target.shape
    rim = (grid_rows - count) // 2
    batch = BATCH
    steps = kernels // batch
    early = spec_far.shape[0]
    late_steps = taps_sems.shape[0]
    late = (kernels - early) // late_steps

    fetch_early = pltpu.make_async_copy(spec_far, spec.at[pl.ds(0, early)], spec_sem)

    def fetch_taps(i):
        here = pl.ds(early + i * late, late)
        return pltpu.make_async_copy(taps_far.at[here], taps.at[here], taps_sems.at[i])

    def fetch_table(i):
        here = pl.ds(sections[i][0], sections[i][1])
        return pltpu.make_async_copy(tables_far.at[here], tables.at[here], table_sems.at[i])

    def table(name):
        start, rows, blocks = layout[name]
        parts = [tables[start + b * rows:start + (b + 1) * rows] for b in range(blocks)]
        return jnp.concatenate(parts, axis=1)

    fetch_table(0).start()
    for i in range(late_steps):
        fetch_taps(i).start()
    fetch_table(1).start()
    fetch_early.start()
    slopes[...] = jnp.zeros(slopes.shape, f32)
    grad_spec[...] = jnp.zeros(grad_spec.shape, f32)
    fetch_table(0).wait()
    row_fwd, head, tail = table("row_fwd"), table("head"), table("tail")

    def spectra(i, carry):
        fetch_taps(i).wait()
        spectra_of(radii, taps, spec, early + i * late, late, row_fwd, head, tail)
        return carry

    lax.fori_loop(0, late_steps, spectra, 0)
    fetch_table(1).wait()
    fetch_early.wait()

    odd = place[0] % 2 == 1
    above, below = [], []
    for c in range(2):
        above.append(jnp.where(odd, near[c, count - rim:], far[c, count - rim:]))
        below.append(jnp.where(odd, far[c, :rim], near[c, :rim]))
    upper, lower = quarters_of(own[0], own[1], rim)
    mask, = row_stage([lower, tuple(below), tuple(above), upper], row_fwd, width)
    m_first, m_rest = to_freqs(mask, table("mask_head"), table("mask_tail"))
    lane = lax.broadcasted_iota(jnp.int32, m_rest.shape, 1)
    real_half = lane < m_rest.shape[1] // 2
    turned = swap(m_rest)
    mask_spec[:, :2 * width] = m_first
    mask_spec[:, 2 * width:3 * width] = jnp.where(real_half, m_rest, turned)
    mask_spec[:, 3 * width:] = jnp.where(real_half, -turned, m_rest)

    col_inv, row_inv = table("col_inv"), table("row_inv")

    def forward(i, carry):
        m_re, m_im = mask_spec[:, :width], mask_spec[:, width:2 * width]
        m_same, m_cross = mask_spec[:, 2 * width:3 * width], mask_spec[:, 3 * width:]

        def cols_of(p):
            planes = []
            for j in range(2):
                k = i * batch + 2 * p + j
                s_re, s_im, s_rest = spec[k, :, :width], spec[k, :, width:2 * width], spec[k, :, 2 * width:]
                product = jnp.concatenate([
                    s_re * m_re - s_im * m_im,
                    s_re * m_im + s_im * m_re,
                    s_rest * m_same + swap(s_rest) * m_cross,
                ], axis=1)
                back = over_lanes(split(product), col_inv)
                planes.append(split(back))
            return [side_by_side(planes, c, width) for c in range(4)]

        def rows_of(p, pair):
            upper, lower = from_row_freqs(pair, row_inv, (0, 1))
            re = jnp.concatenate([upper[0], lower[0]], axis=0)
            im = jnp.concatenate([upper[1], lower[1]], axis=0)
            field[i * (batch // 2) + p, :count] = re
            field[i * (batch // 2) + p, count:] = im
            power = re * re + im * im
            for j in range(2):
                k = i * batch + 2 * p + j
                g = group[k]
                slopes[g] = slopes[g] + weight[k] * power[:, j * width:(j + 1) * width]

        staggered(batch // 2, cols_of, rows_of)
        return carry

    lax.fori_loop(0, steps, forward, 0)

    wanted = target[...].astype(f32)
    for g in range(GROUPS):
        seen = jax.nn.sigmoid(STEEPNESS * (slopes[g] - THRESHOLD))
        resist[g] = seen
        slopes[g] = 2.0 * (seen - wanted) * seen * (1.0 - seen) * STEEPNESS
    out = pltpu.make_async_copy(resist, resist_far, out_sem)
    out.start()

    def backward(i, carry):
        def rows_of(p):
            factors = []
            for j in range(2):
                k = i * batch + 2 * p + j
                factors.append((2.0 * weight[k]) * slopes[group[k]])
            factor = jnp.concatenate(factors, axis=1)
            re = field[i * (batch // 2) + p, :count] * factor
            im = field[i * (batch // 2) + p, count:] * factor
            return row_stage(quarters_of(re, im, rim), row_fwd, width)

        def cols_of(p, tiles):
            total = [grad_spec[:, c * width:(c + 1) * width] for c in range(4)]
            for j in range(2):
                k = i * batch + 2 * p + j
                s_re, s_im, s_rest = spec[k, :, :width], spec[k, :, width:2 * width], spec[k, :, 2 * width:]
                first, rest = to_freqs(tiles[j], head, tail)
                c_re, c_im = first[:, :width], first[:, width:]
                total[0] = total[0] + (s_re * c_re + s_im * c_im)
                total[1] = total[1] + (s_re * c_im - s_im * c_re)
                total[2] = total[2] + s_rest * rest
                total[3] = total[3] + s_rest * swap(rest)
            for c in range(4):
                grad_spec[:, c * width:(c + 1) * width] = total[c]

        staggered(batch // 2, rows_of, cols_of)
        return carry

    lax.fori_loop(0, steps, backward, 0)

    same, cross = grad_spec[:, 2 * width:3 * width], grad_spec[:, 3 * width:]
    tail_sum = jnp.where(real_half, same + swap(same), swap(cross) - cross)
    total = jnp.concatenate([grad_spec[:, :2 * width], tail_sum], axis=1)
    back = split(over_lanes(split(total), table("grad_col")))
    classes = [side_by_side([back], c, width) for c in range(4)]
    rise, upper, lower, fall = from_row_freqs(classes, row_inv, (2, 3, 0, 1))
    for c in range(2):
        near_rim[c] = jnp.where(odd, rise[c], fall[c])
        far_rim[c] = jnp.where(odd, fall[c], rise[c])
        grad_own[c, :rim] = upper[c]
        grad_own[c, rim:] = lower[c]
    out.wait()


def join_body(place, own, near, far, out):
    odd = place[0] % 2 == 1
    rim = near.shape[1]
    count = own.shape[1]
    for c in range(2):
        out[c, :rim] = own[c, :rim] + jnp.where(odd, near[c], far[c])
        if count > 2 * rim:
            out[c, rim:count - rim] = own[c, rim:count - rim]
        out[c, count - rim:] = own[c, count - rim:] + jnp.where(odd, far[c], near[c])


def stacked(groups):
    blocks, layout, sections, at = [], {}, [], 0
    for group in groups:
        start = at
        for name, table in group.items():
            rows, lanes = table.shape
            layout[name] = (at, rows, lanes // 256)
            for b in range(lanes // 256):
                blocks.append(table[:, b * 256:(b + 1) * 256])
            at += rows * (lanes // 256)
        sections.append((start, at - start))
    return np.concatenate(blocks, axis=0), layout, sections


def on_device(mask_field, target, kernel_taps, kernel_radii, kernel_group, kernel_weight):
    _, count, width = mask_field.shape
    kernels, _, span, _ = kernel_taps.shape
    rim = span // 2
    grid_rows = count + 2 * rim
    grid_cols = width + rim
    assert count == span and width == span and kernels % BATCH == 0 and (kernels - EARLY) % LATE_BATCH == 0 and count == 2 * rim

    strips = lax.axis_size("row")
    assert strips % 2 == 0
    at = lax.axis_index("row")
    near_pairs = [(i, i ^ 1) for i in range(strips)]
    far_pairs = [(i, ((i + 1) ^ 1) - 1) for i in range(1, strips - 1)]
    near = lax.ppermute(mask_field, "row", near_pairs)
    far = lax.ppermute(mask_field, "row", far_pairs)
    place = at.astype(jnp.int32).reshape(1)

    scale = 1.0 / (grid_rows * grid_cols)
    order = grouped(grid_cols, width)

    def head_and_tail(shift):
        table = analysis(grid_cols, width, shift).T[:, order]
        return halves(table[:, :2 * width], 0), halves(table[:, 2 * width:], 1)

    quarter = grid_rows // 4
    by_class = [class_table(grid_rows, quarter, c) for c in range(4)]
    row_fwd = np.concatenate([halves(t, 0) for t in by_class], axis=1)
    row_inv = np.concatenate([halves(t.T * scale, 0) for t in by_class], axis=1)
    head, tail = head_and_tail(0)
    mask_head, mask_tail = head_and_tail(rim)
    col_inv = halves(synthesis(grid_cols, width, 0).T[order], 0)
    grad_col = halves(synthesis(grid_cols, width, rim).T[order], 0)

    smem = pl.BlockSpec(memory_space=pltpu.SMEM)
    vmem = pl.BlockSpec(memory_space=pltpu.VMEM)
    hbm = pl.BlockSpec(memory_space=pltpu.HBM)
    spectra = pl.pallas_call(
        spectra_body,
        out_shape=jax.ShapeDtypeStruct((EARLY, grid_rows, 2 * grid_cols), f32),
        in_specs=[smem, hbm, vmem, vmem, vmem],
        out_specs=hbm,
        scratch_shapes=[
            pltpu.VMEM((EARLY,) + kernel_taps.shape[1:], f32),
            pltpu.VMEM((EARLY, grid_rows, 2 * grid_cols), f32),
            pltpu.SemaphoreType.DMA,
            pltpu.SemaphoreType.DMA,
        ],
        compiler_params=pltpu.CompilerParams(vmem_limit_bytes=56 * MIB),
        cost_estimate=pl.CostEstimate(flops=3 * 10**9, bytes_accessed=3 * 10**6, transcendentals=0),
        name="spectra",
    )(kernel_radii, kernel_taps, *map(jnp.asarray, (row_fwd, head, tail)))

    tables, layout, sections = stacked([
        {"row_fwd": row_fwd, "head": head, "tail": tail},
        {"mask_head": mask_head, "mask_tail": mask_tail, "col_inv": col_inv, "row_inv": row_inv, "grad_col": grad_col},
    ])
    resist, own, near_rim, far_rim = pl.pallas_call(
        functools.partial(main_body, layout=layout, sections=sections),
        out_shape=[
            jax.ShapeDtypeStruct((GROUPS, count, width), f32),
            jax.ShapeDtypeStruct((2, count, width), f32),
            jax.ShapeDtypeStruct((2, rim, width), f32),
            jax.ShapeDtypeStruct((2, rim, width), f32),
        ],
        in_specs=[smem] * 4 + [vmem] * 4 + [hbm] * 3,
        out_specs=[hbm] + [vmem] * 3,
        scratch_shapes=[
            pltpu.VMEM((kernels, grid_rows, 2 * grid_cols), f32),
            pltpu.VMEM(kernel_taps.shape, f32),
            pltpu.VMEM((kernels // 2, 2 * count, 2 * width), f32),
            pltpu.VMEM((grid_rows, 4 * width), f32),
            pltpu.VMEM((GROUPS, count, width), f32),
            pltpu.VMEM((GROUPS, count, width), f32),
            pltpu.VMEM((grid_rows, 4 * width), f32),
            pltpu.VMEM(tables.shape, bf16),
            pltpu.SemaphoreType.DMA,
            pltpu.SemaphoreType.DMA(((kernels - EARLY) // LATE_BATCH,)),
            pltpu.SemaphoreType.DMA((len(sections),)),
            pltpu.SemaphoreType.DMA,
        ],
        compiler_params=pltpu.CompilerParams(vmem_limit_bytes=LIMIT * MIB),
        name="fields",
    )(kernel_group, kernel_weight, place, kernel_radii, mask_field, near, far, target, kernel_taps, spectra, jnp.asarray(tables))

    near_in = lax.ppermute(near_rim, "row", near_pairs)
    far_in = lax.ppermute(far_rim, "row", far_pairs)
    gradient = pl.pallas_call(
        join_body,
        out_shape=jax.ShapeDtypeStruct((2, count, width), f32),
        in_specs=[smem] + [vmem] * 3,
        out_specs=vmem,
        compiler_params=pltpu.CompilerParams(vmem_limit_bytes=4 * MIB),
        name="join",
    )(place, own, near_in, far_in)
    return resist, gradient


def solution(mesh):
    in_specs = (P(None, ("win", "row"), None), P(("win", "row"), None), P(), P(), P(), P())
    out_specs = (P(None, ("win", "row"), None), P(None, ("win", "row"), None))
    return jax.shard_map(
        on_device, mesh=mesh, in_specs=in_specs, out_specs=out_specs, check_vma=False
    )
```

```python
import functools
import math

import jax
import jax.numpy as jnp
import ml_dtypes
import numpy as np
from jax import lax
from jax.experimental import pallas as pl
from jax.experimental.pallas import tpu as pltpu
from jax.sharding import PartitionSpec as P

RMAX = 64
GROUPS = 3
STEEPNESS = 1.0
THRESHOLD = 2.0
BATCH = 12
EARLY = 4
LATE_BATCH = 10
PIECE = 256

f32 = jnp.float32
bf16 = jnp.bfloat16
MIB = 1024 * 1024
LIMIT = 53


def halves(table, axis):
    high = table.astype(ml_dtypes.bfloat16)
    low = (table - high.astype(np.float64)).astype(ml_dtypes.bfloat16)
    return np.concatenate([high, low], axis=axis)


def analysis(freqs, points, shift):
    f = np.arange(freqs)[:, None]
    n = np.arange(points)[None, :] - shift
    angle = 2.0 * math.pi * ((f * n) % freqs) / freqs
    cos, sin = np.cos(angle), np.sin(angle)
    return np.block([[cos, sin], [-sin, cos]])


def synthesis(freqs, points, shift, scale=1.0):
    return analysis(freqs, points, shift).T * scale


def class_table(freqs, points, c):
    f = np.arange(c, freqs, 4)[:, None]
    n = np.arange(points)[None, :]
    angle = 2.0 * math.pi * ((f * n) % freqs) / freqs
    cos, sin = np.cos(angle), np.sin(angle)
    return np.block([[cos, sin], [-sin, cos]])


def grouped(freqs, lanes):
    head, tail = np.arange(lanes), np.arange(lanes, freqs)
    return np.concatenate([head, freqs + head, tail, freqs + tail])


def split(x):
    high = x.astype(bf16)
    low = (x - high.astype(f32)).astype(bf16)
    return high, low


def dot(left, right):
    parts = [
        jnp.dot(left[at:at + PIECE], right, preferred_element_type=f32)
        for at in range(0, left.shape[0], PIECE)
    ]
    return jnp.concatenate(parts, axis=0)


def class_product(table, c, parts):
    depth = parts[0].shape[0]
    left = table[:, c * depth:(c + 1) * depth]
    found = dot(jnp.concatenate([left, left], axis=1), jnp.concatenate(parts, axis=0))
    half = found.shape[0] // 2
    return found[:half] + found[half:]


def turned(x, sign):
    re, im = x
    return (-im, re) if sign > 0 else (im, -re)


def plus(x, y):
    return x[0] + y[0], x[1] + y[1]


def minus(x, y):
    return x[0] - y[0], x[1] - y[1]


def to_row_freqs(x, table):
    if len(x) == 2:
        even, odd, even_less, odd_less = x[0], x[1], x[0], x[1]
    else:
        even, odd = plus(x[0], x[2]), plus(x[1], x[3])
        even_less, odd_less = minus(x[0], x[2]), minus(x[1], x[3])
    folded = [
        plus(even, odd),
        plus(even_less, turned(odd_less, -1)),
        minus(even, odd),
        plus(even_less, turned(odd_less, 1)),
    ]
    return [class_product(table, c, split(jnp.concatenate(y, axis=0))) for c, y in enumerate(folded)]


def from_row_freqs(classes, table, quarters):
    v = []
    for c, parts in enumerate(classes):
        found = class_product(table, c, parts)
        half = found.shape[0] // 2
        v.append((found[:half], found[half:]))
    out = []
    for q in quarters:
        if q % 2 == 0:
            even, odd = plus(v[0], v[2]), plus(v[1], v[3])
        else:
            even, odd = minus(v[0], v[2]), turned(minus(v[1], v[3]), 1)
        out.append(plus(even, odd) if q < 2 else minus(even, odd))
    return out


def over_lanes(parts, table):
    high, low = parts
    right = jnp.concatenate([table, table[:high.shape[1]]], axis=0)
    return dot(jnp.concatenate([high, high, low], axis=1), right)


def to_freqs(parts, head, tail):
    high, low = parts
    rows, depth = high.shape
    lanes = tail.shape[1] // 2
    right = jnp.concatenate([head, head[:depth]], axis=0)
    first = dot(jnp.concatenate([high, high, low], axis=1), right)
    rest = dot(jnp.concatenate([high, low], axis=1), jnp.concatenate([tail, tail], axis=0))
    return first, rest[:, :lanes] + rest[:, lanes:]


def beside(classes, at, width):
    tiles = []
    for found in classes:
        half = found.shape[0] // 2
        tiles.append(jnp.concatenate([found[:half, at:at + width], found[half:, at:at + width]], axis=1))
    return split(jnp.concatenate(tiles, axis=0))


def row_stage(quarters, row_fwd, width):
    classes = to_row_freqs(quarters, row_fwd)
    return [beside(classes, at, width) for at in range(0, quarters[0][0].shape[1], width)]


def quarters_of(re, im, quarter):
    return [(re[at:at + quarter], im[at:at + quarter]) for at in range(0, re.shape[0], quarter)]


def staggered(count, first, second):
    held = None
    for i in range(count):
        new = first(i)
        if i:
            second(i - 1, held)
        held = new
    second(count - 1, held)


def side_by_side(planes, c, width):
    quarter = planes[0][0].shape[0] // 4
    rows = slice(c * quarter, (c + 1) * quarter)
    return [
        jnp.concatenate([
            jnp.concatenate([plane[part][rows, at:at + width] for plane in planes], axis=1)
            for at in (0, width)
        ], axis=0)
        for part in range(2)
    ]


def swap(x):
    return pltpu.roll(x, x.shape[1] // 2, 1)


def spectra_of(radii, taps, spec, first, batch, row_fwd, head, tail):
    span = taps.shape[2]
    row_at = lax.broadcasted_iota(jnp.int32, (span, span), 0) - span // 2
    col_at = lax.broadcasted_iota(jnp.int32, (span, span), 1) - span // 2
    reach = jnp.maximum(jnp.maximum(row_at, -1 - row_at), jnp.maximum(col_at, -1 - col_at))

    def rows_of(p):
        planes = [[], []]
        for j in range(2):
            k = first + 2 * p + j
            inside = reach < radii[k]
            for c in range(2):
                planes[c].append(jnp.where(inside, taps[k, c], 0.0))
        re, im = [jnp.concatenate(plane, axis=1) for plane in planes]
        return row_stage(quarters_of(re, im, span // 2), row_fwd, span)

    def cols_of(p, tiles):
        for j in range(2):
            k = first + 2 * p + j
            a, b = to_freqs(tiles[j], head, tail)
            spec[k, :, :a.shape[1]] = a
            spec[k, :, a.shape[1]:] = b

    staggered(batch // 2, rows_of, cols_of)


def spectra_body(radii, taps, row_ref, head_ref, tail_ref, spec):
    spectra_of(radii, taps, spec, 0, spec.shape[0], row_ref[...], head_ref[...], tail_ref[...])


def main_body(
    group, weight, place, radii,
    own, near, far, target, row_ref, head_ref, tail_ref, taps_far, spec_far, tables_far,
    resist_far, grad_own, near_rim, far_rim,
    spec, taps, field, mask_spec, resist, slopes, grad_spec, tables, spec_sem, taps_sems, table_sems, out_sem,
    *, layout, sections,
):
    kernels, grid_rows, _ = spec.shape
    count, width = target.shape
    rim = (grid_rows - count) // 2
    batch = BATCH
    steps = kernels // batch
    early = spec_far.shape[0]
    late_steps = taps_sems.shape[0]
    late = (kernels - early) // late_steps

    fetch_early = pltpu.make_async_copy(spec_far, spec.at[pl.ds(0, early)], spec_sem)

    def fetch_taps(i):
        here = pl.ds(early + i * late, late)
        return pltpu.make_async_copy(taps_far.at[here], taps.at[here], taps_sems.at[i])

    def fetch_table(i):
        here = pl.ds(sections[i][0], sections[i][1])
        return pltpu.make_async_copy(tables_far.at[here], tables.at[here], table_sems.at[i])

    def table(name):
        start, rows, blocks = layout[name]
        parts = [tables[start + b * rows:start + (b + 1) * rows] for b in range(blocks)]
        return jnp.concatenate(parts, axis=1)

    for i in range(late_steps):
        fetch_taps(i).start()
    fetch_table(0).start()
    fetch_early.start()
    slopes[...] = jnp.zeros(slopes.shape, f32)
    grad_spec[...] = jnp.zeros(grad_spec.shape, f32)
    row_fwd, head, tail = row_ref[...], head_ref[...], tail_ref[...]

    def spectra(i, carry):
        fetch_taps(i).wait()
        spectra_of(radii, taps, spec, early + i * late, late, row_fwd, head, tail)
        return carry

    lax.fori_loop(0, late_steps, spectra, 0)
    fetch_table(0).wait()
    fetch_early.wait()

    odd = place[0] % 2 == 1
    above, below = [], []
    for c in range(2):
        above.append(jnp.where(odd, near[c, count - rim:], far[c, count - rim:]))
        below.append(jnp.where(odd, far[c, :rim], near[c, :rim]))
    upper, lower = quarters_of(own[0], own[1], rim)
    mask, = row_stage([lower, tuple(below), tuple(above), upper], row_fwd, width)
    m_first, m_rest = to_freqs(mask, table("mask_head"), table("mask_tail"))
    lane = lax.broadcasted_iota(jnp.int32, m_rest.shape, 1)
    real_half = lane < m_rest.shape[1] // 2
    turned = swap(m_rest)
    mask_spec[:, :2 * width] = m_first
    mask_spec[:, 2 * width:3 * width] = jnp.where(real_half, m_rest, turned)
    mask_spec[:, 3 * width:] = jnp.where(real_half, -turned, m_rest)

    col_inv, row_inv = table("col_inv"), table("row_inv")

    def forward(i, carry):
        m_re, m_im = mask_spec[:, :width], mask_spec[:, width:2 * width]
        m_same, m_cross = mask_spec[:, 2 * width:3 * width], mask_spec[:, 3 * width:]

        def cols_of(p):
            planes = []
            for j in range(2):
                k = i * batch + 2 * p + j
                s_re, s_im, s_rest = spec[k, :, :width], spec[k, :, width:2 * width], spec[k, :, 2 * width:]
                product = jnp.concatenate([
                    s_re * m_re - s_im * m_im,
                    s_re * m_im + s_im * m_re,
                    s_rest * m_same + swap(s_rest) * m_cross,
                ], axis=1)
                back = over_lanes(split(product), col_inv)
                planes.append(split(back))
            return [side_by_side(planes, c, width) for c in range(4)]

        def rows_of(p, pair):
            upper, lower = from_row_freqs(pair, row_inv, (0, 1))
            re = jnp.concatenate([upper[0], lower[0]], axis=0)
            im = jnp.concatenate([upper[1], lower[1]], axis=0)
            field[i * (batch // 2) + p, :count] = re
            field[i * (batch // 2) + p, count:] = im
            power = re * re + im * im
            for j in range(2):
                k = i * batch + 2 * p + j
                g = group[k]
                slopes[g] = slopes[g] + weight[k] * power[:, j * width:(j + 1) * width]

        staggered(batch // 2, cols_of, rows_of)
        return carry

    lax.fori_loop(0, steps, forward, 0)

    wanted = target[...].astype(f32)
    for g in range(GROUPS):
        seen = jax.nn.sigmoid(STEEPNESS * (slopes[g] - THRESHOLD))
        resist[g] = seen
        slopes[g] = 2.0 * (seen - wanted) * seen * (1.0 - seen) * STEEPNESS
    out = pltpu.make_async_copy(resist, resist_far, out_sem)
    out.start()

    def backward(i, carry):
        def rows_of(p):
            factors = []
            for j in range(2):
                k = i * batch + 2 * p + j
                factors.append((2.0 * weight[k]) * slopes[group[k]])
            factor = jnp.concatenate(factors, axis=1)
            re = field[i * (batch // 2) + p, :count] * factor
            im = field[i * (batch // 2) + p, count:] * factor
            return row_stage(quarters_of(re, im, rim), row_fwd, width)

        def cols_of(p, tiles):
            total = [grad_spec[:, c * width:(c + 1) * width] for c in range(4)]
            for j in range(2):
                k = i * batch + 2 * p + j
                s_re, s_im, s_rest = spec[k, :, :width], spec[k, :, width:2 * width], spec[k, :, 2 * width:]
                first, rest = to_freqs(tiles[j], head, tail)
                c_re, c_im = first[:, :width], first[:, width:]
                total[0] = total[0] + (s_re * c_re + s_im * c_im)
                total[1] = total[1] + (s_re * c_im - s_im * c_re)
                total[2] = total[2] + s_rest * rest
                total[3] = total[3] + s_rest * swap(rest)
            for c in range(4):
                grad_spec[:, c * width:(c + 1) * width] = total[c]

        staggered(batch // 2, rows_of, cols_of)
        return carry

    lax.fori_loop(0, steps, backward, 0)

    same, cross = grad_spec[:, 2 * width:3 * width], grad_spec[:, 3 * width:]
    tail_sum = jnp.where(real_half, same + swap(same), swap(cross) - cross)
    total = jnp.concatenate([grad_spec[:, :2 * width], tail_sum], axis=1)
    back = split(over_lanes(split(total), table("grad_col")))
    classes = [side_by_side([back], c, width) for c in range(4)]
    rise, upper, lower, fall = from_row_freqs(classes, row_inv, (2, 3, 0, 1))
    for c in range(2):
        near_rim[c] = jnp.where(odd, rise[c], fall[c])
        far_rim[c] = jnp.where(odd, fall[c], rise[c])
        grad_own[c, :rim] = upper[c]
        grad_own[c, rim:] = lower[c]
    out.wait()


def join_body(place, own, near, far, out):
    odd = place[0] % 2 == 1
    rim = near.shape[1]
    count = own.shape[1]
    for c in range(2):
        out[c, :rim] = own[c, :rim] + jnp.where(odd, near[c], far[c])
        if count > 2 * rim:
            out[c, rim:count - rim] = own[c, rim:count - rim]
        out[c, count - rim:] = own[c, count - rim:] + jnp.where(odd, far[c], near[c])


def stacked(groups):
    blocks, layout, sections, at = [], {}, [], 0
    for group in groups:
        start = at
        for name, table in group.items():
            rows, lanes = table.shape
            layout[name] = (at, rows, lanes // 256)
            for b in range(lanes // 256):
                blocks.append(table[:, b * 256:(b + 1) * 256])
            at += rows * (lanes // 256)
        sections.append((start, at - start))
    return np.concatenate(blocks, axis=0), layout, sections


def on_device(mask_field, target, kernel_taps, kernel_radii, kernel_group, kernel_weight):
    _, count, width = mask_field.shape
    kernels, _, span, _ = kernel_taps.shape
    rim = span // 2
    grid_rows = count + 2 * rim
    grid_cols = width + rim
    assert count == span and width == span and kernels % BATCH == 0 and (kernels - EARLY) % LATE_BATCH == 0 and count == 2 * rim

    strips = lax.axis_size("row")
    assert strips % 2 == 0
    at = lax.axis_index("row")
    near_pairs = [(i, i ^ 1) for i in range(strips)]
    far_pairs = [(i, ((i + 1) ^ 1) - 1) for i in range(1, strips - 1)]
    near = lax.ppermute(mask_field, "row", near_pairs)
    far = lax.ppermute(mask_field, "row", far_pairs)
    place = at.astype(jnp.int32).reshape(1)

    scale = 1.0 / (grid_rows * grid_cols)
    order = grouped(grid_cols, width)

    def head_and_tail(shift):
        table = analysis(grid_cols, width, shift).T[:, order]
        return halves(table[:, :2 * width], 0), halves(table[:, 2 * width:], 1)

    quarter = grid_rows // 4
    by_class = [class_table(grid_rows, quarter, c) for c in range(4)]
    row_fwd = np.concatenate([halves(t, 0) for t in by_class], axis=1)
    row_inv = np.concatenate([halves(t.T * scale, 0) for t in by_class], axis=1)
    head, tail = head_and_tail(0)
    mask_head, mask_tail = head_and_tail(rim)
    col_inv = halves(synthesis(grid_cols, width, 0).T[order], 0)
    grad_col = halves(synthesis(grid_cols, width, rim).T[order], 0)

    smem = pl.BlockSpec(memory_space=pltpu.SMEM)
    vmem = pl.BlockSpec(memory_space=pltpu.VMEM)
    hbm = pl.BlockSpec(memory_space=pltpu.HBM)
    early_tables = [jnp.asarray(t) for t in (row_fwd, head, tail)]
    spectra = pl.pallas_call(
        spectra_body,
        out_shape=jax.ShapeDtypeStruct((EARLY, grid_rows, 2 * grid_cols), f32),
        grid=(1,),
        in_specs=[smem, pl.BlockSpec((EARLY, 2, span, span), lambda i: (0, 0, 0, 0)), vmem, vmem, vmem],
        out_specs=pl.BlockSpec((EARLY, grid_rows, 2 * grid_cols), lambda i: (0, 0, 0)),
        compiler_params=pltpu.CompilerParams(vmem_limit_bytes=56 * MIB),
        cost_estimate=pl.CostEstimate(flops=3 * 10**9, bytes_accessed=3 * 10**6, transcendentals=0),
        name="spectra",
    )(kernel_radii, kernel_taps, *early_tables)

    tables, layout, sections = stacked([
        {"mask_head": mask_head, "mask_tail": mask_tail, "col_inv": col_inv, "row_inv": row_inv, "grad_col": grad_col},
    ])
    resist, own, near_rim, far_rim = pl.pallas_call(
        functools.partial(main_body, layout=layout, sections=sections),
        out_shape=[
            jax.ShapeDtypeStruct((GROUPS, count, width), f32),
            jax.ShapeDtypeStruct((2, count, width), f32),
            jax.ShapeDtypeStruct((2, rim, width), f32),
            jax.ShapeDtypeStruct((2, rim, width), f32),
        ],
        in_specs=[smem] * 4 + [vmem] * 7 + [hbm] * 3,
        out_specs=[hbm] + [vmem] * 3,
        scratch_shapes=[
            pltpu.VMEM((kernels, grid_rows, 2 * grid_cols), f32),
            pltpu.VMEM(kernel_taps.shape, f32),
            pltpu.VMEM((kernels // 2, 2 * count, 2 * width), f32),
            pltpu.VMEM((grid_rows, 4 * width), f32),
            pltpu.VMEM((GROUPS, count, width), f32),
            pltpu.VMEM((GROUPS, count, width), f32),
            pltpu.VMEM((grid_rows, 4 * width), f32),
            pltpu.VMEM(tables.shape, bf16),
            pltpu.SemaphoreType.DMA,
            pltpu.SemaphoreType.DMA(((kernels - EARLY) // LATE_BATCH,)),
            pltpu.SemaphoreType.DMA((len(sections),)),
            pltpu.SemaphoreType.DMA,
        ],
        compiler_params=pltpu.CompilerParams(vmem_limit_bytes=LIMIT * MIB),
        name="fields",
    )(kernel_group, kernel_weight, place, kernel_radii, mask_field, near, far, target, *early_tables, kernel_taps, spectra, jnp.asarray(tables))

    near_in = lax.ppermute(near_rim, "row", near_pairs)
    far_in = lax.ppermute(far_rim, "row", far_pairs)
    gradient = pl.pallas_call(
        join_body,
        out_shape=jax.ShapeDtypeStruct((2, count, width), f32),
        in_specs=[smem] + [vmem] * 3,
        out_specs=vmem,
        compiler_params=pltpu.CompilerParams(vmem_limit_bytes=4 * MIB),
        name="join",
    )(place, own, near_in, far_in)
    return resist, gradient


def solution(mesh):
    in_specs = (P(None, ("win", "row"), None), P(("win", "row"), None), P(), P(), P(), P())
    out_specs = (P(None, ("win", "row"), None), P(None, ("win", "row"), None))
    return jax.shard_map(
        on_device, mesh=mesh, in_specs=in_specs, out_specs=out_specs, check_vma=False
    )
```

```python
import functools
import math

import jax
import jax.numpy as jnp
import ml_dtypes
import numpy as np
from jax import lax
from jax.experimental import pallas as pl
from jax.experimental.pallas import tpu as pltpu
from jax.sharding import PartitionSpec as P

RMAX = 64
GROUPS = 3
STEEPNESS = 1.0
THRESHOLD = 2.0
BATCH = 12
EARLY = 8
LATE_BATCH = 8
PIECE = 256

f32 = jnp.float32
bf16 = jnp.bfloat16
MIB = 1024 * 1024
LIMIT = 53


def halves(table, axis):
    high = table.astype(ml_dtypes.bfloat16)
    low = (table - high.astype(np.float64)).astype(ml_dtypes.bfloat16)
    return np.concatenate([high, low], axis=axis)


def analysis(freqs, points, shift):
    f = np.arange(freqs)[:, None]
    n = np.arange(points)[None, :] - shift
    angle = 2.0 * math.pi * ((f * n) % freqs) / freqs
    cos, sin = np.cos(angle), np.sin(angle)
    return np.block([[cos, sin], [-sin, cos]])


def synthesis(freqs, points, shift, scale=1.0):
    return analysis(freqs, points, shift).T * scale


def class_table(freqs, points, c):
    f = np.arange(c, freqs, 4)[:, None]
    n = np.arange(points)[None, :]
    angle = 2.0 * math.pi * ((f * n) % freqs) / freqs
    cos, sin = np.cos(angle), np.sin(angle)
    return np.block([[cos, sin], [-sin, cos]])


def grouped(freqs, lanes):
    head, tail = np.arange(lanes), np.arange(lanes, freqs)
    return np.concatenate([head, freqs + head, tail, freqs + tail])


def split(x):
    high = x.astype(bf16)
    low = (x - high.astype(f32)).astype(bf16)
    return high, low


def dot(left, right):
    parts = [
        jnp.dot(left[at:at + PIECE], right, preferred_element_type=f32)
        for at in range(0, left.shape[0], PIECE)
    ]
    return jnp.concatenate(parts, axis=0)


def class_product(table, c, parts):
    depth = parts[0].shape[0]
    left = table[:, c * depth:(c + 1) * depth]
    found = dot(jnp.concatenate([left, left], axis=1), jnp.concatenate(parts, axis=0))
    half = found.shape[0] // 2
    return found[:half] + found[half:]


def turned(x, sign):
    re, im = x
    return (-im, re) if sign > 0 else (im, -re)


def plus(x, y):
    return x[0] + y[0], x[1] + y[1]


def minus(x, y):
    return x[0] - y[0], x[1] - y[1]


def to_row_freqs(x, table):
    if len(x) == 2:
        even, odd, even_less, odd_less = x[0], x[1], x[0], x[1]
    else:
        even, odd = plus(x[0], x[2]), plus(x[1], x[3])
        even_less, odd_less = minus(x[0], x[2]), minus(x[1], x[3])
    folded = [
        plus(even, odd),
        plus(even_less, turned(odd_less, -1)),
        minus(even, odd),
        plus(even_less, turned(odd_less, 1)),
    ]
    return [class_product(table, c, split(jnp.concatenate(y, axis=0))) for c, y in enumerate(folded)]


def from_row_freqs(classes, table, quarters):
    v = []
    for c, parts in enumerate(classes):
        found = class_product(table, c, parts)
        half = found.shape[0] // 2
        v.append((found[:half], found[half:]))
    out = []
    for q in quarters:
        if q % 2 == 0:
            even, odd = plus(v[0], v[2]), plus(v[1], v[3])
        else:
            even, odd = minus(v[0], v[2]), turned(minus(v[1], v[3]), 1)
        out.append(plus(even, odd) if q < 2 else minus(even, odd))
    return out


def over_lanes(parts, table):
    high, low = parts
    right = jnp.concatenate([table, table[:high.shape[1]]], axis=0)
    return dot(jnp.concatenate([high, high, low], axis=1), right)


def to_freqs(parts, head, tail):
    high, low = parts
    rows, depth = high.shape
    lanes = tail.shape[1] // 2
    right = jnp.concatenate([head, head[:depth]], axis=0)
    first = dot(jnp.concatenate([high, high, low], axis=1), right)
    rest = dot(jnp.concatenate([high, low], axis=1), jnp.concatenate([tail, tail], axis=0))
    return first, rest[:, :lanes] + rest[:, lanes:]


def beside(classes, at, width):
    tiles = []
    for found in classes:
        half = found.shape[0] // 2
        tiles.append(jnp.concatenate([found[:half, at:at + width], found[half:, at:at + width]], axis=1))
    return split(jnp.concatenate(tiles, axis=0))


def row_stage(quarters, row_fwd, width):
    classes = to_row_freqs(quarters, row_fwd)
    return [beside(classes, at, width) for at in range(0, quarters[0][0].shape[1], width)]


def quarters_of(re, im, quarter):
    return [(re[at:at + quarter], im[at:at + quarter]) for at in range(0, re.shape[0], quarter)]


def staggered(count, first, second):
    held = None
    for i in range(count):
        new = first(i)
        if i:
            second(i - 1, held)
        held = new
    second(count - 1, held)


def side_by_side(planes, c, width):
    quarter = planes[0][0].shape[0] // 4
    rows = slice(c * quarter, (c + 1) * quarter)
    return [
        jnp.concatenate([
            jnp.concatenate([plane[part][rows, at:at + width] for plane in planes], axis=1)
            for at in (0, width)
        ], axis=0)
        for part in range(2)
    ]


def swap(x):
    return pltpu.roll(x, x.shape[1] // 2, 1)


def spectra_of(radii, taps, spec, first, batch, row_fwd, head, tail):
    span = taps.shape[2]
    row_at = lax.broadcasted_iota(jnp.int32, (span, span), 0) - span // 2
    col_at = lax.broadcasted_iota(jnp.int32, (span, span), 1) - span // 2
    reach = jnp.maximum(jnp.maximum(row_at, -1 - row_at), jnp.maximum(col_at, -1 - col_at))

    def rows_of(p):
        planes = [[], []]
        for j in range(2):
            k = first + 2 * p + j
            inside = reach < radii[k]
            for c in range(2):
                planes[c].append(jnp.where(inside, taps[k, c], 0.0))
        re, im = [jnp.concatenate(plane, axis=1) for plane in planes]
        return row_stage(quarters_of(re, im, span // 2), row_fwd, span)

    def cols_of(p, tiles):
        for j in range(2):
            k = first + 2 * p + j
            a, b = to_freqs(tiles[j], head, tail)
            spec[k, :, :a.shape[1]] = a
            spec[k, :, a.shape[1]:] = b

    staggered(batch // 2, rows_of, cols_of)


def spectra_body(radii, taps, row_ref, head_ref, tail_ref, spec):
    spectra_of(radii, taps, spec, 0, spec.shape[0], row_ref[...], head_ref[...], tail_ref[...])


def main_body(
    group, weight, place, radii,
    own, near, far, target, taps_far, spec_far, tables_far,
    resist_far, grad_own, near_rim, far_rim,
    spec, taps, field, mask_spec, resist, slopes, grad_spec, tables, spec_sem, taps_sems, table_sems, out_sem,
    *, layout, sections,
):
    kernels, grid_rows, _ = spec.shape
    count, width = target.shape
    rim = (grid_rows - count) // 2
    batch = BATCH
    steps = kernels // batch
    early = spec_far.shape[0]
    late_steps = taps_sems.shape[0]
    late = (kernels - early) // late_steps

    fetch_early = pltpu.make_async_copy(spec_far, spec.at[pl.ds(0, early)], spec_sem)

    def fetch_taps(i):
        here = pl.ds(early + i * late, late)
        return pltpu.make_async_copy(taps_far.at[here], taps.at[here], taps_sems.at[i])

    def fetch_table(i):
        here = pl.ds(sections[i][0], sections[i][1])
        return pltpu.make_async_copy(tables_far.at[here], tables.at[here], table_sems.at[i])

    def table(name):
        start, rows, blocks = layout[name]
        parts = [tables[start + b * rows:start + (b + 1) * rows] for b in range(blocks)]
        return jnp.concatenate(parts, axis=1)

    fetch_table(0).start()
    for i in range(late_steps):
        fetch_taps(i).start()
    fetch_table(1).start()
    fetch_early.start()
    slopes[...] = jnp.zeros(slopes.shape, f32)
    grad_spec[...] = jnp.zeros(grad_spec.shape, f32)
    fetch_table(0).wait()
    row_fwd, head, tail = table("row_fwd"), table("head"), table("tail")

    def spectra(i, carry):
        fetch_taps(i).wait()
        spectra_of(radii, taps, spec, early + i * late, late, row_fwd, head, tail)
        return carry

    lax.fori_loop(0, late_steps, spectra, 0)
    fetch_table(1).wait()
    fetch_early.wait()

    odd = place[0] % 2 == 1
    above, below = [], []
    for c in range(2):
        above.append(jnp.where(odd, near[c, count - rim:], far[c, count - rim:]))
        below.append(jnp.where(odd, far[c, :rim], near[c, :rim]))
    upper, lower = quarters_of(own[0], own[1], rim)
    mask, = row_stage([lower, tuple(below), tuple(above), upper], row_fwd, width)
    m_first, m_rest = to_freqs(mask, table("mask_head"), table("mask_tail"))
    lane = lax.broadcasted_iota(jnp.int32, m_rest.shape, 1)
    real_half = lane < m_rest.shape[1] // 2
    turned = swap(m_rest)
    mask_spec[:, :2 * width] = m_first
    mask_spec[:, 2 * width:3 * width] = jnp.where(real_half, m_rest, turned)
    mask_spec[:, 3 * width:] = jnp.where(real_half, -turned, m_rest)

    col_inv, row_inv = table("col_inv"), table("row_inv")

    def forward(i, carry):
        m_re, m_im = mask_spec[:, :width], mask_spec[:, width:2 * width]
        m_same, m_cross = mask_spec[:, 2 * width:3 * width], mask_spec[:, 3 * width:]

        def cols_of(p):
            planes = []
            for j in range(2):
                k = i * batch + 2 * p + j
                s_re, s_im, s_rest = spec[k, :, :width], spec[k, :, width:2 * width], spec[k, :, 2 * width:]
                product = jnp.concatenate([
                    s_re * m_re - s_im * m_im,
                    s_re * m_im + s_im * m_re,
                    s_rest * m_same + swap(s_rest) * m_cross,
                ], axis=1)
                back = over_lanes(split(product), col_inv)
                planes.append(split(back))
            return [side_by_side(planes, c, width) for c in range(4)]

        def rows_of(p, pair):
            upper, lower = from_row_freqs(pair, row_inv, (0, 1))
            re = jnp.concatenate([upper[0], lower[0]], axis=0)
            im = jnp.concatenate([upper[1], lower[1]], axis=0)
            field[i * (batch // 2) + p, :count] = re
            field[i * (batch // 2) + p, count:] = im
            power = re * re + im * im
            for j in range(2):
                k = i * batch + 2 * p + j
                g = group[k]
                slopes[g] = slopes[g] + weight[k] * power[:, j * width:(j + 1) * width]

        staggered(batch // 2, cols_of, rows_of)
        return carry

    lax.fori_loop(0, steps, forward, 0)

    wanted = target[...].astype(f32)
    for g in range(GROUPS):
        seen = jax.nn.sigmoid(STEEPNESS * (slopes[g] - THRESHOLD))
        resist[g] = seen
        slopes[g] = 2.0 * (seen - wanted) * seen * (1.0 - seen) * STEEPNESS
    out = pltpu.make_async_copy(resist, resist_far, out_sem)
    out.start()

    def backward(i, carry):
        def rows_of(p):
            factors = []
            for j in range(2):
                k = i * batch + 2 * p + j
                factors.append((2.0 * weight[k]) * slopes[group[k]])
            factor = jnp.concatenate(factors, axis=1)
            re = field[i * (batch // 2) + p, :count] * factor
            im = field[i * (batch // 2) + p, count:] * factor
            return row_stage(quarters_of(re, im, rim), row_fwd, width)

        def cols_of(p, tiles):
            total = [grad_spec[:, c * width:(c + 1) * width] for c in range(4)]
            for j in range(2):
                k = i * batch + 2 * p + j
                s_re, s_im, s_rest = spec[k, :, :width], spec[k, :, width:2 * width], spec[k, :, 2 * width:]
                first, rest = to_freqs(tiles[j], head, tail)
                c_re, c_im = first[:, :width], first[:, width:]
                total[0] = total[0] + (s_re * c_re + s_im * c_im)
                total[1] = total[1] + (s_re * c_im - s_im * c_re)
                total[2] = total[2] + s_rest * rest
                total[3] = total[3] + s_rest * swap(rest)
            for c in range(4):
                grad_spec[:, c * width:(c + 1) * width] = total[c]

        staggered(batch // 2, rows_of, cols_of)
        return carry

    lax.fori_loop(0, steps, backward, 0)

    same, cross = grad_spec[:, 2 * width:3 * width], grad_spec[:, 3 * width:]
    tail_sum = jnp.where(real_half, same + swap(same), swap(cross) - cross)
    total = jnp.concatenate([grad_spec[:, :2 * width], tail_sum], axis=1)
    back = split(over_lanes(split(total), table("grad_col")))
    classes = [side_by_side([back], c, width) for c in range(4)]
    rise, upper, lower, fall = from_row_freqs(classes, row_inv, (2, 3, 0, 1))
    for c in range(2):
        near_rim[c] = jnp.where(odd, rise[c], fall[c])
        far_rim[c] = jnp.where(odd, fall[c], rise[c])
        grad_own[c, :rim] = upper[c]
        grad_own[c, rim:] = lower[c]
    out.wait()


def join_body(place, own, near, far, out):
    odd = place[0] % 2 == 1
    rim = near.shape[1]
    count = own.shape[1]
    for c in range(2):
        out[c, :rim] = own[c, :rim] + jnp.where(odd, near[c], far[c])
        if count > 2 * rim:
            out[c, rim:count - rim] = own[c, rim:count - rim]
        out[c, count - rim:] = own[c, count - rim:] + jnp.where(odd, far[c], near[c])


def stacked(groups):
    blocks, layout, sections, at = [], {}, [], 0
    for group in groups:
        start = at
        for name, table in group.items():
            rows, lanes = table.shape
            layout[name] = (at, rows, lanes // 256)
            for b in range(lanes // 256):
                blocks.append(table[:, b * 256:(b + 1) * 256])
            at += rows * (lanes // 256)
        sections.append((start, at - start))
    return np.concatenate(blocks, axis=0), layout, sections


def on_device(mask_field, target, kernel_taps, kernel_radii, kernel_group, kernel_weight):
    _, count, width = mask_field.shape
    kernels, _, span, _ = kernel_taps.shape
    rim = span // 2
    grid_rows = count + 2 * rim
    grid_cols = width + rim
    assert count == span and width == span and kernels % BATCH == 0 and (kernels - EARLY) % LATE_BATCH == 0 and count == 2 * rim

    strips = lax.axis_size("row")
    assert strips % 2 == 0
    at = lax.axis_index("row")
    near_pairs = [(i, i ^ 1) for i in range(strips)]
    far_pairs = [(i, ((i + 1) ^ 1) - 1) for i in range(1, strips - 1)]
    near = lax.ppermute(mask_field, "row", near_pairs)
    far = lax.ppermute(mask_field, "row", far_pairs)
    place = at.astype(jnp.int32).reshape(1)

    scale = 1.0 / (grid_rows * grid_cols)
    order = grouped(grid_cols, width)

    def head_and_tail(shift):
        table = analysis(grid_cols, width, shift).T[:, order]
        return halves(table[:, :2 * width], 0), halves(table[:, 2 * width:], 1)

    quarter = grid_rows // 4
    by_class = [class_table(grid_rows, quarter, c) for c in range(4)]
    row_fwd = np.concatenate([halves(t, 0) for t in by_class], axis=1)
    row_inv = np.concatenate([halves(t.T * scale, 0) for t in by_class], axis=1)
    head, tail = head_and_tail(0)
    mask_head, mask_tail = head_and_tail(rim)
    col_inv = halves(synthesis(grid_cols, width, 0).T[order], 0)
    grad_col = halves(synthesis(grid_cols, width, rim).T[order], 0)

    smem = pl.BlockSpec(memory_space=pltpu.SMEM)
    vmem = pl.BlockSpec(memory_space=pltpu.VMEM)
    hbm = pl.BlockSpec(memory_space=pltpu.HBM)
    spectra = pl.pallas_call(
        spectra_body,
        out_shape=jax.ShapeDtypeStruct((EARLY, grid_rows, 2 * grid_cols), f32),
        grid=(1,),
        in_specs=[smem, pl.BlockSpec((EARLY, 2, span, span), lambda i: (0, 0, 0, 0)), vmem, vmem, vmem],
        out_specs=pl.BlockSpec((EARLY, grid_rows, 2 * grid_cols), lambda i: (0, 0, 0)),
        compiler_params=pltpu.CompilerParams(vmem_limit_bytes=56 * MIB),
        cost_estimate=pl.CostEstimate(flops=3 * 10**9, bytes_accessed=3 * 10**6, transcendentals=0),
        name="spectra",
    )(kernel_radii, kernel_taps, *map(jnp.asarray, (row_fwd, head, tail)))

    tables, layout, sections = stacked([
        {"row_fwd": row_fwd, "head": head, "tail": tail},
        {"mask_head": mask_head, "mask_tail": mask_tail, "col_inv": col_inv, "row_inv": row_inv, "grad_col": grad_col},
    ])
    resist, own, near_rim, far_rim = pl.pallas_call(
        functools.partial(main_body, layout=layout, sections=sections),
        out_shape=[
            jax.ShapeDtypeStruct((GROUPS, count, width), f32),
            jax.ShapeDtypeStruct((2, count, width), f32),
            jax.ShapeDtypeStruct((2, rim, width), f32),
            jax.ShapeDtypeStruct((2, rim, width), f32),
        ],
        in_specs=[smem] * 4 + [vmem] * 4 + [hbm] * 3,
        out_specs=[hbm] + [vmem] * 3,
        scratch_shapes=[
            pltpu.VMEM((kernels, grid_rows, 2 * grid_cols), f32),
            pltpu.VMEM(kernel_taps.shape, f32),
            pltpu.VMEM((kernels // 2, 2 * count, 2 * width), f32),
            pltpu.VMEM((grid_rows, 4 * width), f32),
            pltpu.VMEM((GROUPS, count, width), f32),
            pltpu.VMEM((GROUPS, count, width), f32),
            pltpu.VMEM((grid_rows, 4 * width), f32),
            pltpu.VMEM(tables.shape, bf16),
            pltpu.SemaphoreType.DMA,
            pltpu.SemaphoreType.DMA(((kernels - EARLY) // LATE_BATCH,)),
            pltpu.SemaphoreType.DMA((len(sections),)),
            pltpu.SemaphoreType.DMA,
        ],
        compiler_params=pltpu.CompilerParams(vmem_limit_bytes=LIMIT * MIB),
        name="fields",
    )(kernel_group, kernel_weight, place, kernel_radii, mask_field, near, far, target, kernel_taps, spectra, jnp.asarray(tables))

    near_in = lax.ppermute(near_rim, "row", near_pairs)
    far_in = lax.ppermute(far_rim, "row", far_pairs)
    gradient = pl.pallas_call(
        join_body,
        out_shape=jax.ShapeDtypeStruct((2, count, width), f32),
        in_specs=[smem] + [vmem] * 3,
        out_specs=vmem,
        compiler_params=pltpu.CompilerParams(vmem_limit_bytes=4 * MIB),
        name="join",
    )(place, own, near_in, far_in)
    return resist, gradient


def solution(mesh):
    in_specs = (P(None, ("win", "row"), None), P(("win", "row"), None), P(), P(), P(), P())
    out_specs = (P(None, ("win", "row"), None), P(None, ("win", "row"), None))
    return jax.shard_map(
        on_device, mesh=mesh, in_specs=in_specs, out_specs=out_specs, check_vma=False
    )
```

```python
import functools
import math

import jax
import jax.numpy as jnp
import ml_dtypes
import numpy as np
from jax import lax
from jax.experimental import pallas as pl
from jax.experimental.pallas import tpu as pltpu
from jax.sharding import PartitionSpec as P

RMAX = 64
GROUPS = 3
STEEPNESS = 1.0
THRESHOLD = 2.0
BATCH = 12
EARLY = 8
LATE_BATCH = 8
PIECE = 256

f32 = jnp.float32
bf16 = jnp.bfloat16
MIB = 1024 * 1024
LIMIT = 53


def halves(table, axis):
    high = table.astype(ml_dtypes.bfloat16)
    low = (table - high.astype(np.float64)).astype(ml_dtypes.bfloat16)
    return np.concatenate([high, low], axis=axis)


def analysis(freqs, points, shift):
    f = np.arange(freqs)[:, None]
    n = np.arange(points)[None, :] - shift
    angle = 2.0 * math.pi * ((f * n) % freqs) / freqs
    cos, sin = np.cos(angle), np.sin(angle)
    return np.block([[cos, sin], [-sin, cos]])


def synthesis(freqs, points, shift, scale=1.0):
    return analysis(freqs, points, shift).T * scale


def class_table(freqs, points, c):
    f = np.arange(c, freqs, 4)[:, None]
    n = np.arange(points)[None, :]
    angle = 2.0 * math.pi * ((f * n) % freqs) / freqs
    cos, sin = np.cos(angle), np.sin(angle)
    return np.block([[cos, sin], [-sin, cos]])


def grouped(freqs, lanes):
    head, tail = np.arange(lanes), np.arange(lanes, freqs)
    return np.concatenate([head, freqs + head, tail, freqs + tail])


def split(x):
    high = x.astype(bf16)
    low = (x - high.astype(f32)).astype(bf16)
    return high, low


def dot(left, right):
    parts = [
        jnp.dot(left[at:at + PIECE], right, preferred_element_type=f32)
        for at in range(0, left.shape[0], PIECE)
    ]
    return jnp.concatenate(parts, axis=0)


def class_product(table, c, parts):
    depth = parts[0].shape[0]
    left = table[:, c * depth:(c + 1) * depth]
    found = dot(jnp.concatenate([left, left], axis=1), jnp.concatenate(parts, axis=0))
    half = found.shape[0] // 2
    return found[:half] + found[half:]


def turned(x, sign):
    re, im = x
    return (-im, re) if sign > 0 else (im, -re)


def plus(x, y):
    return x[0] + y[0], x[1] + y[1]


def minus(x, y):
    return x[0] - y[0], x[1] - y[1]


def to_row_freqs(x, table):
    if len(x) == 2:
        even, odd, even_less, odd_less = x[0], x[1], x[0], x[1]
    else:
        even, odd = plus(x[0], x[2]), plus(x[1], x[3])
        even_less, odd_less = minus(x[0], x[2]), minus(x[1], x[3])
    folded = [
        plus(even, odd),
        plus(even_less, turned(odd_less, -1)),
        minus(even, odd),
        plus(even_less, turned(odd_less, 1)),
    ]
    return [class_product(table, c, split(jnp.concatenate(y, axis=0))) for c, y in enumerate(folded)]


def from_row_freqs(classes, table, quarters):
    v = []
    for c, parts in enumerate(classes):
        found = class_product(table, c, parts)
        half = found.shape[0] // 2
        v.append((found[:half], found[half:]))
    out = []
    for q in quarters:
        if q % 2 == 0:
            even, odd = plus(v[0], v[2]), plus(v[1], v[3])
        else:
            even, odd = minus(v[0], v[2]), turned(minus(v[1], v[3]), 1)
        out.append(plus(even, odd) if q < 2 else minus(even, odd))
    return out


def over_lanes(parts, table):
    high, low = parts
    right = jnp.concatenate([table, table[:high.shape[1]]], axis=0)
    return dot(jnp.concatenate([high, high, low], axis=1), right)


def to_freqs(parts, head, tail):
    high, low = parts
    rows, depth = high.shape
    lanes = tail.shape[1] // 2
    right = jnp.concatenate([head, head[:depth]], axis=0)
    first = dot(jnp.concatenate([high, high, low], axis=1), right)
    rest = dot(jnp.concatenate([high, low], axis=1), jnp.concatenate([tail, tail], axis=0))
    return first, rest[:, :lanes] + rest[:, lanes:]


def beside(classes, at, width):
    tiles = []
    for found in classes:
        half = found.shape[0] // 2
        tiles.append(jnp.concatenate([found[:half, at:at + width], found[half:, at:at + width]], axis=1))
    return split(jnp.concatenate(tiles, axis=0))


def row_stage(quarters, row_fwd, width):
    classes = to_row_freqs(quarters, row_fwd)
    return [beside(classes, at, width) for at in range(0, quarters[0][0].shape[1], width)]


def quarters_of(re, im, quarter):
    return [(re[at:at + quarter], im[at:at + quarter]) for at in range(0, re.shape[0], quarter)]


def staggered(count, first, second):
    held = None
    for i in range(count):
        new = first(i)
        if i:
            second(i - 1, held)
        held = new
    second(count - 1, held)


def side_by_side(planes, c, width):
    quarter = planes[0][0].shape[0] // 4
    rows = slice(c * quarter, (c + 1) * quarter)
    return [
        jnp.concatenate([
            jnp.concatenate([plane[part][rows, at:at + width] for plane in planes], axis=1)
            for at in (0, width)
        ], axis=0)
        for part in range(2)
    ]


def swap(x):
    return pltpu.roll(x, x.shape[1] // 2, 1)


def spectra_of(radii, taps, spec, first, batch, row_fwd, head, tail):
    span = taps.shape[2]
    row_at = lax.broadcasted_iota(jnp.int32, (span, span), 0) - span // 2
    col_at = lax.broadcasted_iota(jnp.int32, (span, span), 1) - span // 2
    reach = jnp.maximum(jnp.maximum(row_at, -1 - row_at), jnp.maximum(col_at, -1 - col_at))

    def rows_of(p):
        planes = [[], []]
        for j in range(2):
            k = first + 2 * p + j
            inside = reach < radii[k]
            for c in range(2):
                planes[c].append(jnp.where(inside, taps[k, c], 0.0))
        re, im = [jnp.concatenate(plane, axis=1) for plane in planes]
        return row_stage(quarters_of(re, im, span // 2), row_fwd, span)

    def cols_of(p, tiles):
        for j in range(2):
            k = first + 2 * p + j
            a, b = to_freqs(tiles[j], head, tail)
            spec[k, :, :a.shape[1]] = a
            spec[k, :, a.shape[1]:] = b

    staggered(batch // 2, rows_of, cols_of)


def spectra_body(radii, taps, row_ref, head_ref, tail_ref, spec):
    spectra_of(radii, taps, spec, 0, spec.shape[0], row_ref[...], head_ref[...], tail_ref[...])


def main_body(
    group, weight, place, radii,
    own, near, far, target, taps_far, spec_far, tables_far,
    resist_far, grad_own, near_rim, far_rim,
    spec, taps, field, mask_spec, resist, slopes, grad_spec, tables, spec_sem, taps_sems, table_sems, out_sem,
    *, layout, sections,
):
    kernels, grid_rows, _ = spec.shape
    count, width = target.shape
    rim = (grid_rows - count) // 2
    batch = BATCH
    steps = kernels // batch
    early = spec_far.shape[0]
    late_steps = taps_sems.shape[0]
    late = (kernels - early) // late_steps

    fetch_early = pltpu.make_async_copy(spec_far, spec.at[pl.ds(0, early)], spec_sem)

    def fetch_taps(i):
        here = pl.ds(early + i * late, late)
        return pltpu.make_async_copy(taps_far.at[here], taps.at[here], taps_sems.at[i])

    def fetch_table(i):
        here = pl.ds(sections[i][0], sections[i][1])
        return pltpu.make_async_copy(tables_far.at[here], tables.at[here], table_sems.at[i])

    def table(name):
        start, rows, blocks = layout[name]
        parts = [tables[start + b * rows:start + (b + 1) * rows] for b in range(blocks)]
        return jnp.concatenate(parts, axis=1)

    fetch_table(0).start()
    for i in range(late_steps):
        fetch_taps(i).start()
    fetch_table(1).start()
    fetch_early.start()
    slopes[...] = jnp.zeros(slopes.shape, f32)
    grad_spec[...] = jnp.zeros(grad_spec.shape, f32)
    fetch_table(0).wait()
    row_fwd, head, tail = table("row_fwd"), table("head"), table("tail")

    def spectra(i, carry):
        fetch_taps(i).wait()
        spectra_of(radii, taps, spec, early + i * late, late, row_fwd, head, tail)
        return carry

    lax.fori_loop(0, late_steps, spectra, 0)
    fetch_table(1).wait()
    fetch_early.wait()

    odd = place[0] % 2 == 1
    above, below = [], []
    for c in range(2):
        above.append(jnp.where(odd, near[c, count - rim:], far[c, count - rim:]))
        below.append(jnp.where(odd, far[c, :rim], near[c, :rim]))
    upper, lower = quarters_of(own[0], own[1], rim)
    mask, = row_stage([lower, tuple(below), tuple(above), upper], row_fwd, width)
    m_first, m_rest = to_freqs(mask, table("mask_head"), table("mask_tail"))
    lane = lax.broadcasted_iota(jnp.int32, m_rest.shape, 1)
    real_half = lane < m_rest.shape[1] // 2
    turned = swap(m_rest)
    mask_spec[:, :2 * width] = m_first
    mask_spec[:, 2 * width:3 * width] = jnp.where(real_half, m_rest, turned)
    mask_spec[:, 3 * width:] = jnp.where(real_half, -turned, m_rest)

    col_inv, row_inv = table("col_inv"), table("row_inv")

    def forward(i, carry):
        m_re, m_im = mask_spec[:, :width], mask_spec[:, width:2 * width]
        m_same, m_cross = mask_spec[:, 2 * width:3 * width], mask_spec[:, 3 * width:]

        def cols_of(p):
            planes = []
            for j in range(2):
                k = i * batch + 2 * p + j
                s_re, s_im, s_rest = spec[k, :, :width], spec[k, :, width:2 * width], spec[k, :, 2 * width:]
                product = jnp.concatenate([
                    s_re * m_re - s_im * m_im,
                    s_re * m_im + s_im * m_re,
                    s_rest * m_same + swap(s_rest) * m_cross,
                ], axis=1)
                back = over_lanes(split(product), col_inv)
                planes.append(split(back))
            return [side_by_side(planes, c, width) for c in range(4)]

        def rows_of(p, pair):
            upper, lower = from_row_freqs(pair, row_inv, (0, 1))
            re = jnp.concatenate([upper[0], lower[0]], axis=0)
            im = jnp.concatenate([upper[1], lower[1]], axis=0)
            field[i * (batch // 2) + p, :count] = re
            field[i * (batch // 2) + p, count:] = im
            power = re * re + im * im
            for j in range(2):
                k = i * batch + 2 * p + j
                g = group[k]
                slopes[g] = slopes[g] + weight[k] * power[:, j * width:(j + 1) * width]

        staggered(batch // 2, cols_of, rows_of)
        return carry

    lax.fori_loop(0, steps, forward, 0)

    wanted = target[...].astype(f32)
    for g in range(GROUPS):
        seen = jax.nn.sigmoid(STEEPNESS * (slopes[g] - THRESHOLD))
        resist[g] = seen
        slopes[g] = 2.0 * (seen - wanted) * seen * (1.0 - seen) * STEEPNESS
    out = pltpu.make_async_copy(resist, resist_far, out_sem)
    out.start()

    def backward(i, carry):
        def rows_of(p):
            factors = []
            for j in range(2):
                k = i * batch + 2 * p + j
                factors.append((2.0 * weight[k]) * slopes[group[k]])
            factor = jnp.concatenate(factors, axis=1)
            re = field[i * (batch // 2) + p, :count] * factor
            im = field[i * (batch // 2) + p, count:] * factor
            return row_stage(quarters_of(re, im, rim), row_fwd, width)

        def cols_of(p, tiles):
            total = [grad_spec[:, c * width:(c + 1) * width] for c in range(4)]
            for j in range(2):
                k = i * batch + 2 * p + j
                s_re, s_im, s_rest = spec[k, :, :width], spec[k, :, width:2 * width], spec[k, :, 2 * width:]
                first, rest = to_freqs(tiles[j], head, tail)
                c_re, c_im = first[:, :width], first[:, width:]
                total[0] = total[0] + (s_re * c_re + s_im * c_im)
                total[1] = total[1] + (s_re * c_im - s_im * c_re)
                total[2] = total[2] + s_rest * rest
                total[3] = total[3] + s_rest * swap(rest)
            for c in range(4):
                grad_spec[:, c * width:(c + 1) * width] = total[c]

        staggered(batch // 2, rows_of, cols_of)
        return carry

    lax.fori_loop(0, steps, backward, 0)

    same, cross = grad_spec[:, 2 * width:3 * width], grad_spec[:, 3 * width:]
    tail_sum = jnp.where(real_half, same + swap(same), swap(cross) - cross)
    total = jnp.concatenate([grad_spec[:, :2 * width], tail_sum], axis=1)
    back = split(over_lanes(split(total), table("grad_col")))
    classes = [side_by_side([back], c, width) for c in range(4)]
    rise, upper, lower, fall = from_row_freqs(classes, row_inv, (2, 3, 0, 1))
    for c in range(2):
        near_rim[c] = jnp.where(odd, rise[c], fall[c])
        far_rim[c] = jnp.where(odd, fall[c], rise[c])
        grad_own[c, :rim] = upper[c]
        grad_own[c, rim:] = lower[c]
    out.wait()


def join_body(place, own, near, far, out):
    odd = place[0] % 2 == 1
    rim = near.shape[1]
    count = own.shape[1]
    for c in range(2):
        out[c, :rim] = own[c, :rim] + jnp.where(odd, near[c], far[c])
        if count > 2 * rim:
            out[c, rim:count - rim] = own[c, rim:count - rim]
        out[c, count - rim:] = own[c, count - rim:] + jnp.where(odd, far[c], near[c])


def stacked(groups):
    blocks, layout, sections, at = [], {}, [], 0
    for group in groups:
        start = at
        for name, table in group.items():
            rows, lanes = table.shape
            layout[name] = (at, rows, lanes // 256)
            for b in range(lanes // 256):
                blocks.append(table[:, b * 256:(b + 1) * 256])
            at += rows * (lanes // 256)
        sections.append((start, at - start))
    return np.concatenate(blocks, axis=0), layout, sections


def on_device(mask_field, target, kernel_taps, kernel_radii, kernel_group, kernel_weight):
    _, count, width = mask_field.shape
    kernels, _, span, _ = kernel_taps.shape
    rim = span // 2
    grid_rows = count + 2 * rim
    grid_cols = width + rim
    assert count == span and width == span and kernels % BATCH == 0 and (kernels - EARLY) % LATE_BATCH == 0 and count == 2 * rim

    strips = lax.axis_size("row")
    assert strips % 2 == 0
    at = lax.axis_index("row")
    near_pairs = [(i, i ^ 1) for i in range(strips)]
    far_pairs = [(i, ((i + 1) ^ 1) - 1) for i in range(1, strips - 1)]
    near = lax.ppermute(mask_field, "row", near_pairs)
    far = lax.ppermute(mask_field, "row", far_pairs)
    place = at.astype(jnp.int32).reshape(1)

    scale = 1.0 / (grid_rows * grid_cols)
    order = grouped(grid_cols, width)

    def head_and_tail(shift):
        table = analysis(grid_cols, width, shift).T[:, order]
        return halves(table[:, :2 * width], 0), halves(table[:, 2 * width:], 1)

    quarter = grid_rows // 4
    by_class = [class_table(grid_rows, quarter, c) for c in range(4)]
    row_fwd = np.concatenate([halves(t, 0) for t in by_class], axis=1)
    row_inv = np.concatenate([halves(t.T * scale, 0) for t in by_class], axis=1)
    head, tail = head_and_tail(0)
    mask_head, mask_tail = head_and_tail(rim)
    col_inv = halves(synthesis(grid_cols, width, 0).T[order], 0)
    grad_col = halves(synthesis(grid_cols, width, rim).T[order], 0)

    smem = pl.BlockSpec(memory_space=pltpu.SMEM)
    vmem = pl.BlockSpec(memory_space=pltpu.VMEM)
    hbm = pl.BlockSpec(memory_space=pltpu.HBM)
    spectra = pl.pallas_call(
        spectra_body,
        out_shape=jax.ShapeDtypeStruct((EARLY, grid_rows, 2 * grid_cols), f32),
        grid=(1,),
        in_specs=[smem, pl.BlockSpec((EARLY, 2, span, span), lambda i: (0, 0, 0, 0)), vmem, vmem, vmem],
        out_specs=pl.BlockSpec((EARLY, grid_rows, 2 * grid_cols), lambda i: (0, 0, 0)),
        compiler_params=pltpu.CompilerParams(vmem_limit_bytes=56 * MIB),
        cost_estimate=pl.CostEstimate(flops=3 * 10**9, bytes_accessed=3 * 10**6, transcendentals=0),
        name="spectra",
    )(kernel_radii, kernel_taps, *map(jnp.asarray, (row_fwd, head, tail)))

    tables, layout, sections = stacked([
        {"row_fwd": row_fwd, "head": head, "tail": tail},
        {"mask_head": mask_head, "mask_tail": mask_tail, "col_inv": col_inv, "row_inv": row_inv, "grad_col": grad_col},
    ])
    resist, own, near_rim, far_rim = pl.pallas_call(
        functools.partial(main_body, layout=layout, sections=sections),
        out_shape=[
            jax.ShapeDtypeStruct((GROUPS, count, width), f32),
            jax.ShapeDtypeStruct((2, count, width), f32),
            jax.ShapeDtypeStruct((2, rim, width), f32),
            jax.ShapeDtypeStruct((2, rim, width), f32),
        ],
        in_specs=[smem] * 4 + [vmem] * 4 + [hbm] * 3,
        out_specs=[hbm] + [vmem] * 3,
        scratch_shapes=[
            pltpu.VMEM((kernels, grid_rows, 2 * grid_cols), f32),
            pltpu.VMEM(kernel_taps.shape, f32),
            pltpu.VMEM((kernels // 2, 2 * count, 2 * width), f32),
            pltpu.VMEM((grid_rows, 4 * width), f32),
            pltpu.VMEM((GROUPS, count, width), f32),
            pltpu.VMEM((GROUPS, count, width), f32),
            pltpu.VMEM((grid_rows, 4 * width), f32),
            pltpu.VMEM(tables.shape, bf16),
            pltpu.SemaphoreType.DMA,
            pltpu.SemaphoreType.DMA(((kernels - EARLY) // LATE_BATCH,)),
            pltpu.SemaphoreType.DMA((len(sections),)),
            pltpu.SemaphoreType.DMA,
        ],
        compiler_params=pltpu.CompilerParams(vmem_limit_bytes=LIMIT * MIB),
        name="fields",
    )(kernel_group, kernel_weight, place, kernel_radii, mask_field, near, far, target, kernel_taps, spectra, jnp.asarray(tables))

    far_in = lax.ppermute(far_rim, "row", far_pairs)
    near_in = lax.ppermute(near_rim, "row", near_pairs)
    gradient = pl.pallas_call(
        join_body,
        out_shape=jax.ShapeDtypeStruct((2, count, width), f32),
        in_specs=[smem] + [vmem] * 3,
        out_specs=vmem,
        compiler_params=pltpu.CompilerParams(vmem_limit_bytes=4 * MIB),
        name="join",
    )(place, own, near_in, far_in)
    return resist, gradient


def solution(mesh):
    in_specs = (P(None, ("win", "row"), None), P(("win", "row"), None), P(), P(), P(), P())
    out_specs = (P(None, ("win", "row"), None), P(None, ("win", "row"), None))
    return jax.shard_map(
        on_device, mesh=mesh, in_specs=in_specs, out_specs=out_specs, check_vma=False
    )
```

```python
import functools
import math

import jax
import jax.numpy as jnp
import ml_dtypes
import numpy as np
from jax import lax
from jax.experimental import pallas as pl
from jax.experimental.pallas import tpu as pltpu
from jax.sharding import PartitionSpec as P

RMAX = 64
GROUPS = 3
STEEPNESS = 1.0
THRESHOLD = 2.0
BATCH = 12
EARLY = 8
LATE_BATCH = 8
PIECE = 256

f32 = jnp.float32
bf16 = jnp.bfloat16
MIB = 1024 * 1024
LIMIT = 53


def halves(table, axis):
    high = table.astype(ml_dtypes.bfloat16)
    low = (table - high.astype(np.float64)).astype(ml_dtypes.bfloat16)
    return np.concatenate([high, low], axis=axis)


def analysis(freqs, points, shift):
    f = np.arange(freqs)[:, None]
    n = np.arange(points)[None, :] - shift
    angle = 2.0 * math.pi * ((f * n) % freqs) / freqs
    cos, sin = np.cos(angle), np.sin(angle)
    return np.block([[cos, sin], [-sin, cos]])


def synthesis(freqs, points, shift, scale=1.0):
    return analysis(freqs, points, shift).T * scale


def class_table(freqs, points, c):
    f = np.arange(c, freqs, 4)[:, None]
    n = np.arange(points)[None, :]
    angle = 2.0 * math.pi * ((f * n) % freqs) / freqs
    cos, sin = np.cos(angle), np.sin(angle)
    return np.block([[cos, sin], [-sin, cos]])


def grouped(freqs, lanes):
    head, tail = np.arange(lanes), np.arange(lanes, freqs)
    return np.concatenate([head, freqs + head, tail, freqs + tail])


def split(x):
    high = x.astype(bf16)
    low = (x - high.astype(f32)).astype(bf16)
    return high, low


def dot(left, right):
    parts = [
        jnp.dot(left[at:at + PIECE], right, preferred_element_type=f32)
        for at in range(0, left.shape[0], PIECE)
    ]
    return jnp.concatenate(parts, axis=0)


def class_product(table, c, parts):
    depth = parts[0].shape[0]
    left = table[:, c * depth:(c + 1) * depth]
    found = dot(jnp.concatenate([left, left], axis=1), jnp.concatenate(parts, axis=0))
    half = found.shape[0] // 2
    return found[:half] + found[half:]


def turned(x, sign):
    re, im = x
    return (-im, re) if sign > 0 else (im, -re)


def plus(x, y):
    return x[0] + y[0], x[1] + y[1]


def minus(x, y):
    return x[0] - y[0], x[1] - y[1]


def to_row_freqs(x, table):
    if len(x) == 2:
        even, odd, even_less, odd_less = x[0], x[1], x[0], x[1]
    else:
        even, odd = plus(x[0], x[2]), plus(x[1], x[3])
        even_less, odd_less = minus(x[0], x[2]), minus(x[1], x[3])
    folded = [
        plus(even, odd),
        plus(even_less, turned(odd_less, -1)),
        minus(even, odd),
        plus(even_less, turned(odd_less, 1)),
    ]
    return [class_product(table, c, split(jnp.concatenate(y, axis=0))) for c, y in enumerate(folded)]


def from_row_freqs(classes, table, quarters):
    v = []
    for c, parts in enumerate(classes):
        found = class_product(table, c, parts)
        half = found.shape[0] // 2
        v.append((found[:half], found[half:]))
    out = []
    for q in quarters:
        if q % 2 == 0:
            even, odd = plus(v[0], v[2]), plus(v[1], v[3])
        else:
            even, odd = minus(v[0], v[2]), turned(minus(v[1], v[3]), 1)
        out.append(plus(even, odd) if q < 2 else minus(even, odd))
    return out


def over_lanes(parts, table):
    high, low = parts
    right = jnp.concatenate([table, table[:high.shape[1]]], axis=0)
    return dot(jnp.concatenate([high, high, low], axis=1), right)


def to_freqs(parts, head, tail):
    high, low = parts
    rows, depth = high.shape
    lanes = tail.shape[1] // 2
    right = jnp.concatenate([head, head[:depth]], axis=0)
    first = dot(jnp.concatenate([high, high, low], axis=1), right)
    rest = dot(jnp.concatenate([high, low], axis=1), jnp.concatenate([tail, tail], axis=0))
    return first, rest[:, :lanes] + rest[:, lanes:]


def beside(classes, at, width):
    tiles = []
    for found in classes:
        half = found.shape[0] // 2
        tiles.append(jnp.concatenate([found[:half, at:at + width], found[half:, at:at + width]], axis=1))
    return split(jnp.concatenate(tiles, axis=0))


def row_stage(quarters, row_fwd, width):
    classes = to_row_freqs(quarters, row_fwd)
    return [beside(classes, at, width) for at in range(0, quarters[0][0].shape[1], width)]


def quarters_of(re, im, quarter):
    return [(re[at:at + quarter], im[at:at + quarter]) for at in range(0, re.shape[0], quarter)]


def staggered(count, first, second):
    held = None
    for i in range(count):
        new = first(i)
        if i:
            second(i - 1, held)
        held = new
    second(count - 1, held)


def side_by_side(planes, c, width):
    quarter = planes[0][0].shape[0] // 4
    rows = slice(c * quarter, (c + 1) * quarter)
    return [
        jnp.concatenate([
            jnp.concatenate([plane[part][rows, at:at + width] for plane in planes], axis=1)
            for at in (0, width)
        ], axis=0)
        for part in range(2)
    ]


def swap(x):
    return pltpu.roll(x, x.shape[1] // 2, 1)


def spectra_of(radii, taps, spec, first, batch, row_fwd, head, tail):
    span = taps.shape[2]
    row_at = lax.broadcasted_iota(jnp.int32, (span, span), 0) - span // 2
    col_at = lax.broadcasted_iota(jnp.int32, (span, span), 1) - span // 2
    reach = jnp.maximum(jnp.maximum(row_at, -1 - row_at), jnp.maximum(col_at, -1 - col_at))

    def rows_of(p):
        planes = [[], []]
        for j in range(2):
            k = first + 2 * p + j
            inside = reach < radii[k]
            for c in range(2):
                planes[c].append(jnp.where(inside, taps[k, c], 0.0))
        re, im = [jnp.concatenate(plane, axis=1) for plane in planes]
        return row_stage(quarters_of(re, im, span // 2), row_fwd, span)

    def cols_of(p, tiles):
        for j in range(2):
            k = first + 2 * p + j
            a, b = to_freqs(tiles[j], head, tail)
            spec[k, :, :a.shape[1]] = a
            spec[k, :, a.shape[1]:] = b

    staggered(batch // 2, rows_of, cols_of)


def spectra_body(radii, taps, row_ref, head_ref, tail_ref, spec):
    spectra_of(radii, taps, spec, 0, spec.shape[0], row_ref[...], head_ref[...], tail_ref[...])


def main_body(
    group, weight, place, radii,
    own, near, far, target, taps_far, spec_far, tables_far,
    resist_far, grad_own, near_rim, far_rim,
    spec, taps, field, mask_spec, resist, slopes, grad_spec, tables, spec_sem, taps_sems, table_sems, out_sem,
    *, layout, sections,
):
    kernels, grid_rows, _ = spec.shape
    count, width = target.shape
    rim = (grid_rows - count) // 2
    batch = BATCH
    steps = kernels // batch
    early = spec_far.shape[0]
    late_steps = taps_sems.shape[0]
    late = (kernels - early) // late_steps

    fetch_early = pltpu.make_async_copy(spec_far, spec.at[pl.ds(0, early)], spec_sem)

    def fetch_taps(i):
        here = pl.ds(early + i * late, late)
        return pltpu.make_async_copy(taps_far.at[here], taps.at[here], taps_sems.at[i])

    def fetch_table(i):
        here = pl.ds(sections[i][0], sections[i][1])
        return pltpu.make_async_copy(tables_far.at[here], tables.at[here], table_sems.at[i])

    def table(name):
        start, rows, blocks = layout[name]
        parts = [tables[start + b * rows:start + (b + 1) * rows] for b in range(blocks)]
        return jnp.concatenate(parts, axis=1)

    fetch_table(0).start()
    fetch_table(1).start()
    for i in range(late_steps):
        fetch_taps(i).start()
    fetch_early.start()
    slopes[...] = jnp.zeros(slopes.shape, f32)
    grad_spec[...] = jnp.zeros(grad_spec.shape, f32)
    fetch_table(0).wait()
    fetch_table(1).wait()
    row_fwd, head, tail = table("row_fwd"), table("head"), table("tail")

    odd = place[0] % 2 == 1
    above, below = [], []
    for c in range(2):
        above.append(jnp.where(odd, near[c, count - rim:], far[c, count - rim:]))
        below.append(jnp.where(odd, far[c, :rim], near[c, :rim]))
    upper, lower = quarters_of(own[0], own[1], rim)
    mask, = row_stage([lower, tuple(below), tuple(above), upper], row_fwd, width)
    m_first, m_rest = to_freqs(mask, table("mask_head"), table("mask_tail"))
    lane = lax.broadcasted_iota(jnp.int32, m_rest.shape, 1)
    real_half = lane < m_rest.shape[1] // 2
    turned = swap(m_rest)
    mask_spec[:, :2 * width] = m_first
    mask_spec[:, 2 * width:3 * width] = jnp.where(real_half, m_rest, turned)
    mask_spec[:, 3 * width:] = jnp.where(real_half, -turned, m_rest)

    def spectra(i, carry):
        fetch_taps(i).wait()
        spectra_of(radii, taps, spec, early + i * late, late, row_fwd, head, tail)
        return carry

    lax.fori_loop(0, late_steps, spectra, 0)
    fetch_early.wait()

    col_inv, row_inv = table("col_inv"), table("row_inv")

    def forward(i, carry):
        m_re, m_im = mask_spec[:, :width], mask_spec[:, width:2 * width]
        m_same, m_cross = mask_spec[:, 2 * width:3 * width], mask_spec[:, 3 * width:]

        def cols_of(p):
            planes = []
            for j in range(2):
                k = i * batch + 2 * p + j
                s_re, s_im, s_rest = spec[k, :, :width], spec[k, :, width:2 * width], spec[k, :, 2 * width:]
                product = jnp.concatenate([
                    s_re * m_re - s_im * m_im,
                    s_re * m_im + s_im * m_re,
                    s_rest * m_same + swap(s_rest) * m_cross,
                ], axis=1)
                back = over_lanes(split(product), col_inv)
                planes.append(split(back))
            return [side_by_side(planes, c, width) for c in range(4)]

        def rows_of(p, pair):
            upper, lower = from_row_freqs(pair, row_inv, (0, 1))
            re = jnp.concatenate([upper[0], lower[0]], axis=0)
            im = jnp.concatenate([upper[1], lower[1]], axis=0)
            field[i * (batch // 2) + p, :count] = re
            field[i * (batch // 2) + p, count:] = im
            power = re * re + im * im
            for j in range(2):
                k = i * batch + 2 * p + j
                g = group[k]
                slopes[g] = slopes[g] + weight[k] * power[:, j * width:(j + 1) * width]

        staggered(batch // 2, cols_of, rows_of)
        return carry

    lax.fori_loop(0, steps, forward, 0)

    wanted = target[...].astype(f32)
    for g in range(GROUPS):
        seen = jax.nn.sigmoid(STEEPNESS * (slopes[g] - THRESHOLD))
        resist[g] = seen
        slopes[g] = 2.0 * (seen - wanted) * seen * (1.0 - seen) * STEEPNESS
    out = pltpu.make_async_copy(resist, resist_far, out_sem)
    out.start()

    def backward(i, carry):
        def rows_of(p):
            factors = []
            for j in range(2):
                k = i * batch + 2 * p + j
                factors.append((2.0 * weight[k]) * slopes[group[k]])
            factor = jnp.concatenate(factors, axis=1)
            re = field[i * (batch // 2) + p, :count] * factor
            im = field[i * (batch // 2) + p, count:] * factor
            return row_stage(quarters_of(re, im, rim), row_fwd, width)

        def cols_of(p, tiles):
            total = [grad_spec[:, c * width:(c + 1) * width] for c in range(4)]
            for j in range(2):
                k = i * batch + 2 * p + j
                s_re, s_im, s_rest = spec[k, :, :width], spec[k, :, width:2 * width], spec[k, :, 2 * width:]
                first, rest = to_freqs(tiles[j], head, tail)
                c_re, c_im = first[:, :width], first[:, width:]
                total[0] = total[0] + (s_re * c_re + s_im * c_im)
                total[1] = total[1] + (s_re * c_im - s_im * c_re)
                total[2] = total[2] + s_rest * rest
                total[3] = total[3] + s_rest * swap(rest)
            for c in range(4):
                grad_spec[:, c * width:(c + 1) * width] = total[c]

        staggered(batch // 2, rows_of, cols_of)
        return carry

    lax.fori_loop(0, steps, backward, 0)

    same, cross = grad_spec[:, 2 * width:3 * width], grad_spec[:, 3 * width:]
    tail_sum = jnp.where(real_half, same + swap(same), swap(cross) - cross)
    total = jnp.concatenate([grad_spec[:, :2 * width], tail_sum], axis=1)
    back = split(over_lanes(split(total), table("grad_col")))
    classes = [side_by_side([back], c, width) for c in range(4)]
    rise, upper, lower, fall = from_row_freqs(classes, row_inv, (2, 3, 0, 1))
    for c in range(2):
        near_rim[c] = jnp.where(odd, rise[c], fall[c])
        far_rim[c] = jnp.where(odd, fall[c], rise[c])
        grad_own[c, :rim] = upper[c]
        grad_own[c, rim:] = lower[c]
    out.wait()


def join_body(place, own, near, far, out):
    odd = place[0] % 2 == 1
    rim = near.shape[1]
    count = own.shape[1]
    for c in range(2):
        out[c, :rim] = own[c, :rim] + jnp.where(odd, near[c], far[c])
        if count > 2 * rim:
            out[c, rim:count - rim] = own[c, rim:count - rim]
        out[c, count - rim:] = own[c, count - rim:] + jnp.where(odd, far[c], near[c])


def stacked(groups):
    blocks, layout, sections, at = [], {}, [], 0
    for group in groups:
        start = at
        for name, table in group.items():
            rows, lanes = table.shape
            layout[name] = (at, rows, lanes // 256)
            for b in range(lanes // 256):
                blocks.append(table[:, b * 256:(b + 1) * 256])
            at += rows * (lanes // 256)
        sections.append((start, at - start))
    return np.concatenate(blocks, axis=0), layout, sections


def on_device(mask_field, target, kernel_taps, kernel_radii, kernel_group, kernel_weight):
    _, count, width = mask_field.shape
    kernels, _, span, _ = kernel_taps.shape
    rim = span // 2
    grid_rows = count + 2 * rim
    grid_cols = width + rim
    assert count == span and width == span and kernels % BATCH == 0 and (kernels - EARLY) % LATE_BATCH == 0 and count == 2 * rim

    strips = lax.axis_size("row")
    assert strips % 2 == 0
    at = lax.axis_index("row")
    near_pairs = [(i, i ^ 1) for i in range(strips)]
    far_pairs = [(i, ((i + 1) ^ 1) - 1) for i in range(1, strips - 1)]
    near = lax.ppermute(mask_field, "row", near_pairs)
    far = lax.ppermute(mask_field, "row", far_pairs)
    place = at.astype(jnp.int32).reshape(1)

    scale = 1.0 / (grid_rows * grid_cols)
    order = grouped(grid_cols, width)

    def head_and_tail(shift):
        table = analysis(grid_cols, width, shift).T[:, order]
        return halves(table[:, :2 * width], 0), halves(table[:, 2 * width:], 1)

    quarter = grid_rows // 4
    by_class = [class_table(grid_rows, quarter, c) for c in range(4)]
    row_fwd = np.concatenate([halves(t, 0) for t in by_class], axis=1)
    row_inv = np.concatenate([halves(t.T * scale, 0) for t in by_class], axis=1)
    head, tail = head_and_tail(0)
    mask_head, mask_tail = head_and_tail(rim)
    col_inv = halves(synthesis(grid_cols, width, 0).T[order], 0)
    grad_col = halves(synthesis(grid_cols, width, rim).T[order], 0)

    smem = pl.BlockSpec(memory_space=pltpu.SMEM)
    vmem = pl.BlockSpec(memory_space=pltpu.VMEM)
    hbm = pl.BlockSpec(memory_space=pltpu.HBM)
    spectra = pl.pallas_call(
        spectra_body,
        out_shape=jax.ShapeDtypeStruct((EARLY, grid_rows, 2 * grid_cols), f32),
        grid=(1,),
        in_specs=[smem, pl.BlockSpec((EARLY, 2, span, span), lambda i: (0, 0, 0, 0)), vmem, vmem, vmem],
        out_specs=pl.BlockSpec((EARLY, grid_rows, 2 * grid_cols), lambda i: (0, 0, 0)),
        compiler_params=pltpu.CompilerParams(vmem_limit_bytes=56 * MIB),
        cost_estimate=pl.CostEstimate(flops=3 * 10**9, bytes_accessed=3 * 10**6, transcendentals=0),
        name="spectra",
    )(kernel_radii, kernel_taps, *map(jnp.asarray, (row_fwd, head, tail)))

    tables, layout, sections = stacked([
        {"row_fwd": row_fwd, "head": head, "tail": tail},
        {"mask_head": mask_head, "mask_tail": mask_tail, "col_inv": col_inv, "row_inv": row_inv, "grad_col": grad_col},
    ])
    resist, own, near_rim, far_rim = pl.pallas_call(
        functools.partial(main_body, layout=layout, sections=sections),
        out_shape=[
            jax.ShapeDtypeStruct((GROUPS, count, width), f32),
            jax.ShapeDtypeStruct((2, count, width), f32),
            jax.ShapeDtypeStruct((2, rim, width), f32),
            jax.ShapeDtypeStruct((2, rim, width), f32),
        ],
        in_specs=[smem] * 4 + [vmem] * 4 + [hbm] * 3,
        out_specs=[hbm] + [vmem] * 3,
        scratch_shapes=[
            pltpu.VMEM((kernels, grid_rows, 2 * grid_cols), f32),
            pltpu.VMEM(kernel_taps.shape, f32),
            pltpu.VMEM((kernels // 2, 2 * count, 2 * width), f32),
            pltpu.VMEM((grid_rows, 4 * width), f32),
            pltpu.VMEM((GROUPS, count, width), f32),
            pltpu.VMEM((GROUPS, count, width), f32),
            pltpu.VMEM((grid_rows, 4 * width), f32),
            pltpu.VMEM(tables.shape, bf16),
            pltpu.SemaphoreType.DMA,
            pltpu.SemaphoreType.DMA(((kernels - EARLY) // LATE_BATCH,)),
            pltpu.SemaphoreType.DMA((len(sections),)),
            pltpu.SemaphoreType.DMA,
        ],
        compiler_params=pltpu.CompilerParams(vmem_limit_bytes=LIMIT * MIB),
        name="fields",
    )(kernel_group, kernel_weight, place, kernel_radii, mask_field, near, far, target, kernel_taps, spectra, jnp.asarray(tables))

    far_in = lax.ppermute(far_rim, "row", far_pairs)
    near_in = lax.ppermute(near_rim, "row", near_pairs)
    gradient = pl.pallas_call(
        join_body,
        out_shape=jax.ShapeDtypeStruct((2, count, width), f32),
        in_specs=[smem] + [vmem] * 3,
        out_specs=vmem,
        compiler_params=pltpu.CompilerParams(vmem_limit_bytes=4 * MIB),
        name="join",
    )(place, own, near_in, far_in)
    return resist, gradient


def solution(mesh):
    in_specs = (P(None, ("win", "row"), None), P(("win", "row"), None), P(), P(), P(), P())
    out_specs = (P(None, ("win", "row"), None), P(None, ("win", "row"), None))
    return jax.shard_map(
        on_device, mesh=mesh, in_specs=in_specs, out_specs=out_specs, check_vma=False
    )
```

```python
import functools
import math

import jax
import jax.numpy as jnp
import ml_dtypes
import numpy as np
from jax import lax
from jax.experimental import pallas as pl
from jax.experimental.pallas import tpu as pltpu
from jax.sharding import PartitionSpec as P

RMAX = 64
GROUPS = 3
STEEPNESS = 1.0
THRESHOLD = 2.0
BATCH = 12
EARLY = 8
LATE_BATCH = 16
PIECE = 256

f32 = jnp.float32
bf16 = jnp.bfloat16
MIB = 1024 * 1024
LIMIT = 53


def halves(table, axis):
    high = table.astype(ml_dtypes.bfloat16)
    low = (table - high.astype(np.float64)).astype(ml_dtypes.bfloat16)
    return np.concatenate([high, low], axis=axis)


def analysis(freqs, points, shift):
    f = np.arange(freqs)[:, None]
    n = np.arange(points)[None, :] - shift
    angle = 2.0 * math.pi * ((f * n) % freqs) / freqs
    cos, sin = np.cos(angle), np.sin(angle)
    return np.block([[cos, sin], [-sin, cos]])


def synthesis(freqs, points, shift, scale=1.0):
    return analysis(freqs, points, shift).T * scale


def class_table(freqs, points, c):
    f = np.arange(c, freqs, 4)[:, None]
    n = np.arange(points)[None, :]
    angle = 2.0 * math.pi * ((f * n) % freqs) / freqs
    cos, sin = np.cos(angle), np.sin(angle)
    return np.block([[cos, sin], [-sin, cos]])


def grouped(freqs, lanes):
    head, tail = np.arange(lanes), np.arange(lanes, freqs)
    return np.concatenate([head, freqs + head, tail, freqs + tail])


def split(x):
    high = x.astype(bf16)
    low = (x - high.astype(f32)).astype(bf16)
    return high, low


def dot(left, right):
    parts = [
        jnp.dot(left[at:at + PIECE], right, preferred_element_type=f32)
        for at in range(0, left.shape[0], PIECE)
    ]
    return jnp.concatenate(parts, axis=0)


def class_product(table, c, parts):
    depth = parts[0].shape[0]
    left = table[:, c * depth:(c + 1) * depth]
    found = dot(jnp.concatenate([left, left], axis=1), jnp.concatenate(parts, axis=0))
    half = found.shape[0] // 2
    return found[:half] + found[half:]


def turned(x, sign):
    re, im = x
    return (-im, re) if sign > 0 else (im, -re)


def plus(x, y):
    return x[0] + y[0], x[1] + y[1]


def minus(x, y):
    return x[0] - y[0], x[1] - y[1]


def to_row_freqs(x, table):
    if len(x) == 2:
        even, odd, even_less, odd_less = x[0], x[1], x[0], x[1]
    else:
        even, odd = plus(x[0], x[2]), plus(x[1], x[3])
        even_less, odd_less = minus(x[0], x[2]), minus(x[1], x[3])
    folded = [
        plus(even, odd),
        plus(even_less, turned(odd_less, -1)),
        minus(even, odd),
        plus(even_less, turned(odd_less, 1)),
    ]
    return [class_product(table, c, split(jnp.concatenate(y, axis=0))) for c, y in enumerate(folded)]


def from_row_freqs(classes, table, quarters):
    v = []
    for c, parts in enumerate(classes):
        found = class_product(table, c, parts)
        half = found.shape[0] // 2
        v.append((found[:half], found[half:]))
    out = []
    for q in quarters:
        if q % 2 == 0:
            even, odd = plus(v[0], v[2]), plus(v[1], v[3])
        else:
            even, odd = minus(v[0], v[2]), turned(minus(v[1], v[3]), 1)
        out.append(plus(even, odd) if q < 2 else minus(even, odd))
    return out


def over_lanes(parts, table):
    high, low = parts
    right = jnp.concatenate([table, table[:high.shape[1]]], axis=0)
    return dot(jnp.concatenate([high, high, low], axis=1), right)


def to_freqs(parts, head, tail):
    high, low = parts
    rows, depth = high.shape
    lanes = tail.shape[1] // 2
    right = jnp.concatenate([head, head[:depth]], axis=0)
    first = dot(jnp.concatenate([high, high, low], axis=1), right)
    rest = dot(jnp.concatenate([high, low], axis=1), jnp.concatenate([tail, tail], axis=0))
    return first, rest[:, :lanes] + rest[:, lanes:]


def beside(classes, at, width):
    tiles = []
    for found in classes:
        half = found.shape[0] // 2
        tiles.append(jnp.concatenate([found[:half, at:at + width], found[half:, at:at + width]], axis=1))
    return split(jnp.concatenate(tiles, axis=0))


def row_stage(quarters, row_fwd, width):
    classes = to_row_freqs(quarters, row_fwd)
    return [beside(classes, at, width) for at in range(0, quarters[0][0].shape[1], width)]


def quarters_of(re, im, quarter):
    return [(re[at:at + quarter], im[at:at + quarter]) for at in range(0, re.shape[0], quarter)]


def staggered(count, first, second):
    held = None
    for i in range(count):
        new = first(i)
        if i:
            second(i - 1, held)
        held = new
    second(count - 1, held)


def side_by_side(planes, c, width):
    quarter = planes[0][0].shape[0] // 4
    rows = slice(c * quarter, (c + 1) * quarter)
    return [
        jnp.concatenate([
            jnp.concatenate([plane[part][rows, at:at + width] for plane in planes], axis=1)
            for at in (0, width)
        ], axis=0)
        for part in range(2)
    ]


def swap(x):
    return pltpu.roll(x, x.shape[1] // 2, 1)


def spectra_of(radii, taps, spec, first, batch, row_fwd, head, tail):
    span = taps.shape[2]
    row_at = lax.broadcasted_iota(jnp.int32, (span, span), 0) - span // 2
    col_at = lax.broadcasted_iota(jnp.int32, (span, span), 1) - span // 2
    reach = jnp.maximum(jnp.maximum(row_at, -1 - row_at), jnp.maximum(col_at, -1 - col_at))

    def rows_of(p):
        planes = [[], []]
        for j in range(2):
            k = first + 2 * p + j
            inside = reach < radii[k]
            for c in range(2):
                planes[c].append(jnp.where(inside, taps[k, c], 0.0))
        re, im = [jnp.concatenate(plane, axis=1) for plane in planes]
        return row_stage(quarters_of(re, im, span // 2), row_fwd, span)

    def cols_of(p, tiles):
        for j in range(2):
            k = first + 2 * p + j
            a, b = to_freqs(tiles[j], head, tail)
            spec[k, :, :a.shape[1]] = a
            spec[k, :, a.shape[1]:] = b

    staggered(batch // 2, rows_of, cols_of)


def spectra_body(radii, taps, row_ref, head_ref, tail_ref, spec):
    spectra_of(radii, taps, spec, 0, spec.shape[0], row_ref[...], head_ref[...], tail_ref[...])


def main_body(
    group, weight, place, radii,
    own, near, far, target, taps_far, spec_far, tables_far,
    resist_far, grad_own, near_rim, far_rim,
    spec, taps, field, mask_spec, resist, slopes, grad_spec, tables, spec_sem, taps_sems, table_sems, out_sem,
    *, layout, sections,
):
    kernels, grid_rows, _ = spec.shape
    count, width = target.shape
    rim = (grid_rows - count) // 2
    batch = BATCH
    steps = kernels // batch
    early = spec_far.shape[0]
    late_steps = taps_sems.shape[0]
    late = (kernels - early) // late_steps

    fetch_early = pltpu.make_async_copy(spec_far, spec.at[pl.ds(0, early)], spec_sem)

    def fetch_taps(i):
        here = pl.ds(early + i * late, late)
        return pltpu.make_async_copy(taps_far.at[here], taps.at[here], taps_sems.at[i])

    def fetch_table(i):
        here = pl.ds(sections[i][0], sections[i][1])
        return pltpu.make_async_copy(tables_far.at[here], tables.at[here], table_sems.at[i])

    def table(name):
        start, rows, blocks = layout[name]
        parts = [tables[start + b * rows:start + (b + 1) * rows] for b in range(blocks)]
        return jnp.concatenate(parts, axis=1)

    fetch_table(0).start()
    for i in range(late_steps):
        fetch_taps(i).start()
    fetch_table(1).start()
    fetch_early.start()
    slopes[...] = jnp.zeros(slopes.shape, f32)
    grad_spec[...] = jnp.zeros(grad_spec.shape, f32)
    fetch_table(0).wait()
    row_fwd, head, tail = table("row_fwd"), table("head"), table("tail")

    def spectra(i, carry):
        fetch_taps(i).wait()
        spectra_of(radii, taps, spec, early + i * late, late, row_fwd, head, tail)
        return carry

    lax.fori_loop(0, late_steps, spectra, 0)
    fetch_table(1).wait()
    fetch_early.wait()

    odd = place[0] % 2 == 1
    above, below = [], []
    for c in range(2):
        above.append(jnp.where(odd, near[c, count - rim:], far[c, count - rim:]))
        below.append(jnp.where(odd, far[c, :rim], near[c, :rim]))
    upper, lower = quarters_of(own[0], own[1], rim)
    mask, = row_stage([lower, tuple(below), tuple(above), upper], row_fwd, width)
    m_first, m_rest = to_freqs(mask, table("mask_head"), table("mask_tail"))
    lane = lax.broadcasted_iota(jnp.int32, m_rest.shape, 1)
    real_half = lane < m_rest.shape[1] // 2
    turned = swap(m_rest)
    mask_spec[:, :2 * width] = m_first
    mask_spec[:, 2 * width:3 * width] = jnp.where(real_half, m_rest, turned)
    mask_spec[:, 3 * width:] = jnp.where(real_half, -turned, m_rest)

    col_inv, row_inv = table("col_inv"), table("row_inv")

    def forward(i, carry):
        m_re, m_im = mask_spec[:, :width], mask_spec[:, width:2 * width]
        m_same, m_cross = mask_spec[:, 2 * width:3 * width], mask_spec[:, 3 * width:]

        def cols_of(p):
            planes = []
            for j in range(2):
                k = i * batch + 2 * p + j
                s_re, s_im, s_rest = spec[k, :, :width], spec[k, :, width:2 * width], spec[k, :, 2 * width:]
                product = jnp.concatenate([
                    s_re * m_re - s_im * m_im,
                    s_re * m_im + s_im * m_re,
                    s_rest * m_same + swap(s_rest) * m_cross,
                ], axis=1)
                back = over_lanes(split(product), col_inv)
                planes.append(split(back))
            return [side_by_side(planes, c, width) for c in range(4)]

        def rows_of(p, pair):
            upper, lower = from_row_freqs(pair, row_inv, (0, 1))
            re = jnp.concatenate([upper[0], lower[0]], axis=0)
            im = jnp.concatenate([upper[1], lower[1]], axis=0)
            field[i * (batch // 2) + p, :count] = re
            field[i * (batch // 2) + p, count:] = im
            power = re * re + im * im
            for j in range(2):
                k = i * batch + 2 * p + j
                g = group[k]
                slopes[g] = slopes[g] + weight[k] * power[:, j * width:(j + 1) * width]

        staggered(batch // 2, cols_of, rows_of)
        return carry

    lax.fori_loop(0, steps, forward, 0)

    wanted = target[...].astype(f32)
    for g in range(GROUPS):
        seen = jax.nn.sigmoid(STEEPNESS * (slopes[g] - THRESHOLD))
        resist[g] = seen
        slopes[g] = 2.0 * (seen - wanted) * seen * (1.0 - seen) * STEEPNESS
    out = pltpu.make_async_copy(resist, resist_far, out_sem)
    out.start()

    def backward(i, carry):
        def rows_of(p):
            factors = []
            for j in range(2):
                k = i * batch + 2 * p + j
                factors.append((2.0 * weight[k]) * slopes[group[k]])
            factor = jnp.concatenate(factors, axis=1)
            re = field[i * (batch // 2) + p, :count] * factor
            im = field[i * (batch // 2) + p, count:] * factor
            return row_stage(quarters_of(re, im, rim), row_fwd, width)

        def cols_of(p, tiles):
            total = [grad_spec[:, c * width:(c + 1) * width] for c in range(4)]
            for j in range(2):
                k = i * batch + 2 * p + j
                s_re, s_im, s_rest = spec[k, :, :width], spec[k, :, width:2 * width], spec[k, :, 2 * width:]
                first, rest = to_freqs(tiles[j], head, tail)
                c_re, c_im = first[:, :width], first[:, width:]
                total[0] = total[0] + (s_re * c_re + s_im * c_im)
                total[1] = total[1] + (s_re * c_im - s_im * c_re)
                total[2] = total[2] + s_rest * rest
                total[3] = total[3] + s_rest * swap(rest)
            for c in range(4):
                grad_spec[:, c * width:(c + 1) * width] = total[c]

        staggered(batch // 2, rows_of, cols_of)
        return carry

    lax.fori_loop(0, steps, backward, 0)

    same, cross = grad_spec[:, 2 * width:3 * width], grad_spec[:, 3 * width:]
    tail_sum = jnp.where(real_half, same + swap(same), swap(cross) - cross)
    total = jnp.concatenate([grad_spec[:, :2 * width], tail_sum], axis=1)
    back = split(over_lanes(split(total), table("grad_col")))
    classes = [side_by_side([back], c, width) for c in range(4)]
    rise, upper, lower, fall = from_row_freqs(classes, row_inv, (2, 3, 0, 1))
    for c in range(2):
        near_rim[c] = jnp.where(odd, rise[c], fall[c])
        far_rim[c] = jnp.where(odd, fall[c], rise[c])
        grad_own[c, :rim] = upper[c]
        grad_own[c, rim:] = lower[c]
    out.wait()


def join_body(place, own, near, far, out):
    odd = place[0] % 2 == 1
    rim = near.shape[1]
    count = own.shape[1]
    for c in range(2):
        out[c, :rim] = own[c, :rim] + jnp.where(odd, near[c], far[c])
        if count > 2 * rim:
            out[c, rim:count - rim] = own[c, rim:count - rim]
        out[c, count - rim:] = own[c, count - rim:] + jnp.where(odd, far[c], near[c])


def stacked(groups):
    blocks, layout, sections, at = [], {}, [], 0
    for group in groups:
        start = at
        for name, table in group.items():
            rows, lanes = table.shape
            layout[name] = (at, rows, lanes // 256)
            for b in range(lanes // 256):
                blocks.append(table[:, b * 256:(b + 1) * 256])
            at += rows * (lanes // 256)
        sections.append((start, at - start))
    return np.concatenate(blocks, axis=0), layout, sections


def on_device(mask_field, target, kernel_taps, kernel_radii, kernel_group, kernel_weight):
    _, count, width = mask_field.shape
    kernels, _, span, _ = kernel_taps.shape
    rim = span // 2
    grid_rows = count + 2 * rim
    grid_cols = width + rim
    assert count == span and width == span and kernels % BATCH == 0 and (kernels - EARLY) % LATE_BATCH == 0 and count == 2 * rim

    strips = lax.axis_size("row")
    assert strips % 2 == 0
    at = lax.axis_index("row")
    near_pairs = [(i, i ^ 1) for i in range(strips)]
    far_pairs = [(i, ((i + 1) ^ 1) - 1) for i in range(1, strips - 1)]
    near = lax.ppermute(mask_field, "row", near_pairs)
    far = lax.ppermute(mask_field, "row", far_pairs)
    place = at.astype(jnp.int32).reshape(1)

    scale = 1.0 / (grid_rows * grid_cols)
    order = grouped(grid_cols, width)

    def head_and_tail(shift):
        table = analysis(grid_cols, width, shift).T[:, order]
        return halves(table[:, :2 * width], 0), halves(table[:, 2 * width:], 1)

    quarter = grid_rows // 4
    by_class = [class_table(grid_rows, quarter, c) for c in range(4)]
    row_fwd = np.concatenate([halves(t, 0) for t in by_class], axis=1)
    row_inv = np.concatenate([halves(t.T * scale, 0) for t in by_class], axis=1)
    head, tail = head_and_tail(0)
    mask_head, mask_tail = head_and_tail(rim)
    col_inv = halves(synthesis(grid_cols, width, 0).T[order], 0)
    grad_col = halves(synthesis(grid_cols, width, rim).T[order], 0)

    smem = pl.BlockSpec(memory_space=pltpu.SMEM)
    vmem = pl.BlockSpec(memory_space=pltpu.VMEM)
    hbm = pl.BlockSpec(memory_space=pltpu.HBM)
    spectra = pl.pallas_call(
        spectra_body,
        out_shape=jax.ShapeDtypeStruct((EARLY, grid_rows, 2 * grid_cols), f32),
        grid=(1,),
        in_specs=[smem, pl.BlockSpec((EARLY, 2, span, span), lambda i: (0, 0, 0, 0)), vmem, vmem, vmem],
        out_specs=pl.BlockSpec((EARLY, grid_rows, 2 * grid_cols), lambda i: (0, 0, 0)),
        compiler_params=pltpu.CompilerParams(vmem_limit_bytes=56 * MIB),
        cost_estimate=pl.CostEstimate(flops=3 * 10**9, bytes_accessed=3 * 10**6, transcendentals=0),
        name="spectra",
    )(kernel_radii, kernel_taps, *map(jnp.asarray, (row_fwd, head, tail)))

    tables, layout, sections = stacked([
        {"row_fwd": row_fwd, "head": head, "tail": tail},
        {"mask_head": mask_head, "mask_tail": mask_tail, "col_inv": col_inv, "row_inv": row_inv, "grad_col": grad_col},
    ])
    resist, own, near_rim, far_rim = pl.pallas_call(
        functools.partial(main_body, layout=layout, sections=sections),
        out_shape=[
            jax.ShapeDtypeStruct((GROUPS, count, width), f32),
            jax.ShapeDtypeStruct((2, count, width), f32),
            jax.ShapeDtypeStruct((2, rim, width), f32),
            jax.ShapeDtypeStruct((2, rim, width), f32),
        ],
        in_specs=[smem] * 4 + [vmem] * 4 + [hbm] * 3,
        out_specs=[hbm] + [vmem] * 3,
        scratch_shapes=[
            pltpu.VMEM((kernels, grid_rows, 2 * grid_cols), f32),
            pltpu.VMEM(kernel_taps.shape, f32),
            pltpu.VMEM((kernels // 2, 2 * count, 2 * width), f32),
            pltpu.VMEM((grid_rows, 4 * width), f32),
            pltpu.VMEM((GROUPS, count, width), f32),
            pltpu.VMEM((GROUPS, count, width), f32),
            pltpu.VMEM((grid_rows, 4 * width), f32),
            pltpu.VMEM(tables.shape, bf16),
            pltpu.SemaphoreType.DMA,
            pltpu.SemaphoreType.DMA(((kernels - EARLY) // LATE_BATCH,)),
            pltpu.SemaphoreType.DMA((len(sections),)),
            pltpu.SemaphoreType.DMA,
        ],
        compiler_params=pltpu.CompilerParams(vmem_limit_bytes=LIMIT * MIB),
        name="fields",
    )(kernel_group, kernel_weight, place, kernel_radii, mask_field, near, far, target, kernel_taps, spectra, jnp.asarray(tables))

    far_in = lax.ppermute(far_rim, "row", far_pairs)
    near_in = lax.ppermute(near_rim, "row", near_pairs)
    gradient = pl.pallas_call(
        join_body,
        out_shape=jax.ShapeDtypeStruct((2, count, width), f32),
        in_specs=[smem] + [vmem] * 3,
        out_specs=vmem,
        compiler_params=pltpu.CompilerParams(vmem_limit_bytes=4 * MIB),
        name="join",
    )(place, own, near_in, far_in)
    return resist, gradient


def solution(mesh):
    in_specs = (P(None, ("win", "row"), None), P(("win", "row"), None), P(), P(), P(), P())
    out_specs = (P(None, ("win", "row"), None), P(None, ("win", "row"), None))
    return jax.shard_map(
        on_device, mesh=mesh, in_specs=in_specs, out_specs=out_specs, check_vma=False
    )
```
